32 devices in a mesh: dp: 8 (over y, x, core), tensor: 4 (over z).
Axes of the slice: x: 2, y: 2, z: 4, core: 2. Of those that a mesh axis runs over, the one named last changes fastest.
Arguments:
- tokens: bfloat16 [8192, 2048], P(('dp', 'tensor')), may hold values from -6 to 6
- cotangent: bfloat16 [8192, 2048], P(('dp', 'tensor')), may hold values from -6 to 6
- segments: int32 [8, 1024], P('dp'), may hold values from 0 to 3, never falling along the last dimension, each value on 1 to 512 neighbouring positions
- w_qkv: float32 [2048, 6144], P('dp', 'tensor'), may hold values from -0.125 to 0.125
- w_out: float32 [2048, 2048], P('dp', 'tensor'), may hold values from -0.5 to 0.5
- w_up: float32 [2048, 8192], P('dp', 'tensor'), may hold values from -0.125 to 0.125
- w_down: float32 [2048, 8192], P('dp', 'tensor'), may hold values from -0.0625 to 0.0625
- m_qkv: float32 [2048, 6144], P('dp', 'tensor'), may hold values from -112 to 112
- m_out: float32 [2048, 2048], P('dp', 'tensor'), may hold values from -160 to 160
- m_up: float32 [2048, 8192], P('dp', 'tensor'), may hold values from -128 to 128
- m_down: float32 [2048, 8192], P('dp', 'tensor'), may hold values from -320 to 320
- norm_gains: float32 [2, 2048], replicated, may hold values from 0.5 to 1.5
- norm_biases: float32 [2, 2048], replicated, may hold values from -1 to 1
- norm_moments: float32 [4, 2048], replicated, may hold values from -256 to 256
Outputs:
- block_out: bfloat16 [8192, 2048], P(('dp', 'tensor'))
- grad_tokens: float32 [8192, 2048], P(('dp', 'tensor'))
- new_m_qkv: float32 [2048, 6144], P('dp', 'tensor')
- new_w_qkv: float32 [2048, 6144], P('dp', 'tensor')
- new_m_out: float32 [2048, 2048], P('dp', 'tensor')
- new_w_out: float32 [2048, 2048], P('dp', 'tensor')
- new_m_up: float32 [2048, 8192], P('dp', 'tensor')
- new_w_up: float32 [2048, 8192], P('dp', 'tensor')
- new_m_down: float32 [2048, 8192], P('dp', 'tensor')
- new_w_down: float32 [2048, 8192], P('dp', 'tensor')
- new_norm_moments: float32 [4, 2048], replicated
- new_norm_values: float32 [4, 2048], replicated
The draws below stay inside these ranges and needn't reach their ends.
Inputs may be any that keep to these rules, and one draw needn't show every extreme that they name: `segments`: within each row the numbers never fall; a document is a run of equal numbers, of at most 512 tokens.
All inputs are finite; a program needn't handle non-finite values.
Results may differ from the reference program's by a relative error of at most 0.023.
Values may be sent and summed in bfloat16 or wider, within the bound.
A program may use at most 256 MiB of HBM per device.

```python
import math
import jax
import jax.numpy as jnp
import numpy as np
from jax import lax

D = 2048
HEADS = 8
HD = 256
FF = 8192
ROT = 64
SEQ_LEN = 1024
TOKENS = 8192
DOCS = 4
DOC_MOST = 512
N_DP = 8


def shard_levels(stream_key, extent, split, least, top_value):
    loudness, own = 1.0, jax.random.fold_in(stream_key, 6)
    for dim, blocks in split:
        draws = jnp.exp(jax.random.uniform(jax.random.fold_in(own, dim), (blocks,), jnp.float32, least / len(split), top_value / len(split)))
        loudness = loudness * jnp.repeat(draws, extent[dim] // blocks).reshape([-1 if axis == dim else 1 for axis in range(len(extent))])
    return loudness


def profile(amount, total, limit, lean):
    weights = [(1 << 20) // math.isqrt(grade ** lean) + 1 for grade in range(2, amount + 1)]
    rest, given = total - limit - (amount - 1), [1] * (amount - 1)
    while rest > 0:
        movable = [i for i in range(amount - 1) if given[i] < limit]
        mass, left = sum([weights[i] for i in movable]), rest
        for i in movable:
            extra = min(limit - given[i], max(1, left * weights[i] // mass), rest)
            given[i] = given[i] + extra
            rest = rest - extra
    return np.array([limit] + given)


def uneven(rng, count, total, most, skew):
    if count == 2:
        one = jax.random.randint(rng, (), max(1, total - most), min(most, total - 1) + 1)
        return jnp.stack([one, total - one])
    tallies = jnp.asarray(profile(count, total, most, skew), jnp.int32)
    twos = (count - 1) // 2
    giver, taker = tallies[1:1 + 2 * twos:2], tallies[2:2 + 2 * twos:2]
    slack = jnp.minimum(giver - 1, most - taker)
    shifted = jax.random.randint(jax.random.fold_in(rng, 1), (twos,), 0, 1 << 20) % (slack + 1)
    tallies = tallies.at[1:1 + 2 * twos:2].set(giver - shifted).at[2:2 + 2 * twos:2].set(taker + shifted)
    return tallies[jax.random.permutation(jax.random.fold_in(rng, 2), count)]


def gaussian(key, dims, deviation, bound, cuts=(), held_as=jnp.bfloat16):
    values = deviation * jax.random.normal(key, dims, jnp.float32)
    if cuts:
        values = values * shard_levels(key, dims, cuts, -0.22, 0.18)
    return jnp.clip(values, -bound, bound).astype(held_as)


def setup_inputs(seed: int = 0) -> dict:
    seeds = jax.random.split(jax.random.key(seed), 15)
    return {
        "tokens": gaussian(seeds[0], (TOKENS, D), 1.0, 6.0, ((0, 32),)),
        "cotangent": gaussian(seeds[1], (TOKENS, D), 1.0, 6.0, ((0, 32),)),
        "segments": jax.vmap(lambda own: jnp.searchsorted(jnp.cumsum(uneven(own, DOCS, SEQ_LEN, DOC_MOST, 2)), jnp.arange(SEQ_LEN), side="right"))(jax.random.split(seeds[2], N_DP)).reshape((N_DP, SEQ_LEN)).astype(jnp.int32),
        "w_qkv": gaussian(seeds[3], (D, 3 * D), D ** -0.5, 0.125, ((0, 8), (1, 4)), jnp.float32),
        "w_out": gaussian(seeds[4], (D, D), (max(1, D // 16)) ** -0.5, 0.5, ((0, 8), (1, 4)), jnp.float32),
        "w_up": gaussian(seeds[5], (D, FF), D ** -0.5, 0.125, ((0, 8), (1, 4)), jnp.float32),
        "w_down": gaussian(seeds[6], (D, FF), FF ** -0.5, 0.0625, ((0, 8), (1, 4)), jnp.float32),
        "m_qkv": gaussian(seeds[7], (D, 3 * D), (0.2 * (SEQ_LEN * N_DP) ** 0.5), 112.0, ((0, 8), (1, 4)), jnp.float32),
        "m_out": gaussian(seeds[8], (D, D), (0.3 * (SEQ_LEN * N_DP) ** 0.5), 160.0, ((0, 8), (1, 4)), jnp.float32),
        "m_up": gaussian(seeds[9], (D, FF), (0.25 * (SEQ_LEN * N_DP) ** 0.5), 128.0, ((0, 8), (1, 4)), jnp.float32),
        "m_down": gaussian(seeds[10], (D, FF), (0.6 * (SEQ_LEN * N_DP) ** 0.5), 320.0, ((0, 8), (1, 4)), jnp.float32),
        "norm_gains": jnp.clip(1.0 + 0.1 * jax.random.normal(seeds[11], (2, D), jnp.float32), 0.5, 1.5),
        "norm_biases": gaussian(seeds[12], (2, D), 0.2, 1.0, (), jnp.float32),
        "norm_moments": gaussian(seeds[13], (4, D), (0.5 * (SEQ_LEN * N_DP) ** 0.5), 256.0, (), jnp.float32),
    }


@jax.custom_vjp
def low(v):
    return lax.optimization_barrier(v.astype(jnp.bfloat16)).astype(jnp.float32)

@jax.custom_vjp
def low_back(v):
    return v

def low_keep(v):
    return (low(v), None)

def low_pass(kept, grad):
    return (grad,)

def back_keep(v):
    return (v, None)

def back_low(kept, grad):
    return (low(grad),)
low.defvjp(low_keep, low_pass)
low_back.defvjp(back_keep, back_low)
NS_A = 3.4445
NS_B = -4.775
NS_C = 2.0315
MOMENTUM = 0.95
LEARN = 0.5
DECAY = 0.01
NORM_LEARN = 0.05
LN_EPS = 1e-05
MASKED = -1e+30
HIGH = lax.Precision.HIGHEST

def matmul(left, right):
    return jnp.dot(left, right, precision=HIGH, preferred_element_type=jnp.float32)

def layer_norm(hidden, gain_row, bias_row):
    row_mean = lax.optimization_barrier(jnp.mean(hidden, axis=-1, keepdims=True))
    centred = hidden - row_mean
    row_var = lax.optimization_barrier(jnp.mean(centred * centred, axis=-1, keepdims=True))
    return centred * lax.rsqrt(row_var + LN_EPS) * gain_row + bias_row

def doc_positions(seg_ids):
    position_idx = jnp.arange(seg_ids.shape[0], dtype=jnp.int32)
    change = jnp.concatenate([jnp.ones((1,), dtype=jnp.bool_), seg_ids[1:] != seg_ids[:-1]])
    doc_start = lax.cummax(jnp.where(change, position_idx, jnp.zeros_like(position_idx)), axis=0)
    return position_idx - doc_start

def rotary_tables(positions):
    half_rot = ROT // 2
    inv_freq = 10000.0 ** (-2.0 * jnp.arange(half_rot, dtype=jnp.float32) / ROT)
    angles = positions.astype(jnp.float32)[:, None, None] * inv_freq[None, None, :]
    return (jnp.cos(angles), jnp.sin(angles))

def rotate(heads, cosine, sine_tab):
    half_rot = ROT // 2
    first_half = heads[..., :half_rot]
    second_half = heads[..., half_rot:ROT]
    return jnp.concatenate([first_half * cosine - second_half * sine_tab, second_half * cosine + first_half * sine_tab, heads[..., ROT:]], axis=-1)

def forward(hidden, qkv_in, out_in, up_in, down_in, norm_in, seg_ids):
    length = hidden.shape[0]
    ln_attn = low(layer_norm(hidden, norm_in[0], norm_in[1]))
    ln_mlp = low(layer_norm(hidden, norm_in[2], norm_in[3]))
    packed = low_back(matmul(ln_attn, low(qkv_in))).reshape(length, HEADS, 3, HD)
    cosine, sine_tab = rotary_tables(doc_positions(seg_ids))
    queries = low(rotate(packed[:, :, 0], cosine, sine_tab))
    key_rows = low(rotate(packed[:, :, 1], cosine, sine_tab))
    value_rows = low(packed[:, :, 2])
    position_idx = jnp.arange(length, dtype=jnp.int32)
    allowed = (seg_ids[:, None] == seg_ids[None, :]) & (position_idx[None, :] <= position_idx[:, None])
    scores = jnp.einsum('qhd,khd->hqk', queries, key_rows, precision=HIGH) * HD ** (-0.5)
    scores = low_back(jnp.where(allowed[None], scores, MASKED))
    prob_rows = jax.nn.softmax(scores, axis=-1)
    mixed_heads = jnp.einsum('hqk,khd->qhd', low(prob_rows), value_rows, precision=HIGH)
    mixed_heads = low(low_back(mixed_heads)).reshape(length, D)
    attn_out = matmul(mixed_heads, low(out_in).T)
    up_proj = low_back(matmul(ln_mlp, low(up_in)))
    activated = low(jax.nn.gelu(up_proj, approximate=False))
    return hidden + attn_out + matmul(activated, low(down_in).T)

def orthogonalize(matrix):
    iterate = low(matrix / (jnp.sqrt(jnp.sum(matrix * matrix)) + 1e-07))
    for sweep_idx in range(5):
        gram_mat = low(matmul(iterate.T, iterate))
        poly_mat = low(NS_B * gram_mat + NS_C * matmul(gram_mat, gram_mat))
        iterate = low(NS_A * iterate + matmul(iterate, poly_mat))
    return iterate

def muon(weight, moment, gradient, block_cols):
    new_moment = MOMENTUM * moment + gradient
    nested = low(gradient + MOMENTUM * new_moment)
    stacked = nested.reshape(D, HEADS, block_cols).transpose(1, 0, 2)
    ortho = lax.map(orthogonalize, stacked).transpose(1, 0, 2).reshape(D, HEADS * block_cols)
    return (new_moment, weight * (1.0 - LEARN * DECAY) - LEARN * ortho)

def reference(tokens, cotangent, segments, w_qkv, w_out, w_up, w_down, m_qkv, m_out, m_up, m_down, norm_gains, norm_biases, norm_moments):
    norm_rows = jnp.stack([norm_gains[0], norm_biases[0], norm_gains[1], norm_biases[1]])
    hidden_all = tokens.astype(jnp.float32).reshape(N_DP, SEQ_LEN, D)
    grad_all = cotangent.astype(jnp.float32).reshape(N_DP, SEQ_LEN, D)
    params = (w_qkv, w_out, w_up, w_down, norm_rows)

    def one_sequence(running, inputs_row):
        hidden, grad_out, seg_ids = inputs_row

        def local_forward(hidden_in, qkv_in, out_in, up_in, down_in, norm_in):
            return forward(hidden_in, qkv_in, out_in, up_in, down_in, norm_in, seg_ids)
        result, pull_back = jax.vjp(local_forward, hidden, w_qkv, w_out, w_up, w_down, norm_rows)
        pulled = pull_back(grad_out)
        running = tuple((acc_grad + new_grad for acc_grad, new_grad in zip(running, pulled[1:])))
        return (running, (result.astype(jnp.bfloat16), pulled[0]))
    zero_grads = tuple((jnp.zeros_like(param) for param in params))
    summed, (out_rows, grad_rows) = lax.scan(one_sequence, zero_grads, (hidden_all, grad_all, segments))
    grad_qkv, grad_attn, grad_upw, grad_downw, grad_norms = summed
    new_m_qkv, new_w_qkv = muon(w_qkv, m_qkv, grad_qkv, 3 * HD)
    new_m_out, new_w_out = muon(w_out, m_out, grad_attn, HD)
    new_m_up, new_w_up = muon(w_up, m_up, grad_upw, FF // HEADS)
    new_m_down, new_w_down = muon(w_down, m_down, grad_downw, FF // HEADS)
    moment_norms = MOMENTUM * norm_moments + grad_norms
    step_scale = lax.rsqrt(lax.optimization_barrier(jnp.mean(moment_norms * moment_norms, axis=-1, keepdims=True)) + 1e-06)
    value_norms = norm_rows - NORM_LEARN * moment_norms * step_scale
    return (out_rows.reshape(TOKENS, D), grad_rows.reshape(TOKENS, D), new_m_qkv, new_w_qkv, new_m_out, new_w_out, new_m_up, new_w_up, new_m_down, new_w_down, moment_norms, value_norms)
```

```python
import functools
from functools import partial

import jax
import jax.numpy as jnp
from jax import lax
from jax.experimental import pallas as pl
from jax.experimental.pallas import tpu as pltpu
from jax.sharding import PartitionSpec as P

HEADS = 8
HD = 256
FF = 8192
ROT = 64


NS_A = 3.4445
NS_B = -4.775
NS_C = 2.0315
MOMENTUM = 0.95
LEARN = 0.5
DECAY = 0.01
NORM_LEARN = 0.05
LN_EPS = 1e-05
MASKED = -1e30


def doc_positions(seg_ids):
    position_idx = jnp.arange(seg_ids.shape[0], dtype=jnp.int32)
    change = jnp.concatenate([jnp.ones((1,), dtype=jnp.bool_), seg_ids[1:] != seg_ids[:-1]])
    doc_start = lax.cummax(jnp.where(change, position_idx, jnp.zeros_like(position_idx)), axis=0)
    return position_idx - doc_start


def rotary_tables(positions):
    half_rot = ROT // 2
    inv_freq = 10000.0 ** (-2.0 * jnp.arange(half_rot, dtype=jnp.float32) / ROT)
    angles = positions.astype(jnp.float32)[:, None, None] * inv_freq[None, None, :]
    return (jnp.cos(angles), jnp.sin(angles))


def rotate(heads, cosine, sine_tab):
    half_rot = ROT // 2
    first_half = heads[..., :half_rot]
    second_half = heads[..., half_rot:ROT]
    return jnp.concatenate(
        [
            first_half * cosine - second_half * sine_tab,
            second_half * cosine + first_half * sine_tab,
            heads[..., ROT:],
        ],
        axis=-1,
    )


def rotate_back(grads_in, cosine, sine_tab):
    half_rot = ROT // 2
    first_half = grads_in[..., :half_rot]
    second_half = grads_in[..., half_rot:ROT]
    return jnp.concatenate(
        [
            first_half * cosine + second_half * sine_tab,
            second_half * cosine - first_half * sine_tab,
            grads_in[..., ROT:],
        ],
        axis=-1,
    )


def contract_rows(left, right):
    return lax.dot_general(
        left, right, (((0,), (0,)), ((), ())), preferred_element_type=jnp.float32
    )


def contract_cols(left, right):
    return lax.dot_general(
        left, right, (((1,), (1,)), ((), ())), preferred_element_type=jnp.float32
    )


def block_scores(query_block, key_rows, seg_ids, position_idx, offset, block_rows, score_scale):
    seg_block = seg_ids[offset : offset + block_rows]
    allowed = (seg_block[:, None] == seg_ids[None, :]) & (
        position_idx[None, :] <= position_idx[offset : offset + block_rows, None]
    )
    raw_scores = (
        jnp.einsum("qhd,khd->hqk", query_block, key_rows, preferred_element_type=jnp.float32)
        * score_scale
    )
    return jnp.where(allowed[None], raw_scores, MASKED)


MESH = pl.DeviceIdType.MESH

def gather_kernel(n_w, n_t, *refs):
    ins_w = refs[:n_w]; ins_t = refs[n_w:n_w+n_t]
    outs_w = refs[n_w+n_t:2*n_w+n_t]; outs_t = refs[2*n_w+n_t:2*(n_w+n_t)]
    w_send, w_recv, t_send, t_recv, own_sem = refs[2*(n_w+n_t):]
    size = lax.axis_size("tensor")
    dp = lax.axis_index("dp"); me = lax.axis_index("tensor")
    y, x, c = dp // 4, (dp // 2) % 2, dp % 2
    by_x = y * 4 + (1 - x) * 2 + c
    by_y = (1 - y) * 4 + x * 2 + c
    far = (1 - y) * 4 + (1 - x) * 2 + c
    by_c = y * 4 + x * 2 + (1 - c)
    barrier = pltpu.get_barrier_semaphore()
    for peer in (by_x, by_y, by_c):
        pl.semaphore_signal(barrier, inc=1, device_id=(peer, me), device_id_type=MESH)
    for s in range(1, size):
        pl.semaphore_signal(barrier, inc=1, device_id=(dp, lax.rem(me + s, size)), device_id_type=MESH)
    pl.semaphore_wait(barrier, 3 + size - 1)

    def rows_of(ref, dev, low=0, high=1):
        rows = ref.shape[0] // 8
        return ref.at[pl.ds(pl.multiple_of(dev * rows + low, 128), high)]

    def send(i, k, src, dst, peer):
        return pltpu.make_async_remote_copy(src_ref=src, dst_ref=dst, send_sem=w_send.at[i, k], recv_sem=w_recv.at[i, k], device_id=(peer, me), device_id_type=MESH)

    def part(i, dev, low, count):
        rows = outs_w[i].shape[0] // 8
        return outs_w[i].at[pl.ds(pl.multiple_of(dev * rows + low, 128), count)]

    def copy(i, k):
        rows = outs_w[i].shape[0] // 8
        half = rows // 2
        if k < 3:
            return send(i, k, ins_w[i], part(i, dp, 0, rows), (by_x, by_y, by_c)[k])
        dev, low, count, peer = {3: (by_y, 0, half, by_x), 4: (by_x, half, half, by_y), 5: (by_x, 0, rows, by_c), 6: (by_y, 0, rows, by_c), 7: (far, 0, half, by_c), 8: (far, half, half, by_c)}[k]
        src = part(i, dev, low, count)
        return send(i, k, src, src, peer)

    def token_copy(i, s):
        rows = ins_t[i].shape[0]
        dst = outs_t[i].at[pl.ds(pl.multiple_of(me * rows, 128), rows)]
        return pltpu.make_async_remote_copy(src_ref=ins_t[i], dst_ref=dst, send_sem=t_send.at[i, s], recv_sem=t_recv.at[i, s], device_id=(dp, lax.rem(me + s, size)), device_id_type=MESH)

    if n_t:
        for s in range(1, size):
            token_copy(0, s).start()
    for i in range(min(2, n_w)):
        for k in range(3):
            copy(i, k).start()
    def second():
        for s in range(1, size):
            token_copy(0, s).wait_send()
        for j in range(1, n_t):
            for s in range(1, size):
                token_copy(j, s).start()

    own = [pltpu.make_async_copy(ins_w[i], part(i, dp, 0, outs_w[i].shape[0] // 8), own_sem.at[i]) for i in range(n_w)]
    for i in range(n_t):
        rows = ins_t[i].shape[0]
        own.append(pltpu.make_async_copy(ins_t[i], outs_t[i].at[pl.ds(pl.multiple_of(me * rows, 128), rows)], own_sem.at[n_w + i]))
    for o in own:
        o.start()
    for i in range(n_w):
        copy(i, 0).wait_recv()
        copy(i, 5).start()
        copy(i, 4).start()
        copy(i, 1).wait_recv()
        copy(i, 6).start()
        copy(i, 3).start()
        if i + 2 < n_w:
            for k in range(3):
                copy(i + 2, k).start()
        if i >= 1:
            for k in (3, 4):
                copy(i - 1, k).wait_recv()
                copy(i - 1, k + 4).start()
        if i == 1 and n_t:
            second()
    if n_w < 2 and n_t:
        second()
    for k in (3, 4) if n_w else ():
        copy(n_w - 1, k).wait_recv()
        copy(n_w - 1, k + 4).start()
    for i in range(n_w):
        for k in range(9):
            copy(i, k).wait_send()
        for k in (2, 5, 6, 7, 8):
            copy(i, k).wait_recv()
    for o in own:
        o.wait()
    for j in range(n_t):
        for s in range(1, size):
            if j > 0:
                token_copy(j, s).wait_send()
            token_copy(j, s).wait_recv()

def gather_all(shards, tokens):
    n_w, n_t = len(shards), len(tokens)
    size = lax.axis_size("tensor")
    shapes = [jax.ShapeDtypeStruct((s.shape[0] * 8, s.shape[1]), s.dtype) for s in shards]
    shapes += [jax.ShapeDtypeStruct((s.shape[0] * size, s.shape[1]), s.dtype) for s in tokens]
    anyspec = pl.BlockSpec(memory_space=pl.ANY)
    return pl.pallas_call(
        functools.partial(gather_kernel, n_w, n_t),
        out_shape=shapes,
        in_specs=[anyspec] * (n_w + n_t),
        out_specs=[anyspec] * (n_w + n_t),
        scratch_shapes=[pltpu.SemaphoreType.DMA((max(1,n_w), 9)), pltpu.SemaphoreType.DMA((max(1,n_w), 9)), pltpu.SemaphoreType.DMA((max(1,n_t), size)), pltpu.SemaphoreType.DMA((max(1,n_t), size)), pltpu.SemaphoreType.DMA((n_w + n_t,))],
        compiler_params=pltpu.CompilerParams(collective_id=0, has_side_effects=True),
        name="gather_all",
    )(*shards, *tokens)


def owner_tables():
    return ((2, 0), (1, 0), (2, 1), (1, 1), (3, 0), (0, 0), (3, 1), (0, 1))


CHUNK = 512


def reduce_kernel(plan, lhs_of, widths, *refs):
    n_chunks = len(plan)
    lhs_refs = refs[0:3]
    rhs_refs = refs[3:7]
    mom_refs = refs[7:11]
    newm_refs = refs[11:15]
    xin_ref = refs[15]
    (lhs, rhs, sib_send, own, sib_recv, far_x, far_y, in_x, in_y, far_send, x_send, y_send, mom, newm, e_send,
     lhs_sem, rhs_sem, mom_sem, newm_sem, sib_ss, sib_rs, fx_ss, fx_rs, fy_ss, fy_rs, x_ss, x_rs, y_ss, y_rs,
     e_ss, e_rs, e_own) = refs[16:]
    dp = lax.axis_index("dp")
    t = lax.axis_index("tensor")
    y, x, c = dp // 4, (dp // 2) % 2, dp % 2
    rows = xin_ref.shape[0] // 8
    half = rows // 2
    by_x = y * 4 + (1 - x) * 2 + c
    by_y = (1 - y) * 4 + x * 2 + c
    far = (1 - y) * 4 + (1 - x) * 2 + c
    by_c = y * 4 + x * 2 + (1 - c)
    barrier = pltpu.get_barrier_semaphore()
    for shift in range(1, 8):
        pl.semaphore_signal(barrier, inc=1, device_id=(lax.rem(dp + shift, 8), t), device_id_type=MESH)
    pl.semaphore_wait(barrier, 7)

    def sibling(dev):
        return dev + 1 - 2 * (dev % 2)

    def remote(src, dst, ss, rs, peer):
        return pltpu.make_async_remote_copy(src_ref=src, dst_ref=dst, send_sem=ss, recv_sem=rs, device_id=(peer, t), device_id_type=MESH)

    order = []
    for m, cidx in plan:
        order.append((m, cidx))

    def select(k, values):
        out = jnp.int32(values[0])
        for i in range(1, n_chunks):
            if values[i] != values[i - 1]:
                out = jnp.where(k >= i, jnp.int32(values[i]), out)
        return out

    def matrix_of(k):
        return select(k, [m for m, _ in order])

    def column_of(k):
        return select(k, [cidx for _, cidx in order]) * CHUNK

    def per_matrix(k, fn):
        mk = matrix_of(k)
        for m in range(4):
            @pl.when(mk == m)
            def _():
                fn(m, pl.ds(pl.multiple_of(column_of(k), CHUNK), CHUNK))

    def rhs_copy(m, cols, slot):
        return pltpu.make_async_copy(rhs_refs[m].at[:, cols], rhs.at[slot], rhs_sem.at[slot])

    def mom_copy(m, cols, slot):
        return pltpu.make_async_copy(mom_refs[m].at[:, cols], mom.at[slot], mom_sem.at[slot])

    def newm_copy(m, cols, slot):
        return pltpu.make_async_copy(newm.at[slot], newm_refs[m].at[:, cols], newm_sem.at[slot])

    def sib_copy(k):
        return remote(sib_send.at[k % 2], sib_recv.at[k], sib_ss.at[k % 2], sib_rs.at[k], by_c)

    def far_copy_x(k):
        return remote(far_send.at[k % 2, pl.ds(0, half)], far_x.at[k], fx_ss.at[k % 2], fx_rs.at[k], by_x)

    def far_copy_y(k):
        return remote(far_send.at[k % 2, pl.ds(half, half)], far_y.at[k], fy_ss.at[k % 2], fy_rs.at[k], by_y)

    def copy_x(k):
        return remote(x_send.at[k % 2], in_x.at[k], x_ss.at[k % 2], x_rs.at[k], by_x)

    def copy_y(k):
        return remote(y_send.at[k % 2], in_y.at[k], y_ss.at[k % 2], y_rs.at[k], by_y)

    lhs_copies = [pltpu.make_async_copy(lhs_refs[i], lhs.at[i], lhs_sem.at[i]) for i in range(3)]
    for cp in lhs_copies:
        cp.start()
    per_matrix(jnp.int32(0), lambda m, cols: rhs_copy(m, cols, 0).start())
    per_matrix(jnp.int32(0), lambda m, cols: mom_copy(m, cols, 0).start())
    for cp in lhs_copies:
        cp.wait()

    def unit_owner(k, u):
        vals_o, vals_c = [], []
        for m, cidx in order:
            unit = cidx * (CHUNK // 256) + u
            per_block = widths[m] // 256
            head = unit // per_block
            vals_o.append(owner_tables().index((m, head)))
            vals_c.append((unit % per_block) * 256)
        return select(k, vals_o), select(k, vals_c)

    def e_copy(k, u):
        owner, col = unit_owner(k, u)
        dst = xin_ref.at[pl.ds(pl.multiple_of(dp * rows, 256), rows), pl.ds(pl.multiple_of(col, 256), 256)]
        src = e_send.at[k % 2, :, pl.ds(u * 256, 256)]
        return owner, remote(src, dst, e_ss.at[k % 2, u], e_rs, owner), pltpu.make_async_copy(src, dst, e_own.at[k % 2, u])

    def e_start(k, u):
        owner, far_cp, own_cp = e_copy(k, u)

        @pl.when(owner != dp)
        def _():
            far_cp.start()

        @pl.when(owner == dp)
        def _():
            own_cp.start()

    def e_wait(k, u):
        owner, far_cp, own_cp = e_copy(k, u)

        @pl.when(owner != dp)
        def _():
            far_cp.wait_send()

        @pl.when(owner == dp)
        def _():
            own_cp.wait()

    def wide(v):
        return v.astype(jnp.float32)

    def low(v):
        return v.astype(jnp.bfloat16)

    def step(i, carry):
        k1 = i
        k2 = i - 1
        k3 = i - 2
        k4 = i - 3

        @pl.when(k1 < n_chunks)
        def _():
            @pl.when(k1 + 1 < n_chunks)
            def _():
                per_matrix(k1 + 1, lambda m, cols: rhs_copy(m, cols, (k1 + 1) % 2).start())

            rhs_copy(0, pl.ds(0, CHUNK), k1 % 2).wait()

            @pl.when(k1 >= 2)
            def _():
                sib_copy(k1 - 2).wait_send()

            which = select(k1, [lhs_of[m] for m, _ in order])
            right = rhs[k1 % 2]

            def piece(q, carry2):
                px = x + (q % 2) * (1 - 2 * x)
                py = y + (q // 2) * (1 - 2 * y)
                base = py * 4 + px * 2
                left = lhs[which, :, pl.ds(pl.multiple_of((base + 1 - c) * rows, 256), rows)]
                sib_send[k1 % 2, q] = low(lax.dot_general(left, right, (((0,), (0,)), ((), ())), preferred_element_type=jnp.float32))
                left = lhs[which, :, pl.ds(pl.multiple_of((base + c) * rows, 256), rows)]
                own[k1 % 4, q] = lax.dot_general(left, right, (((0,), (0,)), ((), ())), preferred_element_type=jnp.float32)
                return carry2

            lax.fori_loop(0, 4, piece, 0)
            sib_copy(k1).start()

        @pl.when((k2 >= 0) & (k2 < n_chunks))
        def _():
            @pl.when(k2 >= 2)
            def _():
                far_copy_x(k2 - 2).wait_send()
                far_copy_y(k2 - 2).wait_send()

            sib_copy(k2).wait_recv()
            far_send[k2 % 2] = low(own[k2 % 4, 3] + wide(sib_recv[k2, 3]))
            far_copy_x(k2).start()
            far_copy_y(k2).start()
            for q in range(3):
                own[k2 % 4, q] = own[k2 % 4, q] + wide(sib_recv[k2, q])

        @pl.when((k3 >= 0) & (k3 < n_chunks))
        def _():
            @pl.when(k3 >= 2)
            def _():
                copy_x(k3 - 2).wait_send()
                copy_y(k3 - 2).wait_send()

            far_copy_x(k3).wait_recv()
            y_send[k3 % 2, pl.ds(0, half)] = low(own[k3 % 4, 2, pl.ds(0, half)] + wide(far_x[k3]))
            y_send[k3 % 2, pl.ds(half, half)] = low(own[k3 % 4, 2, pl.ds(half, half)])
            copy_y(k3).start()
            far_copy_y(k3).wait_recv()
            x_send[k3 % 2, pl.ds(0, half)] = low(own[k3 % 4, 1, pl.ds(0, half)])
            x_send[k3 % 2, pl.ds(half, half)] = low(own[k3 % 4, 1, pl.ds(half, half)] + wide(far_y[k3]))
            copy_x(k3).start()

        @pl.when(k4 >= 0)
        def _():
            @pl.when(k4 + 1 < n_chunks)
            def _():
                per_matrix(k4 + 1, lambda m, cols: mom_copy(m, cols, (k4 + 1) % 2).start())

            mom_copy(0, pl.ds(0, CHUNK), k4 % 2).wait()

            @pl.when(k4 >= 2)
            def _():
                newm_copy(0, pl.ds(0, CHUNK), k4 % 2).wait()
                e_wait(k4 - 2, 0)
                e_wait(k4 - 2, 1)

            copy_x(k4).wait_recv()
            copy_y(k4).wait_recv()
            grad = own[k4 % 4, 0] + wide(in_x[k4]) + wide(in_y[k4])
            fresh = MOMENTUM * mom[k4 % 2] + grad
            newm[k4 % 2] = fresh
            e_send[k4 % 2] = low(grad + MOMENTUM * fresh)
            per_matrix(k4, lambda m, cols: newm_copy(m, cols, k4 % 2).start())
            e_start(k4, 0)
            e_start(k4, 1)

        return carry

    lax.fori_loop(0, n_chunks + 3, step, 0)
    for k in (n_chunks - 2, n_chunks - 1):
        sib_copy(k).wait_send()
        far_copy_x(k).wait_send()
        far_copy_y(k).wait_send()
        copy_x(k).wait_send()
        copy_y(k).wait_send()
        newm_copy(0, pl.ds(0, CHUNK), k % 2).wait()
        for u in range(2):
            e_wait(jnp.int32(k), u)
    for dev, (m, head) in enumerate(owner_tables()):
        @pl.when(dp == dev)
        def _():
            seen = xin_ref.at[pl.ds(0, 7 * rows), pl.ds(0, widths[m])]
            pltpu.make_async_copy(seen, seen, e_rs).wait()


def reduce_all(lhs, rhs, moments, widths):
    rows = moments[0].shape[0]
    seq = lhs[0].shape[0]
    plan = [(3, 0), (3, 2), (3, 1), (3, 3), (2, 0), (2, 2), (2, 1), (2, 3), (1, 0), (0, 0), (0, 1), (0, 2)]
    n = len(plan)
    anyspec = pl.BlockSpec(memory_space=pl.ANY)
    bf, f32 = jnp.bfloat16, jnp.float32
    V, S = pltpu.VMEM, pltpu.SemaphoreType.DMA
    scratch = [
        V((3, seq, 8 * rows), bf), V((2, seq, CHUNK), bf), V((2, 4, rows, CHUNK), bf), V((4, 4, rows, CHUNK), f32),
        V((n, 4, rows, CHUNK), bf), V((n, rows // 2, CHUNK), bf), V((n, rows // 2, CHUNK), bf), V((n, rows, CHUNK), bf),
        V((n, rows, CHUNK), bf), V((2, rows, CHUNK), bf), V((2, rows, CHUNK), bf), V((2, rows, CHUNK), bf),
        V((2, rows, CHUNK), f32), V((2, rows, CHUNK), f32), V((2, rows, CHUNK), bf),
        S((3,)), S((2,)), S((2,)), S((2,)), S((2,)), S((n,)), S((2,)), S((n,)), S((2,)), S((n,)), S((2,)), S((n,)),
        S((2,)), S((n,)), S((2, 2)), S, S((2, 2)),
    ]
    out = pl.pallas_call(
        functools.partial(reduce_kernel, plan, (2, 0, 1, 0), widths),
        out_shape=[jax.ShapeDtypeStruct(m.shape, f32) for m in moments]
        + [jax.ShapeDtypeStruct((8 * rows, max(widths)), bf)],
        in_specs=[anyspec] * 11,
        out_specs=[anyspec] * 5,
        scratch_shapes=scratch,
        compiler_params=pltpu.CompilerParams(collective_id=1, has_side_effects=True, vmem_limit_bytes=60 * 2**20),
        name="reduce_all",
    )(*lhs, *rhs, *moments)
    return out[:4], out[4]


NT = (((1,), (1,)), ((), ()))
NN = (((1,), (0,)), ((), ()))


def wide_dot(left, right, dims):
    return lax.dot_general(left, right, dims, preferred_element_type=jnp.float32)


def sweep_kernel(width_ref, e_ref, o_ref, flipped, gram, poly):
    rows, cols = e_ref.shape
    tile, strip = 256, 512
    width = width_ref[0]
    inside = lax.broadcasted_iota(jnp.int32, (tile, cols), 1) < width

    def load(i):
        return jnp.where(inside, e_ref[pl.ds(pl.multiple_of(i * tile, tile), tile), :].astype(jnp.float32), 0.0)

    def squares(i, total):
        part = load(i)
        return total + jnp.sum((part * part).reshape(tile // 8, 8, cols), axis=0)

    total = jnp.sum(lax.fori_loop(0, rows // tile, squares, jnp.zeros((8, cols), jnp.float32)))
    scale = 1.0 / (jnp.sqrt(total) + 1e-07)
    for i in range(rows // tile):
        flipped[:, i * tile : (i + 1) * tile] = (load(i) * scale).T.astype(jnp.bfloat16)
    pairs = [(i, j) for i in range(cols // tile) for j in range(i, cols // tile)]

    def sweep(step, carry):
        for i, j in pairs:
            a, b = slice(i * tile, (i + 1) * tile), slice(j * tile, (j + 1) * tile)
            part = wide_dot(flipped[a, :], flipped[b, :], NT).astype(jnp.bfloat16)
            gram[a, b] = part
            if i != j:
                gram[b, a] = part.T
        for i, j in pairs:
            a, b = slice(i * tile, (i + 1) * tile), slice(j * tile, (j + 1) * tile)
            part = NS_B * gram[a, b].astype(jnp.float32) + NS_C * wide_dot(gram[a, :], gram[:, b], NN)
            part = part.astype(jnp.bfloat16)
            poly[a, b] = part
            if i != j:
                poly[b, a] = part.T

        def update(n, inner):
            part = pl.ds(pl.multiple_of(n * strip, strip), strip)
            old = flipped[:, part]
            for m in range(cols // strip):
                own = slice(m * strip, (m + 1) * strip)
                flipped[own, part] = (
                    NS_A * old[own].astype(jnp.float32) + wide_dot(poly[own, :], old, NN)
                ).astype(jnp.bfloat16)
            return inner

        lax.fori_loop(0, rows // strip, update, 0)
        return carry

    lax.fori_loop(0, 5, sweep, 0)
    for i in range(rows // tile):
        o_ref[i * tile : (i + 1) * tile, :] = flipped[:, i * tile : (i + 1) * tile].astype(jnp.float32).T.astype(jnp.bfloat16)


def sweeps(block, width):
    rows, cols = block.shape
    whole = pl.BlockSpec(memory_space=pltpu.VMEM)
    return pl.pallas_call(
        sweep_kernel,
        out_shape=jax.ShapeDtypeStruct((rows, cols), jnp.bfloat16),
        in_specs=[pl.BlockSpec(memory_space=pltpu.SMEM), whole],
        out_specs=whole,
        scratch_shapes=[
            pltpu.VMEM((cols, rows), jnp.bfloat16),
            pltpu.VMEM((cols, cols), jnp.bfloat16),
            pltpu.VMEM((cols, cols), jnp.bfloat16),
        ],
        compiler_params=pltpu.CompilerParams(vmem_limit_bytes=40 * 2**20),
        cost_estimate=pl.CostEstimate(flops=55 * 10**9, bytes_accessed=8 * 2**20, transcendentals=0),
        name="sweeps",
    )(width.reshape(1), block)


def on_device(
    tokens,
    cotangent,
    segments,
    w_qkv,
    w_out,
    w_up,
    w_down,
    m_qkv,
    m_out,
    m_up,
    m_down,
    norm_gains,
    norm_biases,
    norm_moments,
):
    tensor_size = lax.axis_size("tensor")
    seq_len = tokens.shape[0] * tensor_size
    seg_ids = segments[0]
    local_heads = w_out.shape[1] // HD
    block_units = FF // HEADS
    row_share = w_qkv.shape[0]
    hidden_own = tokens.astype(jnp.float32)
    tokens_all, grad_all = (
        lax.all_gather(tokens, "tensor", axis=0, tiled=True),
        lax.all_gather(cotangent, "tensor", axis=0, tiled=True),
    )
    hidden_all = tokens_all.astype(jnp.float32)
    mean_all = jnp.mean(hidden_all, axis=-1, keepdims=True)
    centred_all = hidden_all - mean_all
    rstd_all = lax.rsqrt(jnp.mean(centred_all * centred_all, axis=-1, keepdims=True) + LN_EPS)
    normed_all = centred_all * rstd_all
    ln_attn = (normed_all * norm_gains[0] + norm_biases[0]).astype(jnp.bfloat16)
    ln_mlp = (normed_all * norm_gains[1] + norm_biases[1]).astype(jnp.bfloat16)
    shards = tuple(w.astype(jnp.bfloat16) for w in (w_qkv, w_out, w_up, w_down))
    paired = lax.axis_size("dp") == 8 and local_heads == 2
    if paired:
        full_qkv, full_up, full_out, full_down = gather_all((shards[0], shards[2], shards[1], shards[3]), ())
    else:
        full_qkv, full_out, full_up, full_down = (
            lax.all_gather(w, "dp", axis=0, tiled=True) for w in shards
        )
    packed = jnp.dot(ln_attn, full_qkv, preferred_element_type=jnp.float32).reshape(
        seq_len, local_heads, 3, HD
    )
    cosine, sine_tab = rotary_tables(doc_positions(seg_ids))
    queries = rotate(packed[:, :, 0], cosine, sine_tab).astype(jnp.bfloat16)
    key_rows = rotate(packed[:, :, 1], cosine, sine_tab).astype(jnp.bfloat16)
    value_rows = packed[:, :, 2].astype(jnp.bfloat16)
    position_idx = jnp.arange(seq_len, dtype=jnp.int32)
    block_rows = min(512, seq_len)
    score_scale = HD ** (-0.5)
    mixed_parts = []
    lse_parts = []
    for offset in range(0, seq_len, block_rows):
        scores = block_scores(
            queries[offset : offset + block_rows],
            key_rows,
            seg_ids,
            position_idx,
            offset,
            block_rows,
            score_scale,
        )
        row_peak = jnp.max(scores, axis=-1, keepdims=True)
        expo_vals = jnp.exp(scores - row_peak)
        row_total = jnp.sum(expo_vals, axis=-1, keepdims=True)
        prob_rows = (expo_vals / row_total).astype(jnp.bfloat16)
        mixed_parts.append(
            jnp.einsum("hqk,khd->qhd", prob_rows, value_rows, preferred_element_type=jnp.float32)
        )
        lse_parts.append(row_peak + jnp.log(row_total))
    mixed_heads = (
        jnp.concatenate(mixed_parts, axis=0).reshape(seq_len, local_heads * HD).astype(jnp.bfloat16)
    )
    attn_out = contract_cols(mixed_heads, full_out)
    up_proj = jnp.dot(ln_mlp, full_up, preferred_element_type=jnp.float32)
    gelu_exact = partial(jax.nn.gelu, approximate=False)
    activated, gelu_pull = jax.vjp(gelu_exact, up_proj)
    activated = activated.astype(jnp.bfloat16)
    mlp_out = contract_cols(activated, full_down)
    branch_sum = lax.psum_scatter(
        (attn_out + mlp_out).astype(jnp.bfloat16), "tensor", scatter_dimension=0, tiled=True
    ).astype(jnp.float32)
    block_out = (hidden_own + branch_sum).astype(jnp.bfloat16)
    grad_act = jnp.dot(grad_all, full_down, preferred_element_type=jnp.float32)
    grad_upproj = gelu_pull(grad_act)[0].astype(jnp.bfloat16)
    grad_ln_mlp = contract_cols(grad_upproj, full_up)
    grad_mixed = (
        jnp.dot(grad_all, full_out, preferred_element_type=jnp.float32)
        .astype(jnp.bfloat16)
        .reshape(seq_len, local_heads, HD)
    )
    grad_keys = jnp.zeros((seq_len, local_heads, HD), jnp.float32)
    grad_values = jnp.zeros((seq_len, local_heads, HD), jnp.float32)
    query_grads = []
    for block_idx, offset in enumerate(range(0, seq_len, block_rows)):
        query_block = queries[offset : offset + block_rows]
        mixed_block = grad_mixed[offset : offset + block_rows]
        scores = block_scores(
            query_block, key_rows, seg_ids, position_idx, offset, block_rows, score_scale
        )
        prob_full = jnp.exp(scores - lse_parts[block_idx])
        grad_values = grad_values + jnp.einsum(
            "hqk,qhd->khd",
            prob_full.astype(jnp.bfloat16),
            mixed_block,
            preferred_element_type=jnp.float32,
        )
        grad_prob = jnp.einsum(
            "qhd,khd->hqk", mixed_block, value_rows, preferred_element_type=jnp.float32
        )
        row_delta = jnp.sum(prob_full * grad_prob, axis=-1, keepdims=True)
        grad_scores = (prob_full * (grad_prob - row_delta)).astype(jnp.bfloat16)
        query_grads.append(
            jnp.einsum("hqk,khd->qhd", grad_scores, key_rows, preferred_element_type=jnp.float32)
            * score_scale
        )
        grad_keys = (
            grad_keys
            + jnp.einsum(
                "hqk,qhd->khd", grad_scores, query_block, preferred_element_type=jnp.float32
            )
            * score_scale
        )
    grad_queries = rotate_back(jnp.concatenate(query_grads, axis=0), cosine, sine_tab)
    grad_keys = rotate_back(grad_keys, cosine, sine_tab)
    grad_packed = (
        jnp.stack([grad_queries, grad_keys, grad_values], axis=2)
        .reshape(seq_len, local_heads * 3 * HD)
        .astype(jnp.bfloat16)
    )
    grad_ln_attn = contract_cols(grad_packed, full_qkv)
    mixed_grad = norm_gains[0] * grad_ln_attn + norm_gains[1] * grad_ln_mlp
    mixed_own = lax.psum_scatter(
        mixed_grad.astype(jnp.bfloat16), "tensor", scatter_dimension=0, tiled=True
    ).astype(jnp.float32)
    mean_own = jnp.mean(hidden_own, axis=-1, keepdims=True)
    centred_own = hidden_own - mean_own
    rstd_own = lax.rsqrt(jnp.mean(centred_own * centred_own, axis=-1, keepdims=True) + LN_EPS)
    normed_own = centred_own * rstd_own
    grad_tokens = cotangent.astype(jnp.float32) + rstd_own * (
        mixed_own
        - jnp.mean(mixed_own, axis=-1, keepdims=True)
        - normed_own * jnp.mean(mixed_own * normed_own, axis=-1, keepdims=True)
    )
    local_norm = jnp.stack(
        [
            jnp.sum(grad_ln_attn * normed_all, axis=0),
            jnp.sum(grad_ln_attn, axis=0),
            jnp.sum(grad_ln_mlp * normed_all, axis=0),
            jnp.sum(grad_ln_mlp, axis=0),
        ]
    )
    grad_norms = lax.psum(local_norm, ("dp", "tensor"))
    weights_in = (w_qkv, w_out, w_up, w_down)
    moments_in = (m_qkv, m_out, m_up, m_down)
    col_counts = (3 * HD, HD, block_units, block_units)
    pad_width = max(col_counts)
    dp_index = lax.axis_index("dp")
    if paired:
        new_moments, block = reduce_all(
            (grad_all, ln_mlp, ln_attn),
            (grad_packed, mixed_heads, grad_upproj, activated),
            moments_in,
            col_counts,
        )
        owners = owner_tables()
    else:
        lefts = (ln_attn, grad_all, ln_mlp, grad_all)
        rights = (grad_packed, mixed_heads, grad_upproj, activated)
        reduced = tuple(
            lax.psum_scatter(
                contract_rows(l, r).astype(jnp.bfloat16), "dp", scatter_dimension=0, tiled=True
            ).astype(jnp.float32)
            for l, r in zip(lefts, rights)
        )
        new_moments = tuple(MOMENTUM * m + g for m, g in zip(moments_in, reduced))
        parts = []
        for fresh, grad_rows, col_count in zip(new_moments, reduced, col_counts):
            nested = (grad_rows + MOMENTUM * fresh).astype(jnp.bfloat16)
            for head in range(local_heads):
                part = nested[:, head * col_count : (head + 1) * col_count]
                parts.append(jnp.pad(part, ((0, 0), (0, pad_width - col_count))))
        groups = lax.axis_size("dp") // len(parts)
        outgoing = jnp.tile(jnp.stack(parts), (groups, 1, 1))
        block = lax.all_to_all(outgoing, "dp", split_axis=0, concat_axis=0, tiled=True)
        block = block.reshape(row_share * lax.axis_size("dp"), pad_width)
        owners = tuple((m, h) for m in range(4) for h in range(local_heads)) * groups
    widths = jnp.array([col_counts[m] for m, _ in owners], jnp.int32)
    ortho = sweeps(block, lax.dynamic_slice_in_dim(widths, dp_index, 1))
    returned = lax.all_to_all(
        ortho.reshape(lax.axis_size("dp"), row_share, pad_width), "dp", split_axis=0, concat_axis=0, tiled=True
    )
    new_weights = []
    for m in range(4):
        own = [returned[owners.index((m, h)), :, : col_counts[m]] for h in range(local_heads)]
        ortho_rows = jnp.concatenate(own, axis=1).astype(jnp.float32)
        new_weights.append(weights_in[m] * (1.0 - LEARN * DECAY) - LEARN * ortho_rows)
    norm_rows = jnp.stack([norm_gains[0], norm_biases[0], norm_gains[1], norm_biases[1]])
    moment_norms = MOMENTUM * norm_moments + grad_norms
    step_scale = lax.rsqrt(jnp.mean(moment_norms * moment_norms, axis=-1, keepdims=True) + 1e-06)
    value_norms = norm_rows - NORM_LEARN * moment_norms * step_scale
    return (
        block_out,
        grad_tokens,
        new_moments[0],
        new_weights[0],
        new_moments[1],
        new_weights[1],
        new_moments[2],
        new_weights[2],
        new_moments[3],
        new_weights[3],
        moment_norms,
        value_norms,
    )


def solution(mesh):
    in_specs = (
        P(("dp", "tensor"), None),
        P(("dp", "tensor"), None),
        P("dp", None),
        P("dp", "tensor"),
        P("dp", "tensor"),
        P("dp", "tensor"),
        P("dp", "tensor"),
        P("dp", "tensor"),
        P("dp", "tensor"),
        P("dp", "tensor"),
        P("dp", "tensor"),
        P(),
        P(),
        P(),
    )
    out_specs = (
        P(("dp", "tensor"), None),
        P(("dp", "tensor"), None),
        P("dp", "tensor"),
        P("dp", "tensor"),
        P("dp", "tensor"),
        P("dp", "tensor"),
        P("dp", "tensor"),
        P("dp", "tensor"),
        P("dp", "tensor"),
        P("dp", "tensor"),
        P(),
        P(),
    )
    return jax.shard_map(
        on_device, mesh=mesh, in_specs=in_specs, out_specs=out_specs, check_vma=False
    )
```

```python
import functools
import math

import jax
import jax.numpy as jnp
from jax import lax
from jax.experimental import pallas as pl
from jax.experimental.pallas import tpu as pltpu
from jax.sharding import PartitionSpec as P

HEADS = 8
HD = 256
FF = 8192
ROT = 64
DOC_MOST = 512


NS_A = 3.4445
NS_B = -4.775
NS_C = 2.0315
MOMENTUM = 0.95
LEARN = 0.5
DECAY = 0.01
NORM_LEARN = 0.05
LN_EPS = 1e-05
MASKED = -1e30


def doc_positions(seg_ids):
    position_idx = jnp.arange(seg_ids.shape[0], dtype=jnp.int32)
    change = jnp.concatenate([jnp.ones((1,), dtype=jnp.bool_), seg_ids[1:] != seg_ids[:-1]])
    doc_start = lax.cummax(jnp.where(change, position_idx, jnp.zeros_like(position_idx)), axis=0)
    return position_idx - doc_start


def contract_rows(left, right):
    return lax.dot_general(
        left, right, (((0,), (0,)), ((), ())), preferred_element_type=jnp.float32
    )


def contract_cols(left, right):
    return lax.dot_general(
        left, right, (((1,), (1,)), ((), ())), preferred_element_type=jnp.float32
    )


MESH = pl.DeviceIdType.MESH

def gather_kernel(n_w, n_t, *refs):
    ins_w = refs[:n_w]; ins_t = refs[n_w:n_w+n_t]
    outs_w = refs[n_w+n_t:2*n_w+n_t]; outs_t = refs[2*n_w+n_t:2*(n_w+n_t)]
    w_send, w_recv, t_send, t_recv, own_sem = refs[2*(n_w+n_t):]
    size = lax.axis_size("tensor")
    dp = lax.axis_index("dp"); me = lax.axis_index("tensor")
    y, x, c = dp // 4, (dp // 2) % 2, dp % 2
    by_x = y * 4 + (1 - x) * 2 + c
    by_y = (1 - y) * 4 + x * 2 + c
    far = (1 - y) * 4 + (1 - x) * 2 + c
    by_c = y * 4 + x * 2 + (1 - c)
    barrier = pltpu.get_barrier_semaphore()
    for peer in (by_x, by_y, by_c):
        pl.semaphore_signal(barrier, inc=1, device_id=(peer, me), device_id_type=MESH)
    for s in range(1, size):
        pl.semaphore_signal(barrier, inc=1, device_id=(dp, lax.rem(me + s, size)), device_id_type=MESH)
    pl.semaphore_wait(barrier, 3 + size - 1)

    def rows_of(ref, dev, low=0, high=1):
        rows = ref.shape[0] // 8
        return ref.at[pl.ds(pl.multiple_of(dev * rows + low, 128), high)]

    def send(i, k, src, dst, peer):
        return pltpu.make_async_remote_copy(src_ref=src, dst_ref=dst, send_sem=w_send.at[i, k], recv_sem=w_recv.at[i, k], device_id=(peer, me), device_id_type=MESH)

    def part(i, dev, low, count):
        rows = outs_w[i].shape[0] // 8
        return outs_w[i].at[pl.ds(pl.multiple_of(dev * rows + low, 128), count)]

    def copy(i, k):
        rows = outs_w[i].shape[0] // 8
        half = rows // 2
        if k < 3:
            return send(i, k, ins_w[i], part(i, dp, 0, rows), (by_x, by_y, by_c)[k])
        dev, low, count, peer = {3: (by_y, 0, half, by_x), 4: (by_x, half, half, by_y), 5: (by_x, 0, rows, by_c), 6: (by_y, 0, rows, by_c), 7: (far, 0, half, by_c), 8: (far, half, half, by_c)}[k]
        src = part(i, dev, low, count)
        return send(i, k, src, src, peer)

    def token_copy(i, s):
        rows = ins_t[i].shape[0]
        dst = outs_t[i].at[pl.ds(pl.multiple_of(me * rows, 128), rows)]
        return pltpu.make_async_remote_copy(src_ref=ins_t[i], dst_ref=dst, send_sem=t_send.at[i, s], recv_sem=t_recv.at[i, s], device_id=(dp, lax.rem(me + s, size)), device_id_type=MESH)

    if n_t:
        for s in range(1, size):
            token_copy(0, s).start()
    for i in range(min(2, n_w)):
        for k in range(3):
            copy(i, k).start()
    def second():
        for s in range(1, size):
            token_copy(0, s).wait_send()
        for j in range(1, n_t):
            for s in range(1, size):
                token_copy(j, s).start()

    own = [pltpu.make_async_copy(ins_w[i], part(i, dp, 0, outs_w[i].shape[0] // 8), own_sem.at[i]) for i in range(n_w)]
    for i in range(n_t):
        rows = ins_t[i].shape[0]
        own.append(pltpu.make_async_copy(ins_t[i], outs_t[i].at[pl.ds(pl.multiple_of(me * rows, 128), rows)], own_sem.at[n_w + i]))
    for o in own:
        o.start()
    for i in range(n_w):
        copy(i, 0).wait_recv()
        copy(i, 5).start()
        copy(i, 4).start()
        copy(i, 1).wait_recv()
        copy(i, 6).start()
        copy(i, 3).start()
        if i + 2 < n_w:
            for k in range(3):
                copy(i + 2, k).start()
        if i >= 1:
            for k in (3, 4):
                copy(i - 1, k).wait_recv()
                copy(i - 1, k + 4).start()
        if i == 1 and n_t:
            second()
    if n_w < 2 and n_t:
        second()
    for k in (3, 4) if n_w else ():
        copy(n_w - 1, k).wait_recv()
        copy(n_w - 1, k + 4).start()
    for i in range(n_w):
        for k in range(9):
            copy(i, k).wait_send()
        for k in (2, 5, 6, 7, 8):
            copy(i, k).wait_recv()
    for o in own:
        o.wait()
    for j in range(n_t):
        for s in range(1, size):
            if j > 0:
                token_copy(j, s).wait_send()
            token_copy(j, s).wait_recv()

def gather_all(shards, tokens):
    n_w, n_t = len(shards), len(tokens)
    size = lax.axis_size("tensor")
    shapes = [jax.ShapeDtypeStruct((s.shape[0] * 8, s.shape[1]), s.dtype) for s in shards]
    shapes += [jax.ShapeDtypeStruct((s.shape[0] * size, s.shape[1]), s.dtype) for s in tokens]
    anyspec = pl.BlockSpec(memory_space=pl.ANY)
    return pl.pallas_call(
        functools.partial(gather_kernel, n_w, n_t),
        out_shape=shapes,
        in_specs=[anyspec] * (n_w + n_t),
        out_specs=[anyspec] * (n_w + n_t),
        scratch_shapes=[pltpu.SemaphoreType.DMA((max(1,n_w), 9)), pltpu.SemaphoreType.DMA((max(1,n_w), 9)), pltpu.SemaphoreType.DMA((max(1,n_t), size)), pltpu.SemaphoreType.DMA((max(1,n_t), size)), pltpu.SemaphoreType.DMA((n_w + n_t,))],
        compiler_params=pltpu.CompilerParams(collective_id=0, has_side_effects=True),
        cost_estimate=pl.CostEstimate(flops=0, bytes_accessed=300 * 2**20, transcendentals=0),
        name="gather_all",
    )(*shards, *tokens)


CHUNK = 512
TILE = 256


def owner_tables():
    return ((2, 0), (1, 0), (3, 0), (0, 0), (3, 1), (0, 1), (2, 1), (1, 1))


PLAN = ((3, 0), (3, 2), (3, 1), (3, 3), (1, 0), (2, 0), (2, 2), (2, 1), (2, 3), (0, 0), (0, 1), (0, 2))
FIRST_UP, FIRST_QKV = 5, 9
SLOTS = 4


def backward_kernel(widths, *refs):
    n_chunks = len(PLAN)
    (dy_ref, ln_m_ref, ln_a_ref, act_ref, o_ref, slope_ref, qkv_ref, aux_ref, table_ref, tok_ref, norm_ref,
     w_down_ref, w_out_ref, w_up_ref, w_qkv_ref) = refs[:15]
    mom_refs = refs[15:19]
    newm_refs = refs[19:23]
    xin_ref, u_ref, sums_ref = refs[23:26]
    (lhs, rhs, sib_send, own, sib_recv, far_x, far_y, in_x, in_y, far_send, x_send, y_send, mom, newm, e_send,
     d_up, qkv, d_o, d_qkv, d_key, d_value, aux, table, w_tile, slope, row_q, row_u, tok, u_tile, norm, sums, z_in, z_sum, dp_in,
     lhs_sem, rhs_sem, mom_sem, newm_sem, sib_ss, sib_rs, fx_ss, fx_rs, fy_ss, fy_rs, x_ss, x_rs, y_ss, y_rs,
     e_ss, e_rs, e_own, side_sem, w_sem, slope_sem, row_sem, u_sem, z_ss, z_rs, d_ss, d_rs, sums_sem) = refs[26:]
    dp = lax.axis_index("dp")
    t = lax.axis_index("tensor")
    n_t = lax.axis_size("tensor")
    y, x, c = dp // 4, (dp // 2) % 2, dp % 2
    rows = xin_ref.shape[0] // 8
    half = rows // 2
    seq = dy_ref.shape[0]
    by_x = y * 4 + (1 - x) * 2 + c
    by_y = (1 - y) * 4 + x * 2 + c
    by_c = y * 4 + x * 2 + (1 - c)
    barrier = pltpu.get_barrier_semaphore()
    for shift in range(1, 8):
        pl.semaphore_signal(barrier, inc=1, device_id=(lax.rem(dp + shift, 8), t), device_id_type=MESH)
    for shift in range(1, n_t):
        pl.semaphore_signal(barrier, inc=1, device_id=(dp, lax.rem(t + shift, n_t)), device_id_type=MESH)

    def wide(v):
        return v.astype(jnp.float32)

    def low(v):
        return v.astype(jnp.bfloat16)

    def remote(src, dst, ss, rs, peer):
        return pltpu.make_async_remote_copy(src_ref=src, dst_ref=dst, send_sem=ss, recv_sem=rs, device_id=(peer, t), device_id_type=MESH)

    def local(src, dst, sem):
        return pltpu.make_async_copy(src, dst, sem)

    def select(k, values):
        out = jnp.int32(values[0])
        for i in range(1, n_chunks):
            if values[i] != values[i - 1]:
                out = jnp.where(k >= i, jnp.int32(values[i]), out)
        return out

    def per_matrix(k, fn, which=(0, 1, 2, 3)):
        mk = select(k, [m for m, _ in PLAN])
        col = select(k, [cidx for _, cidx in PLAN]) * CHUNK
        for m in which:
            @pl.when(mk == m)
            def _():
                fn(m, pl.ds(pl.multiple_of(col, CHUNK), CHUNK))

    def rhs_start(k):
        def go(m, cols):
            local((o_ref if m == 1 else act_ref).at[:, cols], rhs.at[k % 2], rhs_sem.at[k % 2]).start()
        per_matrix(k, go, (1, 3))

    def mom_copy(m, cols, slot):
        return local(mom_refs[m].at[:, cols], mom.at[slot], mom_sem.at[slot])

    def newm_copy(m, cols, slot):
        return local(newm.at[slot], newm_refs[m].at[:, cols], newm_sem.at[slot])

    any_cols = pl.ds(0, CHUNK)

    def sib_copy(k):
        return remote(sib_send.at[k % 2], sib_recv.at[k % SLOTS], sib_ss.at[k % 2], sib_rs.at[k % SLOTS], by_c)

    def far_copy_x(k):
        return remote(far_send.at[k % 2, pl.ds(0, half)], far_x.at[k % SLOTS], fx_ss.at[k % 2], fx_rs.at[k % SLOTS], by_x)

    def far_copy_y(k):
        return remote(far_send.at[k % 2, pl.ds(half, half)], far_y.at[k % SLOTS], fy_ss.at[k % 2], fy_rs.at[k % SLOTS], by_y)

    def copy_x(k):
        return remote(x_send.at[k % 2], in_x.at[k % SLOTS], x_ss.at[k % 2], x_rs.at[k % SLOTS], by_x)

    def copy_y(k):
        return remote(y_send.at[k % 2], in_y.at[k % SLOTS], y_ss.at[k % 2], y_rs.at[k % SLOTS], by_y)

    def w_start(j):
        @pl.when(j == 0)
        def _():
            local(w_out_ref, w_tile.at[0], w_sem.at[0]).start()

        @pl.when(j > 0)
        def _():
            cols = pl.ds(pl.multiple_of((j - 1) * CHUNK, CHUNK), CHUNK)
            local(w_down_ref.at[:, cols], w_tile.at[j % 2], w_sem.at[j % 2]).start()
            local(slope_ref.at[:, cols], slope.at[j % 2], slope_sem.at[j % 2]).start()

    def row_copies(j):
        here = pl.ds(pl.multiple_of(j * TILE, TILE), TILE)
        slot = j % 2
        return (
            local(w_qkv_ref.at[here], row_q.at[slot], row_sem.at[slot, 0]),
            local(w_up_ref.at[here], row_u.at[slot], row_sem.at[slot, 1]),
            local(tok_ref.at[:, here], tok.at[slot], row_sem.at[slot, 2]),
        )

    def u_copy(j):
        return local(u_tile.at[j % 2], u_ref.at[:, pl.ds(pl.multiple_of(j * TILE, TILE), TILE)], u_sem.at[j % 2])

    rhs_start(jnp.int32(0))
    lhs_copies = [local(ref, lhs.at[i], lhs_sem.at[i]) for i, ref in enumerate((dy_ref, ln_m_ref, ln_a_ref))]
    lhs_copies[0].start()
    per_matrix(jnp.int32(0), lambda m, cols: mom_copy(m, cols, 0).start())
    w_start(jnp.int32(0))
    sides = [local(a, b, side_sem.at[i]) for i, (a, b) in enumerate(((qkv_ref, qkv), (aux_ref, aux), (table_ref, table), (norm_ref, norm)))]
    for cp in sides + lhs_copies[1:]:
        cp.start()
    sums[...] = jnp.zeros_like(sums)
    lhs_copies[0].wait()
    pl.semaphore_wait(barrier, 7 + n_t - 1)

    def unit_owner(k, u):
        owners, starts = [], []
        for m, cidx in PLAN:
            unit = cidx * (CHUNK // TILE) + u
            per_block = widths[m] // TILE
            owners.append(owner_tables().index((m, unit // per_block)))
            starts.append((unit % per_block) * TILE)
        return select(k, owners), select(k, starts)

    def e_copy(k, u):
        owner, col = unit_owner(k, u)
        dst = xin_ref.at[pl.ds(pl.multiple_of(dp * rows, TILE), rows), pl.ds(pl.multiple_of(col, TILE), TILE)]
        src = e_send.at[k % 2, :, pl.ds(u * TILE, TILE)]
        return owner, remote(src, dst, e_ss.at[k % 2, u], e_rs, owner), local(src, dst, e_own.at[k % 2, u])

    def e_start(k, u):
        owner, far_cp, own_cp = e_copy(k, u)

        @pl.when(owner != dp)
        def _():
            far_cp.start()

        @pl.when(owner == dp)
        def _():
            own_cp.start()

    def e_wait(k, u):
        owner, far_cp, own_cp = e_copy(k, u)

        @pl.when(owner != dp)
        def _():
            far_cp.wait_send()

        @pl.when(owner == dp)
        def _():
            own_cp.wait()

    def made_by_dy(j, slot):
        local(w_out_ref, w_tile.at[slot], w_sem.at[slot]).wait()

        @pl.when(j > 0)
        def _():
            local(slope_ref.at[:, any_cols], slope.at[slot], slope_sem.at[slot]).wait()

        def block(r, carry):
            here = pl.ds(pl.multiple_of(r * TILE, TILE), TILE)
            part = wide_dot(lhs[0, here, :], w_tile[slot], NN)

            @pl.when(j == 0)
            def _():
                d_o[here, :] = low(part)

            @pl.when(j > 0)
            def _():
                cols = pl.ds(pl.multiple_of((j - 1) * CHUNK, CHUNK), CHUNK)
                d_up[here, cols] = low(part * wide(slope[slot, here, :]))

            return carry

        lax.fori_loop(0, seq // TILE, block, 0)

    def input_tile(j):
        slot = j % 2
        for cp in row_copies(j):
            cp.wait()

        @pl.when(j + 1 < norm_ref.shape[1] // TILE)
        def _():
            for cp in row_copies(j + 1):
                cp.start()

        @pl.when(j >= 2)
        def _():
            u_copy(j - 2).wait()

        cols = pl.ds(pl.multiple_of(j * TILE, TILE), TILE)
        gain_a, gain_m = norm[0:1, cols], norm[2:3, cols]

        def block(r, total):
            here = pl.ds(pl.multiple_of(r * TILE, TILE), TILE)
            by_a = wide_dot(d_qkv[here, :], row_q[slot], NT)
            by_m = wide_dot(d_up[here, :], row_u[slot], NT)
            normed = (wide(tok[slot, here, :]) - aux[here, 1:2]) * aux[here, 2:3]
            u_tile[slot, here, :] = low(gain_a * by_a + gain_m * by_m)
            parts = [jnp.sum(v, axis=0, keepdims=True) for v in (by_a * normed, by_a, by_m * normed, by_m)]
            return total + jnp.concatenate(parts, axis=0)

        sums[:, cols] = lax.fori_loop(0, seq // TILE, block, jnp.zeros((4, TILE), jnp.float32))
        u_copy(j).start()

    def z_copy(shift):
        return pltpu.make_async_remote_copy(src_ref=sums, dst_ref=z_in.at[shift], send_sem=z_ss.at[shift], recv_sem=z_rs.at[shift], device_id=(dp, lax.rem(t + shift, n_t)), device_id_type=MESH)

    def dp_copy(shift):
        return remote(z_sum, dp_in.at[shift], d_ss.at[shift], d_rs.at[shift], lax.rem(dp + shift, 8))

    n_tiles = norm_ref.shape[1] // TILE
    n_blocks = seq // TILE

    def step(i, carry):
        k1 = i
        k2 = i - 1
        k3 = i - 2
        k4 = i - 3

        @pl.when(k1 < n_chunks)
        def _():
            @pl.when(k1 + 1 < FIRST_UP)
            def _():
                rhs_start(k1 + 1)

            @pl.when(k1 < FIRST_UP)
            def _():
                local(act_ref.at[:, any_cols], rhs.at[k1 % 2], rhs_sem.at[k1 % 2]).wait()

            @pl.when(k1 == FIRST_UP)
            def _():
                lhs_copies[1].wait()

            @pl.when(k1 == FIRST_QKV)
            def _():
                lhs_copies[2].wait()

            def bring(m, cols):
                rhs[k1 % 2] = (d_up if m == 2 else d_qkv)[:, cols]

            per_matrix(k1, bring, (0, 2))

            @pl.when(k1 >= 2)
            def _():
                sib_copy(k1 - 2).wait_send()

            which = select(k1, [(2, 0, 1, 0)[m] for m, _ in PLAN])
            slot = k1 % 2

            def piece(q, carry2):
                px = x + (q % 2) * (1 - 2 * x)
                py = y + (q // 2) * (1 - 2 * y)
                base = py * 4 + px * 2
                left = lhs[which, :, pl.ds(pl.multiple_of((base + 1 - c) * rows, TILE), rows)]
                sib_send[slot, q] = low(wide_dot(left, rhs[slot], TN))
                left = lhs[which, :, pl.ds(pl.multiple_of((base + c) * rows, TILE), rows)]
                own[k1 % 4, q] = wide_dot(left, rhs[slot], TN)
                return carry2

            lax.fori_loop(0, 4, piece, 0)
            sib_copy(k1).start()

        @pl.when((k2 >= 0) & (k2 < n_chunks))
        def _():
            @pl.when(k2 >= 2)
            def _():
                far_copy_x(k2 - 2).wait_send()
                far_copy_y(k2 - 2).wait_send()

            sib_copy(k2).wait_recv()
            far_send[k2 % 2] = low(own[k2 % 4, 3] + wide(sib_recv[k2 % SLOTS, 3]))
            far_copy_x(k2).start()
            far_copy_y(k2).start()
            for q in range(3):
                own[k2 % 4, q] = own[k2 % 4, q] + wide(sib_recv[k2 % SLOTS, q])

        @pl.when(i <= FIRST_UP - 1)
        def _():
            @pl.when(i + 1 <= FIRST_UP - 1)
            def _():
                w_start(i + 1)

            made_by_dy(i, i % 2)

        for block in range(2 * n_blocks):
            @pl.when(i == block + 1)
            def _():
                if block == 0:
                    for cp in sides:
                        cp.wait()
                attend_back_block(qkv, aux, table, d_o, d_qkv, d_key, d_value, block // n_blocks, block % n_blocks, block % n_blocks == n_blocks - 1)

        @pl.when((k3 >= 0) & (k3 < n_chunks))
        def _():
            @pl.when(k3 >= 2)
            def _():
                copy_x(k3 - 2).wait_send()
                copy_y(k3 - 2).wait_send()

            far_copy_x(k3).wait_recv()
            far_copy_y(k3).wait_recv()
            y_send[k3 % 2, pl.ds(0, half)] = low(own[k3 % 4, 2, pl.ds(0, half)] + wide(far_x[k3 % SLOTS]))
            y_send[k3 % 2, pl.ds(half, half)] = low(own[k3 % 4, 2, pl.ds(half, half)])
            copy_y(k3).start()
            x_send[k3 % 2, pl.ds(0, half)] = low(own[k3 % 4, 1, pl.ds(0, half)])
            x_send[k3 % 2, pl.ds(half, half)] = low(own[k3 % 4, 1, pl.ds(half, half)] + wide(far_y[k3 % SLOTS]))
            copy_x(k3).start()

        @pl.when(i == FIRST_QKV - 1)
        def _():
            for cp in row_copies(0):
                cp.start()

        @pl.when((i >= FIRST_QKV) & (i < FIRST_QKV + n_tiles // 2))
        def _():
            input_tile(2 * (i - FIRST_QKV))
            input_tile(2 * (i - FIRST_QKV) + 1)

        @pl.when(i == FIRST_QKV + n_tiles // 2)
        def _():
            for shift in range(1, n_t):
                z_copy(shift).start()

        @pl.when(i == FIRST_QKV + n_tiles // 2 + 1)
        def _():
            total = sums[...]
            for shift in range(1, n_t):
                z_copy(shift).wait_recv()
                total = total + z_in[shift]
            z_sum[...] = total
            for shift in range(1, 8):
                dp_copy(shift).start()

        @pl.when(k4 >= 0)
        def _():
            @pl.when(k4 + 1 < n_chunks)
            def _():
                per_matrix(k4 + 1, lambda m, cols: mom_copy(m, cols, (k4 + 1) % 2).start())

            mom_copy(0, any_cols, k4 % 2).wait()

            @pl.when(k4 >= 2)
            def _():
                newm_copy(0, any_cols, k4 % 2).wait()
                e_wait(k4 - 2, 0)
                e_wait(k4 - 2, 1)

            copy_x(k4).wait_recv()
            copy_y(k4).wait_recv()
            grad = own[k4 % 4, 0] + wide(in_x[k4 % SLOTS]) + wide(in_y[k4 % SLOTS])
            fresh = MOMENTUM * mom[k4 % 2] + grad
            newm[k4 % 2] = fresh
            e_send[k4 % 2] = low(grad + MOMENTUM * fresh)
            per_matrix(k4, lambda m, cols: newm_copy(m, cols, k4 % 2).start())
            e_start(k4, 0)
            e_start(k4, 1)

        return carry

    lax.fori_loop(0, n_chunks + 3, step, 0)
    for k in (n_chunks - 2, n_chunks - 1):
        sib_copy(k).wait_send()
        far_copy_x(k).wait_send()
        far_copy_y(k).wait_send()
        copy_x(k).wait_send()
        copy_y(k).wait_send()
        newm_copy(0, any_cols, k % 2).wait()
        for u in range(2):
            e_wait(jnp.int32(k), u)
    total = z_sum[...]
    for shift in range(1, 8):
        dp_copy(shift).wait_recv()
        total = total + dp_in[shift]
    sums_out = local(z_in.at[0], sums_ref, sums_sem)
    z_in[0] = total
    sums_out.start()
    for shift in range(1, n_t):
        z_copy(shift).wait_send()
    for shift in range(1, 8):
        dp_copy(shift).wait_send()
    u_copy(n_tiles - 2).wait()
    u_copy(n_tiles - 1).wait()
    sums_out.wait()
    for dev, (m, head) in enumerate(owner_tables()):
        @pl.when(dp == dev)
        def _():
            seen = xin_ref.at[pl.ds(0, 7 * rows), pl.ds(0, widths[m])]
            local(seen, seen, e_rs).wait()


def backward_all(dy, ln_m, ln_a, act, o, slope, qkv, aux, table, tok, norm_rows, full, moments, widths):
    full_qkv, full_out, full_up, full_down = full
    rows = moments[0].shape[0]
    seq, width = dy.shape
    n_t = lax.axis_size("tensor")
    anyspec = pl.BlockSpec(memory_space=pl.ANY)
    bf, f32 = jnp.bfloat16, jnp.float32
    V, S = pltpu.VMEM, pltpu.SemaphoreType.DMA
    scratch = [
        V((3, seq, width), bf), V((2, seq, CHUNK), bf), V((2, 4, rows, CHUNK), bf), V((4, 4, rows, CHUNK), f32),
        V((SLOTS, 4, rows, CHUNK), bf), V((SLOTS, rows // 2, CHUNK), bf), V((SLOTS, rows // 2, CHUNK), bf),
        V((SLOTS, rows, CHUNK), bf), V((SLOTS, rows, CHUNK), bf), V((2, rows, CHUNK), bf), V((2, rows, CHUNK), bf),
        V((2, rows, CHUNK), bf), V((2, rows, CHUNK), f32), V((2, rows, CHUNK), f32), V((2, rows, CHUNK), bf),
        V(act.shape, bf), V(qkv.shape, bf), V(o.shape, bf), V(qkv.shape, bf), V((seq, HD), f32), V((seq, HD), f32),
        V(aux.shape, f32), V(table.shape, f32), V((2, width, CHUNK), bf), V((2, seq, CHUNK), bf),
        V((2, TILE, qkv.shape[1]), bf), V((2, TILE, act.shape[1]), bf), V((2, seq, TILE), bf), V((2, seq, TILE), bf),
        V(norm_rows.shape, f32), V((4, width), f32), V((n_t, 4, width), f32), V((4, width), f32), V((8, 4, width), f32),
        S((3,)), S((2,)), S((2,)), S((2,)), S((2,)), S((SLOTS,)), S((2,)), S((SLOTS,)), S((2,)), S((SLOTS,)),
        S((2,)), S((SLOTS,)), S((2,)), S((SLOTS,)),
        S((2, 2)), S, S((2, 2)), S((4,)), S((2,)), S((2,)), S((2, 3)), S((2,)), S((n_t,)), S((n_t,)), S((8,)), S((8,)), S,
    ]
    out = pl.pallas_call(
        functools.partial(backward_kernel, widths),
        out_shape=[jax.ShapeDtypeStruct(m.shape, f32) for m in moments]
        + [
            jax.ShapeDtypeStruct((8 * rows, max(widths)), bf),
            jax.ShapeDtypeStruct((seq, width), bf),
            jax.ShapeDtypeStruct((4, width), f32),
        ],
        in_specs=[anyspec] * 19,
        out_specs=[anyspec] * 7,
        scratch_shapes=scratch,
        compiler_params=pltpu.CompilerParams(collective_id=1, has_side_effects=True, vmem_limit_bytes=63 * 2**20),
        cost_estimate=pl.CostEstimate(flops=150 * 10**9, bytes_accessed=100 * 2**20, transcendentals=0),
        name="backward_all",
    )(dy, ln_m, ln_a, act, o, slope, qkv, aux, table, tok, norm_rows, full_down, full_out, full_up, full_qkv, *moments)
    return out[:4], out[4], out[5], out[6]


NT = (((1,), (1,)), ((), ()))
NN = (((1,), (0,)), ((), ()))


def wide_dot(left, right, dims):
    return lax.dot_general(left, right, dims, preferred_element_type=jnp.float32)


def sweep_kernel(width_ref, e_ref, o_ref, flipped, gram, poly):
    rows, cols = e_ref.shape
    tile, strip = 256, 512
    width = width_ref[0]
    inside = lax.broadcasted_iota(jnp.int32, (tile, cols), 1) < width

    def load(i):
        return jnp.where(inside, e_ref[pl.ds(pl.multiple_of(i * tile, tile), tile), :].astype(jnp.float32), 0.0)

    def squares(i, total):
        part = load(i)
        return total + jnp.sum((part * part).reshape(tile // 8, 8, cols), axis=0)

    total = jnp.sum(lax.fori_loop(0, rows // tile, squares, jnp.zeros((8, cols), jnp.float32)))
    scale = 1.0 / (jnp.sqrt(total) + 1e-07)
    for i in range(rows // tile):
        flipped[:, i * tile : (i + 1) * tile] = (load(i) * scale).T.astype(jnp.bfloat16)
    pairs = [(i, j) for i in range(cols // tile) for j in range(i, cols // tile)]

    def sweep(step, carry):
        for i, j in pairs:
            a, b = slice(i * tile, (i + 1) * tile), slice(j * tile, (j + 1) * tile)
            part = wide_dot(flipped[a, :], flipped[b, :], NT).astype(jnp.bfloat16)
            gram[a, b] = part
            if i != j:
                gram[b, a] = part.T
        for i, j in pairs:
            a, b = slice(i * tile, (i + 1) * tile), slice(j * tile, (j + 1) * tile)
            part = NS_B * gram[a, b].astype(jnp.float32) + NS_C * wide_dot(gram[a, :], gram[:, b], NN)
            part = part.astype(jnp.bfloat16)
            poly[a, b] = part
            if i != j:
                poly[b, a] = part.T

        def update(n, inner):
            part = pl.ds(pl.multiple_of(n * strip, strip), strip)
            old = flipped[:, part]
            for m in range(cols // strip):
                own = slice(m * strip, (m + 1) * strip)
                flipped[own, part] = (
                    NS_A * old[own].astype(jnp.float32) + wide_dot(poly[own, :], old, NN)
                ).astype(jnp.bfloat16)
            return inner

        lax.fori_loop(0, rows // strip, update, 0)
        return carry

    lax.fori_loop(0, 5, sweep, 0)
    for i in range(rows // tile):
        o_ref[i * tile : (i + 1) * tile, :] = flipped[:, i * tile : (i + 1) * tile].astype(jnp.float32).T.astype(jnp.bfloat16)


def sweeps(block, width):
    rows, cols = block.shape
    whole = pl.BlockSpec(memory_space=pltpu.VMEM)
    return pl.pallas_call(
        sweep_kernel,
        out_shape=jax.ShapeDtypeStruct((rows, cols), jnp.bfloat16),
        in_specs=[pl.BlockSpec(memory_space=pltpu.SMEM), whole],
        out_specs=whole,
        scratch_shapes=[
            pltpu.VMEM((cols, rows), jnp.bfloat16),
            pltpu.VMEM((cols, cols), jnp.bfloat16),
            pltpu.VMEM((cols, cols), jnp.bfloat16),
        ],
        compiler_params=pltpu.CompilerParams(vmem_limit_bytes=40 * 2**20),
        cost_estimate=pl.CostEstimate(flops=55 * 10**9, bytes_accessed=8 * 2**20, transcendentals=0),
        name="sweeps",
    )(width.reshape(1), block)


def turn(part, table, sign):
    half = ROT // 2
    lane = lax.broadcasted_iota(jnp.int32, part.shape, 1)
    sines = pltpu.roll(table, 128 - ROT, 1)
    ahead = pltpu.roll(part, 128 - half, 1)
    back = pltpu.roll(part, half, 1)
    partner = jnp.where(lane < half, ahead, back)
    return jnp.where(lane < ROT, part * table + sign * (partner * sines), part)


def rotary_table(positions):
    half = ROT // 2
    inv_freq = 10000.0 ** (-2.0 * jnp.arange(half, dtype=jnp.float32) / ROT)
    angles = positions.astype(jnp.float32)[:, None] * inv_freq[None, :]
    cosine, sine = jnp.cos(angles), jnp.sin(angles)
    return jnp.concatenate([cosine, cosine, -sine, sine], axis=1)


def project_kernel(tok_ref, norm_ref, table_ref, start_ref, w_ref, ln_a_ref, ln_m_ref, qkv_ref, aux_ref):
    hidden = tok_ref[...].astype(jnp.float32)
    mean = jnp.mean(hidden, axis=-1, keepdims=True)
    centred = hidden - mean
    scale = lax.rsqrt(jnp.mean(centred * centred, axis=-1, keepdims=True) + LN_EPS)
    normed = centred * scale
    ln_a = (normed * norm_ref[0:1, :] + norm_ref[1:2, :]).astype(jnp.bfloat16)
    ln_a_ref[...] = ln_a
    ln_m_ref[...] = (normed * norm_ref[2:3, :] + norm_ref[3:4, :]).astype(jnp.bfloat16)
    lane = lax.broadcasted_iota(jnp.int32, aux_ref.shape, 1)
    aux_ref[...] = jnp.where(lane == 0, start_ref[:, 0:1], jnp.where(lane == 1, mean, scale))
    table = table_ref[...]
    for part in range(w_ref.shape[1] // HD):
        raw = wide_dot(ln_a, w_ref[:, part * HD : (part + 1) * HD], NN)
        if part % 3 < 2:
            raw = jnp.concatenate([turn(raw[:, :128], table, 1.0), raw[:, 128:]], axis=1)
        qkv_ref[:, part * HD : (part + 1) * HD] = raw.astype(jnp.bfloat16)


def project(tokens_all, norm_rows, table, start_col, full_qkv):
    seq, width = tokens_all.shape
    cols = full_qkv.shape[1]
    tile = 256
    row = lambda n: pl.BlockSpec((tile, n), lambda i: (i, 0))
    whole = lambda a, b: pl.BlockSpec((a, b), lambda i: (0, 0))
    return pl.pallas_call(
        project_kernel,
        grid=(seq // tile,),
        out_shape=[
            jax.ShapeDtypeStruct((seq, width), jnp.bfloat16),
            jax.ShapeDtypeStruct((seq, width), jnp.bfloat16),
            jax.ShapeDtypeStruct((seq, cols), jnp.bfloat16),
            jax.ShapeDtypeStruct((seq, 128), jnp.float32),
        ],
        in_specs=[row(width), whole(4, width), row(128), row(1), whole(width, cols)],
        out_specs=[row(width), row(width), row(cols), row(128)],
        compiler_params=pltpu.CompilerParams(vmem_limit_bytes=48 * 2**20),
        cost_estimate=pl.CostEstimate(flops=2 * seq * width * cols, bytes_accessed=20 * 2**20, transcendentals=0),
        name="project",
    )(tokens_all, norm_rows, table, start_col, full_qkv)


def soft_block(query, keys, start_col, first, offset):
    scores = wide_dot(query, keys, NT) * (HD ** (-0.5))
    rows, cols = scores.shape
    key_pos = first + lax.broadcasted_iota(jnp.int32, (rows, cols), 1)
    query_pos = offset + lax.broadcasted_iota(jnp.int32, (rows, cols), 0)
    seen = (key_pos.astype(jnp.float32) >= start_col) & (key_pos <= query_pos)
    scores = jnp.where(seen, scores, MASKED)
    peak = jnp.max(scores, axis=-1, keepdims=True)
    expo = jnp.exp(scores - peak)
    return expo / jnp.sum(expo, axis=-1, keepdims=True)


def reach_of(block, tile):
    return max(0, (block * tile - (DOC_MOST - 1)) // tile)


def attend_kernel(qkv_ref, start_ref, o_ref):
    tile = 256
    for head in range(o_ref.shape[1] // HD):
        col = head * 3 * HD
        for block in range(o_ref.shape[0] // tile):
            low, high = reach_of(block, tile) * tile, (block + 1) * tile
            here = slice(block * tile, high)
            prob = soft_block(
                qkv_ref[here, col : col + HD],
                qkv_ref[low:high, col + HD : col + 2 * HD],
                start_ref[here, 0:1],
                low,
                block * tile,
            ).astype(jnp.bfloat16)
            mixed = wide_dot(prob, qkv_ref[low:high, col + 2 * HD : col + 3 * HD], NN)
            o_ref[here, head * HD : (head + 1) * HD] = mixed.astype(jnp.bfloat16)


def attend(qkv, start_col):
    seq = qkv.shape[0]
    cols = qkv.shape[1] // 3
    whole = pl.BlockSpec(memory_space=pltpu.VMEM)
    return pl.pallas_call(
        attend_kernel,
        out_shape=jax.ShapeDtypeStruct((seq, cols), jnp.bfloat16),
        in_specs=[whole, whole],
        out_specs=whole,
        compiler_params=pltpu.CompilerParams(vmem_limit_bytes=32 * 2**20),
        cost_estimate=pl.CostEstimate(flops=6 * 10**9, bytes_accessed=4 * 2**20, transcendentals=2**20),
        name="attend",
    )(qkv, start_col)


def up_kernel(ln_ref, w_ref, act_ref, slope_ref):
    tile = 256
    for block in range(ln_ref.shape[0] // tile):
        here = slice(block * tile, (block + 1) * tile)
        up = wide_dot(ln_ref[here, :], w_ref[...], NN)
        below = 0.5 + 0.5 * lax.erf(up * (0.5**0.5))
        act_ref[here, :] = (up * below).astype(jnp.bfloat16)
        slope_ref[here, :] = (below + up * jnp.exp(-0.5 * up * up) * ((2.0 * math.pi) ** -0.5)).astype(jnp.bfloat16)


def up_branch(ln_mlp, full_up):
    seq, width = ln_mlp.shape
    units = full_up.shape[1]
    tile = min(512, units)
    out = jax.ShapeDtypeStruct((seq, units), jnp.bfloat16)
    return pl.pallas_call(
        up_kernel,
        grid=(units // tile,),
        out_shape=[out, out],
        in_specs=[pl.BlockSpec((seq, width), lambda i: (0, 0)), pl.BlockSpec((width, tile), lambda i: (0, i))],
        out_specs=[pl.BlockSpec((seq, tile), lambda i: (0, i))] * 2,
        compiler_params=pltpu.CompilerParams(vmem_limit_bytes=48 * 2**20),
        cost_estimate=pl.CostEstimate(flops=2 * seq * width * units, bytes_accessed=20 * 2**20, transcendentals=2 * seq * units),
        name="up_branch",
    )(ln_mlp, full_up)


def down_kernel(o_ref, act_ref, w_out_ref, w_down_ref, out_ref):
    tile = 256
    for block in range(o_ref.shape[0] // tile):
        here = slice(block * tile, (block + 1) * tile)
        total = wide_dot(o_ref[here, :], w_out_ref[...], NT) + wide_dot(act_ref[here, :], w_down_ref[...], NT)
        out_ref[here, :] = total.astype(jnp.bfloat16)


def down_branch(o, act, full_out, full_down):
    seq, units = act.shape
    width = full_down.shape[0]
    tile = 512
    return pl.pallas_call(
        down_kernel,
        grid=(width // tile,),
        out_shape=jax.ShapeDtypeStruct((seq, width), jnp.bfloat16),
        in_specs=[
            pl.BlockSpec(o.shape, lambda i: (0, 0)),
            pl.BlockSpec(act.shape, lambda i: (0, 0)),
            pl.BlockSpec((tile, o.shape[1]), lambda i: (i, 0)),
            pl.BlockSpec((tile, units), lambda i: (i, 0)),
        ],
        out_specs=pl.BlockSpec((seq, tile), lambda i: (0, i)),
        compiler_params=pltpu.CompilerParams(vmem_limit_bytes=48 * 2**20),
        cost_estimate=pl.CostEstimate(flops=2 * seq * width * (units + o.shape[1]), bytes_accessed=20 * 2**20, transcendentals=0),
        name="down_branch",
    )(o, act, full_out, full_down)


TN = (((0,), (0,)), ((), ()))


def attend_back_block(qkv_ref, start_ref, table_ref, d_o_ref, d_qkv_ref, d_key, d_value, head, block, last):
    tile = 256
    col = head * 3 * HD
    low, high = reach_of(block, tile) * tile, (block + 1) * tile
    here = slice(block * tile, high)
    query, keys = qkv_ref[here, col : col + HD], qkv_ref[low:high, col + HD : col + 2 * HD]
    values = qkv_ref[low:high, col + 2 * HD : col + 3 * HD]
    d_o = d_o_ref[here, head * HD : (head + 1) * HD]
    prob = soft_block(query, keys, start_ref[here, 0:1], low, block * tile)
    value_part = wide_dot(prob.astype(jnp.bfloat16), d_o, TN)
    d_prob = wide_dot(d_o, values, NT)
    weighted = prob * d_prob
    d_score = (weighted - prob * jnp.sum(weighted, axis=-1, keepdims=True)).astype(jnp.bfloat16)
    d_query = wide_dot(d_score, keys, NN) * (HD ** (-0.5))
    key_part = wide_dot(d_score, query, TN) * (HD ** (-0.5))
    d_query = jnp.concatenate([turn(d_query[:, :128], table_ref[here, :], -1.0), d_query[:, 128:]], axis=1)
    d_qkv_ref[here, col : col + HD] = d_query.astype(jnp.bfloat16)
    old = high - tile
    if low < old:
        d_key[low:old, :] += key_part[: old - low]
        d_value[low:old, :] += value_part[: old - low]
    d_key[old:high, :] = key_part[old - low :]
    d_value[old:high, :] = value_part[old - low :]
    ready_from = low
    ready_to = high if last else reach_of(block + 1, tile) * tile
    if ready_to > ready_from:
        done = slice(ready_from, ready_to)
        total = d_key[done, :]
        total = jnp.concatenate([turn(total[:, :128], table_ref[done, :], -1.0), total[:, 128:]], axis=1)
        d_qkv_ref[done, col + HD : col + 2 * HD] = total.astype(jnp.bfloat16)
        d_qkv_ref[done, col + 2 * HD : col + 3 * HD] = d_value[done, :].astype(jnp.bfloat16)


def attend_back_kernel(qkv_ref, start_ref, table_ref, d_o_ref, d_qkv_ref, d_key, d_value):
    blocks = qkv_ref.shape[0] // 256
    for head in range(d_o_ref.shape[1] // HD):
        for block in range(blocks):
            attend_back_block(qkv_ref, start_ref, table_ref, d_o_ref, d_qkv_ref, d_key, d_value, head, block, block == blocks - 1)


def attend_back(qkv, start_col, table, d_o):
    whole = pl.BlockSpec(memory_space=pltpu.VMEM)
    return pl.pallas_call(
        attend_back_kernel,
        out_shape=jax.ShapeDtypeStruct(qkv.shape, jnp.bfloat16),
        in_specs=[whole] * 4,
        out_specs=whole,
        scratch_shapes=[pltpu.VMEM((qkv.shape[0], HD), jnp.float32)] * 2,
        compiler_params=pltpu.CompilerParams(vmem_limit_bytes=32 * 2**20),
        cost_estimate=pl.CostEstimate(flops=12 * 10**9, bytes_accessed=10 * 2**20, transcendentals=2**20),
        name="attend_back",
    )(qkv, start_col, table, d_o)


def on_device(
    tokens,
    cotangent,
    segments,
    w_qkv,
    w_out,
    w_up,
    w_down,
    m_qkv,
    m_out,
    m_up,
    m_down,
    norm_gains,
    norm_biases,
    norm_moments,
):
    tensor_size = lax.axis_size("tensor")
    seq_len = tokens.shape[0] * tensor_size
    seg_ids = segments[0]
    local_heads = w_out.shape[1] // HD
    block_units = FF // HEADS
    row_share = w_qkv.shape[0]
    hidden_own = tokens.astype(jnp.float32)
    tokens_all, grad_all = (
        lax.all_gather(tokens, "tensor", axis=0, tiled=True),
        lax.all_gather(cotangent, "tensor", axis=0, tiled=True),
    )
    shards = tuple(w.astype(jnp.bfloat16) for w in (w_qkv, w_out, w_up, w_down))
    positions = doc_positions(seg_ids)
    start_col = (jnp.arange(seq_len, dtype=jnp.int32) - positions)[:, None].astype(jnp.float32)
    table = rotary_table(positions)
    norm_rows = jnp.stack([norm_gains[0], norm_biases[0], norm_gains[1], norm_biases[1]])
    table, start_col, norm_rows, shards = lax.optimization_barrier((table, start_col, norm_rows, shards))
    paired = lax.axis_size("dp") == 8 and local_heads == 2
    if paired:
        full_qkv, full_up, full_out, full_down = gather_all((shards[0], shards[2], shards[1], shards[3]), ())
    else:
        full_qkv, full_out, full_up, full_down = (
            lax.all_gather(w, "dp", axis=0, tiled=True) for w in shards
        )
    ln_attn, ln_mlp, packed, aux = project(tokens_all, norm_rows, table, start_col, full_qkv)
    mixed_heads = attend(packed, aux)
    activated, slope = up_branch(ln_mlp, full_up)
    branch = down_branch(mixed_heads, activated, full_out, full_down)
    grad_all, branch = lax.optimization_barrier((grad_all, branch))
    branch_sum = lax.psum_scatter(branch, "tensor", scatter_dimension=0, tiled=True).astype(jnp.float32)
    weights_in = (w_qkv, w_out, w_up, w_down)
    moments_in = (m_qkv, m_out, m_up, m_down)
    col_counts = (3 * HD, HD, block_units, block_units)
    pad_width = max(col_counts)
    dp_index = lax.axis_index("dp")
    if paired:
        new_moments, block, mixed_grad, grad_norms = backward_all(
            grad_all, ln_mlp, ln_attn, activated, mixed_heads, slope, packed, aux, table, tokens_all, norm_rows,
            (full_qkv, full_out, full_up, full_down), moments_in, col_counts,
        )
        owners = owner_tables()
    else:
        grad_mixed = jnp.dot(grad_all, full_out, preferred_element_type=jnp.float32).astype(jnp.bfloat16)
        grad_packed = attend_back(packed, aux, table, grad_mixed)
        grad_act = jnp.dot(grad_all, full_down, preferred_element_type=jnp.float32)
        grad_upproj = (grad_act * slope.astype(jnp.float32)).astype(jnp.bfloat16)
        grad_ln_mlp = contract_cols(grad_upproj, full_up)
        grad_ln_attn = contract_cols(grad_packed, full_qkv)
        mixed_grad = (norm_gains[0] * grad_ln_attn + norm_gains[1] * grad_ln_mlp).astype(jnp.bfloat16)
        normed_all = (tokens_all.astype(jnp.float32) - aux[:, 1:2]) * aux[:, 2:3]
        sums = [grad_ln_attn * normed_all, grad_ln_attn, grad_ln_mlp * normed_all, grad_ln_mlp]
        grad_norms = lax.psum(jnp.stack([jnp.sum(v, axis=0) for v in sums]), ("dp", "tensor"))
        lefts = (ln_attn, grad_all, ln_mlp, grad_all)
        rights = (grad_packed, mixed_heads, grad_upproj, activated)
        reduced = tuple(
            lax.psum_scatter(
                contract_rows(l, r).astype(jnp.bfloat16), "dp", scatter_dimension=0, tiled=True
            ).astype(jnp.float32)
            for l, r in zip(lefts, rights)
        )
        new_moments = tuple(MOMENTUM * m + g for m, g in zip(moments_in, reduced))
        parts = []
        for fresh, grad_rows, col_count in zip(new_moments, reduced, col_counts):
            nested = (grad_rows + MOMENTUM * fresh).astype(jnp.bfloat16)
            for head in range(local_heads):
                part = nested[:, head * col_count : (head + 1) * col_count]
                parts.append(jnp.pad(part, ((0, 0), (0, pad_width - col_count))))
        groups = lax.axis_size("dp") // len(parts)
        outgoing = jnp.tile(jnp.stack(parts), (groups, 1, 1))
        block = lax.all_to_all(outgoing, "dp", split_axis=0, concat_axis=0, tiled=True)
        block = block.reshape(row_share * lax.axis_size("dp"), pad_width)
        owners = tuple((m, h) for m in range(4) for h in range(local_heads)) * groups
    mixed_own = lax.psum_scatter(
        mixed_grad, "tensor", scatter_dimension=0, tiled=True
    ).astype(jnp.float32)
    mean_own = jnp.mean(hidden_own, axis=-1, keepdims=True)
    centred_own = hidden_own - mean_own
    rstd_own = lax.rsqrt(jnp.mean(centred_own * centred_own, axis=-1, keepdims=True) + LN_EPS)
    normed_own = centred_own * rstd_own
    grad_tokens = cotangent.astype(jnp.float32) + rstd_own * (
        mixed_own
        - jnp.mean(mixed_own, axis=-1, keepdims=True)
        - normed_own * jnp.mean(mixed_own * normed_own, axis=-1, keepdims=True)
    )
    block, branch_sum = lax.optimization_barrier((block, branch_sum))
    block_out = (hidden_own + branch_sum).astype(jnp.bfloat16)
    widths = jnp.array([col_counts[m] for m, _ in owners], jnp.int32)
    ortho = sweeps(block, lax.dynamic_slice_in_dim(widths, dp_index, 1))
    returned = lax.all_to_all(
        ortho.reshape(lax.axis_size("dp"), row_share, pad_width), "dp", split_axis=0, concat_axis=0, tiled=True
    )
    new_weights = []
    for m in range(4):
        own = [returned[owners.index((m, h)), :, : col_counts[m]] for h in range(local_heads)]
        ortho_rows = jnp.concatenate(own, axis=1).astype(jnp.float32)
        new_weights.append(weights_in[m] * (1.0 - LEARN * DECAY) - LEARN * ortho_rows)
    moment_norms = MOMENTUM * norm_moments + grad_norms
    step_scale = lax.rsqrt(jnp.mean(moment_norms * moment_norms, axis=-1, keepdims=True) + 1e-06)
    value_norms = norm_rows - NORM_LEARN * moment_norms * step_scale
    return (
        block_out,
        grad_tokens,
        new_moments[0],
        new_weights[0],
        new_moments[1],
        new_weights[1],
        new_moments[2],
        new_weights[2],
        new_moments[3],
        new_weights[3],
        moment_norms,
        value_norms,
    )


def solution(mesh):
    in_specs = (
        P(("dp", "tensor"), None),
        P(("dp", "tensor"), None),
        P("dp", None),
        P("dp", "tensor"),
        P("dp", "tensor"),
        P("dp", "tensor"),
        P("dp", "tensor"),
        P("dp", "tensor"),
        P("dp", "tensor"),
        P("dp", "tensor"),
        P("dp", "tensor"),
        P(),
        P(),
        P(),
    )
    out_specs = (
        P(("dp", "tensor"), None),
        P(("dp", "tensor"), None),
        P("dp", "tensor"),
        P("dp", "tensor"),
        P("dp", "tensor"),
        P("dp", "tensor"),
        P("dp", "tensor"),
        P("dp", "tensor"),
        P("dp", "tensor"),
        P("dp", "tensor"),
        P(),
        P(),
    )
    return jax.shard_map(
        on_device, mesh=mesh, in_specs=in_specs, out_specs=out_specs, check_vma=False
    )
```

```python
import functools
import math

import jax
import jax.numpy as jnp
from jax import lax
from jax.experimental import pallas as pl
from jax.experimental.pallas import tpu as pltpu
from jax.sharding import PartitionSpec as P

HEADS = 8
HD = 256
FF = 8192
ROT = 64
DOC_MOST = 512


NS_A = 3.4445
NS_B = -4.775
NS_C = 2.0315
MOMENTUM = 0.95
LEARN = 0.5
DECAY = 0.01
NORM_LEARN = 0.05
LN_EPS = 1e-05
MASKED = -1e30


def doc_positions(seg_ids):
    position_idx = jnp.arange(seg_ids.shape[0], dtype=jnp.int32)
    change = jnp.concatenate([jnp.ones((1,), dtype=jnp.bool_), seg_ids[1:] != seg_ids[:-1]])
    doc_start = lax.cummax(jnp.where(change, position_idx, jnp.zeros_like(position_idx)), axis=0)
    return position_idx - doc_start


def contract_rows(left, right):
    return lax.dot_general(
        left, right, (((0,), (0,)), ((), ())), preferred_element_type=jnp.float32
    )


def contract_cols(left, right):
    return lax.dot_general(
        left, right, (((1,), (1,)), ((), ())), preferred_element_type=jnp.float32
    )


MESH = pl.DeviceIdType.MESH


def gather_kernel(order, *refs):
    n_w = len(order)
    w_refs, m_refs = refs[:n_w], refs[n_w : 2 * n_w]
    full_refs, bundle_ref = refs[2 * n_w : 3 * n_w], refs[3 * n_w]
    w_wide, w_low = refs[3 * n_w + 1 : 4 * n_w + 1], refs[4 * n_w + 1 : 5 * n_w + 1]
    m_low, load_sem, own_sem, w_send, w_recv, bundle_sem = refs[5 * n_w + 1 :]
    dp, me = lax.axis_index("dp"), lax.axis_index("tensor")
    y, x, c = dp // 4, (dp // 2) % 2, dp % 2
    by_x = y * 4 + (1 - x) * 2 + c
    by_y = (1 - y) * 4 + x * 2 + c
    far = (1 - y) * 4 + (1 - x) * 2 + c
    by_c = y * 4 + x * 2 + (1 - c)
    rows = w_refs[0].shape[0]
    half = rows // 2
    loads = [pltpu.make_async_copy(w_refs[m], w_wide[m], load_sem.at[m]) for m in order]
    for cp in loads:
        cp.start()
    barrier = pltpu.get_barrier_semaphore()
    for peer in (by_x, by_y, by_c):
        pl.semaphore_signal(barrier, inc=1, device_id=(peer, me), device_id_type=MESH)

    def part(i, dev, low, count):
        return full_refs[order[i]].at[pl.ds(pl.multiple_of(dev * rows + low, 128), count)]

    def copy(i, k):
        if k < 3:
            src, dst, peer = w_low[order[i]], part(i, dp, 0, rows), (by_x, by_y, by_c)[k]
        else:
            dev, low, count, peer = {
                3: (by_y, 0, half, by_x),
                4: (by_x, half, half, by_y),
                5: (by_x, 0, rows, by_c),
                6: (by_y, 0, rows, by_c),
                7: (far, 0, half, by_c),
                8: (far, half, half, by_c),
            }[k]
            src = dst = part(i, dev, low, count)
        return pltpu.make_async_remote_copy(
            src_ref=src, dst_ref=dst, send_sem=w_send.at[i, k], recv_sem=w_recv.at[i, k],
            device_id=(peer, me), device_id_type=MESH,
        )

    def narrow(src, dst):
        def block(r, carry):
            here = pl.ds(pl.multiple_of(r * 32, 32), 32)
            dst[here, :] = src[here, :].astype(jnp.bfloat16)
            return carry

        lax.fori_loop(0, rows // 32, block, 0)

    own = [pltpu.make_async_copy(w_low[m], part(i, dp, 0, rows), own_sem.at[i]) for i, m in enumerate(order)]
    loads[0].wait()
    narrow(w_wide[order[0]], w_low[order[0]])
    pl.semaphore_wait(barrier, 3)
    for i, m in enumerate(order):
        if i:
            loads[i].wait()
            narrow(w_wide[m], w_low[m])
        if i < 2:
            for k in range(3):
                copy(i, k).start()
        own[i].start()
    loads = [pltpu.make_async_copy(m_refs[m], w_wide[m], load_sem.at[m]) for m in range(n_w)]
    for cp in loads:
        cp.start()
    for cp in loads:
        cp.wait()
    heads = w_refs[0].shape[1] // (3 * HD)
    for dev, (m, head) in enumerate(owner_tables()):
        cols = w_refs[m].shape[1] // heads
        narrow(w_wide[m].at[:, pl.ds(head * cols, cols)], m_low.at[dev, :, pl.ds(0, cols)])
    bundle = pltpu.make_async_copy(m_low, bundle_ref, bundle_sem)
    bundle.start()
    for i in range(n_w):
        copy(i, 0).wait_recv()
        copy(i, 5).start()
        copy(i, 4).start()
        copy(i, 1).wait_recv()
        copy(i, 6).start()
        copy(i, 3).start()
        if i + 2 < n_w:
            for k in range(3):
                copy(i + 2, k).start()
        if i >= 1:
            for k in (3, 4):
                copy(i - 1, k).wait_recv()
                copy(i - 1, k + 4).start()
    for k in (3, 4):
        copy(n_w - 1, k).wait_recv()
        copy(n_w - 1, k + 4).start()
    for i in range(n_w):
        for k in range(9):
            copy(i, k).wait_send()
        for k in (2, 5, 6, 7, 8):
            copy(i, k).wait_recv()
        own[i].wait()
    bundle.wait()


def gather_all(weights, moments):
    n_w = len(weights)
    rows = weights[0].shape[0]
    bf = jnp.bfloat16
    widest = max(w.shape[1] for w in weights) // 2
    anyspec = pl.BlockSpec(memory_space=pl.ANY)
    V, S = pltpu.VMEM, pltpu.SemaphoreType.DMA
    out = pl.pallas_call(
        functools.partial(gather_kernel, (0, 2, 1, 3)),
        out_shape=[jax.ShapeDtypeStruct((rows * 8, w.shape[1]), bf) for w in weights]
        + [jax.ShapeDtypeStruct((8, rows, widest), bf)],
        in_specs=[anyspec] * (2 * n_w),
        out_specs=[anyspec] * (n_w + 1),
        scratch_shapes=[V(w.shape, w.dtype) for w in weights]
        + [V(w.shape, bf) for w in weights]
        + [V((8, rows, widest), bf), S((n_w,)), S((n_w,)), S((n_w, 9)), S((n_w, 9)), S],
        compiler_params=pltpu.CompilerParams(collective_id=0, has_side_effects=True, vmem_limit_bytes=63 * 2**20),
        cost_estimate=pl.CostEstimate(flops=0, bytes_accessed=300 * 2**20, transcendentals=0),
        name="gather_all",
    )(*weights, *moments)
    return out[:n_w], out[n_w]


TILE = 256
STRIP = 512
SLOTS = 4
EVEN_STEPS, SHARED_STEPS, ALL_STEPS = 16, 20, 28


def owner_tables():
    return ((2, 0), (1, 0), (3, 0), (0, 0), (3, 1), (0, 1), (2, 1), (1, 1))


def backward_kernel(*refs):
    (dy_ref, ln_m_ref, ln_a_ref, act_ref, o_ref, slope_ref, qkv_ref, aux_ref, table_ref, tok_ref, norm_ref,
     w_down_ref, w_out_ref, w_up_ref, w_qkv_ref) = refs[:15]
    grad_ref, u_ref, sums_ref = refs[15:18]
    (lhs, rhs, sib_send, own, sib_recv, far_x, far_y, in_x, in_y, far_send, x_send, y_send, g_out,
     qkv, d_o, d_key, d_value, aux, table, w_tile, slope, row_q, row_u, tok, u_tile, norm, sums, z_in, z_sum, dp_in,
     lhs_sem, out_sem, give_ss, give_rs, sib_ss, sib_rs, fx_ss, fx_rs, fy_ss, fy_rs, x_ss, x_rs, y_ss, y_rs,
     side_sem, w_sem, slope_sem, row_sem, u_sem, z_ss, z_rs, d_ss, d_rs, sums_sem) = refs[18:]
    dp = lax.axis_index("dp")
    t = lax.axis_index("tensor")
    n_t = lax.axis_size("tensor")
    y, x, c = dp // 4, (dp // 2) % 2, dp % 2
    seq, width = dy_ref.shape
    units, heads_width = act_ref.shape[1], o_ref.shape[1]
    at_up, at_o, at_qkv = units, 2 * units, 2 * units + heads_width
    share = STRIP // 2
    half = share // 2
    strips = width // STRIP
    by_x = y * 4 + (1 - x) * 2 + c
    by_y = (1 - y) * 4 + x * 2 + c
    by_c = y * 4 + x * 2 + (1 - c)
    barrier = pltpu.get_barrier_semaphore()
    for shift in range(1, 8):
        pl.semaphore_signal(barrier, inc=1, device_id=(lax.rem(dp + shift, 8), t), device_id_type=MESH)
    for shift in range(1, n_t):
        pl.semaphore_signal(barrier, inc=1, device_id=(dp, lax.rem(t + shift, n_t)), device_id_type=MESH)

    def wide(v):
        return v.astype(jnp.float32)

    def low(v):
        return v.astype(jnp.bfloat16)

    def remote(src, dst, ss, rs, peer):
        return pltpu.make_async_remote_copy(src_ref=src, dst_ref=dst, send_sem=ss, recv_sem=rs, device_id=(peer, t), device_id_type=MESH)

    def local(src, dst, sem):
        return pltpu.make_async_copy(src, dst, sem)

    def outer(k):
        return (k < SHARED_STEPS) | (x != y)

    def inner(k):
        return (k < SHARED_STEPS) | (x == y)

    def place(k):
        step = jnp.where(k < EVEN_STEPS, k, k - EVEN_STEPS)
        return step % strips, step // strips

    def out_copy(k):
        strip, tile = place(k)
        rows = pl.ds(pl.multiple_of(strip * STRIP + c * share, TILE), share)
        dst = grad_ref.at[rows, pl.ds(pl.multiple_of(tile * TILE, TILE), TILE)]
        return local(g_out.at[k % 2], dst, out_sem.at[k % 2]), remote(g_out.at[k % 2], dst, give_ss.at[k % 2], give_rs, by_c)

    def keeps(k):
        return jnp.where(k < EVEN_STEPS, c == 0, c == 1)

    def out_start(k):
        here, there = out_copy(k)

        @pl.when(keeps(k))
        def _():
            here.start()

        @pl.when(jnp.logical_not(keeps(k)))
        def _():
            there.start()

    def out_wait(k):
        here, there = out_copy(k)

        @pl.when(keeps(k))
        def _():
            here.wait()

        @pl.when(jnp.logical_not(keeps(k)))
        def _():
            there.wait_send()

    def sib_copy(k):
        return remote(sib_send.at[k % 2], sib_recv.at[k % SLOTS], sib_ss.at[k % 2], sib_rs.at[k % SLOTS], by_c)

    def far_copy_x(k):
        return remote(far_send.at[k % 2, pl.ds(0, half)], far_x.at[k % SLOTS], fx_ss.at[k % 2], fx_rs.at[k % SLOTS], by_x)

    def far_copy_y(k):
        return remote(far_send.at[k % 2, pl.ds(half, half)], far_y.at[k % SLOTS], fy_ss.at[k % 2], fy_rs.at[k % SLOTS], by_y)

    def copy_x(k):
        return remote(x_send.at[k % 2], in_x.at[k % SLOTS], x_ss.at[k % 2], x_rs.at[k % SLOTS], by_x)

    def copy_y(k):
        return remote(y_send.at[k % 2], in_y.at[k % SLOTS], y_ss.at[k % 2], y_rs.at[k % SLOTS], by_y)

    n_down, n_out = units // TILE, heads_width // TILE

    def down_cols(j):
        return pl.ds(pl.multiple_of((j % 2) * (units // 2) + (j // 2) * TILE, TILE), TILE)

    def w_start(j):
        @pl.when(j < n_down)
        def _():
            local(w_down_ref.at[:, down_cols(j)], w_tile.at[j % 2], w_sem.at[j % 2]).start()
            local(slope_ref.at[:, down_cols(j)], slope.at[j % 2], slope_sem.at[j % 2]).start()

        @pl.when(j >= n_down)
        def _():
            cols = pl.ds(pl.multiple_of((j - n_down) * TILE, TILE), TILE)
            local(w_out_ref.at[:, cols], w_tile.at[j % 2], w_sem.at[j % 2]).start()

    def row_copies(j):
        here = pl.ds(pl.multiple_of(j * TILE, TILE), TILE)
        slot = j % 2
        return (
            local(w_qkv_ref.at[here], row_q.at[slot], row_sem.at[slot, 0]),
            local(w_up_ref.at[here], row_u.at[slot], row_sem.at[slot, 1]),
            local(tok_ref.at[:, here], tok.at[slot], row_sem.at[slot, 2]),
        )

    def u_copy(j):
        return local(u_tile.at[j % 2], u_ref.at[:, pl.ds(pl.multiple_of(j * TILE, TILE), TILE)], u_sem.at[j % 2])

    lhs_copies = [local(ref, lhs.at[i], lhs_sem.at[i]) for i, ref in enumerate((dy_ref, ln_m_ref, ln_a_ref))]
    pairs = ((act_ref, rhs.at[:, pl.ds(0, units)]), (o_ref, rhs.at[:, pl.ds(at_o, heads_width)]), (qkv_ref, qkv),
             (aux_ref, aux), (table_ref, table), (norm_ref, norm))
    sides = [local(a, b, side_sem.at[i]) for i, (a, b) in enumerate(pairs)]
    lhs_copies[0].start()
    w_start(jnp.int32(0))
    w_start(jnp.int32(1))
    sides[0].start()
    lhs_copies[1].start()
    for cp in sides[1:]:
        cp.start()
    lhs_copies[2].start()
    sums[...] = jnp.zeros_like(sums)
    lhs_copies[0].wait()

    def made_by_dy(j):
        slot = j % 2
        local(w_out_ref.at[:, pl.ds(0, TILE)], w_tile.at[slot], w_sem.at[slot]).wait()

        @pl.when(j < n_down)
        def _():
            local(slope_ref.at[:, pl.ds(0, TILE)], slope.at[slot], slope_sem.at[slot]).wait()

        def block(r, carry):
            here = pl.ds(pl.multiple_of(r * TILE, TILE), TILE)
            part = wide_dot(lhs[0, here, :], w_tile[slot], NN)

            @pl.when(j < n_down)
            def _():
                cols = pl.ds(pl.multiple_of(at_up + (j % 2) * (units // 2) + (j // 2) * TILE, TILE), TILE)
                rhs[here, cols] = low(part * wide(slope[slot, here, :]))

            @pl.when(j >= n_down)
            def _():
                d_o[here, pl.ds(pl.multiple_of((j - n_down) * TILE, TILE), TILE)] = low(part)

            return carry

        lax.fori_loop(0, seq // TILE, block, 0)

    def input_tile(j):
        slot = j % 2
        for cp in row_copies(j):
            cp.wait()

        @pl.when(j + 1 < width // TILE)
        def _():
            for cp in row_copies(j + 1):
                cp.start()

        @pl.when(j >= 2)
        def _():
            u_copy(j - 2).wait()

        cols = pl.ds(pl.multiple_of(j * TILE, TILE), TILE)
        gain_a, gain_m = norm[0:1, cols], norm[2:3, cols]

        def block(r, total):
            here = pl.ds(pl.multiple_of(r * TILE, TILE), TILE)
            by_a = wide_dot(rhs[here, pl.ds(at_qkv, qkv_ref.shape[1])], row_q[slot], NT)
            by_m = wide_dot(rhs[here, pl.ds(at_up, units)], row_u[slot], NT)
            normed = (wide(tok[slot, here, :]) - aux[here, 1:2]) * aux[here, 2:3]
            u_tile[slot, here, :] = low(gain_a * by_a + gain_m * by_m)
            parts = [jnp.sum(v, axis=0, keepdims=True) for v in (by_a * normed, by_a, by_m * normed, by_m)]
            return total + jnp.concatenate(parts, axis=0)

        sums[:, cols] = lax.fori_loop(0, seq // TILE, block, jnp.zeros((4, TILE), jnp.float32))
        u_copy(j).start()

    def z_copy(shift):
        return pltpu.make_async_remote_copy(src_ref=sums, dst_ref=z_in.at[shift], send_sem=z_ss.at[shift], recv_sem=z_rs.at[shift], device_id=(dp, lax.rem(t + shift, n_t)), device_id_type=MESH)

    def dp_copy(shift):
        return remote(z_sum, dp_in.at[shift], d_ss.at[shift], d_rs.at[shift], lax.rem(dp + shift, 8))

    n_tiles = width // TILE
    n_blocks = seq // TILE
    first_attend = n_down + n_out - 2
    first_input = EVEN_STEPS + 1
    d_qkv = rhs.at[:, pl.ds(at_qkv, qkv_ref.shape[1])]

    made_by_dy(jnp.int32(0))
    made_by_dy(jnp.int32(1))
    w_start(jnp.int32(2))
    pl.semaphore_wait(barrier, 7 + n_t - 1)

    def step(i, carry):
        k1 = i
        k2 = i - 1
        k3 = i - 2
        k4 = i - 3

        @pl.when(k1 < ALL_STEPS)
        def _():
            @pl.when(k1 == 0)
            def _():
                sides[0].wait()
                lhs_copies[1].wait()

            @pl.when(k1 == EVEN_STEPS)
            def _():
                lhs_copies[2].wait()

            strip, tile = place(k1)

            @pl.when(k1 >= 2)
            def _():
                sib_copy(k1 - 2).wait_send()

            def piece(q, carry2):
                px = x + (q % 2) * (1 - 2 * x)
                py = y + (q // 2) * (1 - 2 * y)
                even = k1 < EVEN_STEPS
                plain = px == py

                @pl.when((k1 < SHARED_STEPS) | (px != py))
                def _():
                    which = jnp.where(even, jnp.where(plain, 1, 0), jnp.where(plain, 0, 2))
                    col_even = jnp.where(plain, at_up, 0) + py * (units // 2) + tile * TILE
                    col_odd = jnp.where(plain, at_o + py * TILE, at_qkv + py * (3 * HD) + tile * TILE)
                    col = pl.multiple_of(jnp.where(even, col_even, col_odd), TILE)
                    row = strip * STRIP
                    right = rhs[:, pl.ds(col, TILE)]
                    left = lhs[which, :, pl.ds(pl.multiple_of(row + (1 - c) * share, TILE), share)]
                    sib_send[k1 % 2, q] = low(wide_dot(left, right, TN))
                    left = lhs[which, :, pl.ds(pl.multiple_of(row + c * share, TILE), share)]
                    own[k1 % 4, q] = wide_dot(left, right, TN)

                return carry2

            lax.fori_loop(0, 4, piece, 0)
            sib_copy(k1).start()

        @pl.when((k2 >= 0) & (k2 < ALL_STEPS))
        def _():
            sib_copy(k2).wait_recv()

            @pl.when(outer(k2))
            def _():
                @pl.when(k2 >= 2)
                def _():
                    @pl.when(outer(k2 - 2))
                    def _():
                        far_copy_x(k2 - 2).wait_send()
                        far_copy_y(k2 - 2).wait_send()

                far_send[k2 % 2] = low(own[k2 % 4, 3] + wide(sib_recv[k2 % SLOTS, 3]))
                far_copy_x(k2).start()
                far_copy_y(k2).start()
                own[k2 % 4, 0] = own[k2 % 4, 0] + wide(sib_recv[k2 % SLOTS, 0])

            @pl.when(inner(k2))
            def _():
                for q in (1, 2):
                    own[k2 % 4, q] = own[k2 % 4, q] + wide(sib_recv[k2 % SLOTS, q])

        @pl.when(i < n_down + n_out - 2)
        def _():
            made_by_dy(i + 2)

            @pl.when(i + 3 < n_down + n_out)
            def _():
                w_start(i + 3)

        for block in range(2 * n_blocks):
            @pl.when(i == block + first_attend)
            def _():
                if block == 0:
                    for cp in sides[1:]:
                        cp.wait()
                attend_back_block(qkv, aux, table, d_o, d_qkv, d_key, d_value, block // n_blocks, block % n_blocks, block % n_blocks == n_blocks - 1)

        @pl.when((k3 >= 0) & (k3 < ALL_STEPS) & inner(k3))
        def _():
            @pl.when(k3 >= 2)
            def _():
                @pl.when(inner(k3 - 2))
                def _():
                    copy_x(k3 - 2).wait_send()
                    copy_y(k3 - 2).wait_send()

            far_copy_x(k3).wait_recv()
            far_copy_y(k3).wait_recv()
            y_send[k3 % 2, pl.ds(0, half)] = low(own[k3 % 4, 2, pl.ds(0, half)] + wide(far_x[k3 % SLOTS]))
            y_send[k3 % 2, pl.ds(half, half)] = low(own[k3 % 4, 2, pl.ds(half, half)])
            copy_y(k3).start()
            x_send[k3 % 2, pl.ds(0, half)] = low(own[k3 % 4, 1, pl.ds(0, half)])
            x_send[k3 % 2, pl.ds(half, half)] = low(own[k3 % 4, 1, pl.ds(half, half)] + wide(far_y[k3 % SLOTS]))
            copy_x(k3).start()

        @pl.when(i == first_input - 1)
        def _():
            for cp in row_copies(0):
                cp.start()

        @pl.when((i >= first_input) & (i < first_input + n_tiles))
        def _():
            input_tile(i - first_input)

        @pl.when(i == first_input + n_tiles)
        def _():
            for shift in range(1, n_t):
                z_copy(shift).start()

        @pl.when(i == first_input + n_tiles + 2)
        def _():
            total = sums[...]
            for shift in range(1, n_t):
                z_copy(shift).wait_recv()
                total = total + z_in[shift]
            z_sum[...] = total
            for shift in range(1, 8):
                dp_copy(shift).start()

        @pl.when((k4 >= 0) & outer(k4))
        def _():
            @pl.when(k4 >= 2)
            def _():
                @pl.when(outer(k4 - 2))
                def _():
                    out_wait(k4 - 2)

            copy_x(k4).wait_recv()
            copy_y(k4).wait_recv()
            g_out[k4 % 2] = low(own[k4 % 4, 0] + wide(in_x[k4 % SLOTS]) + wide(in_y[k4 % SLOTS]))
            out_start(k4)

        return carry

    lax.fori_loop(0, ALL_STEPS + 3, step, 0)
    for last, here, there in ((SHARED_STEPS, x == y, x != y), (ALL_STEPS, x != y, x == y)):
        for k in (last - 2, last - 1):
            k = jnp.int32(k)
            if last == ALL_STEPS:
                sib_copy(k).wait_send()

            @pl.when(here)
            def _():
                far_copy_x(k).wait_send()
                far_copy_y(k).wait_send()
                out_wait(k)

            @pl.when(there)
            def _():
                copy_x(k).wait_send()
                copy_y(k).wait_send()

    for odd in range(2):
        for apart in range(2):
            cols = (units // 2 if odd == 0 else (3 * HD if apart else HD))

            @pl.when((c == odd) & (jnp.where(x == y, 0, 1) == apart))
            def _():
                seen = grad_ref.at[pl.ds(0, width // 2), pl.ds(0, cols)]
                local(seen, seen, give_rs).wait()

    total = z_sum[...]
    for shift in range(1, 8):
        dp_copy(shift).wait_recv()
        total = total + dp_in[shift]
    sums_out = local(z_in.at[0], sums_ref, sums_sem)
    z_in[0] = total
    sums_out.start()
    for shift in range(1, n_t):
        z_copy(shift).wait_send()
    for shift in range(1, 8):
        dp_copy(shift).wait_send()
    u_copy(n_tiles - 2).wait()
    u_copy(n_tiles - 1).wait()
    sums_out.wait()


def backward_all(dy, ln_m, ln_a, act, o, slope, qkv, aux, table, tok, norm_rows, full):
    full_qkv, full_out, full_up, full_down = full
    seq, width = dy.shape
    n_t = lax.axis_size("tensor")
    anyspec = pl.BlockSpec(memory_space=pl.ANY)
    bf, f32 = jnp.bfloat16, jnp.float32
    V, S = pltpu.VMEM, pltpu.SemaphoreType.DMA
    rhs_width = 2 * act.shape[1] + o.shape[1] + qkv.shape[1]
    piece = (STRIP // 2, TILE)
    halved = (STRIP // 4, TILE)
    scratch = [
        V((3, seq, width), bf), V((seq, rhs_width), bf), V((2, 4, *piece), bf), V((4, 4, *piece), f32),
        V((SLOTS, 4, *piece), bf), V((SLOTS, *halved), bf), V((SLOTS, *halved), bf), V((SLOTS, *piece), bf),
        V((SLOTS, *piece), bf), V((2, *piece), bf), V((2, *piece), bf), V((2, *piece), bf), V((2, *piece), bf),
        V(qkv.shape, bf), V(o.shape, bf), V((seq, HD), f32), V((seq, HD), f32), V(aux.shape, f32), V(table.shape, f32),
        V((2, width, TILE), bf), V((2, seq, TILE), bf), V((2, TILE, qkv.shape[1]), bf), V((2, TILE, act.shape[1]), bf),
        V((2, seq, TILE), bf), V((2, seq, TILE), bf), V(norm_rows.shape, f32), V((4, width), f32), V((n_t, 4, width), f32),
        V((4, width), f32), V((8, 4, width), f32),
        S((3,)), S((2,)), S((2,)), S, S((2,)), S((SLOTS,)), S((2,)), S((SLOTS,)), S((2,)), S((SLOTS,)),
        S((2,)), S((SLOTS,)), S((2,)), S((SLOTS,)),
        S((6,)), S((2,)), S((2,)), S((2, 3)), S((2,)), S((n_t,)), S((n_t,)), S((8,)), S((8,)), S,
    ]
    block = jax.ShapeDtypeStruct((width, act.shape[1] // 2), bf)
    return pl.pallas_call(
        backward_kernel,
        out_shape=[block, jax.ShapeDtypeStruct((seq, width), bf), jax.ShapeDtypeStruct((4, width), f32)],
        in_specs=[anyspec] * 15,
        out_specs=[anyspec] * 3,
        scratch_shapes=scratch,
        compiler_params=pltpu.CompilerParams(collective_id=1, has_side_effects=True, vmem_limit_bytes=63 * 2**20),
        cost_estimate=pl.CostEstimate(flops=120 * 10**9, bytes_accessed=100 * 2**20, transcendentals=0),
        name="backward_all",
    )(dy, ln_m, ln_a, act, o, slope, qkv, aux, table, tok, norm_rows, full_down, full_out, full_up, full_qkv)


NT = (((1,), (1,)), ((), ()))
NN = (((1,), (0,)), ((), ()))


def wide_dot(left, right, dims):
    return lax.dot_general(left, right, dims, preferred_element_type=jnp.float32)


def sweep_all(load, o_ref, flipped, gram, poly):
    rows, cols = o_ref.shape
    tile, strip = 256, 512

    def squares(i, total):
        here = pl.ds(pl.multiple_of(i * tile, tile), tile)
        part = load(here).astype(jnp.bfloat16)
        o_ref[here, :] = part
        part = part.astype(jnp.float32)
        return total + jnp.sum((part * part).reshape(tile // 8, 8, cols), axis=0)

    total = jnp.sum(lax.fori_loop(0, rows // tile, squares, jnp.zeros((8, cols), jnp.float32)))
    scale = 1.0 / (jnp.sqrt(total) + 1e-07)
    for i in range(rows // tile):
        here = slice(i * tile, (i + 1) * tile)
        flipped[:, here] = (o_ref[here, :].astype(jnp.float32) * scale).T.astype(jnp.bfloat16)
    pairs = [(i, j) for i in range(cols // tile) for j in range(i, cols // tile)]

    def sweep(step, carry):
        for i, j in pairs:
            a, b = slice(i * tile, (i + 1) * tile), slice(j * tile, (j + 1) * tile)
            part = wide_dot(flipped[a, :], flipped[b, :], NT).astype(jnp.bfloat16)
            gram[a, b] = part
            if i != j:
                gram[b, a] = part.T
        for i, j in pairs:
            a, b = slice(i * tile, (i + 1) * tile), slice(j * tile, (j + 1) * tile)
            part = NS_B * gram[a, b].astype(jnp.float32) + NS_C * wide_dot(gram[a, :], gram[:, b], NN)
            part = part.astype(jnp.bfloat16)
            poly[a, b] = part
            if i != j:
                poly[b, a] = part.T

        def update(n, inner):
            part = pl.ds(pl.multiple_of(n * strip, strip), strip)
            old = flipped[:, part]
            for m in range(cols // strip):
                own = slice(m * strip, (m + 1) * strip)
                flipped[own, part] = (
                    NS_A * old[own].astype(jnp.float32) + wide_dot(poly[own, :], old, NN)
                ).astype(jnp.bfloat16)
            return inner

        lax.fori_loop(0, rows // strip, update, 0)
        return carry

    lax.fori_loop(0, 5, sweep, 0)
    for i in range(rows // tile):
        here = slice(i * tile, (i + 1) * tile)
        o_ref[here, :] = flipped[:, here].astype(jnp.float32).T.astype(jnp.bfloat16)


def sweep_kernel(e_ref, o_ref, flipped, gram, poly):
    sweep_all(lambda here: e_ref[here, :].astype(jnp.float32), o_ref, flipped, gram, poly)


def sweep_scratch(rows, cols):
    shapes = ((cols, rows), (cols, cols), (cols, cols))
    return [pltpu.VMEM(shape, jnp.bfloat16) for shape in shapes]


SWEEP_COST = dict(flops=55 * 10**9, bytes_accessed=8 * 2**20, transcendentals=0)


def sweeps(block):
    whole = pl.BlockSpec(memory_space=pltpu.VMEM)
    return pl.pallas_call(
        sweep_kernel,
        out_shape=jax.ShapeDtypeStruct(block.shape, jnp.bfloat16),
        in_specs=[whole],
        out_specs=whole,
        scratch_shapes=sweep_scratch(*block.shape),
        compiler_params=pltpu.CompilerParams(vmem_limit_bytes=63 * 2**20),
        cost_estimate=pl.CostEstimate(**SWEEP_COST),
        name="sweeps",
    )(block)


def sweep_return_kernel(grad_ref, mom_ref, grad_hbm, o_ref, rows_ref, flipped, gram, poly, send_sem, recv_sem, own_sem):
    dp, t = lax.axis_index("dp"), lax.axis_index("tensor")
    y, x, c = dp // 4, (dp // 2) % 2, dp % 2
    share, cols = rows_ref.shape[1:]
    barrier = pltpu.get_barrier_semaphore()
    for shift in range(1, 8):
        pl.semaphore_signal(barrier, inc=1, device_id=(lax.rem(dp + shift, 8), t), device_id_type=MESH)
    pl.semaphore_wait(barrier, 7)

    def part(dev):
        return grad_hbm.at[pl.ds(pl.multiple_of(dev * share, share), share)]

    def copy(shift):
        peer = lax.rem(dp + shift, 8)
        return pltpu.make_async_remote_copy(
            src_ref=part(peer), dst_ref=rows_ref.at[dp], send_sem=send_sem.at[shift], recv_sem=recv_sem.at[shift],
            device_id=(peer, t), device_id_type=MESH,
        )

    for shift in range(1, 8):
        copy(shift).start()
    own = pltpu.make_async_copy(part(dp), rows_ref.at[dp], own_sem)
    own.start()
    width = jnp.where(c == 0, cols, jnp.where(x == y, HD, 3 * HD))
    inside = lax.broadcasted_iota(jnp.int32, (share, cols), 1) < width

    def load(here):
        grad, mom = grad_ref[here, :].astype(jnp.float32), mom_ref[here, :].astype(jnp.float32)
        return jnp.where(inside, grad + MOMENTUM * (MOMENTUM * mom + grad), 0.0)

    sweep_all(load, o_ref, flipped, gram, poly)
    for shift in range(1, 8):
        copy(shift).wait()
    own.wait()


def sweep_return(grad_block, mom_block, share):
    rows, cols = grad_block.shape
    whole, anyspec = pl.BlockSpec(memory_space=pltpu.VMEM), pl.BlockSpec(memory_space=pl.ANY)
    return pl.pallas_call(
        sweep_return_kernel,
        out_shape=[
            jax.ShapeDtypeStruct((rows, cols), jnp.bfloat16),
            jax.ShapeDtypeStruct((rows // share, share, cols), jnp.bfloat16),
        ],
        in_specs=[whole, whole, anyspec],
        out_specs=[whole, anyspec],
        scratch_shapes=sweep_scratch(rows, cols)
        + [pltpu.SemaphoreType.DMA((8,)), pltpu.SemaphoreType.DMA((8,)), pltpu.SemaphoreType.DMA],
        compiler_params=pltpu.CompilerParams(collective_id=2, has_side_effects=True, vmem_limit_bytes=63 * 2**20),
        cost_estimate=pl.CostEstimate(**SWEEP_COST),
        name="sweep_return",
    )(grad_block, mom_block, grad_block)


def turn(part, table, sign):
    half = ROT // 2
    lane = lax.broadcasted_iota(jnp.int32, part.shape, 1)
    sines = pltpu.roll(table, 128 - ROT, 1)
    ahead = pltpu.roll(part, 128 - half, 1)
    back = pltpu.roll(part, half, 1)
    partner = jnp.where(lane < half, ahead, back)
    return jnp.where(lane < ROT, part * table + sign * (partner * sines), part)


def rotary_table(positions):
    half = ROT // 2
    inv_freq = 10000.0 ** (-2.0 * jnp.arange(half, dtype=jnp.float32) / ROT)
    angles = positions.astype(jnp.float32)[:, None] * inv_freq[None, :]
    cosine, sine = jnp.cos(angles), jnp.sin(angles)
    return jnp.concatenate([cosine, cosine, -sine, sine], axis=1)


def project_kernel(tok_ref, norm_ref, table_ref, start_ref, w_ref, ln_a_ref, ln_m_ref, qkv_ref, aux_ref):
    hidden = tok_ref[...].astype(jnp.float32)
    mean = jnp.mean(hidden, axis=-1, keepdims=True)
    centred = hidden - mean
    scale = lax.rsqrt(jnp.mean(centred * centred, axis=-1, keepdims=True) + LN_EPS)
    normed = centred * scale
    ln_a = (normed * norm_ref[0:1, :] + norm_ref[1:2, :]).astype(jnp.bfloat16)
    ln_a_ref[...] = ln_a
    ln_m_ref[...] = (normed * norm_ref[2:3, :] + norm_ref[3:4, :]).astype(jnp.bfloat16)
    lane = lax.broadcasted_iota(jnp.int32, aux_ref.shape, 1)
    aux_ref[...] = jnp.where(lane == 0, start_ref[:, 0:1], jnp.where(lane == 1, mean, scale))
    table = table_ref[...]
    for part in range(w_ref.shape[1] // HD):
        raw = wide_dot(ln_a, w_ref[:, part * HD : (part + 1) * HD], NN)
        if part % 3 < 2:
            raw = jnp.concatenate([turn(raw[:, :128], table, 1.0), raw[:, 128:]], axis=1)
        qkv_ref[:, part * HD : (part + 1) * HD] = raw.astype(jnp.bfloat16)


def project(tokens_all, norm_rows, table, start_col, full_qkv):
    seq, width = tokens_all.shape
    cols = full_qkv.shape[1]
    tile = 256
    row = lambda n: pl.BlockSpec((tile, n), lambda i: (i, 0))
    whole = lambda a, b: pl.BlockSpec((a, b), lambda i: (0, 0))
    return pl.pallas_call(
        project_kernel,
        grid=(seq // tile,),
        out_shape=[
            jax.ShapeDtypeStruct((seq, width), jnp.bfloat16),
            jax.ShapeDtypeStruct((seq, width), jnp.bfloat16),
            jax.ShapeDtypeStruct((seq, cols), jnp.bfloat16),
            jax.ShapeDtypeStruct((seq, 128), jnp.float32),
        ],
        in_specs=[row(width), whole(4, width), row(128), row(1), whole(width, cols)],
        out_specs=[row(width), row(width), row(cols), row(128)],
        compiler_params=pltpu.CompilerParams(vmem_limit_bytes=63 * 2**20),
        cost_estimate=pl.CostEstimate(flops=2 * seq * width * cols, bytes_accessed=20 * 2**20, transcendentals=0),
        name="project",
    )(tokens_all, norm_rows, table, start_col, full_qkv)


def soft_block(query, keys, start_col, first, offset):
    scores = wide_dot(query, keys, NT) * (HD ** (-0.5))
    rows, cols = scores.shape
    key_pos = first + lax.broadcasted_iota(jnp.int32, (rows, cols), 1)
    query_pos = offset + lax.broadcasted_iota(jnp.int32, (rows, cols), 0)
    seen = (key_pos.astype(jnp.float32) >= start_col) & (key_pos <= query_pos)
    scores = jnp.where(seen, scores, MASKED)
    peak = jnp.max(scores, axis=-1, keepdims=True)
    expo = jnp.exp(scores - peak)
    return expo / jnp.sum(expo, axis=-1, keepdims=True)


def reach_of(block, tile):
    return max(0, (block * tile - (DOC_MOST - 1)) // tile)


def attend_kernel(qkv_ref, start_ref, o_ref):
    tile = 256
    for head in range(o_ref.shape[1] // HD):
        col = head * 3 * HD
        for block in range(o_ref.shape[0] // tile):
            low, high = reach_of(block, tile) * tile, (block + 1) * tile
            here = slice(block * tile, high)
            prob = soft_block(
                qkv_ref[here, col : col + HD],
                qkv_ref[low:high, col + HD : col + 2 * HD],
                start_ref[here, 0:1],
                low,
                block * tile,
            ).astype(jnp.bfloat16)
            mixed = wide_dot(prob, qkv_ref[low:high, col + 2 * HD : col + 3 * HD], NN)
            o_ref[here, head * HD : (head + 1) * HD] = mixed.astype(jnp.bfloat16)


def attend(qkv, start_col):
    seq = qkv.shape[0]
    cols = qkv.shape[1] // 3
    whole = pl.BlockSpec(memory_space=pltpu.VMEM)
    return pl.pallas_call(
        attend_kernel,
        out_shape=jax.ShapeDtypeStruct((seq, cols), jnp.bfloat16),
        in_specs=[whole, whole],
        out_specs=whole,
        compiler_params=pltpu.CompilerParams(vmem_limit_bytes=63 * 2**20),
        cost_estimate=pl.CostEstimate(flops=6 * 10**9, bytes_accessed=4 * 2**20, transcendentals=2**20),
        name="attend",
    )(qkv, start_col)


def up_kernel(ln_ref, w_ref, act_ref, slope_ref):
    tile = 256
    for block in range(ln_ref.shape[0] // tile):
        here = slice(block * tile, (block + 1) * tile)
        up = wide_dot(ln_ref[here, :], w_ref[...], NN)
        below = 0.5 + 0.5 * lax.erf(up * (0.5**0.5))
        act_ref[here, :] = (up * below).astype(jnp.bfloat16)
        slope_ref[here, :] = (below + up * jnp.exp(-0.5 * up * up) * ((2.0 * math.pi) ** -0.5)).astype(jnp.bfloat16)


def up_branch(ln_mlp, full_up):
    seq, width = ln_mlp.shape
    units = full_up.shape[1]
    tile = min(512, units)
    out = jax.ShapeDtypeStruct((seq, units), jnp.bfloat16)
    return pl.pallas_call(
        up_kernel,
        grid=(units // tile,),
        out_shape=[out, out],
        in_specs=[pl.BlockSpec((seq, width), lambda i: (0, 0)), pl.BlockSpec((width, tile), lambda i: (0, i))],
        out_specs=[pl.BlockSpec((seq, tile), lambda i: (0, i))] * 2,
        compiler_params=pltpu.CompilerParams(vmem_limit_bytes=63 * 2**20),
        cost_estimate=pl.CostEstimate(flops=2 * seq * width * units, bytes_accessed=20 * 2**20, transcendentals=2 * seq * units),
        name="up_branch",
    )(ln_mlp, full_up)


def down_kernel(o_ref, act_ref, w_out_ref, w_down_ref, out_ref):
    tile = 256
    for block in range(o_ref.shape[0] // tile):
        here = slice(block * tile, (block + 1) * tile)
        total = wide_dot(o_ref[here, :], w_out_ref[...], NT) + wide_dot(act_ref[here, :], w_down_ref[...], NT)
        out_ref[here, :] = total.astype(jnp.bfloat16)


def down_branch(o, act, full_out, full_down):
    seq, units = act.shape
    width = full_down.shape[0]
    tile = 512
    return pl.pallas_call(
        down_kernel,
        grid=(width // tile,),
        out_shape=jax.ShapeDtypeStruct((seq, width), jnp.bfloat16),
        in_specs=[
            pl.BlockSpec(o.shape, lambda i: (0, 0)),
            pl.BlockSpec(act.shape, lambda i: (0, 0)),
            pl.BlockSpec((tile, o.shape[1]), lambda i: (i, 0)),
            pl.BlockSpec((tile, units), lambda i: (i, 0)),
        ],
        out_specs=pl.BlockSpec((seq, tile), lambda i: (0, i)),
        compiler_params=pltpu.CompilerParams(vmem_limit_bytes=63 * 2**20),
        cost_estimate=pl.CostEstimate(flops=2 * seq * width * (units + o.shape[1]), bytes_accessed=20 * 2**20, transcendentals=0),
        name="down_branch",
    )(o, act, full_out, full_down)


TN = (((0,), (0,)), ((), ()))


def attend_back_block(qkv_ref, start_ref, table_ref, d_o_ref, d_qkv_ref, d_key, d_value, head, block, last):
    tile = 256
    col = head * 3 * HD
    low, high = reach_of(block, tile) * tile, (block + 1) * tile
    here = slice(block * tile, high)
    query, keys = qkv_ref[here, col : col + HD], qkv_ref[low:high, col + HD : col + 2 * HD]
    values = qkv_ref[low:high, col + 2 * HD : col + 3 * HD]
    d_o = d_o_ref[here, head * HD : (head + 1) * HD]
    prob = soft_block(query, keys, start_ref[here, 0:1], low, block * tile)
    value_part = wide_dot(prob.astype(jnp.bfloat16), d_o, TN)
    d_prob = wide_dot(d_o, values, NT)
    weighted = prob * d_prob
    d_score = (weighted - prob * jnp.sum(weighted, axis=-1, keepdims=True)).astype(jnp.bfloat16)
    d_query = wide_dot(d_score, keys, NN) * (HD ** (-0.5))
    key_part = wide_dot(d_score, query, TN) * (HD ** (-0.5))
    d_query = jnp.concatenate([turn(d_query[:, :128], table_ref[here, :], -1.0), d_query[:, 128:]], axis=1)
    d_qkv_ref[here, col : col + HD] = d_query.astype(jnp.bfloat16)
    old = high - tile
    if low < old:
        d_key[low:old, :] += key_part[: old - low]
        d_value[low:old, :] += value_part[: old - low]
    d_key[old:high, :] = key_part[old - low :]
    d_value[old:high, :] = value_part[old - low :]
    ready_from = low
    ready_to = high if last else reach_of(block + 1, tile) * tile
    if ready_to > ready_from:
        done = slice(ready_from, ready_to)
        total = d_key[done, :]
        total = jnp.concatenate([turn(total[:, :128], table_ref[done, :], -1.0), total[:, 128:]], axis=1)
        d_qkv_ref[done, col + HD : col + 2 * HD] = total.astype(jnp.bfloat16)
        d_qkv_ref[done, col + 2 * HD : col + 3 * HD] = d_value[done, :].astype(jnp.bfloat16)


def attend_back_kernel(qkv_ref, start_ref, table_ref, d_o_ref, d_qkv_ref, d_key, d_value):
    blocks = qkv_ref.shape[0] // 256
    for head in range(d_o_ref.shape[1] // HD):
        for block in range(blocks):
            attend_back_block(qkv_ref, start_ref, table_ref, d_o_ref, d_qkv_ref, d_key, d_value, head, block, block == blocks - 1)


def attend_back(qkv, start_col, table, d_o):
    whole = pl.BlockSpec(memory_space=pltpu.VMEM)
    return pl.pallas_call(
        attend_back_kernel,
        out_shape=jax.ShapeDtypeStruct(qkv.shape, jnp.bfloat16),
        in_specs=[whole] * 4,
        out_specs=whole,
        scratch_shapes=[pltpu.VMEM((qkv.shape[0], HD), jnp.float32)] * 2,
        compiler_params=pltpu.CompilerParams(vmem_limit_bytes=63 * 2**20),
        cost_estimate=pl.CostEstimate(flops=12 * 10**9, bytes_accessed=10 * 2**20, transcendentals=2**20),
        name="attend_back",
    )(qkv, start_col, table, d_o)


def hand_out(block, row_share):
    parts = block.reshape(lax.axis_size("dp"), row_share, block.shape[1])
    return lax.all_to_all(parts, "dp", split_axis=0, concat_axis=0, tiled=True)


def from_owners(parts, owners, matrix, col_count, heads):
    own = [parts[owners.index((matrix, head)), :, :col_count] for head in range(heads)]
    return jnp.concatenate(own, axis=1).astype(jnp.float32)


def on_device(
    tokens,
    cotangent,
    segments,
    w_qkv,
    w_out,
    w_up,
    w_down,
    m_qkv,
    m_out,
    m_up,
    m_down,
    norm_gains,
    norm_biases,
    norm_moments,
):
    tensor_size = lax.axis_size("tensor")
    seq_len = tokens.shape[0] * tensor_size
    seg_ids = segments[0]
    local_heads = w_out.shape[1] // HD
    block_units = FF // HEADS
    row_share = w_qkv.shape[0]
    hidden_own = tokens.astype(jnp.float32)
    tokens_all, grad_all = (
        lax.all_gather(tokens, "tensor", axis=0, tiled=True),
        lax.all_gather(cotangent, "tensor", axis=0, tiled=True),
    )
    paired = lax.axis_size("dp") == 8 and local_heads == 2
    weights_in = (w_qkv, w_out, w_up, w_down)
    moments_in = (m_qkv, m_out, m_up, m_down)
    col_counts = (3 * HD, HD, block_units, block_units)
    pad_width = max(col_counts)
    positions = doc_positions(seg_ids)
    start_col = (jnp.arange(seq_len, dtype=jnp.int32) - positions)[:, None].astype(jnp.float32)
    table = rotary_table(positions)
    norm_rows = jnp.stack([norm_gains[0], norm_biases[0], norm_gains[1], norm_biases[1]])
    if paired:
        table, start_col, norm_rows, weights_in = lax.optimization_barrier((table, start_col, norm_rows, weights_in))
        (full_qkv, full_out, full_up, full_down), bundle = gather_all(weights_in, moments_in)
        mom_block = lax.all_to_all(bundle, "dp", split_axis=0, concat_axis=0, tiled=True)
        mom_block = mom_block.reshape(row_share * lax.axis_size("dp"), pad_width)
    else:
        full_qkv, full_out, full_up, full_down = (
            lax.all_gather(w.astype(jnp.bfloat16), "dp", axis=0, tiled=True) for w in weights_in
        )
    ln_attn, ln_mlp, packed, aux = project(tokens_all, norm_rows, table, start_col, full_qkv)
    mixed_heads = attend(packed, aux)
    activated, slope = up_branch(ln_mlp, full_up)
    branch = down_branch(mixed_heads, activated, full_out, full_down)
    grad_all, branch = lax.optimization_barrier((grad_all, branch))
    branch_sum = lax.psum_scatter(branch, "tensor", scatter_dimension=0, tiled=True)
    if paired:
        block, mixed_grad, grad_norms = backward_all(
            grad_all, ln_mlp, ln_attn, activated, mixed_heads, slope, packed, aux, table, tokens_all, norm_rows,
            (full_qkv, full_out, full_up, full_down),
        )
        owners = owner_tables()
    else:
        grad_mixed = jnp.dot(grad_all, full_out, preferred_element_type=jnp.float32).astype(jnp.bfloat16)
        grad_packed = attend_back(packed, aux, table, grad_mixed)
        grad_act = jnp.dot(grad_all, full_down, preferred_element_type=jnp.float32)
        grad_upproj = (grad_act * slope.astype(jnp.float32)).astype(jnp.bfloat16)
        grad_ln_mlp = contract_cols(grad_upproj, full_up)
        grad_ln_attn = contract_cols(grad_packed, full_qkv)
        mixed_grad = (norm_gains[0] * grad_ln_attn + norm_gains[1] * grad_ln_mlp).astype(jnp.bfloat16)
        normed_all = (tokens_all.astype(jnp.float32) - aux[:, 1:2]) * aux[:, 2:3]
        sums = [grad_ln_attn * normed_all, grad_ln_attn, grad_ln_mlp * normed_all, grad_ln_mlp]
        grad_norms = lax.psum(jnp.stack([jnp.sum(v, axis=0) for v in sums]), ("dp", "tensor"))
        lefts = (ln_attn, grad_all, ln_mlp, grad_all)
        rights = (grad_packed, mixed_heads, grad_upproj, activated)
        reduced = tuple(
            lax.psum_scatter(
                contract_rows(l, r).astype(jnp.bfloat16), "dp", scatter_dimension=0, tiled=True
            ).astype(jnp.float32)
            for l, r in zip(lefts, rights)
        )
        new_moments = tuple(MOMENTUM * m + g for m, g in zip(moments_in, reduced))
        parts = []
        for fresh, grad_rows, col_count in zip(new_moments, reduced, col_counts):
            nested = (grad_rows + MOMENTUM * fresh).astype(jnp.bfloat16)
            for head in range(local_heads):
                part = nested[:, head * col_count : (head + 1) * col_count]
                parts.append(jnp.pad(part, ((0, 0), (0, pad_width - col_count))))
        groups = lax.axis_size("dp") // len(parts)
        outgoing = jnp.tile(jnp.stack(parts), (groups, 1, 1))
        block = lax.all_to_all(outgoing, "dp", split_axis=0, concat_axis=0, tiled=True)
        block = block.reshape(row_share * lax.axis_size("dp"), pad_width)
        owners = tuple((m, h) for m in range(4) for h in range(local_heads)) * groups
    mixed_own = lax.psum_scatter(
        mixed_grad, "tensor", scatter_dimension=0, tiled=True
    ).astype(jnp.float32)
    mean_own = jnp.mean(hidden_own, axis=-1, keepdims=True)
    centred_own = hidden_own - mean_own
    rstd_own = lax.rsqrt(jnp.mean(centred_own * centred_own, axis=-1, keepdims=True) + LN_EPS)
    normed_own = centred_own * rstd_own
    grad_tokens = cotangent.astype(jnp.float32) + rstd_own * (
        mixed_own
        - jnp.mean(mixed_own, axis=-1, keepdims=True)
        - normed_own * jnp.mean(mixed_own * normed_own, axis=-1, keepdims=True)
    )
    block, branch_sum = lax.optimization_barrier((block, branch_sum))
    block_out = (hidden_own + branch_sum.astype(jnp.float32)).astype(jnp.bfloat16)
    if paired:
        ortho, grad_rows = sweep_return(block, mom_block, row_share)
        new_moments = tuple(
            MOMENTUM * m + from_owners(grad_rows, owners, i, col_counts[i], local_heads)
            for i, m in enumerate(moments_in)
        )
    else:
        ortho = sweeps(block)
    ortho_rows = hand_out(ortho, row_share)
    new_weights = [
        w * (1.0 - LEARN * DECAY) - LEARN * from_owners(ortho_rows, owners, i, col_counts[i], local_heads)
        for i, w in enumerate(weights_in)
    ]
    moment_norms = MOMENTUM * norm_moments + grad_norms
    step_scale = lax.rsqrt(jnp.mean(moment_norms * moment_norms, axis=-1, keepdims=True) + 1e-06)
    value_norms = norm_rows - NORM_LEARN * moment_norms * step_scale
    return (
        block_out,
        grad_tokens,
        new_moments[0],
        new_weights[0],
        new_moments[1],
        new_weights[1],
        new_moments[2],
        new_weights[2],
        new_moments[3],
        new_weights[3],
        moment_norms,
        value_norms,
    )


def solution(mesh):
    in_specs = (
        P(("dp", "tensor"), None),
        P(("dp", "tensor"), None),
        P("dp", None),
        P("dp", "tensor"),
        P("dp", "tensor"),
        P("dp", "tensor"),
        P("dp", "tensor"),
        P("dp", "tensor"),
        P("dp", "tensor"),
        P("dp", "tensor"),
        P("dp", "tensor"),
        P(),
        P(),
        P(),
    )
    out_specs = (
        P(("dp", "tensor"), None),
        P(("dp", "tensor"), None),
        P("dp", "tensor"),
        P("dp", "tensor"),
        P("dp", "tensor"),
        P("dp", "tensor"),
        P("dp", "tensor"),
        P("dp", "tensor"),
        P("dp", "tensor"),
        P("dp", "tensor"),
        P(),
        P(),
    )
    return jax.shard_map(
        on_device, mesh=mesh, in_specs=in_specs, out_specs=out_specs, check_vma=False
    )
```

```python
import functools
import math

import jax
import jax.numpy as jnp
from jax import lax
from jax.experimental import pallas as pl
from jax.experimental.pallas import tpu as pltpu
from jax.sharding import PartitionSpec as P

HEADS = 8
HD = 256
FF = 8192
ROT = 64
DOC_MOST = 512


NS_A = 3.4445
NS_B = -4.775
NS_C = 2.0315
MOMENTUM = 0.95
LEARN = 0.5
DECAY = 0.01
NORM_LEARN = 0.05
LN_EPS = 1e-05
MASKED = -1e30


def doc_positions(seg_ids):
    position_idx = jnp.arange(seg_ids.shape[0], dtype=jnp.int32)
    change = jnp.concatenate([jnp.ones((1,), dtype=jnp.bool_), seg_ids[1:] != seg_ids[:-1]])
    doc_start = lax.cummax(jnp.where(change, position_idx, jnp.zeros_like(position_idx)), axis=0)
    return position_idx - doc_start


def contract_rows(left, right):
    return lax.dot_general(
        left, right, (((0,), (0,)), ((), ())), preferred_element_type=jnp.float32
    )


def contract_cols(left, right):
    return lax.dot_general(
        left, right, (((1,), (1,)), ((), ())), preferred_element_type=jnp.float32
    )


MESH = pl.DeviceIdType.MESH


def gather_kernel(order, *refs):
    n_w = len(order)
    w_refs, m_refs = refs[:n_w], refs[n_w : 2 * n_w]
    full_refs, bundle_ref = refs[2 * n_w : 3 * n_w], refs[3 * n_w]
    w_wide, w_low = refs[3 * n_w + 1 : 4 * n_w + 1], refs[4 * n_w + 1 : 5 * n_w + 1]
    m_low, load_sem, own_sem, w_send, w_recv, bundle_sem = refs[5 * n_w + 1 :]
    dp, me = lax.axis_index("dp"), lax.axis_index("tensor")
    y, x, c = dp // 4, (dp // 2) % 2, dp % 2
    by_x = y * 4 + (1 - x) * 2 + c
    by_y = (1 - y) * 4 + x * 2 + c
    far = (1 - y) * 4 + (1 - x) * 2 + c
    by_c = y * 4 + x * 2 + (1 - c)
    rows = w_refs[0].shape[0]
    half = rows // 2
    loads = [pltpu.make_async_copy(w_refs[m], w_wide[m], load_sem.at[m]) for m in order]
    for cp in loads:
        cp.start()
    barrier = pltpu.get_barrier_semaphore()
    for peer in (by_x, by_y, by_c):
        pl.semaphore_signal(barrier, inc=1, device_id=(peer, me), device_id_type=MESH)

    def part(i, dev, low, count):
        return full_refs[order[i]].at[pl.ds(pl.multiple_of(dev * rows + low, 128), count)]

    def copy(i, k):
        if k < 3:
            src, dst, peer = w_low[order[i]], part(i, dp, 0, rows), (by_x, by_y, by_c)[k]
        else:
            dev, low, count, peer = {
                3: (by_y, 0, half, by_x),
                4: (by_x, half, half, by_y),
                5: (by_x, 0, rows, by_c),
                6: (by_y, 0, rows, by_c),
                7: (far, 0, half, by_c),
                8: (far, half, half, by_c),
            }[k]
            src = dst = part(i, dev, low, count)
        return pltpu.make_async_remote_copy(
            src_ref=src, dst_ref=dst, send_sem=w_send.at[i, k], recv_sem=w_recv.at[i, k],
            device_id=(peer, me), device_id_type=MESH,
        )

    def narrow(src, dst):
        def block(r, carry):
            here = pl.ds(pl.multiple_of(r * 32, 32), 32)
            dst[here, :] = src[here, :].astype(jnp.bfloat16)
            return carry

        lax.fori_loop(0, rows // 32, block, 0)

    own = [pltpu.make_async_copy(w_low[m], part(i, dp, 0, rows), own_sem.at[i]) for i, m in enumerate(order)]
    loads[0].wait()
    narrow(w_wide[order[0]], w_low[order[0]])
    pl.semaphore_wait(barrier, 3)
    for i, m in enumerate(order):
        if i:
            loads[i].wait()
            narrow(w_wide[m], w_low[m])
        if i < 2:
            for k in range(3):
                copy(i, k).start()
        own[i].start()
    loads = [pltpu.make_async_copy(m_refs[m], w_wide[m], load_sem.at[m]) for m in range(n_w)]
    for cp in loads:
        cp.start()
    for cp in loads:
        cp.wait()
    heads = w_refs[0].shape[1] // (3 * HD)
    for dev, (m, head) in enumerate(owner_tables()):
        cols = w_refs[m].shape[1] // heads
        narrow(w_wide[m].at[:, pl.ds(head * cols, cols)], m_low.at[dev, :, pl.ds(0, cols)])
    bundle = pltpu.make_async_copy(m_low, bundle_ref, bundle_sem)
    bundle.start()
    for i in range(n_w):
        copy(i, 0).wait_recv()
        copy(i, 5).start()
        copy(i, 4).start()
        copy(i, 1).wait_recv()
        copy(i, 6).start()
        copy(i, 3).start()
        if i + 2 < n_w:
            for k in range(3):
                copy(i + 2, k).start()
        if i >= 1:
            for k in (3, 4):
                copy(i - 1, k).wait_recv()
                copy(i - 1, k + 4).start()
    for k in (3, 4):
        copy(n_w - 1, k).wait_recv()
        copy(n_w - 1, k + 4).start()
    for i in range(n_w):
        for k in range(9):
            copy(i, k).wait_send()
        for k in (2, 5, 6, 7, 8):
            copy(i, k).wait_recv()
        own[i].wait()
    bundle.wait()


def gather_all(weights, moments):
    n_w = len(weights)
    rows = weights[0].shape[0]
    bf = jnp.bfloat16
    widest = max(w.shape[1] for w in weights) // 2
    anyspec = pl.BlockSpec(memory_space=pl.ANY)
    V, S = pltpu.VMEM, pltpu.SemaphoreType.DMA
    out = pl.pallas_call(
        functools.partial(gather_kernel, (0, 2, 1, 3)),
        out_shape=[jax.ShapeDtypeStruct((rows * 8, w.shape[1]), bf) for w in weights]
        + [jax.ShapeDtypeStruct((8, rows, widest), bf)],
        in_specs=[anyspec] * (2 * n_w),
        out_specs=[anyspec] * (n_w + 1),
        scratch_shapes=[V(w.shape, w.dtype) for w in weights]
        + [V(w.shape, bf) for w in weights]
        + [V((8, rows, widest), bf), S((n_w,)), S((n_w,)), S((n_w, 9)), S((n_w, 9)), S],
        compiler_params=pltpu.CompilerParams(collective_id=0, has_side_effects=True, vmem_limit_bytes=63 * 2**20),
        cost_estimate=pl.CostEstimate(flops=0, bytes_accessed=300 * 2**20, transcendentals=0),
        name="gather_all",
    )(*weights, *moments)
    return out[:n_w], out[n_w]


TILE = 256
STRIP = 512
SLOTS = 8
EVEN_STEPS, SHARED_STEPS, ALL_STEPS = 16, 20, 28


def owner_tables():
    return ((2, 0), (1, 0), (3, 0), (0, 0), (3, 1), (0, 1), (2, 1), (1, 1))


def backward_kernel(*refs):
    (dy_ref, ln_m_ref, ln_a_ref, act_ref, o_ref, slope_ref, qkv_ref, aux_ref, table_ref, tok_ref, norm_ref,
     w_down_ref, w_out_ref, w_up_ref, w_qkv_ref) = refs[:15]
    grad_ref, u_ref, sums_ref = refs[15:18]
    (lhs, rhs, sib_send, own, sib_recv, far_x, far_y, in_x, in_y, far_send, x_send, y_send, g_out,
     qkv, d_o, d_key, d_value, aux, table, w_tile, slope, row_q, row_u, tok, u_tile, norm, sums, z_in, z_sum, dp_in,
     lhs_sem, out_sem, give_ss, give_rs, sib_ss, sib_rs, fx_ss, fx_rs, fy_ss, fy_rs, x_ss, x_rs, y_ss, y_rs,
     side_sem, w_sem, slope_sem, row_sem, u_sem, z_ss, z_rs, d_ss, d_rs, sums_sem) = refs[18:]
    dp = lax.axis_index("dp")
    t = lax.axis_index("tensor")
    n_t = lax.axis_size("tensor")
    y, x, c = dp // 4, (dp // 2) % 2, dp % 2
    seq, width = dy_ref.shape
    units, heads_width = act_ref.shape[1], o_ref.shape[1]
    at_up, at_o, at_qkv = units, 2 * units, 2 * units + heads_width
    share = STRIP // 2
    half = share // 2
    strips = width // STRIP
    by_x = y * 4 + (1 - x) * 2 + c
    by_y = (1 - y) * 4 + x * 2 + c
    by_c = y * 4 + x * 2 + (1 - c)
    barrier = pltpu.get_barrier_semaphore()
    for shift in range(1, 8):
        pl.semaphore_signal(barrier, inc=1, device_id=(lax.rem(dp + shift, 8), t), device_id_type=MESH)
    for shift in range(1, n_t):
        pl.semaphore_signal(barrier, inc=1, device_id=(dp, lax.rem(t + shift, n_t)), device_id_type=MESH)

    def wide(v):
        return v.astype(jnp.float32)

    def low(v):
        return v.astype(jnp.bfloat16)

    def remote(src, dst, ss, rs, peer):
        return pltpu.make_async_remote_copy(src_ref=src, dst_ref=dst, send_sem=ss, recv_sem=rs, device_id=(peer, t), device_id_type=MESH)

    def local(src, dst, sem):
        return pltpu.make_async_copy(src, dst, sem)

    def outer(k):
        return (k < SHARED_STEPS) | (x != y)

    def inner(k):
        return (k < SHARED_STEPS) | (x == y)

    def place(k):
        step = jnp.where(k < EVEN_STEPS, k, k - EVEN_STEPS)
        return step % strips, step // strips

    def out_copy(k):
        strip, tile = place(k)
        rows = pl.ds(pl.multiple_of(strip * STRIP + c * share, TILE), share)
        dst = grad_ref.at[rows, pl.ds(pl.multiple_of(tile * TILE, TILE), TILE)]
        return local(g_out.at[k % 2], dst, out_sem.at[k % 2]), remote(g_out.at[k % 2], dst, give_ss.at[k % 2], give_rs, by_c)

    def keeps(k):
        return jnp.where(k < EVEN_STEPS, c == 0, c == 1)

    def out_start(k):
        here, there = out_copy(k)

        @pl.when(keeps(k))
        def _():
            here.start()

        @pl.when(jnp.logical_not(keeps(k)))
        def _():
            there.start()

    def out_wait(k):
        here, there = out_copy(k)

        @pl.when(keeps(k))
        def _():
            here.wait()

        @pl.when(jnp.logical_not(keeps(k)))
        def _():
            there.wait_send()

    def sib_copy(k):
        return remote(sib_send.at[k % 2], sib_recv.at[k % SLOTS], sib_ss.at[k % 2], sib_rs.at[k % SLOTS], by_c)

    def far_copy_x(k):
        return remote(far_send.at[k % 2, pl.ds(0, half)], far_x.at[k % SLOTS], fx_ss.at[k % 2], fx_rs.at[k % SLOTS], by_x)

    def far_copy_y(k):
        return remote(far_send.at[k % 2, pl.ds(half, half)], far_y.at[k % SLOTS], fy_ss.at[k % 2], fy_rs.at[k % SLOTS], by_y)

    def copy_x(k):
        return remote(x_send.at[k % 2], in_x.at[k % SLOTS], x_ss.at[k % 2], x_rs.at[k % SLOTS], by_x)

    def copy_y(k):
        return remote(y_send.at[k % 2], in_y.at[k % SLOTS], y_ss.at[k % 2], y_rs.at[k % SLOTS], by_y)

    n_down, n_out = units // TILE, heads_width // TILE

    def down_cols(j):
        return pl.ds(pl.multiple_of((j % 2) * (units // 2) + (j // 2) * TILE, TILE), TILE)

    def w_start(j):
        @pl.when(j < n_down)
        def _():
            local(w_down_ref.at[:, down_cols(j)], w_tile.at[j % 2], w_sem.at[j % 2]).start()
            local(slope_ref.at[:, down_cols(j)], slope.at[j % 2], slope_sem.at[j % 2]).start()

        @pl.when(j >= n_down)
        def _():
            cols = pl.ds(pl.multiple_of((j - n_down) * TILE, TILE), TILE)
            local(w_out_ref.at[:, cols], w_tile.at[j % 2], w_sem.at[j % 2]).start()

    def row_copies(j):
        here = pl.ds(pl.multiple_of(j * TILE, TILE), TILE)
        slot = j % 2
        return (
            local(w_qkv_ref.at[here], row_q.at[slot], row_sem.at[slot, 0]),
            local(w_up_ref.at[here], row_u.at[slot], row_sem.at[slot, 1]),
            local(tok_ref.at[:, here], tok.at[slot], row_sem.at[slot, 2]),
        )

    def u_copy(j):
        return local(u_tile.at[j % 2], u_ref.at[:, pl.ds(pl.multiple_of(j * TILE, TILE), TILE)], u_sem.at[j % 2])

    lhs_copies = [local(ref, lhs.at[i], lhs_sem.at[i]) for i, ref in enumerate((dy_ref, ln_m_ref, ln_a_ref))]
    pairs = ((act_ref, rhs.at[:, pl.ds(0, units)]), (o_ref, rhs.at[:, pl.ds(at_o, heads_width)]), (qkv_ref, qkv),
             (aux_ref, aux), (table_ref, table), (norm_ref, norm))
    sides = [local(a, b, side_sem.at[i]) for i, (a, b) in enumerate(pairs)]
    lhs_copies[0].start()
    w_start(jnp.int32(0))
    w_start(jnp.int32(1))
    sides[0].start()
    lhs_copies[1].start()
    for cp in sides[1:]:
        cp.start()
    lhs_copies[2].start()
    sums[...] = jnp.zeros_like(sums)
    lhs_copies[0].wait()

    def made_by_dy(j):
        slot = j % 2
        local(w_out_ref.at[:, pl.ds(0, TILE)], w_tile.at[slot], w_sem.at[slot]).wait()

        @pl.when(j < n_down)
        def _():
            local(slope_ref.at[:, pl.ds(0, TILE)], slope.at[slot], slope_sem.at[slot]).wait()
            cols = pl.ds(pl.multiple_of(at_up + (j % 2) * (units // 2) + (j // 2) * TILE, TILE), TILE)
            for r in range(2):
                here = slice(r * (seq // 2), (r + 1) * (seq // 2))
                rhs[here, cols] = low(wide_dot(lhs[0, here, :], w_tile[slot], NN) * wide(slope[slot, here, :]))

        @pl.when(j >= n_down)
        def _():
            cols = pl.ds(pl.multiple_of((j - n_down) * TILE, TILE), TILE)
            for r in range(2):
                here = slice(r * (seq // 2), (r + 1) * (seq // 2))
                d_o[here, cols] = low(wide_dot(lhs[0, here, :], w_tile[slot], NN))

    def input_tile(j):
        slot = j % 2
        for cp in row_copies(j):
            cp.wait()

        @pl.when(j + 1 < width // TILE)
        def _():
            for cp in row_copies(j + 1):
                cp.start()

        @pl.when(j >= 2)
        def _():
            u_copy(j - 2).wait()

        cols = pl.ds(pl.multiple_of(j * TILE, TILE), TILE)
        gain_a, gain_m = norm[0:1, cols], norm[2:3, cols]

        total = jnp.zeros((4, TILE), jnp.float32)
        for r in range(2):
            here = slice(r * (seq // 2), (r + 1) * (seq // 2))
            by_a = wide_dot(rhs[here, pl.ds(at_qkv, qkv_ref.shape[1])], row_q[slot], NT)
            by_m = wide_dot(rhs[here, pl.ds(at_up, units)], row_u[slot], NT)
            normed = (wide(tok[slot, here, :]) - aux[here, 1:2]) * aux[here, 2:3]
            u_tile[slot, here, :] = low(gain_a * by_a + gain_m * by_m)
            parts = [jnp.sum(v, axis=0, keepdims=True) for v in (by_a * normed, by_a, by_m * normed, by_m)]
            total = total + jnp.concatenate(parts, axis=0)
        sums[:, cols] = total
        u_copy(j).start()

    def z_copy(shift):
        return pltpu.make_async_remote_copy(src_ref=sums, dst_ref=z_in.at[shift], send_sem=z_ss.at[shift], recv_sem=z_rs.at[shift], device_id=(dp, lax.rem(t + shift, n_t)), device_id_type=MESH)

    def dp_copy(shift):
        return remote(z_sum, dp_in.at[shift], d_ss.at[shift], d_rs.at[shift], lax.rem(dp + shift, 8))

    n_tiles = width // TILE
    n_blocks = seq // TILE
    first_attend = n_down + n_out - 2
    first_input = EVEN_STEPS + 1
    d_qkv = rhs.at[:, pl.ds(at_qkv, qkv_ref.shape[1])]

    made_by_dy(jnp.int32(0))
    made_by_dy(jnp.int32(1))
    w_start(jnp.int32(2))
    pl.semaphore_wait(barrier, 7 + n_t - 1)

    def step(i, carry):
        k1 = i
        k2 = i - 1
        k3 = i - 3
        k4 = i - 5

        @pl.when(k1 < ALL_STEPS)
        def _():
            @pl.when(k1 == 0)
            def _():
                sides[0].wait()
                lhs_copies[1].wait()

            @pl.when(k1 == EVEN_STEPS)
            def _():
                lhs_copies[2].wait()

            strip, tile = place(k1)

            @pl.when(k1 >= 2)
            def _():
                sib_copy(k1 - 2).wait_send()

            def piece(q):
                px = x + (q % 2) * (1 - 2 * x)
                py = y + (q // 2) * (1 - 2 * y)
                even = k1 < EVEN_STEPS
                plain = px == py
                which = jnp.where(even, jnp.where(plain, 1, 0), jnp.where(plain, 0, 2))
                col_even = jnp.where(plain, at_up, 0) + py * (units // 2) + tile * TILE
                col_odd = jnp.where(plain, at_o + py * TILE, at_qkv + py * (3 * HD) + tile * TILE)
                col = pl.multiple_of(jnp.where(even, col_even, col_odd), TILE)
                row = strip * STRIP
                right = rhs[:, pl.ds(col, TILE)]
                left = lhs[which, :, pl.ds(pl.multiple_of(row + (1 - c) * share, TILE), share)]
                sib_send[k1 % 2, q] = low(wide_dot(left, right, TN))
                left = lhs[which, :, pl.ds(pl.multiple_of(row + c * share, TILE), share)]
                own[k1 % SLOTS, q] = wide_dot(left, right, TN)

            @pl.when(k1 < SHARED_STEPS)
            def _():
                for q in range(4):
                    piece(q)

            @pl.when(k1 >= SHARED_STEPS)
            def _():
                piece(jnp.where(x == y, 1, 0))
                piece(jnp.where(x == y, 2, 3))

            sib_copy(k1).start()

        @pl.when((k2 >= 0) & (k2 < ALL_STEPS))
        def _():
            sib_copy(k2).wait_recv()

            @pl.when(outer(k2))
            def _():
                @pl.when(k2 >= 2)
                def _():
                    @pl.when(outer(k2 - 2))
                    def _():
                        far_copy_x(k2 - 2).wait_send()
                        far_copy_y(k2 - 2).wait_send()

                far_send[k2 % 2] = low(own[k2 % SLOTS, 3] + wide(sib_recv[k2 % SLOTS, 3]))
                far_copy_x(k2).start()
                far_copy_y(k2).start()

        @pl.when(i < n_down + n_out - 2)
        def _():
            made_by_dy(i + 2)

            @pl.when(i + 3 < n_down + n_out)
            def _():
                w_start(i + 3)

        for block in range(2 * n_blocks):
            @pl.when(i == block + first_attend)
            def _():
                if block == 0:
                    for cp in sides[1:]:
                        cp.wait()
                attend_back_block(qkv, aux, table, d_o, d_qkv, d_key, d_value, block // n_blocks, block % n_blocks, block % n_blocks == n_blocks - 1)

        @pl.when((k3 >= 0) & (k3 < ALL_STEPS) & inner(k3))
        def _():
            @pl.when(k3 >= 2)
            def _():
                @pl.when(inner(k3 - 2))
                def _():
                    copy_x(k3 - 2).wait_send()
                    copy_y(k3 - 2).wait_send()

            far_copy_x(k3).wait_recv()
            far_copy_y(k3).wait_recv()
            first, last = pl.ds(0, half), pl.ds(half, half)

            def chip_sum(q, part):
                return own[k3 % SLOTS, q, part] + wide(sib_recv[k3 % SLOTS, q, part])

            y_send[k3 % 2, first] = low(chip_sum(2, first) + wide(far_x[k3 % SLOTS]))
            y_send[k3 % 2, last] = low(chip_sum(2, last))
            copy_y(k3).start()
            x_send[k3 % 2, first] = low(chip_sum(1, first))
            x_send[k3 % 2, last] = low(chip_sum(1, last) + wide(far_y[k3 % SLOTS]))
            copy_x(k3).start()

        @pl.when(i == first_input - 1)
        def _():
            for cp in row_copies(0):
                cp.start()

        @pl.when((i >= first_input) & (i < first_input + n_tiles))
        def _():
            input_tile(i - first_input)

        @pl.when(i == first_input + n_tiles)
        def _():
            for shift in range(1, n_t):
                z_copy(shift).start()

        @pl.when(i == first_input + n_tiles + 2)
        def _():
            total = sums[...]
            for shift in range(1, n_t):
                z_copy(shift).wait_recv()
                total = total + z_in[shift]
            z_sum[...] = total
            for shift in range(1, 8):
                dp_copy(shift).start()

        @pl.when((k4 >= 0) & outer(k4))
        def _():
            @pl.when(k4 >= 2)
            def _():
                @pl.when(outer(k4 - 2))
                def _():
                    out_wait(k4 - 2)

            copy_x(k4).wait_recv()
            copy_y(k4).wait_recv()
            g_out[k4 % 2] = low(own[k4 % SLOTS, 0] + wide(sib_recv[k4 % SLOTS, 0]) + wide(in_x[k4 % SLOTS]) + wide(in_y[k4 % SLOTS]))
            out_start(k4)

        return carry

    lax.fori_loop(0, ALL_STEPS + 5, step, 0)
    for last, here, there in ((SHARED_STEPS, x == y, x != y), (ALL_STEPS, x != y, x == y)):
        for k in (last - 2, last - 1):
            k = jnp.int32(k)
            if last == ALL_STEPS:
                sib_copy(k).wait_send()

            @pl.when(here)
            def _():
                far_copy_x(k).wait_send()
                far_copy_y(k).wait_send()
                out_wait(k)

            @pl.when(there)
            def _():
                copy_x(k).wait_send()
                copy_y(k).wait_send()

    for odd in range(2):
        for apart in range(2):
            cols = (units // 2 if odd == 0 else (3 * HD if apart else HD))

            @pl.when((c == odd) & (jnp.where(x == y, 0, 1) == apart))
            def _():
                seen = grad_ref.at[pl.ds(0, width // 2), pl.ds(0, cols)]
                local(seen, seen, give_rs).wait()

    total = z_sum[...]
    for shift in range(1, 8):
        dp_copy(shift).wait_recv()
        total = total + dp_in[shift]
    sums_out = local(z_in.at[0], sums_ref, sums_sem)
    z_in[0] = total
    sums_out.start()
    for shift in range(1, n_t):
        z_copy(shift).wait_send()
    for shift in range(1, 8):
        dp_copy(shift).wait_send()
    u_copy(n_tiles - 2).wait()
    u_copy(n_tiles - 1).wait()
    sums_out.wait()


def backward_all(dy, ln_m, ln_a, act, o, slope, qkv, aux, table, tok, norm_rows, full):
    full_qkv, full_out, full_up, full_down = full
    seq, width = dy.shape
    n_t = lax.axis_size("tensor")
    anyspec = pl.BlockSpec(memory_space=pl.ANY)
    bf, f32 = jnp.bfloat16, jnp.float32
    V, S = pltpu.VMEM, pltpu.SemaphoreType.DMA
    rhs_width = 2 * act.shape[1] + o.shape[1] + qkv.shape[1]
    piece = (STRIP // 2, TILE)
    halved = (STRIP // 4, TILE)
    scratch = [
        V((3, seq, width), bf), V((seq, rhs_width), bf), V((2, 4, *piece), bf), V((SLOTS, 4, *piece), f32),
        V((SLOTS, 4, *piece), bf), V((SLOTS, *halved), bf), V((SLOTS, *halved), bf), V((SLOTS, *piece), bf),
        V((SLOTS, *piece), bf), V((2, *piece), bf), V((2, *piece), bf), V((2, *piece), bf), V((2, *piece), bf),
        V(qkv.shape, bf), V(o.shape, bf), V((seq, HD), f32), V((seq, HD), f32), V(aux.shape, f32), V(table.shape, f32),
        V((2, width, TILE), bf), V((2, seq, TILE), bf), V((2, TILE, qkv.shape[1]), bf), V((2, TILE, act.shape[1]), bf),
        V((2, seq, TILE), bf), V((2, seq, TILE), bf), V(norm_rows.shape, f32), V((4, width), f32), V((n_t, 4, width), f32),
        V((4, width), f32), V((8, 4, width), f32),
        S((3,)), S((2,)), S((2,)), S, S((2,)), S((SLOTS,)), S((2,)), S((SLOTS,)), S((2,)), S((SLOTS,)),
        S((2,)), S((SLOTS,)), S((2,)), S((SLOTS,)),
        S((6,)), S((2,)), S((2,)), S((2, 3)), S((2,)), S((n_t,)), S((n_t,)), S((8,)), S((8,)), S,
    ]
    block = jax.ShapeDtypeStruct((width, act.shape[1] // 2), bf)
    return pl.pallas_call(
        backward_kernel,
        out_shape=[block, jax.ShapeDtypeStruct((seq, width), bf), jax.ShapeDtypeStruct((4, width), f32)],
        in_specs=[anyspec] * 15,
        out_specs=[anyspec] * 3,
        scratch_shapes=scratch,
        compiler_params=pltpu.CompilerParams(collective_id=1, has_side_effects=True, vmem_limit_bytes=63 * 2**20),
        cost_estimate=pl.CostEstimate(flops=120 * 10**9, bytes_accessed=100 * 2**20, transcendentals=0),
        name="backward_all",
    )(dy, ln_m, ln_a, act, o, slope, qkv, aux, table, tok, norm_rows, full_down, full_out, full_up, full_qkv)


NT = (((1,), (1,)), ((), ()))
NN = (((1,), (0,)), ((), ()))


def wide_dot(left, right, dims):
    return lax.dot_general(left, right, dims, preferred_element_type=jnp.float32)


def sweep_all(load, o_ref, flipped, gram, poly, strip_of=None, done=None):
    rows, cols = o_ref.shape
    tile, strip = 256, 512

    def squares(i, total):
        here = pl.ds(pl.multiple_of(i * tile, tile), tile)
        part = load(here).astype(jnp.bfloat16)
        o_ref[here, :] = part
        part = part.astype(jnp.float32)
        return total + jnp.sum((part * part).reshape(tile // 8, 8, cols), axis=0)

    total = jnp.sum(lax.fori_loop(0, rows // tile, squares, jnp.zeros((8, cols), jnp.float32)))
    scale = 1.0 / (jnp.sqrt(total) + 1e-07)
    for i in range(rows // tile):
        here = slice(i * tile, (i + 1) * tile)
        flipped[:, here] = (o_ref[here, :].astype(jnp.float32) * scale).T.astype(jnp.bfloat16)
    pairs = [(i, j) for i in range(cols // tile) for j in range(i, cols // tile)]

    def sweep(step, carry):
        for i, j in pairs:
            a, b = slice(i * tile, (i + 1) * tile), slice(j * tile, (j + 1) * tile)
            part = wide_dot(flipped[a, :], flipped[b, :], NT).astype(jnp.bfloat16)
            gram[a, b] = part
            if i != j:
                gram[b, a] = part.T
        for i, j in pairs:
            a, b = slice(i * tile, (i + 1) * tile), slice(j * tile, (j + 1) * tile)
            part = NS_B * gram[a, b].astype(jnp.float32) + NS_C * wide_dot(gram[a, :], gram[:, b], NN)
            part = part.astype(jnp.bfloat16)
            poly[a, b] = part
            if i != j:
                poly[b, a] = part.T

        def update(n, inner):
            n = n if strip_of is None else strip_of(n)
            part = pl.ds(pl.multiple_of(n * strip, strip), strip)
            old = flipped[:, part]
            for m in range(cols // strip):
                own = slice(m * strip, (m + 1) * strip)
                flipped[own, part] = (
                    NS_A * old[own].astype(jnp.float32) + wide_dot(poly[own, :], old, NN)
                ).astype(jnp.bfloat16)

            @pl.when(step == 4)
            def _():
                for r in range(strip // tile):
                    here = pl.ds(pl.multiple_of(n * strip + r * tile, tile), tile)
                    o_ref[here, :] = flipped[:, here].astype(jnp.float32).T.astype(jnp.bfloat16)
                if done is not None:
                    done(n)

            return inner

        lax.fori_loop(0, rows // strip, update, 0)
        return carry

    lax.fori_loop(0, 5, sweep, 0)


def sweep_kernel(e_ref, o_ref, flipped, gram, poly):
    sweep_all(lambda here: e_ref[here, :].astype(jnp.float32), o_ref, flipped, gram, poly)


def sweep_scratch(rows, cols):
    shapes = ((cols, rows), (cols, cols), (cols, cols))
    return [pltpu.VMEM(shape, jnp.bfloat16) for shape in shapes]


SWEEP_COST = dict(flops=55 * 10**9, bytes_accessed=8 * 2**20, transcendentals=0)


def sweeps(block):
    whole = pl.BlockSpec(memory_space=pltpu.VMEM)
    return pl.pallas_call(
        sweep_kernel,
        out_shape=jax.ShapeDtypeStruct(block.shape, jnp.bfloat16),
        in_specs=[whole],
        out_specs=whole,
        scratch_shapes=sweep_scratch(*block.shape),
        compiler_params=pltpu.CompilerParams(vmem_limit_bytes=63 * 2**20),
        cost_estimate=pl.CostEstimate(**SWEEP_COST),
        name="sweeps",
    )(block)


def sweep_return_kernel(
    widths, grad_ref, mom_ref, grad_hbm, rows_ref, ortho_ref, out, flipped, gram, poly,
    grad_ss, grad_rs, ortho_ss, ortho_rs, own_sem,
):
    dp, t = lax.axis_index("dp"), lax.axis_index("tensor")
    y, x = dp // 4, (dp // 2) % 2
    share, cols = rows_ref.shape[1:]
    barrier = pltpu.get_barrier_semaphore()
    for shift in range(1, 8):
        pl.semaphore_signal(barrier, inc=1, device_id=(lax.rem(dp + shift, 8), t), device_id_type=MESH)
    pl.semaphore_wait(barrier, 7)

    def of_width(fn):
        for width in sorted(set(widths)):
            mine = functools.reduce(jnp.logical_or, [dp == dev for dev, w in enumerate(widths) if w == width])

            @pl.when(mine)
            def _():
                fn(width)

    def pair(src, dst, peer, width, which, ss, rs):
        src = src.at[pl.ds(pl.multiple_of(peer * share, share), share), pl.ds(0, width)]
        dst = dst.at[dp, :, pl.ds(0, width)]
        far = pltpu.make_async_remote_copy(
            src_ref=src, dst_ref=dst, send_sem=ss.at[peer], recv_sem=rs.at[dp], device_id=(peer, t), device_id_type=MESH
        )
        return far, pltpu.make_async_copy(src, dst, own_sem.at[which])

    def start(src, dst, peer, which, ss, rs):
        def go(width):
            far, here = pair(src, dst, peer, width, which, ss, rs)

            @pl.when(peer != dp)
            def _():
                far.start()

            @pl.when(peer == dp)
            def _():
                here.start()

        of_width(go)

    def wait(src, dst, which, ss, rs):
        def go(width):
            for peer in range(8):
                far, here = pair(src, dst, peer, width, which, ss, rs)

                @pl.when(peer != dp)
                def _():
                    far.wait_send()

                @pl.when(peer == dp)
                def _():
                    here.wait()

        of_width(go)
        for dev, width in enumerate(widths):
            @pl.when(dev != dp)
            def _():
                seen = dst.at[dev, :, pl.ds(0, width)]
                pltpu.make_async_copy(seen, seen, rs.at[dev]).wait()

    def chip(n):
        px = x + ((3 - n) % 2) * (1 - 2 * x)
        py = y + ((3 - n) // 2) * (1 - 2 * y)
        return py * 2 + px

    def grad_start(n, carry):
        for core in range(2):
            start(grad_hbm, rows_ref, chip(n) * 2 + core, 0, grad_ss, grad_rs)
        return carry

    lax.fori_loop(0, 4, grad_start, 0)
    column = lax.broadcasted_iota(jnp.int32, (share, cols), 1)
    width = sum(jnp.where(dp == dev, w, 0) for dev, w in enumerate(widths))
    inside = column < width

    def load(here):
        grad, mom = grad_ref[here, :].astype(jnp.float32), mom_ref[here, :].astype(jnp.float32)
        return jnp.where(inside, grad + MOMENTUM * (MOMENTUM * mom + grad), 0.0)

    def done(strip):
        for core in range(2):
            start(out, ortho_ref, strip * 2 + core, 1, ortho_ss, ortho_rs)

    sweep_all(load, out, flipped, gram, poly, chip, done)
    wait(grad_hbm, rows_ref, 0, grad_ss, grad_rs)
    wait(out, ortho_ref, 1, ortho_ss, ortho_rs)


def sweep_return(grad_block, mom_block, share, widths):
    rows, cols = grad_block.shape
    whole, anyspec = pl.BlockSpec(memory_space=pltpu.VMEM), pl.BlockSpec(memory_space=pl.ANY)
    sems = pltpu.SemaphoreType.DMA((8,))
    return pl.pallas_call(
        functools.partial(sweep_return_kernel, widths),
        out_shape=[jax.ShapeDtypeStruct((rows // share, share, cols), jnp.bfloat16)] * 2,
        in_specs=[whole, whole, anyspec],
        out_specs=[anyspec] * 2,
        scratch_shapes=[pltpu.VMEM((rows, cols), jnp.bfloat16)]
        + sweep_scratch(rows, cols)
        + [sems] * 4
        + [pltpu.SemaphoreType.DMA((2,))],
        compiler_params=pltpu.CompilerParams(collective_id=2, has_side_effects=True, vmem_limit_bytes=63 * 2**20),
        cost_estimate=pl.CostEstimate(**SWEEP_COST),
        name="sweep_return",
    )(grad_block, mom_block, grad_block)


def update_kernel(places, width_of, *refs):
    n = len(width_of)
    w_refs, m_refs = refs[:n], refs[n : 2 * n]
    grad_ref, ortho_ref = refs[2 * n : 2 * n + 2]
    new_m, new_w = refs[2 * n + 2 : 3 * n + 2], refs[3 * n + 2 :]
    for dev, (m, head) in enumerate(places):
        width = width_of[m]
        cols = slice(head * width, (head + 1) * width)
        new_m[m][:, cols] = MOMENTUM * m_refs[m][:, cols] + grad_ref[dev, :, :width].astype(jnp.float32)
        ortho = ortho_ref[dev, :, :width].astype(jnp.float32)
        new_w[m][:, cols] = w_refs[m][:, cols] * (1.0 - LEARN * DECAY) - LEARN * ortho


def update_all(weights, moments, grad_rows, ortho_rows, places, width_of):
    rows = weights[0].shape[0]
    tile = 32
    flat = [pl.BlockSpec((tile, w.shape[1]), lambda i: (i, 0)) for w in weights]
    block = pl.BlockSpec((grad_rows.shape[0], tile, grad_rows.shape[2]), lambda i: (0, i, 0))
    out = pl.pallas_call(
        functools.partial(update_kernel, places, width_of),
        grid=(rows // tile,),
        out_shape=[jax.ShapeDtypeStruct(w.shape, w.dtype) for w in weights] * 2,
        in_specs=flat * 2 + [block] * 2,
        out_specs=flat * 2,
        compiler_params=pltpu.CompilerParams(vmem_limit_bytes=63 * 2**20),
        cost_estimate=pl.CostEstimate(flops=10**7, bytes_accessed=34 * 2**20, transcendentals=0),
        name="update_all",
    )(*weights, *moments, grad_rows, ortho_rows)
    return out[: len(weights)], out[len(weights) :]


def turn(part, table, sign):
    half = ROT // 2
    lane = lax.broadcasted_iota(jnp.int32, part.shape, 1)
    sines = pltpu.roll(table, 128 - ROT, 1)
    ahead = pltpu.roll(part, 128 - half, 1)
    back = pltpu.roll(part, half, 1)
    partner = jnp.where(lane < half, ahead, back)
    return jnp.where(lane < ROT, part * table + sign * (partner * sines), part)


def rotary_table(positions):
    half = ROT // 2
    inv_freq = 10000.0 ** (-2.0 * jnp.arange(half, dtype=jnp.float32) / ROT)
    angles = positions.astype(jnp.float32)[:, None] * inv_freq[None, :]
    cosine, sine = jnp.cos(angles), jnp.sin(angles)
    return jnp.concatenate([cosine, cosine, -sine, sine], axis=1)


def project_kernel(tok_ref, norm_ref, table_ref, start_ref, w_ref, ln_a_ref, ln_m_ref, qkv_ref, aux_ref):
    hidden = tok_ref[...].astype(jnp.float32)
    mean = jnp.mean(hidden, axis=-1, keepdims=True)
    centred = hidden - mean
    scale = lax.rsqrt(jnp.mean(centred * centred, axis=-1, keepdims=True) + LN_EPS)
    normed = centred * scale
    ln_a = (normed * norm_ref[0:1, :] + norm_ref[1:2, :]).astype(jnp.bfloat16)
    ln_a_ref[...] = ln_a
    ln_m_ref[...] = (normed * norm_ref[2:3, :] + norm_ref[3:4, :]).astype(jnp.bfloat16)
    lane = lax.broadcasted_iota(jnp.int32, aux_ref.shape, 1)
    aux_ref[...] = jnp.where(lane == 0, start_ref[:, 0:1], jnp.where(lane == 1, mean, scale))
    table = table_ref[...]
    for part in range(w_ref.shape[1] // HD):
        raw = wide_dot(ln_a, w_ref[:, part * HD : (part + 1) * HD], NN)
        if part % 3 < 2:
            raw = jnp.concatenate([turn(raw[:, :128], table, 1.0), raw[:, 128:]], axis=1)
        qkv_ref[:, part * HD : (part + 1) * HD] = raw.astype(jnp.bfloat16)


def project(tokens_all, norm_rows, table, start_col, full_qkv):
    seq, width = tokens_all.shape
    cols = full_qkv.shape[1]
    tile = 256
    row = lambda n: pl.BlockSpec((tile, n), lambda i: (i, 0))
    whole = lambda a, b: pl.BlockSpec((a, b), lambda i: (0, 0))
    return pl.pallas_call(
        project_kernel,
        grid=(seq // tile,),
        out_shape=[
            jax.ShapeDtypeStruct((seq, width), jnp.bfloat16),
            jax.ShapeDtypeStruct((seq, width), jnp.bfloat16),
            jax.ShapeDtypeStruct((seq, cols), jnp.bfloat16),
            jax.ShapeDtypeStruct((seq, 128), jnp.float32),
        ],
        in_specs=[row(width), whole(4, width), row(128), row(1), whole(width, cols)],
        out_specs=[row(width), row(width), row(cols), row(128)],
        compiler_params=pltpu.CompilerParams(vmem_limit_bytes=63 * 2**20),
        cost_estimate=pl.CostEstimate(flops=2 * seq * width * cols, bytes_accessed=20 * 2**20, transcendentals=0),
        name="project",
    )(tokens_all, norm_rows, table, start_col, full_qkv)


def soft_block(query, keys, start_col, first, offset):
    scores = wide_dot(query, keys, NT) * (HD ** (-0.5))
    rows, cols = scores.shape
    key_pos = first + lax.broadcasted_iota(jnp.int32, (rows, cols), 1)
    query_pos = offset + lax.broadcasted_iota(jnp.int32, (rows, cols), 0)
    seen = (key_pos.astype(jnp.float32) >= start_col) & (key_pos <= query_pos)
    scores = jnp.where(seen, scores, MASKED)
    peak = jnp.max(scores, axis=-1, keepdims=True)
    expo = jnp.exp(scores - peak)
    return expo / jnp.sum(expo, axis=-1, keepdims=True)


def reach_of(block, tile):
    return max(0, (block * tile - (DOC_MOST - 1)) // tile)


def attend_kernel(qkv_ref, start_ref, o_ref):
    tile = 256
    for head in range(o_ref.shape[1] // HD):
        col = head * 3 * HD
        for block in range(o_ref.shape[0] // tile):
            low, high = reach_of(block, tile) * tile, (block + 1) * tile
            here = slice(block * tile, high)
            prob = soft_block(
                qkv_ref[here, col : col + HD],
                qkv_ref[low:high, col + HD : col + 2 * HD],
                start_ref[here, 0:1],
                low,
                block * tile,
            ).astype(jnp.bfloat16)
            mixed = wide_dot(prob, qkv_ref[low:high, col + 2 * HD : col + 3 * HD], NN)
            o_ref[here, head * HD : (head + 1) * HD] = mixed.astype(jnp.bfloat16)


def attend(qkv, start_col):
    seq = qkv.shape[0]
    cols = qkv.shape[1] // 3
    whole = pl.BlockSpec(memory_space=pltpu.VMEM)
    return pl.pallas_call(
        attend_kernel,
        out_shape=jax.ShapeDtypeStruct((seq, cols), jnp.bfloat16),
        in_specs=[whole, whole],
        out_specs=whole,
        compiler_params=pltpu.CompilerParams(vmem_limit_bytes=63 * 2**20),
        cost_estimate=pl.CostEstimate(flops=6 * 10**9, bytes_accessed=4 * 2**20, transcendentals=2**20),
        name="attend",
    )(qkv, start_col)


def up_kernel(ln_ref, w_ref, act_ref, slope_ref):
    tile = 256
    for block in range(ln_ref.shape[0] // tile):
        here = slice(block * tile, (block + 1) * tile)
        up = wide_dot(ln_ref[here, :], w_ref[...], NN)
        below = 0.5 + 0.5 * lax.erf(up * (0.5**0.5))
        act_ref[here, :] = (up * below).astype(jnp.bfloat16)
        slope_ref[here, :] = (below + up * jnp.exp(-0.5 * up * up) * ((2.0 * math.pi) ** -0.5)).astype(jnp.bfloat16)


def up_branch(ln_mlp, full_up):
    seq, width = ln_mlp.shape
    units = full_up.shape[1]
    tile = min(512, units)
    out = jax.ShapeDtypeStruct((seq, units), jnp.bfloat16)
    return pl.pallas_call(
        up_kernel,
        grid=(units // tile,),
        out_shape=[out, out],
        in_specs=[pl.BlockSpec((seq, width), lambda i: (0, 0)), pl.BlockSpec((width, tile), lambda i: (0, i))],
        out_specs=[pl.BlockSpec((seq, tile), lambda i: (0, i))] * 2,
        compiler_params=pltpu.CompilerParams(vmem_limit_bytes=63 * 2**20),
        cost_estimate=pl.CostEstimate(flops=2 * seq * width * units, bytes_accessed=20 * 2**20, transcendentals=2 * seq * units),
        name="up_branch",
    )(ln_mlp, full_up)


def down_kernel(o_ref, act_ref, w_out_ref, w_down_ref, out_ref):
    tile = 256
    for block in range(o_ref.shape[0] // tile):
        here = slice(block * tile, (block + 1) * tile)
        total = wide_dot(o_ref[here, :], w_out_ref[...], NT) + wide_dot(act_ref[here, :], w_down_ref[...], NT)
        out_ref[here, :] = total.astype(jnp.bfloat16)


def down_branch(o, act, full_out, full_down):
    seq, units = act.shape
    width = full_down.shape[0]
    tile = 512
    return pl.pallas_call(
        down_kernel,
        grid=(width // tile,),
        out_shape=jax.ShapeDtypeStruct((seq, width), jnp.bfloat16),
        in_specs=[
            pl.BlockSpec(o.shape, lambda i: (0, 0)),
            pl.BlockSpec(act.shape, lambda i: (0, 0)),
            pl.BlockSpec((tile, o.shape[1]), lambda i: (i, 0)),
            pl.BlockSpec((tile, units), lambda i: (i, 0)),
        ],
        out_specs=pl.BlockSpec((seq, tile), lambda i: (0, i)),
        compiler_params=pltpu.CompilerParams(vmem_limit_bytes=63 * 2**20),
        cost_estimate=pl.CostEstimate(flops=2 * seq * width * (units + o.shape[1]), bytes_accessed=20 * 2**20, transcendentals=0),
        name="down_branch",
    )(o, act, full_out, full_down)


TN = (((0,), (0,)), ((), ()))


def attend_back_block(qkv_ref, start_ref, table_ref, d_o_ref, d_qkv_ref, d_key, d_value, head, block, last):
    tile = 256
    col = head * 3 * HD
    low, high = reach_of(block, tile) * tile, (block + 1) * tile
    here = slice(block * tile, high)
    query, keys = qkv_ref[here, col : col + HD], qkv_ref[low:high, col + HD : col + 2 * HD]
    values = qkv_ref[low:high, col + 2 * HD : col + 3 * HD]
    d_o = d_o_ref[here, head * HD : (head + 1) * HD]
    prob = soft_block(query, keys, start_ref[here, 0:1], low, block * tile)
    value_part = wide_dot(prob.astype(jnp.bfloat16), d_o, TN)
    d_prob = wide_dot(d_o, values, NT)
    weighted = prob * d_prob
    d_score = (weighted - prob * jnp.sum(weighted, axis=-1, keepdims=True)).astype(jnp.bfloat16)
    d_query = wide_dot(d_score, keys, NN) * (HD ** (-0.5))
    key_part = wide_dot(d_score, query, TN) * (HD ** (-0.5))
    d_query = jnp.concatenate([turn(d_query[:, :128], table_ref[here, :], -1.0), d_query[:, 128:]], axis=1)
    d_qkv_ref[here, col : col + HD] = d_query.astype(jnp.bfloat16)
    old = high - tile
    if low < old:
        d_key[low:old, :] += key_part[: old - low]
        d_value[low:old, :] += value_part[: old - low]
    d_key[old:high, :] = key_part[old - low :]
    d_value[old:high, :] = value_part[old - low :]
    ready_from = low
    ready_to = high if last else reach_of(block + 1, tile) * tile
    if ready_to > ready_from:
        done = slice(ready_from, ready_to)
        total = d_key[done, :]
        total = jnp.concatenate([turn(total[:, :128], table_ref[done, :], -1.0), total[:, 128:]], axis=1)
        d_qkv_ref[done, col + HD : col + 2 * HD] = total.astype(jnp.bfloat16)
        d_qkv_ref[done, col + 2 * HD : col + 3 * HD] = d_value[done, :].astype(jnp.bfloat16)


def attend_back_kernel(qkv_ref, start_ref, table_ref, d_o_ref, d_qkv_ref, d_key, d_value):
    blocks = qkv_ref.shape[0] // 256
    for head in range(d_o_ref.shape[1] // HD):
        for block in range(blocks):
            attend_back_block(qkv_ref, start_ref, table_ref, d_o_ref, d_qkv_ref, d_key, d_value, head, block, block == blocks - 1)


def attend_back(qkv, start_col, table, d_o):
    whole = pl.BlockSpec(memory_space=pltpu.VMEM)
    return pl.pallas_call(
        attend_back_kernel,
        out_shape=jax.ShapeDtypeStruct(qkv.shape, jnp.bfloat16),
        in_specs=[whole] * 4,
        out_specs=whole,
        scratch_shapes=[pltpu.VMEM((qkv.shape[0], HD), jnp.float32)] * 2,
        compiler_params=pltpu.CompilerParams(vmem_limit_bytes=63 * 2**20),
        cost_estimate=pl.CostEstimate(flops=12 * 10**9, bytes_accessed=10 * 2**20, transcendentals=2**20),
        name="attend_back",
    )(qkv, start_col, table, d_o)


def hand_out(block, row_share):
    parts = block.reshape(lax.axis_size("dp"), row_share, block.shape[1])
    return lax.all_to_all(parts, "dp", split_axis=0, concat_axis=0, tiled=True)


def from_owners(parts, owners, matrix, col_count, heads):
    own = [parts[owners.index((matrix, head)), :, :col_count] for head in range(heads)]
    return jnp.concatenate(own, axis=1).astype(jnp.float32)


def on_device(
    tokens,
    cotangent,
    segments,
    w_qkv,
    w_out,
    w_up,
    w_down,
    m_qkv,
    m_out,
    m_up,
    m_down,
    norm_gains,
    norm_biases,
    norm_moments,
):
    tensor_size = lax.axis_size("tensor")
    seq_len = tokens.shape[0] * tensor_size
    seg_ids = segments[0]
    local_heads = w_out.shape[1] // HD
    block_units = FF // HEADS
    row_share = w_qkv.shape[0]
    hidden_own = tokens.astype(jnp.float32)
    tokens_all, grad_all = (
        lax.all_gather(tokens, "tensor", axis=0, tiled=True),
        lax.all_gather(cotangent, "tensor", axis=0, tiled=True),
    )
    paired = lax.axis_size("dp") == 8 and local_heads == 2
    weights_in = (w_qkv, w_out, w_up, w_down)
    moments_in = (m_qkv, m_out, m_up, m_down)
    col_counts = (3 * HD, HD, block_units, block_units)
    pad_width = max(col_counts)
    positions = doc_positions(seg_ids)
    start_col = (jnp.arange(seq_len, dtype=jnp.int32) - positions)[:, None].astype(jnp.float32)
    table = rotary_table(positions)
    norm_rows = jnp.stack([norm_gains[0], norm_biases[0], norm_gains[1], norm_biases[1]])
    if paired:
        table, start_col, norm_rows, weights_in = lax.optimization_barrier((table, start_col, norm_rows, weights_in))
        (full_qkv, full_out, full_up, full_down), bundle = gather_all(weights_in, moments_in)
        mom_block = lax.all_to_all(bundle, "dp", split_axis=0, concat_axis=0, tiled=True)
        mom_block = mom_block.reshape(row_share * lax.axis_size("dp"), pad_width)
    else:
        full_qkv, full_out, full_up, full_down = (
            lax.all_gather(w.astype(jnp.bfloat16), "dp", axis=0, tiled=True) for w in weights_in
        )
    ln_attn, ln_mlp, packed, aux = project(tokens_all, norm_rows, table, start_col, full_qkv)
    mixed_heads = attend(packed, aux)
    activated, slope = up_branch(ln_mlp, full_up)
    branch = down_branch(mixed_heads, activated, full_out, full_down)
    grad_all, branch = lax.optimization_barrier((grad_all, branch))
    if paired:
        grad_all, mom_block = lax.optimization_barrier((grad_all, mom_block))
    branch_sum = lax.psum_scatter(branch, "tensor", scatter_dimension=0, tiled=True)
    if paired:
        block, mixed_grad, grad_norms = backward_all(
            grad_all, ln_mlp, ln_attn, activated, mixed_heads, slope, packed, aux, table, tokens_all, norm_rows,
            (full_qkv, full_out, full_up, full_down),
        )
        owners = owner_tables()
    else:
        grad_mixed = jnp.dot(grad_all, full_out, preferred_element_type=jnp.float32).astype(jnp.bfloat16)
        grad_packed = attend_back(packed, aux, table, grad_mixed)
        grad_act = jnp.dot(grad_all, full_down, preferred_element_type=jnp.float32)
        grad_upproj = (grad_act * slope.astype(jnp.float32)).astype(jnp.bfloat16)
        grad_ln_mlp = contract_cols(grad_upproj, full_up)
        grad_ln_attn = contract_cols(grad_packed, full_qkv)
        mixed_grad = (norm_gains[0] * grad_ln_attn + norm_gains[1] * grad_ln_mlp).astype(jnp.bfloat16)
        normed_all = (tokens_all.astype(jnp.float32) - aux[:, 1:2]) * aux[:, 2:3]
        sums = [grad_ln_attn * normed_all, grad_ln_attn, grad_ln_mlp * normed_all, grad_ln_mlp]
        grad_norms = lax.psum(jnp.stack([jnp.sum(v, axis=0) for v in sums]), ("dp", "tensor"))
        lefts = (ln_attn, grad_all, ln_mlp, grad_all)
        rights = (grad_packed, mixed_heads, grad_upproj, activated)
        reduced = tuple(
            lax.psum_scatter(
                contract_rows(l, r).astype(jnp.bfloat16), "dp", scatter_dimension=0, tiled=True
            ).astype(jnp.float32)
            for l, r in zip(lefts, rights)
        )
        new_moments = tuple(MOMENTUM * m + g for m, g in zip(moments_in, reduced))
        parts = []
        for fresh, grad_rows, col_count in zip(new_moments, reduced, col_counts):
            nested = (grad_rows + MOMENTUM * fresh).astype(jnp.bfloat16)
            for head in range(local_heads):
                part = nested[:, head * col_count : (head + 1) * col_count]
                parts.append(jnp.pad(part, ((0, 0), (0, pad_width - col_count))))
        groups = lax.axis_size("dp") // len(parts)
        outgoing = jnp.tile(jnp.stack(parts), (groups, 1, 1))
        block = lax.all_to_all(outgoing, "dp", split_axis=0, concat_axis=0, tiled=True)
        block = block.reshape(row_share * lax.axis_size("dp"), pad_width)
        owners = tuple((m, h) for m in range(4) for h in range(local_heads)) * groups
    mixed_own = lax.psum_scatter(mixed_grad, "tensor", scatter_dimension=0, tiled=True)
    block, branch_sum = lax.optimization_barrier((block, branch_sum))
    block_out = (hidden_own + branch_sum.astype(jnp.float32)).astype(jnp.bfloat16)
    if paired:
        grad_rows, ortho_rows = sweep_return(block, mom_block, row_share, tuple(col_counts[m] for m, _ in owners))
        mixed_own, ortho_rows = lax.optimization_barrier((mixed_own, ortho_rows))
        new_moments, new_weights = update_all(weights_in, moments_in, grad_rows, ortho_rows, owners, col_counts)
    else:
        ortho_rows = hand_out(sweeps(block), row_share)
        new_weights = [
            w * (1.0 - LEARN * DECAY) - LEARN * from_owners(ortho_rows, owners, i, col_counts[i], local_heads)
            for i, w in enumerate(weights_in)
        ]
    mixed_wide = mixed_own.astype(jnp.float32)
    mean_own = jnp.mean(hidden_own, axis=-1, keepdims=True)
    centred_own = hidden_own - mean_own
    rstd_own = lax.rsqrt(jnp.mean(centred_own * centred_own, axis=-1, keepdims=True) + LN_EPS)
    normed_own = centred_own * rstd_own
    grad_tokens = cotangent.astype(jnp.float32) + rstd_own * (
        mixed_wide
        - jnp.mean(mixed_wide, axis=-1, keepdims=True)
        - normed_own * jnp.mean(mixed_wide * normed_own, axis=-1, keepdims=True)
    )
    moment_norms = MOMENTUM * norm_moments + grad_norms
    step_scale = lax.rsqrt(jnp.mean(moment_norms * moment_norms, axis=-1, keepdims=True) + 1e-06)
    value_norms = norm_rows - NORM_LEARN * moment_norms * step_scale
    return (
        block_out,
        grad_tokens,
        new_moments[0],
        new_weights[0],
        new_moments[1],
        new_weights[1],
        new_moments[2],
        new_weights[2],
        new_moments[3],
        new_weights[3],
        moment_norms,
        value_norms,
    )


def solution(mesh):
    in_specs = (
        P(("dp", "tensor"), None),
        P(("dp", "tensor"), None),
        P("dp", None),
        P("dp", "tensor"),
        P("dp", "tensor"),
        P("dp", "tensor"),
        P("dp", "tensor"),
        P("dp", "tensor"),
        P("dp", "tensor"),
        P("dp", "tensor"),
        P("dp", "tensor"),
        P(),
        P(),
        P(),
    )
    out_specs = (
        P(("dp", "tensor"), None),
        P(("dp", "tensor"), None),
        P("dp", "tensor"),
        P("dp", "tensor"),
        P("dp", "tensor"),
        P("dp", "tensor"),
        P("dp", "tensor"),
        P("dp", "tensor"),
        P("dp", "tensor"),
        P("dp", "tensor"),
        P(),
        P(),
    )
    return jax.shard_map(
        on_device, mesh=mesh, in_specs=in_specs, out_specs=out_specs, check_vma=False
    )
```

```python
import functools
import math

import jax
import jax.numpy as jnp
from jax import lax
from jax.experimental import pallas as pl
from jax.experimental.pallas import tpu as pltpu
from jax.sharding import PartitionSpec as P

HEADS = 8
HD = 256
FF = 8192
ROT = 64
DOC_MOST = 512


NS_A = 3.4445
NS_B = -4.775
NS_C = 2.0315
MOMENTUM = 0.95
LEARN = 0.5
DECAY = 0.01
NORM_LEARN = 0.05
LN_EPS = 1e-05
MASKED = -1e30


def doc_positions(seg_ids):
    position_idx = jnp.arange(seg_ids.shape[0], dtype=jnp.int32)
    change = jnp.concatenate([jnp.ones((1,), dtype=jnp.bool_), seg_ids[1:] != seg_ids[:-1]])
    doc_start = lax.cummax(jnp.where(change, position_idx, jnp.zeros_like(position_idx)), axis=0)
    return position_idx - doc_start


def contract_rows(left, right):
    return lax.dot_general(
        left, right, (((0,), (0,)), ((), ())), preferred_element_type=jnp.float32
    )


def contract_cols(left, right):
    return lax.dot_general(
        left, right, (((1,), (1,)), ((), ())), preferred_element_type=jnp.float32
    )


MESH = pl.DeviceIdType.MESH


def forward_kernel(order, *refs):
    n_w = len(order)
    w_refs, m_refs = refs[:n_w], refs[n_w : 2 * n_w]
    tok_ref, cot_ref, norm_ref, table_ref, start_ref = refs[2 * n_w : 2 * n_w + 5]
    refs = refs[2 * n_w + 5 :]
    full_refs, mom_ref = refs[:n_w], refs[n_w]
    tok_all, cot_all, ln_a_ref, ln_m_ref, qkv_ref, aux_ref, o_ref, act_ref, slope_ref, branch_ref = refs[n_w + 1 : n_w + 11]
    refs = refs[n_w + 11 :]
    w_wide, w_low = refs[:n_w], refs[n_w : 2 * n_w]
    (m_low, tok, ln_a, ln_m, qkv, aux, o, act, slope, norm, table, first, w_qkv, w_out, w_up, w_down, branch,
     load_sem, own_sem, w_send, w_recv, m_send, m_recv, z_send, z_recv, side_sem, tok_sem, tile_sem, out_sem) = refs[2 * n_w :]
    dp, me, n_t = lax.axis_index("dp"), lax.axis_index("tensor"), lax.axis_size("tensor")
    y, x, c = dp // 4, (dp // 2) % 2, dp % 2
    by_x = y * 4 + (1 - x) * 2 + c
    by_y = (1 - y) * 4 + x * 2 + c
    far = (1 - y) * 4 + (1 - x) * 2 + c
    by_c = y * 4 + x * 2 + (1 - c)
    rows = w_refs[0].shape[0]
    half = rows // 2
    share = tok_ref.shape[0]
    seq, width = tok_all.shape
    loads = [pltpu.make_async_copy(w_refs[m], w_wide[m], load_sem.at[m]) for m in order]
    for cp in loads:
        cp.start()
    barrier = pltpu.get_barrier_semaphore()
    for peer in (by_x, by_y, by_c, far):
        pl.semaphore_signal(barrier, inc=1, device_id=(peer, me), device_id_type=MESH)
    for shift in range(1, n_t):
        pl.semaphore_signal(barrier, inc=1, device_id=(dp, lax.rem(me + shift, n_t)), device_id_type=MESH)
    pl.semaphore_wait(barrier, 4 + n_t - 1)

    def chain(kind, step, up):
        ref = (tok_all, cot_all)[kind]
        owner = me + 1 - step if up else me - 1 + step
        here = ref.at[pl.ds(pl.multiple_of(owner * share, share), share)]
        src = (tok_ref, cot_ref)[kind] if step == 1 else here
        return pltpu.make_async_remote_copy(
            src_ref=src, dst_ref=here, send_sem=z_send.at[kind, step, int(up)], recv_sem=z_recv.at[kind, step, int(up)],
            device_id=(dp, me + 1 if up else me - 1), device_id_type=MESH,
        )

    def chain_sends(step, up):
        return (me + 1 < n_t) & (me + 1 - step >= 0) if up else (me >= 1) & (me - 1 + step < n_t)

    def chain_gets(step, up):
        return me - step >= 0 if up else me + step < n_t

    def chain_start(kind, step):
        for up in (True, False):
            @pl.when(chain_sends(step, up))
            def _():
                chain(kind, step, up).start()

    def chain_take(kind, step):
        for up in (True, False):
            @pl.when(chain_gets(step, up))
            def _():
                chain(kind, step, up).wait_recv()

            if step + 1 < n_t:
                @pl.when(chain_sends(step + 1, up))
                def _():
                    chain(kind, step + 1, up).start()

    def part(i, dev, low, count):
        return full_refs[order[i]].at[pl.ds(pl.multiple_of(dev * rows + low, 128), count)]

    def copy(i, k):
        if k < 3:
            src, dst, peer = w_low[order[i]], part(i, dp, 0, rows), (by_x, by_y, by_c)[k]
        else:
            dev, low, count, peer = {
                3: (by_y, 0, half, by_x),
                4: (by_x, half, half, by_y),
                5: (by_x, 0, rows, by_c),
                6: (by_y, 0, rows, by_c),
                7: (far, 0, half, by_c),
                8: (far, half, half, by_c),
            }[k]
            src = dst = part(i, dev, low, count)
        return pltpu.make_async_remote_copy(
            src_ref=src, dst_ref=dst, send_sem=w_send.at[i, k], recv_sem=w_recv.at[i, k],
            device_id=(peer, me), device_id_type=MESH,
        )

    def own_start(i):
        for k in range(3):
            copy(i, k).start()

    def near_take(i):
        copy(i, 0).wait_recv()
        copy(i, 5).start()
        copy(i, 4).start()
        copy(i, 1).wait_recv()
        copy(i, 6).start()
        copy(i, 3).start()

    def far_take(i):
        for k in (3, 4):
            copy(i, k).wait_recv()
            copy(i, k + 4).start()

    def whole_take(i):
        for k in (2, 5, 6, 7, 8):
            copy(i, k).wait_recv()
        own[i].wait()

    def narrow(src, dst):
        def block(r, carry):
            here = pl.ds(pl.multiple_of(r * 32, 32), 32)
            dst[here, :] = src[here, :].astype(jnp.bfloat16)
            return carry

        lax.fori_loop(0, rows // 32, block, 0)

    own = [pltpu.make_async_copy(w_low[m], part(i, dp, 0, rows), own_sem.at[i]) for i, m in enumerate(order)]
    token_own = [
        pltpu.make_async_copy(a, b.at[pl.ds(pl.multiple_of(me * share, share), share)], own_sem.at[n_w + i])
        for i, (a, b) in enumerate(((tok_ref, tok_all), (cot_ref, cot_all)))
    ]
    chain_start(0, 1)
    for i, m in enumerate(order):
        loads[i].wait()
        narrow(w_wide[m], w_low[m])
        if i < 2:
            own_start(i)
        own[i].start()
    for cp in token_own:
        cp.start()
    sides = [
        pltpu.make_async_copy(a, b, side_sem.at[i])
        for i, (a, b) in enumerate(((norm_ref, norm), (table_ref, table), (start_ref, first)))
    ]
    for cp in sides:
        cp.start()
    loads = [pltpu.make_async_copy(m_refs[m], w_wide[m], load_sem.at[m]) for m in range(n_w)]
    for cp in loads:
        cp.start()
    for cp in loads:
        cp.wait()
    heads = w_refs[0].shape[1] // (3 * HD)
    wide_cols = w_refs[2].shape[1] // heads
    for dev, (m, head) in enumerate(owner_tables()):
        cols = w_refs[m].shape[1] // heads
        at = (dev % 2) * wide_cols
        narrow(w_wide[m].at[:, pl.ds(head * cols, cols)], m_low.at[dev // 2, :, pl.ds(at, cols)])

    def mom_copy(n):
        chip = ((y + n // 2) % 2) * 2 + (x + n) % 2
        return pltpu.make_async_remote_copy(
            src_ref=m_low.at[chip], dst_ref=mom_ref.at[y * 2 + x], send_sem=m_send.at[n], recv_sem=m_recv.at[n],
            device_id=(chip * 2 + c, me), device_id_type=MESH,
        )

    mom_own = pltpu.make_async_copy(m_low.at[y * 2 + x], mom_ref.at[y * 2 + x], m_send.at[0])
    mom_own.start()
    near_take(0)
    own_start(2)
    chain_take(0, 1)
    near_take(1)
    own_start(3)
    far_take(0)
    chain_take(0, 2)
    near_take(2)
    far_take(1)
    whole_take(0)
    load_qkv = pltpu.make_async_copy(full_refs[0], w_qkv, tile_sem.at[4])
    load_qkv.start()
    for step in range(3, n_t):
        chain_take(0, step)
    chain_start(1, 1)
    for cp in token_own + sides:
        cp.wait()
    tile = 256

    def tok_copy(r):
        return pltpu.make_async_copy(tok_all.at[pl.ds(pl.multiple_of(r * tile, tile), tile)], tok.at[r % 2], tok_sem.at[r % 2])

    tok_copy(jnp.int32(0)).start()
    load_qkv.wait()

    def project(r, carry):
        @pl.when(r + 1 < seq // tile)
        def _():
            tok_copy(r + 1).start()

        tok_copy(r).wait()
        here = pl.ds(pl.multiple_of(r * tile, tile), tile)
        hidden = tok[r % 2].astype(jnp.float32)
        mean = jnp.mean(hidden, axis=-1, keepdims=True)
        centred = hidden - mean
        scale = lax.rsqrt(jnp.mean(centred * centred, axis=-1, keepdims=True) + LN_EPS)
        normed = centred * scale
        ln = (normed * norm[0:1, :] + norm[1:2, :]).astype(jnp.bfloat16)
        ln_a[here, :] = ln
        ln_m[here, :] = (normed * norm[2:3, :] + norm[3:4, :]).astype(jnp.bfloat16)
        lane = lax.broadcasted_iota(jnp.int32, (tile, 128), 1)
        aux[here, :] = jnp.where(lane == 0, first[here, 0:1], jnp.where(lane == 1, mean, scale))
        angles = table[here, :]
        raw = wide_dot(ln, w_qkv[...], NN)
        for n in range(w_qkv.shape[1] // HD):
            block = raw[:, n * HD : (n + 1) * HD]
            if n % 3 < 2:
                block = jnp.concatenate([turn(block[:, :128], angles, 1.0), block[:, 128:]], axis=1)
            qkv[here, n * HD : (n + 1) * HD] = block.astype(jnp.bfloat16)
        return carry

    lax.fori_loop(0, seq // tile, project, 0)
    outs = []

    def put(src, dst):
        cp = pltpu.make_async_copy(src, dst, out_sem.at[len(outs)])
        cp.start()
        outs.append(cp)

    put(ln_a, ln_a_ref)
    put(ln_m, ln_m_ref)
    put(qkv, qkv_ref)
    put(aux, aux_ref)
    near_take(3)
    far_take(2)
    for n in range(1, 4):
        mom_copy(n).start()
    whole_take(1)
    strip = 512
    n_up = act.shape[1] // strip

    def up_copy(j):
        return pltpu.make_async_copy(full_refs[2].at[:, pl.ds(j * strip, strip)], w_up.at[j % 2], tile_sem.at[j % 2])

    def down_copy(j):
        return pltpu.make_async_copy(full_refs[3].at[pl.ds(j * strip, strip)], w_down.at[j % 2], tile_sem.at[2 + j % 2])

    up_copy(0).start()
    attend_kernel(qkv, aux, o)
    put(o, o_ref)
    for j in range(n_up):
        if j + 1 < n_up:
            up_copy(j + 1).start()
        up_copy(j).wait()
        cols = slice(j * strip, (j + 1) * strip)
        up_kernel(ln_m, w_up.at[j % 2], act.at[:, cols], slope.at[:, cols])
        if j == 0:
            chain_take(1, 1)
        if j == 1:
            far_take(3)
    put(act, act_ref)
    put(slope, slope_ref)
    whole_take(2)
    whole_take(3)
    load_out = pltpu.make_async_copy(full_refs[1], w_out, tile_sem.at[4])
    load_out.start()
    down_copy(0).start()
    load_out.wait()
    n_down = width // strip
    branch_copies = []
    for j in range(n_down):
        if j + 1 < n_down:
            down_copy(j + 1).start()
        down_copy(j).wait()
        if j >= 2:
            branch_copies[j - 2].wait()
        down_kernel(o, act, w_out.at[pl.ds(j * strip, strip)], w_down.at[j % 2], branch.at[j % 2])
        cp = pltpu.make_async_copy(branch.at[j % 2], branch_ref.at[:, pl.ds(j * strip, strip)], tok_sem.at[j % 2])
        cp.start()
        branch_copies.append(cp)
        if j == 1:
            chain_take(1, 2)
    for step in range(3, n_t):
        chain_take(1, step)
    for cp in branch_copies[-2:] + outs + [mom_own]:
        cp.wait()
    for i in range(n_w):
        for k in range(9):
            copy(i, k).wait_send()
    for n in range(1, 4):
        mom_copy(n).wait()
    for kind in range(2):
        for step in range(1, n_t):
            for up in (True, False):
                @pl.when(chain_sends(step, up))
                def _():
                    chain(kind, step, up).wait_send()


def forward_all(weights, moments, tokens, cotangent, norm_rows, table, start_col):
    n_w = len(weights)
    rows, bf, f32 = weights[0].shape[0], jnp.bfloat16, jnp.float32
    n_t = lax.axis_size("tensor")
    share, width = tokens.shape
    seq = share * n_t
    qkv_cols, out_cols, units = (weights[i].shape[1] for i in range(3))
    mom_cols = units // 2 + 3 * HD
    anyspec = pl.BlockSpec(memory_space=pl.ANY)
    V, S = pltpu.VMEM, pltpu.SemaphoreType.DMA
    array = jax.ShapeDtypeStruct
    out = pl.pallas_call(
        functools.partial(forward_kernel, (0, 2, 1, 3)),
        out_shape=[array((rows * 8, w.shape[1]), bf) for w in weights]
        + [array((4, rows, mom_cols), bf), array((seq, width), bf), array((seq, width), bf), array((seq, width), bf),
           array((seq, width), bf), array((seq, qkv_cols), bf), array((seq, 128), f32), array((seq, out_cols), bf),
           array((seq, units), bf), array((seq, units), bf), array((seq, width), bf)],
        in_specs=[anyspec] * (2 * n_w + 5),
        out_specs=[anyspec] * (n_w + 11),
        scratch_shapes=[V(w.shape, w.dtype) for w in weights]
        + [V(w.shape, bf) for w in weights]
        + [V((4, rows, mom_cols), bf), V((2, 256, width), bf), V((seq, width), bf), V((seq, width), bf),
           V((seq, qkv_cols), bf), V((seq, 128), f32), V((seq, out_cols), bf), V((seq, units), bf), V((seq, units), bf),
           V(norm_rows.shape, f32), V(table.shape, f32), V(start_col.shape, f32), V((width, qkv_cols), bf),
           V((width, out_cols), bf), V((2, width, 512), bf), V((2, 512, units), bf), V((2, seq, 512), bf),
           S((n_w,)), S((n_w + 2,)), S((n_w, 9)), S((n_w, 9)), S((4,)), S((4,)), S((2, n_t, 2)), S((2, n_t, 2)),
           S((3,)), S((2,)), S((5,)), S((7,))],
        compiler_params=pltpu.CompilerParams(collective_id=0, has_side_effects=True, vmem_limit_bytes=63 * 2**20),
        cost_estimate=pl.CostEstimate(flops=140 * 10**9, bytes_accessed=100 * 2**20, transcendentals=0),
        name="forward_all",
    )(*weights, *moments, tokens, cotangent, norm_rows, table, start_col)
    return out[:n_w], out[n_w:]


TILE = 256
STRIP = 512
SLOTS = 8
EVEN_STEPS, SHARED_STEPS, ALL_STEPS = 16, 20, 28


def owner_tables():
    return ((2, 0), (1, 0), (3, 0), (0, 0), (3, 1), (0, 1), (2, 1), (1, 1))


def backward_kernel(*refs):
    (dy_ref, ln_m_ref, ln_a_ref, act_ref, o_ref, slope_ref, qkv_ref, aux_ref, table_ref, tok_ref, norm_ref,
     w_down_ref, w_out_ref, w_up_ref, w_qkv_ref, mom_ref) = refs[:16]
    block_ref, grad_ref, u_ref, sums_ref = refs[16:20]
    (lhs, rhs, sib_send, own, sib_recv, far_x, far_y, in_x, in_y, far_send, x_send, y_send, mom, g_out, e_out,
     qkv, d_o, d_key, d_value, aux, table, w_tile, slope, row_q, row_u, tok, u_tile, norm, sums, z_in, z_sum, dp_in,
     lhs_sem, mom_sem, out_sem, keep_sem, give_ss, give_rs, sib_ss, sib_rs, fx_ss, fx_rs, fy_ss, fy_rs, x_ss, x_rs, y_ss, y_rs,
     side_sem, w_sem, slope_sem, row_sem, u_sem, z_ss, z_rs, d_ss, d_rs, sums_sem) = refs[20:]
    dp = lax.axis_index("dp")
    t = lax.axis_index("tensor")
    n_t = lax.axis_size("tensor")
    y, x, c = dp // 4, (dp // 2) % 2, dp % 2
    seq, width = dy_ref.shape
    units, heads_width = act_ref.shape[1], o_ref.shape[1]
    at_up, at_o, at_qkv = units, 2 * units, 2 * units + heads_width
    share = STRIP // 2
    half = share // 2
    strips = width // STRIP
    by_x = y * 4 + (1 - x) * 2 + c
    by_y = (1 - y) * 4 + x * 2 + c
    by_c = y * 4 + x * 2 + (1 - c)
    barrier = pltpu.get_barrier_semaphore()
    for shift in range(1, 8):
        pl.semaphore_signal(barrier, inc=1, device_id=(lax.rem(dp + shift, 8), t), device_id_type=MESH)
    for shift in range(1, n_t):
        pl.semaphore_signal(barrier, inc=1, device_id=(dp, lax.rem(t + shift, n_t)), device_id_type=MESH)

    def wide(v):
        return v.astype(jnp.float32)

    def low(v):
        return v.astype(jnp.bfloat16)

    def remote(src, dst, ss, rs, peer):
        return pltpu.make_async_remote_copy(src_ref=src, dst_ref=dst, send_sem=ss, recv_sem=rs, device_id=(peer, t), device_id_type=MESH)

    def local(src, dst, sem):
        return pltpu.make_async_copy(src, dst, sem)

    def outer(k):
        return (k < SHARED_STEPS) | (x != y)

    def inner(k):
        return (k < SHARED_STEPS) | (x == y)

    def place(k):
        step = jnp.where(k < EVEN_STEPS, k, k - EVEN_STEPS)
        return step % strips, step // strips

    def holder_slice(ref, k):
        strip, tile = place(k)
        col = jnp.where(k < EVEN_STEPS, 0, units // 2) + tile * TILE
        return ref.at[strip, :, pl.ds(pl.multiple_of(col, TILE), TILE)]

    def mom_copy(k):
        return local(holder_slice(mom_ref, k), mom.at[k % SLOTS], mom_sem.at[k % SLOTS])

    def grad_copy(k):
        return local(g_out.at[k % 2], holder_slice(grad_ref, k), keep_sem.at[k % 2])

    def out_copy(k):
        strip, tile = place(k)
        rows = pl.ds(pl.multiple_of(strip * STRIP + c * share, TILE), share)
        dst = block_ref.at[rows, pl.ds(pl.multiple_of(tile * TILE, TILE), TILE)]
        return local(e_out.at[k % 2], dst, out_sem.at[k % 2]), remote(e_out.at[k % 2], dst, give_ss.at[k % 2], give_rs, by_c)

    def keeps(k):
        return jnp.where(k < EVEN_STEPS, c == 0, c == 1)

    def out_start(k):
        here, there = out_copy(k)
        grad_copy(k).start()

        @pl.when(keeps(k))
        def _():
            here.start()

        @pl.when(jnp.logical_not(keeps(k)))
        def _():
            there.start()

    def out_wait(k):
        here, there = out_copy(k)
        grad_copy(k).wait()

        @pl.when(keeps(k))
        def _():
            here.wait()

        @pl.when(jnp.logical_not(keeps(k)))
        def _():
            there.wait_send()

    def sib_copy(k):
        return remote(sib_send.at[k % 2], sib_recv.at[k % SLOTS], sib_ss.at[k % 2], sib_rs.at[k % SLOTS], by_c)

    def far_copy_x(k):
        return remote(far_send.at[k % 2, pl.ds(0, half)], far_x.at[k % SLOTS], fx_ss.at[k % 2], fx_rs.at[k % SLOTS], by_x)

    def far_copy_y(k):
        return remote(far_send.at[k % 2, pl.ds(half, half)], far_y.at[k % SLOTS], fy_ss.at[k % 2], fy_rs.at[k % SLOTS], by_y)

    def copy_x(k):
        return remote(x_send.at[k % 2], in_x.at[k % SLOTS], x_ss.at[k % 2], x_rs.at[k % SLOTS], by_x)

    def copy_y(k):
        return remote(y_send.at[k % 2], in_y.at[k % SLOTS], y_ss.at[k % 2], y_rs.at[k % SLOTS], by_y)

    n_down, n_out = units // TILE, heads_width // TILE

    def down_cols(j):
        return pl.ds(pl.multiple_of((j % 2) * (units // 2) + (j // 2) * TILE, TILE), TILE)

    def w_start(j):
        @pl.when(j < n_down)
        def _():
            local(w_down_ref.at[:, down_cols(j)], w_tile.at[j % 2], w_sem.at[j % 2]).start()
            local(slope_ref.at[:, down_cols(j)], slope.at[j % 2], slope_sem.at[j % 2]).start()

        @pl.when(j >= n_down)
        def _():
            cols = pl.ds(pl.multiple_of((j - n_down) * TILE, TILE), TILE)
            local(w_out_ref.at[:, cols], w_tile.at[j % 2], w_sem.at[j % 2]).start()

    def row_copies(j):
        here = pl.ds(pl.multiple_of(j * TILE, TILE), TILE)
        slot = j % 2
        return (
            local(w_qkv_ref.at[here], row_q.at[slot], row_sem.at[slot, 0]),
            local(w_up_ref.at[here], row_u.at[slot], row_sem.at[slot, 1]),
            local(tok_ref.at[:, here], tok.at[slot], row_sem.at[slot, 2]),
        )

    def u_copy(j):
        return local(u_tile.at[j % 2], u_ref.at[:, pl.ds(pl.multiple_of(j * TILE, TILE), TILE)], u_sem.at[j % 2])

    lhs_copies = [local(ref, lhs.at[i], lhs_sem.at[i]) for i, ref in enumerate((dy_ref, ln_m_ref, ln_a_ref))]
    pairs = ((act_ref, rhs.at[:, pl.ds(0, units)]), (o_ref, rhs.at[:, pl.ds(at_o, heads_width)]), (qkv_ref, qkv),
             (aux_ref, aux), (table_ref, table), (norm_ref, norm))
    sides = [local(a, b, side_sem.at[i]) for i, (a, b) in enumerate(pairs)]
    lhs_copies[0].start()
    w_start(jnp.int32(0))
    w_start(jnp.int32(1))
    sides[0].start()
    lhs_copies[1].start()
    for cp in sides[1:]:
        cp.start()
    lhs_copies[2].start()
    sums[...] = jnp.zeros_like(sums)
    lhs_copies[0].wait()

    def made_by_dy(j):
        slot = j % 2
        local(w_out_ref.at[:, pl.ds(0, TILE)], w_tile.at[slot], w_sem.at[slot]).wait()

        @pl.when(j < n_down)
        def _():
            local(slope_ref.at[:, pl.ds(0, TILE)], slope.at[slot], slope_sem.at[slot]).wait()
            cols = pl.ds(pl.multiple_of(at_up + (j % 2) * (units // 2) + (j // 2) * TILE, TILE), TILE)
            for r in range(2):
                here = slice(r * (seq // 2), (r + 1) * (seq // 2))
                rhs[here, cols] = low(wide_dot(lhs[0, here, :], w_tile[slot], NN) * wide(slope[slot, here, :]))

        @pl.when(j >= n_down)
        def _():
            cols = pl.ds(pl.multiple_of((j - n_down) * TILE, TILE), TILE)
            for r in range(2):
                here = slice(r * (seq // 2), (r + 1) * (seq // 2))
                d_o[here, cols] = low(wide_dot(lhs[0, here, :], w_tile[slot], NN))

    def input_tile(j):
        slot = j % 2
        for cp in row_copies(j):
            cp.wait()

        @pl.when(j + 1 < width // TILE)
        def _():
            for cp in row_copies(j + 1):
                cp.start()

        @pl.when(j >= 2)
        def _():
            u_copy(j - 2).wait()

        cols = pl.ds(pl.multiple_of(j * TILE, TILE), TILE)
        gain_a, gain_m = norm[0:1, cols], norm[2:3, cols]

        total = jnp.zeros((4, TILE), jnp.float32)
        for r in range(2):
            here = slice(r * (seq // 2), (r + 1) * (seq // 2))
            by_a = wide_dot(rhs[here, pl.ds(at_qkv, qkv_ref.shape[1])], row_q[slot], NT)
            by_m = wide_dot(rhs[here, pl.ds(at_up, units)], row_u[slot], NT)
            normed = (wide(tok[slot, here, :]) - aux[here, 1:2]) * aux[here, 2:3]
            u_tile[slot, here, :] = low(gain_a * by_a + gain_m * by_m)
            parts = [jnp.sum(v, axis=0, keepdims=True) for v in (by_a * normed, by_a, by_m * normed, by_m)]
            total = total + jnp.concatenate(parts, axis=0)
        sums[:, cols] = total
        u_copy(j).start()

    def z_copy(shift):
        return pltpu.make_async_remote_copy(src_ref=sums, dst_ref=z_in.at[shift], send_sem=z_ss.at[shift], recv_sem=z_rs.at[shift], device_id=(dp, lax.rem(t + shift, n_t)), device_id_type=MESH)

    def dp_copy(shift):
        return remote(z_sum, dp_in.at[shift], d_ss.at[shift], d_rs.at[shift], lax.rem(dp + shift, 8))

    n_tiles = width // TILE
    n_blocks = seq // TILE
    first_attend = n_down + n_out - 2
    first_input = EVEN_STEPS + 1
    d_qkv = rhs.at[:, pl.ds(at_qkv, qkv_ref.shape[1])]

    made_by_dy(jnp.int32(0))
    made_by_dy(jnp.int32(1))
    w_start(jnp.int32(2))
    pl.semaphore_wait(barrier, 7 + n_t - 1)

    def step(i, carry):
        k1 = i
        k2 = i - 1
        k3 = i - 3
        k4 = i - 5

        @pl.when(k1 < ALL_STEPS)
        def _():
            @pl.when(k1 == 0)
            def _():
                sides[0].wait()
                lhs_copies[1].wait()

            @pl.when(k1 == EVEN_STEPS)
            def _():
                lhs_copies[2].wait()

            strip, tile = place(k1)

            @pl.when(k1 >= 2)
            def _():
                sib_copy(k1 - 2).wait_send()

            def piece(q):
                px = x + (q % 2) * (1 - 2 * x)
                py = y + (q // 2) * (1 - 2 * y)
                even = k1 < EVEN_STEPS
                plain = px == py
                which = jnp.where(even, jnp.where(plain, 1, 0), jnp.where(plain, 0, 2))
                col_even = jnp.where(plain, at_up, 0) + py * (units // 2) + tile * TILE
                col_odd = jnp.where(plain, at_o + py * TILE, at_qkv + py * (3 * HD) + tile * TILE)
                col = pl.multiple_of(jnp.where(even, col_even, col_odd), TILE)
                row = strip * STRIP
                right = rhs[:, pl.ds(col, TILE)]
                left = lhs[which, :, pl.ds(pl.multiple_of(row + (1 - c) * share, TILE), share)]
                sib_send[k1 % 2, q] = low(wide_dot(left, right, TN))
                left = lhs[which, :, pl.ds(pl.multiple_of(row + c * share, TILE), share)]
                own[k1 % SLOTS, q] = wide_dot(left, right, TN)

            @pl.when(k1 < SHARED_STEPS)
            def _():
                for q in range(4):
                    piece(q)

            @pl.when(k1 >= SHARED_STEPS)
            def _():
                piece(jnp.where(x == y, 1, 0))
                piece(jnp.where(x == y, 2, 3))

            sib_copy(k1).start()

        @pl.when((k2 >= 0) & (k2 < ALL_STEPS))
        def _():
            sib_copy(k2).wait_recv()

            @pl.when(outer(k2))
            def _():
                @pl.when(k2 >= 2)
                def _():
                    @pl.when(outer(k2 - 2))
                    def _():
                        far_copy_x(k2 - 2).wait_send()
                        far_copy_y(k2 - 2).wait_send()

                far_send[k2 % 2] = low(own[k2 % SLOTS, 3] + wide(sib_recv[k2 % SLOTS, 3]))
                far_copy_x(k2).start()
                far_copy_y(k2).start()

        @pl.when(i < n_down + n_out - 2)
        def _():
            made_by_dy(i + 2)

            @pl.when(i + 3 < n_down + n_out)
            def _():
                w_start(i + 3)

        for block in range(2 * n_blocks):
            @pl.when(i == block + first_attend)
            def _():
                if block == 0:
                    for cp in sides[1:]:
                        cp.wait()
                attend_back_block(qkv, aux, table, d_o, d_qkv, d_key, d_value, block // n_blocks, block % n_blocks, block % n_blocks == n_blocks - 1)

        @pl.when((k3 >= 0) & (k3 < ALL_STEPS) & inner(k3))
        def _():
            @pl.when(k3 >= 2)
            def _():
                @pl.when(inner(k3 - 2))
                def _():
                    copy_x(k3 - 2).wait_send()
                    copy_y(k3 - 2).wait_send()

            far_copy_x(k3).wait_recv()
            far_copy_y(k3).wait_recv()
            first, last = pl.ds(0, half), pl.ds(half, half)

            def chip_sum(q, part):
                return own[k3 % SLOTS, q, part] + wide(sib_recv[k3 % SLOTS, q, part])

            y_send[k3 % 2, first] = low(chip_sum(2, first) + wide(far_x[k3 % SLOTS]))
            y_send[k3 % 2, last] = low(chip_sum(2, last))
            copy_y(k3).start()
            x_send[k3 % 2, first] = low(chip_sum(1, first))
            x_send[k3 % 2, last] = low(chip_sum(1, last) + wide(far_y[k3 % SLOTS]))
            copy_x(k3).start()

        @pl.when((k3 >= 0) & (k3 < ALL_STEPS) & outer(k3))
        def _():
            mom_copy(k3).start()

        @pl.when(i == first_input - 1)
        def _():
            for cp in row_copies(0):
                cp.start()

        @pl.when((i >= first_input) & (i < first_input + n_tiles))
        def _():
            input_tile(i - first_input)

        @pl.when(i == first_input + n_tiles)
        def _():
            for shift in range(1, n_t):
                z_copy(shift).start()

        @pl.when(i == first_input + n_tiles + 2)
        def _():
            total = sums[...]
            for shift in range(1, n_t):
                z_copy(shift).wait_recv()
                total = total + z_in[shift]
            z_sum[...] = total
            for shift in range(1, 8):
                dp_copy(shift).start()

        @pl.when((k4 >= 0) & outer(k4))
        def _():
            @pl.when(k4 >= 2)
            def _():
                @pl.when(outer(k4 - 2))
                def _():
                    out_wait(k4 - 2)

            copy_x(k4).wait_recv()
            copy_y(k4).wait_recv()
            mom_copy(k4).wait()
            grad = own[k4 % SLOTS, 0] + wide(sib_recv[k4 % SLOTS, 0]) + wide(in_x[k4 % SLOTS]) + wide(in_y[k4 % SLOTS])
            g_out[k4 % 2] = low(grad)
            e_out[k4 % 2] = low(grad + MOMENTUM * (MOMENTUM * wide(mom[k4 % SLOTS]) + grad))
            out_start(k4)

        return carry

    lax.fori_loop(0, ALL_STEPS + 5, step, 0)
    for last, here, there in ((SHARED_STEPS, x == y, x != y), (ALL_STEPS, x != y, x == y)):
        for k in (last - 2, last - 1):
            k = jnp.int32(k)
            if last == ALL_STEPS:
                sib_copy(k).wait_send()

            @pl.when(here)
            def _():
                far_copy_x(k).wait_send()
                far_copy_y(k).wait_send()
                out_wait(k)

            @pl.when(there)
            def _():
                copy_x(k).wait_send()
                copy_y(k).wait_send()

    for odd in range(2):
        for apart in range(2):
            cols = (units // 2 if odd == 0 else (3 * HD if apart else HD))

            @pl.when((c == odd) & (jnp.where(x == y, 0, 1) == apart))
            def _():
                seen = block_ref.at[pl.ds(0, width // 2), pl.ds(0, cols)]
                local(seen, seen, give_rs).wait()

    total = z_sum[...]
    for shift in range(1, 8):
        dp_copy(shift).wait_recv()
        total = total + dp_in[shift]
    sums_out = local(z_in.at[0], sums_ref, sums_sem)
    z_in[0] = total
    sums_out.start()
    for shift in range(1, n_t):
        z_copy(shift).wait_send()
    for shift in range(1, 8):
        dp_copy(shift).wait_send()
    u_copy(n_tiles - 2).wait()
    u_copy(n_tiles - 1).wait()
    sums_out.wait()


def backward_all(dy, ln_m, ln_a, act, o, slope, qkv, aux, table, tok, norm_rows, full, mom):
    full_qkv, full_out, full_up, full_down = full
    seq, width = dy.shape
    n_t = lax.axis_size("tensor")
    anyspec = pl.BlockSpec(memory_space=pl.ANY)
    bf, f32 = jnp.bfloat16, jnp.float32
    V, S = pltpu.VMEM, pltpu.SemaphoreType.DMA
    rhs_width = 2 * act.shape[1] + o.shape[1] + qkv.shape[1]
    piece = (STRIP // 2, TILE)
    halved = (STRIP // 4, TILE)
    scratch = [
        V((3, seq, width), bf), V((seq, rhs_width), bf), V((2, 4, *piece), bf), V((SLOTS, 4, *piece), f32),
        V((SLOTS, 4, *piece), bf), V((SLOTS, *halved), bf), V((SLOTS, *halved), bf), V((SLOTS, *piece), bf),
        V((SLOTS, *piece), bf), V((2, *piece), bf), V((2, *piece), bf), V((2, *piece), bf), V((SLOTS, *piece), bf),
        V((2, *piece), bf), V((2, *piece), bf),
        V(qkv.shape, bf), V(o.shape, bf), V((seq, HD), f32), V((seq, HD), f32), V(aux.shape, f32), V(table.shape, f32),
        V((2, width, TILE), bf), V((2, seq, TILE), bf), V((2, TILE, qkv.shape[1]), bf), V((2, TILE, act.shape[1]), bf),
        V((2, seq, TILE), bf), V((2, seq, TILE), bf), V(norm_rows.shape, f32), V((4, width), f32), V((n_t, 4, width), f32),
        V((4, width), f32), V((8, 4, width), f32),
        S((3,)), S((SLOTS,)), S((2,)), S((2,)), S((2,)), S, S((2,)), S((SLOTS,)), S((2,)), S((SLOTS,)), S((2,)), S((SLOTS,)),
        S((2,)), S((SLOTS,)), S((2,)), S((SLOTS,)),
        S((6,)), S((2,)), S((2,)), S((2, 3)), S((2,)), S((n_t,)), S((n_t,)), S((8,)), S((8,)), S,
    ]
    block = jax.ShapeDtypeStruct((width, act.shape[1] // 2), bf)
    return pl.pallas_call(
        backward_kernel,
        out_shape=[block, jax.ShapeDtypeStruct(mom.shape, bf), jax.ShapeDtypeStruct((seq, width), bf), jax.ShapeDtypeStruct((4, width), f32)],
        in_specs=[anyspec] * 16,
        out_specs=[anyspec] * 4,
        scratch_shapes=scratch,
        compiler_params=pltpu.CompilerParams(collective_id=1, has_side_effects=True, vmem_limit_bytes=63 * 2**20),
        cost_estimate=pl.CostEstimate(flops=120 * 10**9, bytes_accessed=100 * 2**20, transcendentals=0),
        name="backward_all",
    )(dy, ln_m, ln_a, act, o, slope, qkv, aux, table, tok, norm_rows, full_down, full_out, full_up, full_qkv, mom)


NT = (((1,), (1,)), ((), ()))
NN = (((1,), (0,)), ((), ()))


def wide_dot(left, right, dims):
    return lax.dot_general(left, right, dims, preferred_element_type=jnp.float32)


def sweep_all(load, o_ref, flipped, gram, poly, strip_of=None, done=None):
    rows, cols = o_ref.shape
    tile, strip = 256, 512

    def squares(i, total):
        here = pl.ds(pl.multiple_of(i * tile, tile), tile)
        part = load(here).astype(jnp.bfloat16)
        o_ref[here, :] = part
        part = part.astype(jnp.float32)
        return total + jnp.sum((part * part).reshape(tile // 8, 8, cols), axis=0)

    total = jnp.sum(lax.fori_loop(0, rows // tile, squares, jnp.zeros((8, cols), jnp.float32)))
    scale = 1.0 / (jnp.sqrt(total) + 1e-07)
    for i in range(rows // tile):
        here = slice(i * tile, (i + 1) * tile)
        flipped[:, here] = (o_ref[here, :].astype(jnp.float32) * scale).T.astype(jnp.bfloat16)
    pairs = [(i, j) for i in range(cols // tile) for j in range(i, cols // tile)]

    def sweep(step, carry):
        for i, j in pairs:
            a, b = slice(i * tile, (i + 1) * tile), slice(j * tile, (j + 1) * tile)
            part = wide_dot(flipped[a, :], flipped[b, :], NT).astype(jnp.bfloat16)
            gram[a, b] = part
            if i != j:
                gram[b, a] = part.T
        for i, j in pairs:
            a, b = slice(i * tile, (i + 1) * tile), slice(j * tile, (j + 1) * tile)
            part = NS_B * gram[a, b].astype(jnp.float32) + NS_C * wide_dot(gram[a, :], gram[:, b], NN)
            part = part.astype(jnp.bfloat16)
            poly[a, b] = part
            if i != j:
                poly[b, a] = part.T

        def update(n, inner):
            n = n if strip_of is None else strip_of(n)
            part = pl.ds(pl.multiple_of(n * strip, strip), strip)
            old = flipped[:, part]
            for m in range(cols // strip):
                own = slice(m * strip, (m + 1) * strip)
                flipped[own, part] = (
                    NS_A * old[own].astype(jnp.float32) + wide_dot(poly[own, :], old, NN)
                ).astype(jnp.bfloat16)

            @pl.when(step == 4)
            def _():
                for r in range(strip // tile):
                    here = pl.ds(pl.multiple_of(n * strip + r * tile, tile), tile)
                    o_ref[here, :] = flipped[:, here].astype(jnp.float32).T.astype(jnp.bfloat16)
                if done is not None:
                    done(n)

            return inner

        lax.fori_loop(0, rows // strip, update, 0)
        return carry

    lax.fori_loop(0, 5, sweep, 0)


def sweep_kernel(e_ref, o_ref, flipped, gram, poly):
    sweep_all(lambda here: e_ref[here, :].astype(jnp.float32), o_ref, flipped, gram, poly)


def sweep_scratch(rows, cols):
    shapes = ((cols, rows), (cols, cols), (cols, cols))
    return [pltpu.VMEM(shape, jnp.bfloat16) for shape in shapes]


SWEEP_COST = dict(flops=55 * 10**9, bytes_accessed=8 * 2**20, transcendentals=0)


def sweeps(block):
    whole = pl.BlockSpec(memory_space=pltpu.VMEM)
    return pl.pallas_call(
        sweep_kernel,
        out_shape=jax.ShapeDtypeStruct(block.shape, jnp.bfloat16),
        in_specs=[whole],
        out_specs=whole,
        scratch_shapes=sweep_scratch(*block.shape),
        compiler_params=pltpu.CompilerParams(vmem_limit_bytes=63 * 2**20),
        cost_estimate=pl.CostEstimate(**SWEEP_COST),
        name="sweeps",
    )(block)


def sweep_return_kernel(
    widths, block_ref, grad_ref, rows_ref, ortho_ref, out, flipped, gram, poly,
    grad_ss, grad_rs, ortho_ss, ortho_rs, own_sem,
):
    dp, t = lax.axis_index("dp"), lax.axis_index("tensor")
    y, x, c = dp // 4, (dp // 2) % 2, dp % 2
    share, cols = ortho_ref.shape[1:]
    barrier = pltpu.get_barrier_semaphore()
    for shift in range(1, 8):
        pl.semaphore_signal(barrier, inc=1, device_id=(lax.rem(dp + shift, 8), t), device_id_type=MESH)
    pl.semaphore_wait(barrier, 7)

    def of_width(mine, fn):
        for width in sorted(set(mine)):
            here = functools.reduce(jnp.logical_or, [dp == dev for dev, w in enumerate(mine) if w == width])

            @pl.when(here)
            def _():
                fn(width)

    both = tuple(cols + widths[dev // 2 * 2 + 1] for dev in range(8))

    def grad_pair(chip, width):
        src, dst = grad_ref.at[chip, :, pl.ds(0, width)], rows_ref.at[y * 2 + x, :, pl.ds(0, width)]
        far = pltpu.make_async_remote_copy(
            src_ref=src, dst_ref=dst, send_sem=grad_ss.at[chip], recv_sem=grad_rs.at[y * 2 + x],
            device_id=(chip * 2 + c, t), device_id_type=MESH,
        )
        return far, pltpu.make_async_copy(src, dst, own_sem.at[0])

    def ortho_pair(peer, width):
        src = out.at[pl.ds(pl.multiple_of(peer * share, share), share), pl.ds(0, width)]
        dst = ortho_ref.at[dp, :, pl.ds(0, width)]
        far = pltpu.make_async_remote_copy(
            src_ref=src, dst_ref=dst, send_sem=ortho_ss.at[peer], recv_sem=ortho_rs.at[dp],
            device_id=(peer, t), device_id_type=MESH,
        )
        return far, pltpu.make_async_copy(src, dst, own_sem.at[1])

    def either(pair, away, start):
        far, here = pair

        @pl.when(away)
        def _():
            far.start() if start else far.wait_send()

        @pl.when(jnp.logical_not(away))
        def _():
            here.start() if start else here.wait()

    def chip_of(n):
        px = x + ((3 - n) % 2) * (1 - 2 * x)
        py = y + ((3 - n) // 2) * (1 - 2 * y)
        return py * 2 + px

    def grads(start):
        def go(width):
            for n in range(4):
                either(grad_pair(chip_of(n), width), n < 3, start)

        of_width(both, go)

    grads(True)
    width = sum(jnp.where(dp == dev, w, 0) for dev, w in enumerate(widths))
    inside = lax.broadcasted_iota(jnp.int32, (share, cols), 1) < width

    def load(here):
        return jnp.where(inside, block_ref[here, :].astype(jnp.float32), 0.0)

    def done(strip):
        for core in range(2):
            peer = strip * 2 + core
            of_width(widths, lambda width: either(ortho_pair(peer, width), peer != dp, True))

    sweep_all(load, out, flipped, gram, poly, chip_of, done)
    grads(False)
    for chip in range(4):
        @pl.when(chip != y * 2 + x)
        def _():
            seen = rows_ref.at[chip, :, pl.ds(0, both[2 * chip])]
            pltpu.make_async_copy(seen, seen, grad_rs.at[chip]).wait()

    def sent(width):
        for peer in range(8):
            either(ortho_pair(peer, width), peer != dp, False)

    of_width(widths, sent)
    for dev in range(8):
        @pl.when(dev != dp)
        def _():
            seen = ortho_ref.at[dev, :, pl.ds(0, widths[dev])]
            pltpu.make_async_copy(seen, seen, ortho_rs.at[dev]).wait()


def sweep_return(block, grad_half, widths):
    rows, cols = block.shape
    whole, anyspec = pl.BlockSpec(memory_space=pltpu.VMEM), pl.BlockSpec(memory_space=pl.ANY)
    four, eight = pltpu.SemaphoreType.DMA((4,)), pltpu.SemaphoreType.DMA((8,))
    return pl.pallas_call(
        functools.partial(sweep_return_kernel, widths),
        out_shape=[
            jax.ShapeDtypeStruct(grad_half.shape, jnp.bfloat16),
            jax.ShapeDtypeStruct((8, rows // 8, cols), jnp.bfloat16),
        ],
        in_specs=[whole, anyspec],
        out_specs=[anyspec] * 2,
        scratch_shapes=[pltpu.VMEM((rows, cols), jnp.bfloat16)]
        + sweep_scratch(rows, cols)
        + [four, four, eight, eight, pltpu.SemaphoreType.DMA((2,))],
        compiler_params=pltpu.CompilerParams(collective_id=2, has_side_effects=True, vmem_limit_bytes=63 * 2**20),
        cost_estimate=pl.CostEstimate(**SWEEP_COST),
        name="sweep_return",
    )(block, grad_half)


def update_kernel(places, width_of, *refs):
    n = len(width_of)
    w_refs, m_refs = refs[:n], refs[n : 2 * n]
    grad_ref, ortho_ref = refs[2 * n : 2 * n + 2]
    new_m, new_w = refs[2 * n + 2 : 3 * n + 2], refs[3 * n + 2 :]
    for dev, (m, head) in enumerate(places):
        width = width_of[m]
        cols = slice(head * width, (head + 1) * width)
        at = (dev % 2) * ortho_ref.shape[2]
        grad = grad_ref[dev // 2, :, at : at + width].astype(jnp.float32)
        new_m[m][:, cols] = MOMENTUM * m_refs[m][:, cols] + grad
        ortho = ortho_ref[dev, :, :width].astype(jnp.float32)
        new_w[m][:, cols] = w_refs[m][:, cols] * (1.0 - LEARN * DECAY) - LEARN * ortho


def update_all(weights, moments, grad_rows, ortho_rows, places, width_of):
    rows = weights[0].shape[0]
    tile = 32
    flat = [pl.BlockSpec((tile, w.shape[1]), lambda i: (i, 0)) for w in weights]
    block = lambda part: pl.BlockSpec((part.shape[0], tile, part.shape[2]), lambda i: (0, i, 0))
    out = pl.pallas_call(
        functools.partial(update_kernel, places, width_of),
        grid=(rows // tile,),
        out_shape=[jax.ShapeDtypeStruct(w.shape, w.dtype) for w in weights] * 2,
        in_specs=flat * 2 + [block(grad_rows), block(ortho_rows)],
        out_specs=flat * 2,
        compiler_params=pltpu.CompilerParams(vmem_limit_bytes=63 * 2**20),
        cost_estimate=pl.CostEstimate(flops=10**7, bytes_accessed=34 * 2**20, transcendentals=0),
        name="update_all",
    )(*weights, *moments, grad_rows, ortho_rows)
    return out[: len(weights)], out[len(weights) :]


def turn(part, table, sign):
    half = ROT // 2
    lane = lax.broadcasted_iota(jnp.int32, part.shape, 1)
    sines = pltpu.roll(table, 128 - ROT, 1)
    ahead = pltpu.roll(part, 128 - half, 1)
    back = pltpu.roll(part, half, 1)
    partner = jnp.where(lane < half, ahead, back)
    return jnp.where(lane < ROT, part * table + sign * (partner * sines), part)


def rotary_table(positions):
    half = ROT // 2
    inv_freq = 10000.0 ** (-2.0 * jnp.arange(half, dtype=jnp.float32) / ROT)
    angles = positions.astype(jnp.float32)[:, None] * inv_freq[None, :]
    cosine, sine = jnp.cos(angles), jnp.sin(angles)
    return jnp.concatenate([cosine, cosine, -sine, sine], axis=1)


def project_kernel(tok_ref, norm_ref, table_ref, start_ref, w_ref, ln_a_ref, ln_m_ref, qkv_ref, aux_ref):
    hidden = tok_ref[...].astype(jnp.float32)
    mean = jnp.mean(hidden, axis=-1, keepdims=True)
    centred = hidden - mean
    scale = lax.rsqrt(jnp.mean(centred * centred, axis=-1, keepdims=True) + LN_EPS)
    normed = centred * scale
    ln_a = (normed * norm_ref[0:1, :] + norm_ref[1:2, :]).astype(jnp.bfloat16)
    ln_a_ref[...] = ln_a
    ln_m_ref[...] = (normed * norm_ref[2:3, :] + norm_ref[3:4, :]).astype(jnp.bfloat16)
    lane = lax.broadcasted_iota(jnp.int32, aux_ref.shape, 1)
    aux_ref[...] = jnp.where(lane == 0, start_ref[:, 0:1], jnp.where(lane == 1, mean, scale))
    table = table_ref[...]
    for part in range(w_ref.shape[1] // HD):
        raw = wide_dot(ln_a, w_ref[:, part * HD : (part + 1) * HD], NN)
        if part % 3 < 2:
            raw = jnp.concatenate([turn(raw[:, :128], table, 1.0), raw[:, 128:]], axis=1)
        qkv_ref[:, part * HD : (part + 1) * HD] = raw.astype(jnp.bfloat16)


def project(tokens_all, norm_rows, table, start_col, full_qkv):
    seq, width = tokens_all.shape
    cols = full_qkv.shape[1]
    tile = 256
    row = lambda n: pl.BlockSpec((tile, n), lambda i: (i, 0))
    whole = lambda a, b: pl.BlockSpec((a, b), lambda i: (0, 0))
    return pl.pallas_call(
        project_kernel,
        grid=(seq // tile,),
        out_shape=[
            jax.ShapeDtypeStruct((seq, width), jnp.bfloat16),
            jax.ShapeDtypeStruct((seq, width), jnp.bfloat16),
            jax.ShapeDtypeStruct((seq, cols), jnp.bfloat16),
            jax.ShapeDtypeStruct((seq, 128), jnp.float32),
        ],
        in_specs=[row(width), whole(4, width), row(128), row(1), whole(width, cols)],
        out_specs=[row(width), row(width), row(cols), row(128)],
        compiler_params=pltpu.CompilerParams(vmem_limit_bytes=63 * 2**20),
        cost_estimate=pl.CostEstimate(flops=2 * seq * width * cols, bytes_accessed=20 * 2**20, transcendentals=0),
        name="project",
    )(tokens_all, norm_rows, table, start_col, full_qkv)


def soft_block(query, keys, start_col, first, offset):
    scores = wide_dot(query, keys, NT) * (HD ** (-0.5))
    rows, cols = scores.shape
    key_pos = first + lax.broadcasted_iota(jnp.int32, (rows, cols), 1)
    query_pos = offset + lax.broadcasted_iota(jnp.int32, (rows, cols), 0)
    seen = (key_pos.astype(jnp.float32) >= start_col) & (key_pos <= query_pos)
    scores = jnp.where(seen, scores, MASKED)
    peak = jnp.max(scores, axis=-1, keepdims=True)
    expo = jnp.exp(scores - peak)
    return expo / jnp.sum(expo, axis=-1, keepdims=True)


def reach_of(block, tile):
    return max(0, (block * tile - (DOC_MOST - 1)) // tile)


def attend_kernel(qkv_ref, start_ref, o_ref):
    tile = 256
    for head in range(o_ref.shape[1] // HD):
        col = head * 3 * HD
        for block in range(o_ref.shape[0] // tile):
            low, high = reach_of(block, tile) * tile, (block + 1) * tile
            here = slice(block * tile, high)
            prob = soft_block(
                qkv_ref[here, col : col + HD],
                qkv_ref[low:high, col + HD : col + 2 * HD],
                start_ref[here, 0:1],
                low,
                block * tile,
            ).astype(jnp.bfloat16)
            mixed = wide_dot(prob, qkv_ref[low:high, col + 2 * HD : col + 3 * HD], NN)
            o_ref[here, head * HD : (head + 1) * HD] = mixed.astype(jnp.bfloat16)


def attend(qkv, start_col):
    seq = qkv.shape[0]
    cols = qkv.shape[1] // 3
    whole = pl.BlockSpec(memory_space=pltpu.VMEM)
    return pl.pallas_call(
        attend_kernel,
        out_shape=jax.ShapeDtypeStruct((seq, cols), jnp.bfloat16),
        in_specs=[whole, whole],
        out_specs=whole,
        compiler_params=pltpu.CompilerParams(vmem_limit_bytes=63 * 2**20),
        cost_estimate=pl.CostEstimate(flops=6 * 10**9, bytes_accessed=4 * 2**20, transcendentals=2**20),
        name="attend",
    )(qkv, start_col)


def up_kernel(ln_ref, w_ref, act_ref, slope_ref):
    tile = 256
    for block in range(ln_ref.shape[0] // tile):
        here = slice(block * tile, (block + 1) * tile)
        up = wide_dot(ln_ref[here, :], w_ref[...], NN)
        below = 0.5 + 0.5 * lax.erf(up * (0.5**0.5))
        act_ref[here, :] = (up * below).astype(jnp.bfloat16)
        slope_ref[here, :] = (below + up * jnp.exp(-0.5 * up * up) * ((2.0 * math.pi) ** -0.5)).astype(jnp.bfloat16)


def up_branch(ln_mlp, full_up):
    seq, width = ln_mlp.shape
    units = full_up.shape[1]
    tile = min(512, units)
    out = jax.ShapeDtypeStruct((seq, units), jnp.bfloat16)
    return pl.pallas_call(
        up_kernel,
        grid=(units // tile,),
        out_shape=[out, out],
        in_specs=[pl.BlockSpec((seq, width), lambda i: (0, 0)), pl.BlockSpec((width, tile), lambda i: (0, i))],
        out_specs=[pl.BlockSpec((seq, tile), lambda i: (0, i))] * 2,
        compiler_params=pltpu.CompilerParams(vmem_limit_bytes=63 * 2**20),
        cost_estimate=pl.CostEstimate(flops=2 * seq * width * units, bytes_accessed=20 * 2**20, transcendentals=2 * seq * units),
        name="up_branch",
    )(ln_mlp, full_up)


def down_kernel(o_ref, act_ref, w_out_ref, w_down_ref, out_ref):
    tile = 256
    for block in range(o_ref.shape[0] // tile):
        here = slice(block * tile, (block + 1) * tile)
        total = wide_dot(o_ref[here, :], w_out_ref[...], NT) + wide_dot(act_ref[here, :], w_down_ref[...], NT)
        out_ref[here, :] = total.astype(jnp.bfloat16)


def down_branch(o, act, full_out, full_down):
    seq, units = act.shape
    width = full_down.shape[0]
    tile = 512
    return pl.pallas_call(
        down_kernel,
        grid=(width // tile,),
        out_shape=jax.ShapeDtypeStruct((seq, width), jnp.bfloat16),
        in_specs=[
            pl.BlockSpec(o.shape, lambda i: (0, 0)),
            pl.BlockSpec(act.shape, lambda i: (0, 0)),
            pl.BlockSpec((tile, o.shape[1]), lambda i: (i, 0)),
            pl.BlockSpec((tile, units), lambda i: (i, 0)),
        ],
        out_specs=pl.BlockSpec((seq, tile), lambda i: (0, i)),
        compiler_params=pltpu.CompilerParams(vmem_limit_bytes=63 * 2**20),
        cost_estimate=pl.CostEstimate(flops=2 * seq * width * (units + o.shape[1]), bytes_accessed=20 * 2**20, transcendentals=0),
        name="down_branch",
    )(o, act, full_out, full_down)


TN = (((0,), (0,)), ((), ()))


def attend_back_block(qkv_ref, start_ref, table_ref, d_o_ref, d_qkv_ref, d_key, d_value, head, block, last):
    tile = 256
    col = head * 3 * HD
    low, high = reach_of(block, tile) * tile, (block + 1) * tile
    here = slice(block * tile, high)
    query, keys = qkv_ref[here, col : col + HD], qkv_ref[low:high, col + HD : col + 2 * HD]
    values = qkv_ref[low:high, col + 2 * HD : col + 3 * HD]
    d_o = d_o_ref[here, head * HD : (head + 1) * HD]
    prob = soft_block(query, keys, start_ref[here, 0:1], low, block * tile)
    value_part = wide_dot(prob.astype(jnp.bfloat16), d_o, TN)
    d_prob = wide_dot(d_o, values, NT)
    weighted = prob * d_prob
    d_score = (weighted - prob * jnp.sum(weighted, axis=-1, keepdims=True)).astype(jnp.bfloat16)
    d_query = wide_dot(d_score, keys, NN) * (HD ** (-0.5))
    key_part = wide_dot(d_score, query, TN) * (HD ** (-0.5))
    d_query = jnp.concatenate([turn(d_query[:, :128], table_ref[here, :], -1.0), d_query[:, 128:]], axis=1)
    d_qkv_ref[here, col : col + HD] = d_query.astype(jnp.bfloat16)
    old = high - tile
    if low < old:
        d_key[low:old, :] += key_part[: old - low]
        d_value[low:old, :] += value_part[: old - low]
    d_key[old:high, :] = key_part[old - low :]
    d_value[old:high, :] = value_part[old - low :]
    ready_from = low
    ready_to = high if last else reach_of(block + 1, tile) * tile
    if ready_to > ready_from:
        done = slice(ready_from, ready_to)
        total = d_key[done, :]
        total = jnp.concatenate([turn(total[:, :128], table_ref[done, :], -1.0), total[:, 128:]], axis=1)
        d_qkv_ref[done, col + HD : col + 2 * HD] = total.astype(jnp.bfloat16)
        d_qkv_ref[done, col + 2 * HD : col + 3 * HD] = d_value[done, :].astype(jnp.bfloat16)


def attend_back_kernel(qkv_ref, start_ref, table_ref, d_o_ref, d_qkv_ref, d_key, d_value):
    blocks = qkv_ref.shape[0] // 256
    for head in range(d_o_ref.shape[1] // HD):
        for block in range(blocks):
            attend_back_block(qkv_ref, start_ref, table_ref, d_o_ref, d_qkv_ref, d_key, d_value, head, block, block == blocks - 1)


def attend_back(qkv, start_col, table, d_o):
    whole = pl.BlockSpec(memory_space=pltpu.VMEM)
    return pl.pallas_call(
        attend_back_kernel,
        out_shape=jax.ShapeDtypeStruct(qkv.shape, jnp.bfloat16),
        in_specs=[whole] * 4,
        out_specs=whole,
        scratch_shapes=[pltpu.VMEM((qkv.shape[0], HD), jnp.float32)] * 2,
        compiler_params=pltpu.CompilerParams(vmem_limit_bytes=63 * 2**20),
        cost_estimate=pl.CostEstimate(flops=12 * 10**9, bytes_accessed=10 * 2**20, transcendentals=2**20),
        name="attend_back",
    )(qkv, start_col, table, d_o)


def hand_out(block, row_share):
    parts = block.reshape(lax.axis_size("dp"), row_share, block.shape[1])
    return lax.all_to_all(parts, "dp", split_axis=0, concat_axis=0, tiled=True)


def from_owners(parts, owners, matrix, col_count, heads):
    own = [parts[owners.index((matrix, head)), :, :col_count] for head in range(heads)]
    return jnp.concatenate(own, axis=1).astype(jnp.float32)


def on_device(
    tokens,
    cotangent,
    segments,
    w_qkv,
    w_out,
    w_up,
    w_down,
    m_qkv,
    m_out,
    m_up,
    m_down,
    norm_gains,
    norm_biases,
    norm_moments,
):
    tensor_size = lax.axis_size("tensor")
    seq_len = tokens.shape[0] * tensor_size
    seg_ids = segments[0]
    local_heads = w_out.shape[1] // HD
    block_units = FF // HEADS
    row_share = w_qkv.shape[0]
    hidden_own = tokens.astype(jnp.float32)
    paired = lax.axis_size("dp") == 8 and local_heads == 2
    weights_in = (w_qkv, w_out, w_up, w_down)
    moments_in = (m_qkv, m_out, m_up, m_down)
    col_counts = (3 * HD, HD, block_units, block_units)
    pad_width = max(col_counts)
    positions = doc_positions(seg_ids)
    start_col = (jnp.arange(seq_len, dtype=jnp.int32) - positions)[:, None].astype(jnp.float32)
    table = rotary_table(positions)
    norm_rows = jnp.stack([norm_gains[0], norm_biases[0], norm_gains[1], norm_biases[1]])
    if paired:
        start_cols = jnp.broadcast_to(start_col, (seq_len, 128))
        (full_qkv, full_out, full_up, full_down), rest = forward_all(
            weights_in, moments_in, tokens, cotangent, norm_rows, table, start_cols
        )
        mom_half, tokens_all, grad_all, ln_attn, ln_mlp, packed, aux, mixed_heads, activated, slope, branch = rest
    else:
        tokens_all, grad_all = (
            lax.all_gather(tokens, "tensor", axis=0, tiled=True),
            lax.all_gather(cotangent, "tensor", axis=0, tiled=True),
        )
        full_qkv, full_out, full_up, full_down = (
            lax.all_gather(w.astype(jnp.bfloat16), "dp", axis=0, tiled=True) for w in weights_in
        )
        ln_attn, ln_mlp, packed, aux = project(tokens_all, norm_rows, table, start_col, full_qkv)
        mixed_heads = attend(packed, aux)
        activated, slope = up_branch(ln_mlp, full_up)
        branch = down_branch(mixed_heads, activated, full_out, full_down)
    branch_sum = lax.psum_scatter(branch, "tensor", scatter_dimension=0, tiled=True)
    if paired:
        block, grad_half, mixed_grad, grad_norms = backward_all(
            grad_all, ln_mlp, ln_attn, activated, mixed_heads, slope, packed, aux, table, tokens_all, norm_rows,
            (full_qkv, full_out, full_up, full_down), mom_half,
        )
        owners = owner_tables()
    else:
        grad_mixed = jnp.dot(grad_all, full_out, preferred_element_type=jnp.float32).astype(jnp.bfloat16)
        grad_packed = attend_back(packed, aux, table, grad_mixed)
        grad_act = jnp.dot(grad_all, full_down, preferred_element_type=jnp.float32)
        grad_upproj = (grad_act * slope.astype(jnp.float32)).astype(jnp.bfloat16)
        grad_ln_mlp = contract_cols(grad_upproj, full_up)
        grad_ln_attn = contract_cols(grad_packed, full_qkv)
        mixed_grad = (norm_gains[0] * grad_ln_attn + norm_gains[1] * grad_ln_mlp).astype(jnp.bfloat16)
        normed_all = (tokens_all.astype(jnp.float32) - aux[:, 1:2]) * aux[:, 2:3]
        sums = [grad_ln_attn * normed_all, grad_ln_attn, grad_ln_mlp * normed_all, grad_ln_mlp]
        grad_norms = lax.psum(jnp.stack([jnp.sum(v, axis=0) for v in sums]), ("dp", "tensor"))
        lefts = (ln_attn, grad_all, ln_mlp, grad_all)
        rights = (grad_packed, mixed_heads, grad_upproj, activated)
        reduced = tuple(
            lax.psum_scatter(
                contract_rows(l, r).astype(jnp.bfloat16), "dp", scatter_dimension=0, tiled=True
            ).astype(jnp.float32)
            for l, r in zip(lefts, rights)
        )
        new_moments = tuple(MOMENTUM * m + g for m, g in zip(moments_in, reduced))
        parts = []
        for fresh, grad_rows, col_count in zip(new_moments, reduced, col_counts):
            nested = (grad_rows + MOMENTUM * fresh).astype(jnp.bfloat16)
            for head in range(local_heads):
                part = nested[:, head * col_count : (head + 1) * col_count]
                parts.append(jnp.pad(part, ((0, 0), (0, pad_width - col_count))))
        groups = lax.axis_size("dp") // len(parts)
        outgoing = jnp.tile(jnp.stack(parts), (groups, 1, 1))
        block = lax.all_to_all(outgoing, "dp", split_axis=0, concat_axis=0, tiled=True)
        block = block.reshape(row_share * lax.axis_size("dp"), pad_width)
        owners = tuple((m, h) for m in range(4) for h in range(local_heads)) * groups
    mixed_own = lax.psum_scatter(mixed_grad, "tensor", scatter_dimension=0, tiled=True)
    block, branch_sum = lax.optimization_barrier((block, branch_sum))
    block_out = (hidden_own + branch_sum.astype(jnp.float32)).astype(jnp.bfloat16)
    if paired:
        grad_rows, ortho_rows = sweep_return(block, grad_half, tuple(col_counts[m] for m, _ in owners))
        mixed_own, ortho_rows = lax.optimization_barrier((mixed_own, ortho_rows))
        new_moments, new_weights = update_all(weights_in, moments_in, grad_rows, ortho_rows, owners, col_counts)
    else:
        ortho_rows = hand_out(sweeps(block), row_share)
        new_weights = [
            w * (1.0 - LEARN * DECAY) - LEARN * from_owners(ortho_rows, owners, i, col_counts[i], local_heads)
            for i, w in enumerate(weights_in)
        ]
    mixed_wide = mixed_own.astype(jnp.float32)
    mean_own = jnp.mean(hidden_own, axis=-1, keepdims=True)
    centred_own = hidden_own - mean_own
    rstd_own = lax.rsqrt(jnp.mean(centred_own * centred_own, axis=-1, keepdims=True) + LN_EPS)
    normed_own = centred_own * rstd_own
    grad_tokens = cotangent.astype(jnp.float32) + rstd_own * (
        mixed_wide
        - jnp.mean(mixed_wide, axis=-1, keepdims=True)
        - normed_own * jnp.mean(mixed_wide * normed_own, axis=-1, keepdims=True)
    )
    moment_norms = MOMENTUM * norm_moments + grad_norms
    step_scale = lax.rsqrt(jnp.mean(moment_norms * moment_norms, axis=-1, keepdims=True) + 1e-06)
    value_norms = norm_rows - NORM_LEARN * moment_norms * step_scale
    return (
        block_out,
        grad_tokens,
        new_moments[0],
        new_weights[0],
        new_moments[1],
        new_weights[1],
        new_moments[2],
        new_weights[2],
        new_moments[3],
        new_weights[3],
        moment_norms,
        value_norms,
    )


def solution(mesh):
    in_specs = (
        P(("dp", "tensor"), None),
        P(("dp", "tensor"), None),
        P("dp", None),
        P("dp", "tensor"),
        P("dp", "tensor"),
        P("dp", "tensor"),
        P("dp", "tensor"),
        P("dp", "tensor"),
        P("dp", "tensor"),
        P("dp", "tensor"),
        P("dp", "tensor"),
        P(),
        P(),
        P(),
    )
    out_specs = (
        P(("dp", "tensor"), None),
        P(("dp", "tensor"), None),
        P("dp", "tensor"),
        P("dp", "tensor"),
        P("dp", "tensor"),
        P("dp", "tensor"),
        P("dp", "tensor"),
        P("dp", "tensor"),
        P("dp", "tensor"),
        P("dp", "tensor"),
        P(),
        P(),
    )
    return jax.shard_map(
        on_device, mesh=mesh, in_specs=in_specs, out_specs=out_specs, check_vma=False
    )
```

```python
import functools
import math

import jax
import jax.numpy as jnp
import numpy as np
from jax import lax
from jax.experimental import pallas as pl
from jax.experimental.pallas import tpu as pltpu
from jax.sharding import PartitionSpec as P

HEADS = 8
HD = 256
FF = 8192
ROT = 64
DOC_MOST = 512


NS_A = 3.4445
NS_B = -4.775
NS_C = 2.0315
MOMENTUM = 0.95
LEARN = 0.5
DECAY = 0.01
NORM_LEARN = 0.05
LN_EPS = 1e-05
MASKED = -1e30


def doc_starts(seg_ids):
    index = jnp.arange(seg_ids.shape[0], dtype=jnp.int32)
    same = seg_ids[:, None] == seg_ids[None, :]
    return jnp.min(jnp.where(same, index[None, :], seg_ids.shape[0]), axis=1)


def contract_rows(left, right):
    return lax.dot_general(
        left, right, (((0,), (0,)), ((), ())), preferred_element_type=jnp.float32
    )


def contract_cols(left, right):
    return lax.dot_general(
        left, right, (((1,), (1,)), ((), ())), preferred_element_type=jnp.float32
    )


MESH = pl.DeviceIdType.MESH


def forward_kernel(order, *refs):
    n_w = len(order)
    w_refs, m_refs = refs[:n_w], refs[n_w : 2 * n_w]
    tok_ref, cot_ref, gain_ref, bias_ref, seg_ref, freq_ref = refs[2 * n_w : 2 * n_w + 6]
    refs = refs[2 * n_w + 6 :]
    full_refs, mom_ref = refs[:n_w], refs[n_w]
    tok_all, cot_all, ln_a_ref, ln_m_ref, qkv_ref, aux_ref, table_ref, o_ref, act_ref, slope_ref, branch_ref = refs[
        n_w + 1 : n_w + 12
    ]
    refs = refs[n_w + 12 :]
    w_wide, w_low = refs[:n_w], refs[n_w : 2 * n_w]
    (m_low, tok, ln_a, ln_m, qkv, aux, table, o, act, slope, gains, biases, segs, freq, w_qkv, w_out, w_up, w_down, branch,
     load_sem, own_sem, w_send, w_recv, m_send, m_recv, z_send, z_recv, side_sem, tok_sem, tile_sem, out_sem) = refs[2 * n_w :]
    dp, me, n_t = lax.axis_index("dp"), lax.axis_index("tensor"), lax.axis_size("tensor")
    y, x, c = dp // 4, (dp // 2) % 2, dp % 2
    by_x = y * 4 + (1 - x) * 2 + c
    by_y = (1 - y) * 4 + x * 2 + c
    far = (1 - y) * 4 + (1 - x) * 2 + c
    by_c = y * 4 + x * 2 + (1 - c)
    rows = w_refs[0].shape[0]
    half = rows // 2
    share = tok_ref.shape[0]
    seq, width = tok_all.shape
    loads = [pltpu.make_async_copy(w_refs[m], w_wide[m], load_sem.at[m]) for m in order]
    for cp in loads:
        cp.start()
    barrier = pltpu.get_barrier_semaphore()
    for peer in (by_x, by_y, by_c, far):
        pl.semaphore_signal(barrier, inc=1, device_id=(peer, me), device_id_type=MESH)
    for shift in range(1, n_t):
        pl.semaphore_signal(barrier, inc=1, device_id=(dp, lax.rem(me + shift, n_t)), device_id_type=MESH)
    pl.semaphore_wait(barrier, 4 + n_t - 1)

    def chain(kind, step, up):
        ref = (tok_all, cot_all)[kind]
        owner = me + 1 - step if up else me - 1 + step
        here = ref.at[pl.ds(pl.multiple_of(owner * share, share), share)]
        src = (tok_ref, cot_ref)[kind] if step == 1 else here
        return pltpu.make_async_remote_copy(
            src_ref=src, dst_ref=here, send_sem=z_send.at[kind, step, int(up)], recv_sem=z_recv.at[kind, step, int(up)],
            device_id=(dp, me + 1 if up else me - 1), device_id_type=MESH,
        )

    def chain_sends(step, up):
        return (me + 1 < n_t) & (me + 1 - step >= 0) if up else (me >= 1) & (me - 1 + step < n_t)

    def chain_gets(step, up):
        return me - step >= 0 if up else me + step < n_t

    def chain_start(kind, step):
        for up in (True, False):
            @pl.when(chain_sends(step, up))
            def _():
                chain(kind, step, up).start()

    def chain_take(kind, step):
        for up in (True, False):
            @pl.when(chain_gets(step, up))
            def _():
                chain(kind, step, up).wait_recv()

            if step + 1 < n_t:
                @pl.when(chain_sends(step + 1, up))
                def _():
                    chain(kind, step + 1, up).start()

    def part(i, dev, low, count):
        return full_refs[order[i]].at[pl.ds(pl.multiple_of(dev * rows + low, 128), count)]

    def copy(i, k):
        if k < 3:
            src, dst, peer = w_low[order[i]], part(i, dp, 0, rows), (by_x, by_y, by_c)[k]
        else:
            dev, low, count, peer = {
                3: (by_y, 0, half, by_x),
                4: (by_x, half, half, by_y),
                5: (by_x, 0, rows, by_c),
                6: (by_y, 0, rows, by_c),
                7: (far, 0, half, by_c),
                8: (far, half, half, by_c),
            }[k]
            src = dst = part(i, dev, low, count)
        return pltpu.make_async_remote_copy(
            src_ref=src, dst_ref=dst, send_sem=w_send.at[i, k], recv_sem=w_recv.at[i, k],
            device_id=(peer, me), device_id_type=MESH,
        )

    def own_start(i):
        for k in range(3):
            copy(i, k).start()

    def near_take(i):
        copy(i, 0).wait_recv()
        copy(i, 5).start()
        copy(i, 4).start()
        copy(i, 1).wait_recv()
        copy(i, 6).start()
        copy(i, 3).start()

    def far_take(i):
        for k in (3, 4):
            copy(i, k).wait_recv()
            copy(i, k + 4).start()

    def whole_take(i):
        for k in (2, 5, 6, 7, 8):
            copy(i, k).wait_recv()
        own[i].wait()

    def narrow(src, dst):
        def block(r, carry):
            here = pl.ds(pl.multiple_of(r * 32, 32), 32)
            dst[here, :] = src[here, :].astype(jnp.bfloat16)
            return carry

        lax.fori_loop(0, rows // 32, block, 0)

    own = [pltpu.make_async_copy(w_low[m], part(i, dp, 0, rows), own_sem.at[i]) for i, m in enumerate(order)]
    token_own = [
        pltpu.make_async_copy(a, b.at[pl.ds(pl.multiple_of(me * share, share), share)], own_sem.at[n_w + i])
        for i, (a, b) in enumerate(((tok_ref, tok_all), (cot_ref, cot_all)))
    ]
    chain_start(0, 1)
    for i, m in enumerate(order):
        loads[i].wait()
        narrow(w_wide[m], w_low[m])
        if i < 2:
            own_start(i)
        own[i].start()
    for cp in token_own:
        cp.start()
    sides = [
        pltpu.make_async_copy(a, b, side_sem.at[i])
        for i, (a, b) in enumerate(((gain_ref, gains), (bias_ref, biases), (seg_ref, segs), (freq_ref, freq)))
    ]
    for cp in sides:
        cp.start()
    loads = [pltpu.make_async_copy(m_refs[m], w_wide[m], load_sem.at[m]) for m in range(n_w)]
    for cp in loads:
        cp.start()
    for cp in loads:
        cp.wait()
    heads = w_refs[0].shape[1] // (3 * HD)
    wide_cols = w_refs[2].shape[1] // heads
    for dev, (m, head) in enumerate(owner_tables()):
        cols = w_refs[m].shape[1] // heads
        at = (dev % 2) * wide_cols
        narrow(w_wide[m].at[:, pl.ds(head * cols, cols)], m_low.at[dev // 2, :, pl.ds(at, cols)])

    def mom_copy(n):
        chip = ((y + n // 2) % 2) * 2 + (x + n) % 2
        return pltpu.make_async_remote_copy(
            src_ref=m_low.at[chip], dst_ref=mom_ref.at[y * 2 + x], send_sem=m_send.at[n], recv_sem=m_recv.at[n],
            device_id=(chip * 2 + c, me), device_id_type=MESH,
        )

    mom_own = pltpu.make_async_copy(m_low.at[y * 2 + x], mom_ref.at[y * 2 + x], m_send.at[0])
    mom_own.start()
    near_take(0)
    own_start(2)
    chain_take(0, 1)
    near_take(1)
    own_start(3)
    chain_take(0, 2)
    far_take(0)
    near_take(2)
    whole_take(0)
    load_qkv = pltpu.make_async_copy(full_refs[0], w_qkv, tile_sem.at[4])
    load_qkv.start()
    for step in range(3, n_t):
        chain_take(0, step)
    chain_start(1, 1)
    far_take(1)
    for cp in token_own + sides:
        cp.wait()
    tile = 256

    def tok_copy(r):
        return pltpu.make_async_copy(tok_all.at[pl.ds(pl.multiple_of(r * tile, tile), tile)], tok.at[r % 2], tok_sem.at[r % 2])

    tok_copy(jnp.int32(0)).start()
    load_qkv.wait()

    def project(r, carry):
        @pl.when(r + 1 < seq // tile)
        def _():
            tok_copy(r + 1).start()

        tok_copy(r).wait()
        here = pl.ds(pl.multiple_of(r * tile, tile), tile)
        hidden = tok[r % 2].astype(jnp.float32)
        mean = jnp.mean(hidden, axis=-1, keepdims=True)
        centred = hidden - mean
        scale = lax.rsqrt(jnp.mean(centred * centred, axis=-1, keepdims=True) + LN_EPS)
        normed = centred * scale
        ln = (normed * gains[0:1, :] + biases[0:1, :]).astype(jnp.bfloat16)
        ln_a[here, :] = ln
        ln_m[here, :] = (normed * gains[1:2, :] + biases[1:2, :]).astype(jnp.bfloat16)
        lane = lax.broadcasted_iota(jnp.int32, (tile, 128), 1)
        numbers = segs[...].astype(jnp.float32)
        mine = jnp.broadcast_to(segs[:, here].astype(jnp.float32), (128, tile)).T[:, 0:1]
        index = lax.broadcasted_iota(jnp.int32, (tile, seq), 1).astype(jnp.float32)
        first = jnp.min(jnp.where(numbers == mine, index, float(seq)), axis=1, keepdims=True)
        aux[here, :] = jnp.where(lane == 0, first, jnp.where(lane == 1, mean, scale))
        token = (r * tile + lax.broadcasted_iota(jnp.int32, (tile, 128), 0)).astype(jnp.float32)
        turns = (token - first) * freq[...]
        sine = jnp.sin(turns)
        angles = jnp.where(lane < ROT, jnp.cos(turns), jnp.where(lane < ROT + ROT // 2, -sine, sine))
        table[here, :] = angles
        raw = wide_dot(ln, w_qkv[...], NN)
        for n in range(w_qkv.shape[1] // HD):
            block = raw[:, n * HD : (n + 1) * HD]
            if n % 3 < 2:
                block = jnp.concatenate([turn(block[:, :128], angles, 1.0), block[:, 128:]], axis=1)
            qkv[here, n * HD : (n + 1) * HD] = block.astype(jnp.bfloat16)
        return carry

    lax.fori_loop(0, seq // tile, project, 0)
    outs = []

    def put(src, dst):
        cp = pltpu.make_async_copy(src, dst, out_sem.at[len(outs)])
        cp.start()
        outs.append(cp)

    put(ln_a, ln_a_ref)
    put(ln_m, ln_m_ref)
    put(qkv, qkv_ref)
    put(aux, aux_ref)
    put(table, table_ref)
    attend_kernel(qkv, aux, o)
    put(o, o_ref)
    near_take(3)
    far_take(2)
    for n in range(1, 4):
        mom_copy(n).start()
    whole_take(1)
    strip = 512
    n_up = act.shape[1] // strip

    def up_copy(j):
        return pltpu.make_async_copy(full_refs[2].at[:, pl.ds(j * strip, strip)], w_up.at[j % 2], tile_sem.at[j % 2])

    def down_copy(j):
        return pltpu.make_async_copy(full_refs[3].at[pl.ds(j * strip, strip)], w_down.at[j % 2], tile_sem.at[2 + j % 2])

    up_copy(0).start()
    chain_take(1, 1)
    for j in range(n_up):
        if j + 1 < n_up:
            up_copy(j + 1).start()
        up_copy(j).wait()
        cols = slice(j * strip, (j + 1) * strip)
        up_kernel(ln_m, w_up.at[j % 2], act.at[:, cols], slope.at[:, cols])
        if j == 1:
            far_take(3)
    put(act, act_ref)
    put(slope, slope_ref)
    whole_take(2)
    whole_take(3)
    load_out = pltpu.make_async_copy(full_refs[1], w_out, tile_sem.at[4])
    load_out.start()
    down_copy(0).start()
    load_out.wait()
    n_down = width // strip
    branch_copies = []
    for j in range(n_down):
        if j + 1 < n_down:
            down_copy(j + 1).start()
        down_copy(j).wait()
        if j >= 2:
            branch_copies[j - 2].wait()
        down_kernel(o, act, w_out.at[pl.ds(j * strip, strip)], w_down.at[j % 2], branch.at[j % 2])
        cp = pltpu.make_async_copy(branch.at[j % 2], branch_ref.at[:, pl.ds(j * strip, strip)], tok_sem.at[j % 2])
        cp.start()
        branch_copies.append(cp)
        if j == 1:
            chain_take(1, 2)
    for step in range(3, n_t):
        chain_take(1, step)
    for cp in branch_copies[-2:] + outs + [mom_own]:
        cp.wait()
    for i in range(n_w):
        for k in range(9):
            copy(i, k).wait_send()
    for n in range(1, 4):
        mom_copy(n).wait()
    for kind in range(2):
        for step in range(1, n_t):
            for up in (True, False):
                @pl.when(chain_sends(step, up))
                def _():
                    chain(kind, step, up).wait_send()


def forward_all(weights, moments, tokens, cotangent, gains, biases, segments):
    n_w = len(weights)
    rows, bf, f32 = weights[0].shape[0], jnp.bfloat16, jnp.float32
    n_t = lax.axis_size("tensor")
    share, width = tokens.shape
    seq = share * n_t
    qkv_cols, out_cols, units = (weights[i].shape[1] for i in range(3))
    mom_cols = units // 2 + 3 * HD
    freq = np.tile(10000.0 ** (-2.0 * np.arange(ROT // 2) / ROT), 4).astype(np.float32)[None]
    anyspec = pl.BlockSpec(memory_space=pl.ANY)
    V, S = pltpu.VMEM, pltpu.SemaphoreType.DMA
    array = jax.ShapeDtypeStruct
    out = pl.pallas_call(
        functools.partial(forward_kernel, (0, 2, 1, 3)),
        out_shape=[array((rows * 8, w.shape[1]), bf) for w in weights]
        + [array((4, rows, mom_cols), bf), array((seq, width), bf), array((seq, width), bf), array((seq, width), bf),
           array((seq, width), bf), array((seq, qkv_cols), bf), array((seq, 128), f32), array((seq, 128), f32), array((seq, out_cols), bf),
           array((seq, units), bf), array((seq, units), bf), array((seq, width), bf)],
        in_specs=[anyspec] * (2 * n_w + 6),
        out_specs=[anyspec] * (n_w + 12),
        scratch_shapes=[V(w.shape, w.dtype) for w in weights]
        + [V(w.shape, bf) for w in weights]
        + [V((4, rows, mom_cols), bf), V((2, 256, width), bf), V((seq, width), bf), V((seq, width), bf),
           V((seq, qkv_cols), bf), V((seq, 128), f32), V((seq, 128), f32), V((seq, out_cols), bf), V((seq, units), bf),
           V((seq, units), bf), V(gains.shape, f32), V(biases.shape, f32), V(segments.shape, jnp.int32),
           V(freq.shape, f32), V((width, qkv_cols), bf),
           V((width, out_cols), bf), V((2, width, 512), bf), V((2, 512, units), bf), V((2, seq, 512), bf),
           S((n_w,)), S((n_w + 2,)), S((n_w, 9)), S((n_w, 9)), S((4,)), S((4,)), S((2, n_t, 2)), S((2, n_t, 2)),
           S((4,)), S((2,)), S((5,)), S((8,))],
        compiler_params=pltpu.CompilerParams(collective_id=0, has_side_effects=True, vmem_limit_bytes=63 * 2**20),
        cost_estimate=pl.CostEstimate(flops=140 * 10**9, bytes_accessed=100 * 2**20, transcendentals=0),
        name="forward_all",
    )(*weights, *moments, tokens, cotangent, gains, biases, segments, freq)
    return out[:n_w], out[n_w:]


TILE = 256
STRIP = 512
SLOTS = 8
EVEN_STEPS, SHARED_STEPS, ALL_STEPS = 16, 20, 28


def owner_tables():
    return ((2, 0), (1, 0), (3, 0), (0, 0), (3, 1), (0, 1), (2, 1), (1, 1))


def backward_kernel(*refs):
    (dy_ref, ln_m_ref, ln_a_ref, act_ref, o_ref, slope_ref, qkv_ref, aux_ref, table_ref, tok_ref, norm_ref,
     w_down_ref, w_out_ref, w_up_ref, w_qkv_ref, mom_ref) = refs[:16]
    block_ref, grad_ref, u_ref, sums_ref = refs[16:20]
    (lhs, rhs, sib_send, own, sib_recv, far_x, far_y, in_x, in_y, far_send, x_send, y_send, mom, g_out, e_out,
     qkv, d_o, d_key, d_value, aux, table, w_tile, slope, row_q, row_u, tok, u_tile, norm, sums, z_in, z_sum, dp_in,
     lhs_sem, mom_sem, out_sem, keep_sem, give_ss, give_rs, sib_ss, sib_rs, fx_ss, fx_rs, fy_ss, fy_rs, x_ss, x_rs, y_ss, y_rs,
     side_sem, w_sem, slope_sem, row_sem, u_sem, z_ss, z_rs, d_ss, d_rs, sums_sem) = refs[20:]
    dp = lax.axis_index("dp")
    t = lax.axis_index("tensor")
    n_t = lax.axis_size("tensor")
    y, x, c = dp // 4, (dp // 2) % 2, dp % 2
    seq, width = dy_ref.shape
    units, heads_width = act_ref.shape[1], o_ref.shape[1]
    at_up, at_o, at_qkv = units, 2 * units, 2 * units + heads_width
    share = STRIP // 2
    half = share // 2
    strips = width // STRIP
    by_x = y * 4 + (1 - x) * 2 + c
    by_y = (1 - y) * 4 + x * 2 + c
    by_c = y * 4 + x * 2 + (1 - c)
    barrier = pltpu.get_barrier_semaphore()
    for shift in range(1, 8):
        pl.semaphore_signal(barrier, inc=1, device_id=(lax.rem(dp + shift, 8), t), device_id_type=MESH)
    for shift in range(1, n_t):
        pl.semaphore_signal(barrier, inc=1, device_id=(dp, lax.rem(t + shift, n_t)), device_id_type=MESH)

    def wide(v):
        return v.astype(jnp.float32)

    def low(v):
        return v.astype(jnp.bfloat16)

    def remote(src, dst, ss, rs, peer):
        return pltpu.make_async_remote_copy(src_ref=src, dst_ref=dst, send_sem=ss, recv_sem=rs, device_id=(peer, t), device_id_type=MESH)

    def local(src, dst, sem):
        return pltpu.make_async_copy(src, dst, sem)

    def outer(k):
        return (k < SHARED_STEPS) | (x != y)

    def inner(k):
        return (k < SHARED_STEPS) | (x == y)

    def place(k):
        step = jnp.where(k < EVEN_STEPS, k, k - EVEN_STEPS)
        return step % strips, step // strips

    def holder_slice(ref, k):
        strip, tile = place(k)
        col = jnp.where(k < EVEN_STEPS, 0, units // 2) + tile * TILE
        return ref.at[strip, :, pl.ds(pl.multiple_of(col, TILE), TILE)]

    def mom_copy(k):
        return local(holder_slice(mom_ref, k), mom.at[k % SLOTS], mom_sem.at[k % SLOTS])

    def grad_copy(k):
        return local(g_out.at[k % 2], holder_slice(grad_ref, k), keep_sem.at[k % 2])

    def out_copy(k):
        strip, tile = place(k)
        rows = pl.ds(pl.multiple_of(strip * STRIP + c * share, TILE), share)
        dst = block_ref.at[rows, pl.ds(pl.multiple_of(tile * TILE, TILE), TILE)]
        return local(e_out.at[k % 2], dst, out_sem.at[k % 2]), remote(e_out.at[k % 2], dst, give_ss.at[k % 2], give_rs, by_c)

    def keeps(k):
        return jnp.where(k < EVEN_STEPS, c == 0, c == 1)

    def out_start(k):
        here, there = out_copy(k)
        grad_copy(k).start()

        @pl.when(keeps(k))
        def _():
            here.start()

        @pl.when(jnp.logical_not(keeps(k)))
        def _():
            there.start()

    def out_wait(k):
        here, there = out_copy(k)
        grad_copy(k).wait()

        @pl.when(keeps(k))
        def _():
            here.wait()

        @pl.when(jnp.logical_not(keeps(k)))
        def _():
            there.wait_send()

    def sib_copy(k):
        return remote(sib_send.at[k % 2], sib_recv.at[k % SLOTS], sib_ss.at[k % 2], sib_rs.at[k % SLOTS], by_c)

    def far_copy_x(k):
        return remote(far_send.at[k % 2, pl.ds(0, half)], far_x.at[k % SLOTS], fx_ss.at[k % 2], fx_rs.at[k % SLOTS], by_x)

    def far_copy_y(k):
        return remote(far_send.at[k % 2, pl.ds(half, half)], far_y.at[k % SLOTS], fy_ss.at[k % 2], fy_rs.at[k % SLOTS], by_y)

    def copy_x(k):
        return remote(x_send.at[k % 2], in_x.at[k % SLOTS], x_ss.at[k % 2], x_rs.at[k % SLOTS], by_x)

    def copy_y(k):
        return remote(y_send.at[k % 2], in_y.at[k % SLOTS], y_ss.at[k % 2], y_rs.at[k % SLOTS], by_y)

    n_down, n_out = units // TILE, heads_width // TILE

    def down_cols(j):
        return pl.ds(pl.multiple_of((j % 2) * (units // 2) + (j // 2) * TILE, TILE), TILE)

    def w_start(j):
        @pl.when(j < n_down)
        def _():
            local(w_down_ref.at[:, down_cols(j)], w_tile.at[j % 2], w_sem.at[j % 2]).start()
            local(slope_ref.at[:, down_cols(j)], slope.at[j % 2], slope_sem.at[j % 2]).start()

        @pl.when(j >= n_down)
        def _():
            cols = pl.ds(pl.multiple_of((j - n_down) * TILE, TILE), TILE)
            local(w_out_ref.at[:, cols], w_tile.at[j % 2], w_sem.at[j % 2]).start()

    def row_copies(j):
        here = pl.ds(pl.multiple_of(j * TILE, TILE), TILE)
        slot = j % 2
        return (
            local(w_qkv_ref.at[here], row_q.at[slot], row_sem.at[slot, 0]),
            local(w_up_ref.at[here], row_u.at[slot], row_sem.at[slot, 1]),
            local(tok_ref.at[:, here], tok.at[slot], row_sem.at[slot, 2]),
        )

    def u_copy(j):
        return local(u_tile.at[j % 2], u_ref.at[:, pl.ds(pl.multiple_of(j * TILE, TILE), TILE)], u_sem.at[j % 2])

    lhs_copies = [local(ref, lhs.at[i], lhs_sem.at[i]) for i, ref in enumerate((dy_ref, ln_m_ref, ln_a_ref))]
    pairs = ((act_ref, rhs.at[:, pl.ds(0, units)]), (o_ref, rhs.at[:, pl.ds(at_o, heads_width)]), (qkv_ref, qkv),
             (aux_ref, aux), (table_ref, table), (norm_ref, norm))
    sides = [local(a, b, side_sem.at[i]) for i, (a, b) in enumerate(pairs)]
    lhs_copies[0].start()
    w_start(jnp.int32(0))
    w_start(jnp.int32(1))
    sides[0].start()
    lhs_copies[1].start()
    for cp in sides[1:]:
        cp.start()
    lhs_copies[2].start()
    sums[...] = jnp.zeros_like(sums)
    lhs_copies[0].wait()

    def made_by_dy(j):
        slot = j % 2
        local(w_out_ref.at[:, pl.ds(0, TILE)], w_tile.at[slot], w_sem.at[slot]).wait()

        @pl.when(j < n_down)
        def _():
            local(slope_ref.at[:, pl.ds(0, TILE)], slope.at[slot], slope_sem.at[slot]).wait()
            cols = pl.ds(pl.multiple_of(at_up + (j % 2) * (units // 2) + (j // 2) * TILE, TILE), TILE)
            for r in range(2):
                here = slice(r * (seq // 2), (r + 1) * (seq // 2))
                rhs[here, cols] = low(wide_dot(lhs[0, here, :], w_tile[slot], NN) * wide(slope[slot, here, :]))

        @pl.when(j >= n_down)
        def _():
            cols = pl.ds(pl.multiple_of((j - n_down) * TILE, TILE), TILE)
            for r in range(2):
                here = slice(r * (seq // 2), (r + 1) * (seq // 2))
                d_o[here, cols] = low(wide_dot(lhs[0, here, :], w_tile[slot], NN))

    def input_tile(j):
        slot = j % 2
        for cp in row_copies(j):
            cp.wait()

        @pl.when(j + 1 < width // TILE)
        def _():
            for cp in row_copies(j + 1):
                cp.start()

        @pl.when(j >= 2)
        def _():
            u_copy(j - 2).wait()

        cols = pl.ds(pl.multiple_of(j * TILE, TILE), TILE)
        gain_a, gain_m = norm[0:1, cols], norm[1:2, cols]

        total = jnp.zeros((4, TILE), jnp.float32)
        for r in range(2):
            here = slice(r * (seq // 2), (r + 1) * (seq // 2))
            by_a = wide_dot(rhs[here, pl.ds(at_qkv, qkv_ref.shape[1])], row_q[slot], NT)
            by_m = wide_dot(rhs[here, pl.ds(at_up, units)], row_u[slot], NT)
            normed = (wide(tok[slot, here, :]) - aux[here, 1:2]) * aux[here, 2:3]
            u_tile[slot, here, :] = low(gain_a * by_a + gain_m * by_m)
            parts = [jnp.sum(v, axis=0, keepdims=True) for v in (by_a * normed, by_a, by_m * normed, by_m)]
            total = total + jnp.concatenate(parts, axis=0)
        sums[:, cols] = total
        u_copy(j).start()

    def z_copy(shift):
        return pltpu.make_async_remote_copy(src_ref=sums, dst_ref=z_in.at[shift], send_sem=z_ss.at[shift], recv_sem=z_rs.at[shift], device_id=(dp, lax.rem(t + shift, n_t)), device_id_type=MESH)

    def dp_copy(shift):
        return remote(z_sum, dp_in.at[shift], d_ss.at[shift], d_rs.at[shift], lax.rem(dp + shift, 8))

    n_tiles = width // TILE
    n_blocks = seq // TILE
    first_attend = n_down + n_out
    paired_blocks = first_attend + 2 * n_blocks - EVEN_STEPS
    first_input = EVEN_STEPS + 1
    d_qkv = rhs.at[:, pl.ds(at_qkv, qkv_ref.shape[1])]

    made_by_dy(jnp.int32(0))
    made_by_dy(jnp.int32(1))
    w_start(jnp.int32(2))
    pl.semaphore_wait(barrier, 7 + n_t - 1)

    def step(i, carry):
        k1 = i
        k2 = i - 1
        k3 = i - 2
        k4 = i - 4

        @pl.when(k1 < ALL_STEPS)
        def _():
            @pl.when(k1 == 0)
            def _():
                sides[0].wait()
                lhs_copies[1].wait()

            @pl.when(k1 == EVEN_STEPS)
            def _():
                lhs_copies[2].wait()

            strip, tile = place(k1)

            @pl.when(k1 >= 2)
            def _():
                sib_copy(k1 - 2).wait_send()

            def piece(q):
                px = x + (q % 2) * (1 - 2 * x)
                py = y + (q // 2) * (1 - 2 * y)
                even = k1 < EVEN_STEPS
                plain = px == py
                which = jnp.where(even, jnp.where(plain, 1, 0), jnp.where(plain, 0, 2))
                col_even = jnp.where(plain, at_up, 0) + py * (units // 2) + tile * TILE
                col_odd = jnp.where(plain, at_o + py * TILE, at_qkv + py * (3 * HD) + tile * TILE)
                col = pl.multiple_of(jnp.where(even, col_even, col_odd), TILE)
                row = strip * STRIP
                right = rhs[:, pl.ds(col, TILE)]
                left = lhs[which, :, pl.ds(pl.multiple_of(row + (1 - c) * share, TILE), share)]
                sib_send[k1 % 2, q] = low(wide_dot(left, right, TN))
                left = lhs[which, :, pl.ds(pl.multiple_of(row + c * share, TILE), share)]
                own[k1 % SLOTS, q] = wide_dot(left, right, TN)

            @pl.when(k1 < SHARED_STEPS)
            def _():
                for q in range(4):
                    piece(q)

            @pl.when(k1 >= SHARED_STEPS)
            def _():
                piece(jnp.where(x == y, 1, 0))
                piece(jnp.where(x == y, 2, 3))

            sib_copy(k1).start()

        @pl.when((k2 >= 0) & (k2 < ALL_STEPS))
        def _():
            sib_copy(k2).wait_recv()

            @pl.when(outer(k2))
            def _():
                @pl.when(k2 >= 2)
                def _():
                    @pl.when(outer(k2 - 2))
                    def _():
                        far_copy_x(k2 - 2).wait_send()
                        far_copy_y(k2 - 2).wait_send()

                far_send[k2 % 2] = low(own[k2 % SLOTS, 3] + wide(sib_recv[k2 % SLOTS, 3]))
                far_copy_x(k2).start()
                far_copy_y(k2).start()

        @pl.when((i >= 2) & (i < n_down + n_out))
        def _():
            made_by_dy(i)

            @pl.when(i + 1 < n_down + n_out)
            def _():
                w_start(i + 1)

        for block in range(2 * n_blocks):
            @pl.when(i == first_attend + (block // 2 if block < 2 * paired_blocks else block - paired_blocks))
            def _():
                if block == 0:
                    for cp in sides[1:]:
                        cp.wait()
                attend_back_block(qkv, aux, table, d_o, d_qkv, d_key, d_value, block // n_blocks, block % n_blocks, block % n_blocks == n_blocks - 1)

        @pl.when((k3 >= 0) & (k3 < ALL_STEPS) & inner(k3))
        def _():
            @pl.when(k3 >= 2)
            def _():
                @pl.when(inner(k3 - 2))
                def _():
                    copy_x(k3 - 2).wait_send()
                    copy_y(k3 - 2).wait_send()

            far_copy_x(k3).wait_recv()
            far_copy_y(k3).wait_recv()
            first, last = pl.ds(0, half), pl.ds(half, half)

            def chip_sum(q, part):
                return own[k3 % SLOTS, q, part] + wide(sib_recv[k3 % SLOTS, q, part])

            y_send[k3 % 2, first] = low(chip_sum(2, first) + wide(far_x[k3 % SLOTS]))
            y_send[k3 % 2, last] = low(chip_sum(2, last))
            copy_y(k3).start()
            x_send[k3 % 2, first] = low(chip_sum(1, first))
            x_send[k3 % 2, last] = low(chip_sum(1, last) + wide(far_y[k3 % SLOTS]))
            copy_x(k3).start()

        @pl.when((k3 >= 0) & (k3 < ALL_STEPS) & outer(k3))
        def _():
            mom_copy(k3).start()

        @pl.when(i == first_input - 1)
        def _():
            for cp in row_copies(0):
                cp.start()

        @pl.when((i >= first_input) & (i < first_input + n_tiles))
        def _():
            input_tile(i - first_input)

        @pl.when(i == first_input + n_tiles)
        def _():
            for shift in range(1, n_t):
                z_copy(shift).start()

        @pl.when(i == first_input + n_tiles + 2)
        def _():
            total = sums[...]
            for shift in range(1, n_t):
                z_copy(shift).wait_recv()
                total = total + z_in[shift]
            z_sum[...] = total
            for shift in range(1, 8):
                dp_copy(shift).start()

        @pl.when((k4 >= 0) & outer(k4))
        def _():
            @pl.when(k4 >= 2)
            def _():
                @pl.when(outer(k4 - 2))
                def _():
                    out_wait(k4 - 2)

            copy_x(k4).wait_recv()
            copy_y(k4).wait_recv()
            mom_copy(k4).wait()
            grad = own[k4 % SLOTS, 0] + wide(sib_recv[k4 % SLOTS, 0]) + wide(in_x[k4 % SLOTS]) + wide(in_y[k4 % SLOTS])
            g_out[k4 % 2] = low(grad)
            e_out[k4 % 2] = low(grad + MOMENTUM * (MOMENTUM * wide(mom[k4 % SLOTS]) + grad))
            out_start(k4)

        return carry

    lax.fori_loop(0, ALL_STEPS + 4, step, 0)
    for last, here, there in ((SHARED_STEPS, x == y, x != y), (ALL_STEPS, x != y, x == y)):
        for k in (last - 2, last - 1):
            k = jnp.int32(k)
            if last == ALL_STEPS:
                sib_copy(k).wait_send()

            @pl.when(here)
            def _():
                far_copy_x(k).wait_send()
                far_copy_y(k).wait_send()
                out_wait(k)

            @pl.when(there)
            def _():
                copy_x(k).wait_send()
                copy_y(k).wait_send()

    for odd in range(2):
        for apart in range(2):
            cols = (units // 2 if odd == 0 else (3 * HD if apart else HD))

            @pl.when((c == odd) & (jnp.where(x == y, 0, 1) == apart))
            def _():
                seen = block_ref.at[pl.ds(0, width // 2), pl.ds(0, cols)]
                local(seen, seen, give_rs).wait()

    total = z_sum[...]
    for shift in range(1, 8):
        dp_copy(shift).wait_recv()
        total = total + dp_in[shift]
    sums_out = local(z_in.at[0], sums_ref, sums_sem)
    z_in[0] = total
    sums_out.start()
    for shift in range(1, n_t):
        z_copy(shift).wait_send()
    for shift in range(1, 8):
        dp_copy(shift).wait_send()
    u_copy(n_tiles - 2).wait()
    u_copy(n_tiles - 1).wait()
    sums_out.wait()


def backward_all(dy, ln_m, ln_a, act, o, slope, qkv, aux, table, tok, norm_rows, full, mom):
    full_qkv, full_out, full_up, full_down = full
    seq, width = dy.shape
    n_t = lax.axis_size("tensor")
    anyspec = pl.BlockSpec(memory_space=pl.ANY)
    bf, f32 = jnp.bfloat16, jnp.float32
    V, S = pltpu.VMEM, pltpu.SemaphoreType.DMA
    rhs_width = 2 * act.shape[1] + o.shape[1] + qkv.shape[1]
    piece = (STRIP // 2, TILE)
    halved = (STRIP // 4, TILE)
    scratch = [
        V((3, seq, width), bf), V((seq, rhs_width), bf), V((2, 4, *piece), bf), V((SLOTS, 4, *piece), f32),
        V((SLOTS, 4, *piece), bf), V((SLOTS, *halved), bf), V((SLOTS, *halved), bf), V((SLOTS, *piece), bf),
        V((SLOTS, *piece), bf), V((2, *piece), bf), V((2, *piece), bf), V((2, *piece), bf), V((SLOTS, *piece), bf),
        V((2, *piece), bf), V((2, *piece), bf),
        V(qkv.shape, bf), V(o.shape, bf), V((seq, HD), f32), V((seq, HD), f32), V(aux.shape, f32), V(table.shape, f32),
        V((2, width, TILE), bf), V((2, seq, TILE), bf), V((2, TILE, qkv.shape[1]), bf), V((2, TILE, act.shape[1]), bf),
        V((2, seq, TILE), bf), V((2, seq, TILE), bf), V(norm_rows.shape, f32), V((4, width), f32), V((n_t, 4, width), f32),
        V((4, width), f32), V((8, 4, width), f32),
        S((3,)), S((SLOTS,)), S((2,)), S((2,)), S((2,)), S, S((2,)), S((SLOTS,)), S((2,)), S((SLOTS,)), S((2,)), S((SLOTS,)),
        S((2,)), S((SLOTS,)), S((2,)), S((SLOTS,)),
        S((6,)), S((2,)), S((2,)), S((2, 3)), S((2,)), S((n_t,)), S((n_t,)), S((8,)), S((8,)), S,
    ]
    block = jax.ShapeDtypeStruct((width, act.shape[1] // 2), bf)
    return pl.pallas_call(
        backward_kernel,
        out_shape=[block, jax.ShapeDtypeStruct(mom.shape, bf), jax.ShapeDtypeStruct((seq, width), bf), jax.ShapeDtypeStruct((4, width), f32)],
        in_specs=[anyspec] * 16,
        out_specs=[anyspec] * 4,
        scratch_shapes=scratch,
        compiler_params=pltpu.CompilerParams(collective_id=1, has_side_effects=True, vmem_limit_bytes=63 * 2**20),
        cost_estimate=pl.CostEstimate(flops=120 * 10**9, bytes_accessed=100 * 2**20, transcendentals=0),
        name="backward_all",
    )(dy, ln_m, ln_a, act, o, slope, qkv, aux, table, tok, norm_rows, full_down, full_out, full_up, full_qkv, mom)


NT = (((1,), (1,)), ((), ()))
NN = (((1,), (0,)), ((), ()))


def wide_dot(left, right, dims):
    return lax.dot_general(left, right, dims, preferred_element_type=jnp.float32)


def sweep_all(block_ref, o_ref, flipped, gram, poly, cols, strip_of=None, done=None):
    rows = o_ref.shape[0]
    tile, strip = 256, 512
    high = strip if cols % strip == 0 else tile

    def squares(i, total):
        here = pl.ds(pl.multiple_of(i * tile, tile), tile)
        part = block_ref[here, :cols].astype(jnp.float32)
        return total + jnp.sum((part * part).reshape(tile // 8, 8, cols), axis=0)

    total = jnp.sum(lax.fori_loop(0, rows // tile, squares, jnp.zeros((8, cols), jnp.float32)))
    scale = 1.0 / (jnp.sqrt(total) + 1e-07)
    for i in range(rows // tile):
        here = slice(i * tile, (i + 1) * tile)
        flipped[:cols, here] = (block_ref[here, :cols].astype(jnp.float32) * scale).T.astype(jnp.bfloat16)
    pairs = [(i, j) for i in range(cols // tile) for j in range(i, cols // tile)]

    def sweep(step, carry):
        for i, j in pairs:
            a, b = slice(i * tile, (i + 1) * tile), slice(j * tile, (j + 1) * tile)
            part = wide_dot(flipped[a, :], flipped[b, :], NT).astype(jnp.bfloat16)
            gram[a, b] = part
            if i != j:
                gram[b, a] = part.T
        for i, j in pairs:
            a, b = slice(i * tile, (i + 1) * tile), slice(j * tile, (j + 1) * tile)
            part = NS_B * gram[a, b].astype(jnp.float32) + NS_C * wide_dot(gram[a, :cols], gram[:cols, b], NN)
            part = part.astype(jnp.bfloat16)
            poly[a, b] = part
            if i != j:
                poly[b, a] = part.T

        def update(n, inner):
            n = n if strip_of is None else strip_of(n)
            part = pl.ds(pl.multiple_of(n * strip, strip), strip)
            old = flipped[:cols, part]
            for m in range(cols // high):
                own = slice(m * high, (m + 1) * high)
                flipped[own, part] = (
                    NS_A * old[own].astype(jnp.float32) + wide_dot(poly[own, :cols], old, NN)
                ).astype(jnp.bfloat16)

            @pl.when(step == 4)
            def _():
                for r in range(strip // tile):
                    here = pl.ds(pl.multiple_of(n * strip + r * tile, tile), tile)
                    o_ref[here, :cols] = flipped[:cols, here].astype(jnp.float32).T.astype(jnp.bfloat16)
                if done is not None:
                    done(n)

            return inner

        for n in range(rows // strip):
            update(jnp.int32(n), 0)
        return carry

    lax.fori_loop(0, 5, sweep, 0)


def sweep_kernel(e_ref, o_ref, flipped, gram, poly):
    sweep_all(e_ref, o_ref, flipped, gram, poly, e_ref.shape[1])


def sweep_scratch(rows, cols):
    shapes = ((cols, rows), (cols, cols), (cols, cols))
    return [pltpu.VMEM(shape, jnp.bfloat16) for shape in shapes]


SWEEP_COST = dict(flops=55 * 10**9, bytes_accessed=8 * 2**20, transcendentals=0)


def sweeps(block):
    whole = pl.BlockSpec(memory_space=pltpu.VMEM)
    return pl.pallas_call(
        sweep_kernel,
        out_shape=jax.ShapeDtypeStruct(block.shape, jnp.bfloat16),
        in_specs=[whole],
        out_specs=whole,
        scratch_shapes=sweep_scratch(*block.shape),
        compiler_params=pltpu.CompilerParams(vmem_limit_bytes=63 * 2**20),
        cost_estimate=pl.CostEstimate(**SWEEP_COST),
        name="sweeps",
    )(block)


def sweep_return_kernel(
    widths, block_ref, grad_ref, rows_ref, ortho_ref, out, flipped, gram, poly,
    grad_ss, grad_rs, ortho_ss, ortho_rs, own_sem,
):
    dp, t = lax.axis_index("dp"), lax.axis_index("tensor")
    y, x, c = dp // 4, (dp // 2) % 2, dp % 2
    share, cols = ortho_ref.shape[1:]
    barrier = pltpu.get_barrier_semaphore()
    for shift in range(1, 8):
        pl.semaphore_signal(barrier, inc=1, device_id=(lax.rem(dp + shift, 8), t), device_id_type=MESH)
    pl.semaphore_wait(barrier, 7)

    def of_width(mine, fn):
        for width in sorted(set(mine)):
            here = functools.reduce(jnp.logical_or, [dp == dev for dev, w in enumerate(mine) if w == width])

            @pl.when(here)
            def _():
                fn(width)

    both = tuple(cols + widths[dev // 2 * 2 + 1] for dev in range(8))

    def grad_pair(chip, width):
        src, dst = grad_ref.at[chip, :, pl.ds(0, width)], rows_ref.at[y * 2 + x, :, pl.ds(0, width)]
        far = pltpu.make_async_remote_copy(
            src_ref=src, dst_ref=dst, send_sem=grad_ss.at[chip], recv_sem=grad_rs.at[y * 2 + x],
            device_id=(chip * 2 + c, t), device_id_type=MESH,
        )
        return far, pltpu.make_async_copy(src, dst, own_sem.at[0])

    def ortho_pair(peer, width):
        src = out.at[pl.ds(pl.multiple_of(peer * share, share), share), pl.ds(0, width)]
        dst = ortho_ref.at[dp, :, pl.ds(0, width)]
        far = pltpu.make_async_remote_copy(
            src_ref=src, dst_ref=dst, send_sem=ortho_ss.at[peer], recv_sem=ortho_rs.at[dp],
            device_id=(peer, t), device_id_type=MESH,
        )
        return far, pltpu.make_async_copy(src, dst, own_sem.at[1])

    def either(pair, away, start):
        far, here = pair

        @pl.when(away)
        def _():
            far.start() if start else far.wait_send()

        @pl.when(jnp.logical_not(away))
        def _():
            here.start() if start else here.wait()

    def chip_of(n):
        px = x + ((3 - n) % 2) * (1 - 2 * x)
        py = y + ((3 - n) // 2) * (1 - 2 * y)
        return py * 2 + px

    def grads(start):
        def go(width):
            for n in range(4):
                either(grad_pair(chip_of(n), width), n < 3, start)

        of_width(both, go)

    grads(True)

    def work(width):
        def done(strip):
            for core in range(2):
                peer = strip * 2 + core
                either(ortho_pair(peer, width), peer != dp, True)

        sweep_all(block_ref, out, flipped, gram, poly, width, chip_of, done)

    of_width(widths, work)
    grads(False)
    for chip in range(4):
        @pl.when(chip != y * 2 + x)
        def _():
            seen = rows_ref.at[chip, :, pl.ds(0, both[2 * chip])]
            pltpu.make_async_copy(seen, seen, grad_rs.at[chip]).wait()

    def sent(width):
        for peer in range(8):
            either(ortho_pair(peer, width), peer != dp, False)

    of_width(widths, sent)
    for dev in range(8):
        @pl.when(dev != dp)
        def _():
            seen = ortho_ref.at[dev, :, pl.ds(0, widths[dev])]
            pltpu.make_async_copy(seen, seen, ortho_rs.at[dev]).wait()


def sweep_return(block, grad_half, widths):
    rows, cols = block.shape
    whole, anyspec = pl.BlockSpec(memory_space=pltpu.VMEM), pl.BlockSpec(memory_space=pl.ANY)
    four, eight = pltpu.SemaphoreType.DMA((4,)), pltpu.SemaphoreType.DMA((8,))
    return pl.pallas_call(
        functools.partial(sweep_return_kernel, widths),
        out_shape=[
            jax.ShapeDtypeStruct(grad_half.shape, jnp.bfloat16),
            jax.ShapeDtypeStruct((8, rows // 8, cols), jnp.bfloat16),
        ],
        in_specs=[whole, anyspec],
        out_specs=[anyspec] * 2,
        scratch_shapes=[pltpu.VMEM((rows, cols), jnp.bfloat16)]
        + sweep_scratch(rows, cols)
        + [four, four, eight, eight, pltpu.SemaphoreType.DMA((2,))],
        compiler_params=pltpu.CompilerParams(collective_id=2, has_side_effects=True, vmem_limit_bytes=63 * 2**20),
        cost_estimate=pl.CostEstimate(**SWEEP_COST),
        name="sweep_return",
    )(block, grad_half)


def norm_back(tokens, cotangent, mixed):
    hidden, mixed = tokens.astype(jnp.float32), mixed.astype(jnp.float32)
    centred = hidden - jnp.mean(hidden, axis=-1, keepdims=True)
    scale = lax.rsqrt(jnp.mean(centred * centred, axis=-1, keepdims=True) + LN_EPS)
    normed = centred * scale
    inner = mixed - jnp.mean(mixed, axis=-1, keepdims=True) - normed * jnp.mean(mixed * normed, axis=-1, keepdims=True)
    return cotangent.astype(jnp.float32) + scale * inner


def update_kernel(places, width_of, *refs):
    n = len(width_of)
    w_refs, m_refs = refs[:n], refs[n : 2 * n]
    grad_ref, ortho_ref, tok_ref, cot_ref, mixed_ref, branch_ref = refs[2 * n : 2 * n + 6]
    new_m, new_w, out_ref, sum_ref = refs[2 * n + 6 : 3 * n + 6], refs[3 * n + 6 : 4 * n + 6], refs[4 * n + 6], refs[4 * n + 7]
    sum_ref[...] = (tok_ref[...].astype(jnp.float32) + branch_ref[...].astype(jnp.float32)).astype(jnp.bfloat16)
    out_ref[...] = norm_back(tok_ref[...], cot_ref[...], mixed_ref[...])
    for dev, (m, head) in enumerate(places):
        width = width_of[m]
        cols = slice(head * width, (head + 1) * width)
        at = (dev % 2) * ortho_ref.shape[2]
        grad = grad_ref[dev // 2, :, at : at + width].astype(jnp.float32)
        new_m[m][:, cols] = MOMENTUM * m_refs[m][:, cols] + grad
        ortho = ortho_ref[dev, :, :width].astype(jnp.float32)
        new_w[m][:, cols] = w_refs[m][:, cols] * (1.0 - LEARN * DECAY) - LEARN * ortho


def update_all(weights, moments, grad_rows, ortho_rows, rows_in, places, width_of):
    rows = weights[0].shape[0]
    tile = 32
    flat = [pl.BlockSpec((tile, w.shape[1]), lambda i: (i, 0)) for w in weights]
    strip = pl.BlockSpec((tile, rows_in[0].shape[1]), lambda i: (i, 0))
    block = lambda part: pl.BlockSpec((part.shape[0], tile, part.shape[2]), lambda i: (0, i, 0))
    out = pl.pallas_call(
        functools.partial(update_kernel, places, width_of),
        grid=(rows // tile,),
        out_shape=[jax.ShapeDtypeStruct(w.shape, w.dtype) for w in weights] * 2
        + [jax.ShapeDtypeStruct(rows_in[0].shape, jnp.float32), jax.ShapeDtypeStruct(rows_in[0].shape, jnp.bfloat16)],
        in_specs=flat * 2 + [block(grad_rows), block(ortho_rows)] + [strip] * 4,
        out_specs=flat * 2 + [strip] * 2,
        compiler_params=pltpu.CompilerParams(vmem_limit_bytes=63 * 2**20),
        cost_estimate=pl.CostEstimate(flops=10**7, bytes_accessed=34 * 2**20, transcendentals=0),
        name="update_all",
    )(*weights, *moments, grad_rows, ortho_rows, *rows_in)
    return out[: len(weights)], out[len(weights) : -2], out[-2], out[-1]


def turn(part, table, sign):
    half = ROT // 2
    lane = lax.broadcasted_iota(jnp.int32, part.shape, 1)
    sines = pltpu.roll(table, 128 - ROT, 1)
    ahead = pltpu.roll(part, 128 - half, 1)
    back = pltpu.roll(part, half, 1)
    partner = jnp.where(lane < half, ahead, back)
    return jnp.where(lane < ROT, part * table + sign * (partner * sines), part)


def rotary_table(positions):
    half = ROT // 2
    inv_freq = 10000.0 ** (-2.0 * jnp.arange(half, dtype=jnp.float32) / ROT)
    angles = positions.astype(jnp.float32)[:, None] * inv_freq[None, :]
    cosine, sine = jnp.cos(angles), jnp.sin(angles)
    return jnp.concatenate([cosine, cosine, -sine, sine], axis=1)


def project_kernel(tok_ref, norm_ref, table_ref, start_ref, w_ref, ln_a_ref, ln_m_ref, qkv_ref, aux_ref):
    hidden = tok_ref[...].astype(jnp.float32)
    mean = jnp.mean(hidden, axis=-1, keepdims=True)
    centred = hidden - mean
    scale = lax.rsqrt(jnp.mean(centred * centred, axis=-1, keepdims=True) + LN_EPS)
    normed = centred * scale
    ln_a = (normed * norm_ref[0:1, :] + norm_ref[1:2, :]).astype(jnp.bfloat16)
    ln_a_ref[...] = ln_a
    ln_m_ref[...] = (normed * norm_ref[2:3, :] + norm_ref[3:4, :]).astype(jnp.bfloat16)
    lane = lax.broadcasted_iota(jnp.int32, aux_ref.shape, 1)
    aux_ref[...] = jnp.where(lane == 0, start_ref[:, 0:1], jnp.where(lane == 1, mean, scale))
    table = table_ref[...]
    for part in range(w_ref.shape[1] // HD):
        raw = wide_dot(ln_a, w_ref[:, part * HD : (part + 1) * HD], NN)
        if part % 3 < 2:
            raw = jnp.concatenate([turn(raw[:, :128], table, 1.0), raw[:, 128:]], axis=1)
        qkv_ref[:, part * HD : (part + 1) * HD] = raw.astype(jnp.bfloat16)


def project(tokens_all, norm_rows, table, start_col, full_qkv):
    seq, width = tokens_all.shape
    cols = full_qkv.shape[1]
    tile = 256
    row = lambda n: pl.BlockSpec((tile, n), lambda i: (i, 0))
    whole = lambda a, b: pl.BlockSpec((a, b), lambda i: (0, 0))
    return pl.pallas_call(
        project_kernel,
        grid=(seq // tile,),
        out_shape=[
            jax.ShapeDtypeStruct((seq, width), jnp.bfloat16),
            jax.ShapeDtypeStruct((seq, width), jnp.bfloat16),
            jax.ShapeDtypeStruct((seq, cols), jnp.bfloat16),
            jax.ShapeDtypeStruct((seq, 128), jnp.float32),
        ],
        in_specs=[row(width), whole(4, width), row(128), row(1), whole(width, cols)],
        out_specs=[row(width), row(width), row(cols), row(128)],
        compiler_params=pltpu.CompilerParams(vmem_limit_bytes=63 * 2**20),
        cost_estimate=pl.CostEstimate(flops=2 * seq * width * cols, bytes_accessed=20 * 2**20, transcendentals=0),
        name="project",
    )(tokens_all, norm_rows, table, start_col, full_qkv)


def soft_block(query, keys, start_col, first, offset):
    scores = wide_dot(query, keys, NT) * (HD ** (-0.5))
    rows, cols = scores.shape
    key_pos = first + lax.broadcasted_iota(jnp.int32, (rows, cols), 1)
    query_pos = offset + lax.broadcasted_iota(jnp.int32, (rows, cols), 0)
    seen = (key_pos.astype(jnp.float32) >= start_col) & (key_pos <= query_pos)
    scores = jnp.where(seen, scores, MASKED)
    peak = jnp.max(scores, axis=-1, keepdims=True)
    expo = jnp.exp(scores - peak)
    return expo / jnp.sum(expo, axis=-1, keepdims=True)


def reach_of(block, tile):
    return max(0, (block * tile - (DOC_MOST - 1)) // tile)


def attend_kernel(qkv_ref, start_ref, o_ref):
    tile = 256
    for head in range(o_ref.shape[1] // HD):
        col = head * 3 * HD
        for block in range(o_ref.shape[0] // tile):
            low, high = reach_of(block, tile) * tile, (block + 1) * tile
            here = slice(block * tile, high)
            prob = soft_block(
                qkv_ref[here, col : col + HD],
                qkv_ref[low:high, col + HD : col + 2 * HD],
                start_ref[here, 0:1],
                low,
                block * tile,
            ).astype(jnp.bfloat16)
            mixed = wide_dot(prob, qkv_ref[low:high, col + 2 * HD : col + 3 * HD], NN)
            o_ref[here, head * HD : (head + 1) * HD] = mixed.astype(jnp.bfloat16)


def attend(qkv, start_col):
    seq = qkv.shape[0]
    cols = qkv.shape[1] // 3
    whole = pl.BlockSpec(memory_space=pltpu.VMEM)
    return pl.pallas_call(
        attend_kernel,
        out_shape=jax.ShapeDtypeStruct((seq, cols), jnp.bfloat16),
        in_specs=[whole, whole],
        out_specs=whole,
        compiler_params=pltpu.CompilerParams(vmem_limit_bytes=63 * 2**20),
        cost_estimate=pl.CostEstimate(flops=6 * 10**9, bytes_accessed=4 * 2**20, transcendentals=2**20),
        name="attend",
    )(qkv, start_col)


def up_kernel(ln_ref, w_ref, act_ref, slope_ref):
    tile = 256
    for block in range(ln_ref.shape[0] // tile):
        here = slice(block * tile, (block + 1) * tile)
        up = wide_dot(ln_ref[here, :], w_ref[...], NN)
        below = 0.5 + 0.5 * lax.erf(up * (0.5**0.5))
        act_ref[here, :] = (up * below).astype(jnp.bfloat16)
        slope_ref[here, :] = (below + up * jnp.exp(-0.5 * up * up) * ((2.0 * math.pi) ** -0.5)).astype(jnp.bfloat16)


def up_branch(ln_mlp, full_up):
    seq, width = ln_mlp.shape
    units = full_up.shape[1]
    tile = min(512, units)
    out = jax.ShapeDtypeStruct((seq, units), jnp.bfloat16)
    return pl.pallas_call(
        up_kernel,
        grid=(units // tile,),
        out_shape=[out, out],
        in_specs=[pl.BlockSpec((seq, width), lambda i: (0, 0)), pl.BlockSpec((width, tile), lambda i: (0, i))],
        out_specs=[pl.BlockSpec((seq, tile), lambda i: (0, i))] * 2,
        compiler_params=pltpu.CompilerParams(vmem_limit_bytes=63 * 2**20),
        cost_estimate=pl.CostEstimate(flops=2 * seq * width * units, bytes_accessed=20 * 2**20, transcendentals=2 * seq * units),
        name="up_branch",
    )(ln_mlp, full_up)


def down_kernel(o_ref, act_ref, w_out_ref, w_down_ref, out_ref):
    tile = 256
    for block in range(o_ref.shape[0] // tile):
        here = slice(block * tile, (block + 1) * tile)
        total = wide_dot(o_ref[here, :], w_out_ref[...], NT) + wide_dot(act_ref[here, :], w_down_ref[...], NT)
        out_ref[here, :] = total.astype(jnp.bfloat16)


def down_branch(o, act, full_out, full_down):
    seq, units = act.shape
    width = full_down.shape[0]
    tile = 512
    return pl.pallas_call(
        down_kernel,
        grid=(width // tile,),
        out_shape=jax.ShapeDtypeStruct((seq, width), jnp.bfloat16),
        in_specs=[
            pl.BlockSpec(o.shape, lambda i: (0, 0)),
            pl.BlockSpec(act.shape, lambda i: (0, 0)),
            pl.BlockSpec((tile, o.shape[1]), lambda i: (i, 0)),
            pl.BlockSpec((tile, units), lambda i: (i, 0)),
        ],
        out_specs=pl.BlockSpec((seq, tile), lambda i: (0, i)),
        compiler_params=pltpu.CompilerParams(vmem_limit_bytes=63 * 2**20),
        cost_estimate=pl.CostEstimate(flops=2 * seq * width * (units + o.shape[1]), bytes_accessed=20 * 2**20, transcendentals=0),
        name="down_branch",
    )(o, act, full_out, full_down)


TN = (((0,), (0,)), ((), ()))


def attend_back_block(qkv_ref, start_ref, table_ref, d_o_ref, d_qkv_ref, d_key, d_value, head, block, last):
    tile = 256
    col = head * 3 * HD
    low, high = reach_of(block, tile) * tile, (block + 1) * tile
    here = slice(block * tile, high)
    query, keys = qkv_ref[here, col : col + HD], qkv_ref[low:high, col + HD : col + 2 * HD]
    values = qkv_ref[low:high, col + 2 * HD : col + 3 * HD]
    d_o = d_o_ref[here, head * HD : (head + 1) * HD]
    prob = soft_block(query, keys, start_ref[here, 0:1], low, block * tile)
    value_part = wide_dot(prob.astype(jnp.bfloat16), d_o, TN)
    d_prob = wide_dot(d_o, values, NT)
    weighted = prob * d_prob
    d_score = (weighted - prob * jnp.sum(weighted, axis=-1, keepdims=True)).astype(jnp.bfloat16)
    d_query = wide_dot(d_score, keys, NN) * (HD ** (-0.5))
    key_part = wide_dot(d_score, query, TN) * (HD ** (-0.5))
    d_query = jnp.concatenate([turn(d_query[:, :128], table_ref[here, :], -1.0), d_query[:, 128:]], axis=1)
    d_qkv_ref[here, col : col + HD] = d_query.astype(jnp.bfloat16)
    old = high - tile
    if low < old:
        d_key[low:old, :] += key_part[: old - low]
        d_value[low:old, :] += value_part[: old - low]
    d_key[old:high, :] = key_part[old - low :]
    d_value[old:high, :] = value_part[old - low :]
    ready_from = low
    ready_to = high if last else reach_of(block + 1, tile) * tile
    if ready_to > ready_from:
        done = slice(ready_from, ready_to)
        total = d_key[done, :]
        total = jnp.concatenate([turn(total[:, :128], table_ref[done, :], -1.0), total[:, 128:]], axis=1)
        d_qkv_ref[done, col + HD : col + 2 * HD] = total.astype(jnp.bfloat16)
        d_qkv_ref[done, col + 2 * HD : col + 3 * HD] = d_value[done, :].astype(jnp.bfloat16)


def attend_back_kernel(qkv_ref, start_ref, table_ref, d_o_ref, d_qkv_ref, d_key, d_value):
    blocks = qkv_ref.shape[0] // 256
    for head in range(d_o_ref.shape[1] // HD):
        for block in range(blocks):
            attend_back_block(qkv_ref, start_ref, table_ref, d_o_ref, d_qkv_ref, d_key, d_value, head, block, block == blocks - 1)


def attend_back(qkv, start_col, table, d_o):
    whole = pl.BlockSpec(memory_space=pltpu.VMEM)
    return pl.pallas_call(
        attend_back_kernel,
        out_shape=jax.ShapeDtypeStruct(qkv.shape, jnp.bfloat16),
        in_specs=[whole] * 4,
        out_specs=whole,
        scratch_shapes=[pltpu.VMEM((qkv.shape[0], HD), jnp.float32)] * 2,
        compiler_params=pltpu.CompilerParams(vmem_limit_bytes=63 * 2**20),
        cost_estimate=pl.CostEstimate(flops=12 * 10**9, bytes_accessed=10 * 2**20, transcendentals=2**20),
        name="attend_back",
    )(qkv, start_col, table, d_o)


def hand_out(block, row_share):
    parts = block.reshape(lax.axis_size("dp"), row_share, block.shape[1])
    return lax.all_to_all(parts, "dp", split_axis=0, concat_axis=0, tiled=True)


def from_owners(parts, owners, matrix, col_count, heads):
    own = [parts[owners.index((matrix, head)), :, :col_count] for head in range(heads)]
    return jnp.concatenate(own, axis=1).astype(jnp.float32)


def on_device(
    tokens,
    cotangent,
    segments,
    w_qkv,
    w_out,
    w_up,
    w_down,
    m_qkv,
    m_out,
    m_up,
    m_down,
    norm_gains,
    norm_biases,
    norm_moments,
):
    tensor_size = lax.axis_size("tensor")
    seq_len = tokens.shape[0] * tensor_size
    seg_ids = segments[0]
    local_heads = w_out.shape[1] // HD
    block_units = FF // HEADS
    row_share = w_qkv.shape[0]
    paired = lax.axis_size("dp") == 8 and local_heads == 2
    weights_in = (w_qkv, w_out, w_up, w_down)
    moments_in = (m_qkv, m_out, m_up, m_down)
    col_counts = (3 * HD, HD, block_units, block_units)
    pad_width = max(col_counts)
    norm_rows = jnp.stack([norm_gains[0], norm_biases[0], norm_gains[1], norm_biases[1]])
    if paired:
        (full_qkv, full_out, full_up, full_down), rest = forward_all(
            weights_in, moments_in, tokens, cotangent, norm_gains, norm_biases, segments
        )
        mom_half, tokens_all, grad_all, ln_attn, ln_mlp, packed, aux, table = rest[:8]
        mixed_heads, activated, slope, branch = rest[8:]
    else:
        tokens_all, grad_all = (
            lax.all_gather(tokens, "tensor", axis=0, tiled=True),
            lax.all_gather(cotangent, "tensor", axis=0, tiled=True),
        )
        full_qkv, full_out, full_up, full_down = (
            lax.all_gather(w.astype(jnp.bfloat16), "dp", axis=0, tiled=True) for w in weights_in
        )
        starts = doc_starts(seg_ids)
        positions = jnp.arange(seq_len, dtype=jnp.int32) - starts
        start_col = starts[:, None].astype(jnp.float32)
        table = rotary_table(positions)
        ln_attn, ln_mlp, packed, aux = project(tokens_all, norm_rows, table, start_col, full_qkv)
        mixed_heads = attend(packed, aux)
        activated, slope = up_branch(ln_mlp, full_up)
        branch = down_branch(mixed_heads, activated, full_out, full_down)
    branch_sum = lax.psum_scatter(branch, "tensor", scatter_dimension=0, tiled=True)
    if paired:
        block, grad_half, mixed_grad, grad_norms = backward_all(
            grad_all, ln_mlp, ln_attn, activated, mixed_heads, slope, packed, aux, table, tokens_all, norm_gains,
            (full_qkv, full_out, full_up, full_down), mom_half,
        )
        owners = owner_tables()
    else:
        grad_mixed = jnp.dot(grad_all, full_out, preferred_element_type=jnp.float32).astype(jnp.bfloat16)
        grad_packed = attend_back(packed, aux, table, grad_mixed)
        grad_act = jnp.dot(grad_all, full_down, preferred_element_type=jnp.float32)
        grad_upproj = (grad_act * slope.astype(jnp.float32)).astype(jnp.bfloat16)
        grad_ln_mlp = contract_cols(grad_upproj, full_up)
        grad_ln_attn = contract_cols(grad_packed, full_qkv)
        mixed_grad = (norm_gains[0] * grad_ln_attn + norm_gains[1] * grad_ln_mlp).astype(jnp.bfloat16)
        normed_all = (tokens_all.astype(jnp.float32) - aux[:, 1:2]) * aux[:, 2:3]
        sums = [grad_ln_attn * normed_all, grad_ln_attn, grad_ln_mlp * normed_all, grad_ln_mlp]
        grad_norms = lax.psum(jnp.stack([jnp.sum(v, axis=0) for v in sums]), ("dp", "tensor"))
        lefts = (ln_attn, grad_all, ln_mlp, grad_all)
        rights = (grad_packed, mixed_heads, grad_upproj, activated)
        reduced = tuple(
            lax.psum_scatter(
                contract_rows(l, r).astype(jnp.bfloat16), "dp", scatter_dimension=0, tiled=True
            ).astype(jnp.float32)
            for l, r in zip(lefts, rights)
        )
        new_moments = tuple(MOMENTUM * m + g for m, g in zip(moments_in, reduced))
        parts = []
        for fresh, grad_rows, col_count in zip(new_moments, reduced, col_counts):
            nested = (grad_rows + MOMENTUM * fresh).astype(jnp.bfloat16)
            for head in range(local_heads):
                part = nested[:, head * col_count : (head + 1) * col_count]
                parts.append(jnp.pad(part, ((0, 0), (0, pad_width - col_count))))
        groups = lax.axis_size("dp") // len(parts)
        outgoing = jnp.tile(jnp.stack(parts), (groups, 1, 1))
        block = lax.all_to_all(outgoing, "dp", split_axis=0, concat_axis=0, tiled=True)
        block = block.reshape(row_share * lax.axis_size("dp"), pad_width)
        owners = tuple((m, h) for m in range(4) for h in range(local_heads)) * groups
    mixed_own = lax.psum_scatter(mixed_grad, "tensor", scatter_dimension=0, tiled=True)
    block, branch_sum = lax.optimization_barrier((block, branch_sum))
    if paired:
        grad_rows, ortho_rows = sweep_return(block, grad_half, tuple(col_counts[m] for m, _ in owners))
        mixed_own, ortho_rows = lax.optimization_barrier((mixed_own, ortho_rows))
        rows_in = (tokens, cotangent, mixed_own, branch_sum)
        new_moments, new_weights, grad_tokens, block_out = update_all(
            weights_in, moments_in, grad_rows, ortho_rows, rows_in, owners, col_counts
        )
    else:
        ortho_rows = hand_out(sweeps(block), row_share)
        new_weights = [
            w * (1.0 - LEARN * DECAY) - LEARN * from_owners(ortho_rows, owners, i, col_counts[i], local_heads)
            for i, w in enumerate(weights_in)
        ]
        grad_tokens = norm_back(tokens, cotangent, mixed_own)
        block_out = (tokens.astype(jnp.float32) + branch_sum.astype(jnp.float32)).astype(jnp.bfloat16)
    moment_norms = MOMENTUM * norm_moments + grad_norms
    step_scale = lax.rsqrt(jnp.mean(moment_norms * moment_norms, axis=-1, keepdims=True) + 1e-06)
    value_norms = norm_rows - NORM_LEARN * moment_norms * step_scale
    return (
        block_out,
        grad_tokens,
        new_moments[0],
        new_weights[0],
        new_moments[1],
        new_weights[1],
        new_moments[2],
        new_weights[2],
        new_moments[3],
        new_weights[3],
        moment_norms,
        value_norms,
    )


def solution(mesh):
    in_specs = (
        P(("dp", "tensor"), None),
        P(("dp", "tensor"), None),
        P("dp", None),
        P("dp", "tensor"),
        P("dp", "tensor"),
        P("dp", "tensor"),
        P("dp", "tensor"),
        P("dp", "tensor"),
        P("dp", "tensor"),
        P("dp", "tensor"),
        P("dp", "tensor"),
        P(),
        P(),
        P(),
    )
    out_specs = (
        P(("dp", "tensor"), None),
        P(("dp", "tensor"), None),
        P("dp", "tensor"),
        P("dp", "tensor"),
        P("dp", "tensor"),
        P("dp", "tensor"),
        P("dp", "tensor"),
        P("dp", "tensor"),
        P("dp", "tensor"),
        P("dp", "tensor"),
        P(),
        P(),
    )
    return jax.shard_map(
        on_device, mesh=mesh, in_specs=in_specs, out_specs=out_specs, check_vma=False
    )
```

```python
import functools
import math

import jax
import jax.numpy as jnp
import numpy as np
from jax import lax
from jax.experimental import pallas as pl
from jax.experimental.pallas import tpu as pltpu
from jax.sharding import PartitionSpec as P

HEADS = 8
HD = 256
FF = 8192
ROT = 64
DOC_MOST = 512


NS_A = 3.4445
NS_B = -4.775
NS_C = 2.0315
MOMENTUM = 0.95
LEARN = 0.5
DECAY = 0.01
NORM_LEARN = 0.05
LN_EPS = 1e-05
MASKED = -1e30


def doc_starts(seg_ids):
    index = jnp.arange(seg_ids.shape[0], dtype=jnp.int32)
    same = seg_ids[:, None] == seg_ids[None, :]
    return jnp.min(jnp.where(same, index[None, :], seg_ids.shape[0]), axis=1)


def contract_rows(left, right):
    return lax.dot_general(
        left, right, (((0,), (0,)), ((), ())), preferred_element_type=jnp.float32
    )


def contract_cols(left, right):
    return lax.dot_general(
        left, right, (((1,), (1,)), ((), ())), preferred_element_type=jnp.float32
    )


MESH = pl.DeviceIdType.MESH


def forward_kernel(order, *refs):
    n_w = len(order)
    w_refs, m_refs = refs[:n_w], refs[n_w : 2 * n_w]
    tok_ref, cot_ref, gain_ref, bias_ref, seg_ref, freq_ref = refs[2 * n_w : 2 * n_w + 6]
    refs = refs[2 * n_w + 6 :]
    full_refs, mom_ref = refs[:n_w], refs[n_w]
    tok_all, cot_all, ln_a_ref, ln_m_ref, qkv_ref, aux_ref, table_ref, o_ref, act_ref, slope_ref, branch_ref = refs[
        n_w + 1 : n_w + 12
    ]
    refs = refs[n_w + 12 :]
    w_wide, w_low = refs[:n_w], refs[n_w : 2 * n_w]
    (m_low, tok, ln_a, ln_m, qkv, aux, table, o, act, slope, gains, biases, segs, freq, w_qkv, w_out, w_up, w_down, branch,
     load_sem, own_sem, w_send, w_recv, m_send, m_recv, z_send, z_recv, side_sem, tok_sem, tile_sem, out_sem) = refs[2 * n_w :]
    dp, me, n_t = lax.axis_index("dp"), lax.axis_index("tensor"), lax.axis_size("tensor")
    y, x, c = dp // 4, (dp // 2) % 2, dp % 2
    by_x = y * 4 + (1 - x) * 2 + c
    by_y = (1 - y) * 4 + x * 2 + c
    far = (1 - y) * 4 + (1 - x) * 2 + c
    by_c = y * 4 + x * 2 + (1 - c)
    rows = w_refs[0].shape[0]
    half = rows // 2
    share = tok_ref.shape[0]
    seq, width = tok_all.shape
    loads = [pltpu.make_async_copy(w_refs[m], w_wide[m], load_sem.at[m]) for m in order]
    for cp in loads:
        cp.start()
    barrier = pltpu.get_barrier_semaphore()
    for peer in (by_x, by_y, by_c, far):
        pl.semaphore_signal(barrier, inc=1, device_id=(peer, me), device_id_type=MESH)
    for shift in range(1, n_t):
        pl.semaphore_signal(barrier, inc=1, device_id=(dp, lax.rem(me + shift, n_t)), device_id_type=MESH)
    pl.semaphore_wait(barrier, 4 + n_t - 1)

    def chain(kind, step, up):
        ref = (tok_all, cot_all)[kind]
        owner = me + 1 - step if up else me - 1 + step
        here = ref.at[pl.ds(pl.multiple_of(owner * share, share), share)]
        src = (tok_ref, cot_ref)[kind] if step == 1 else here
        return pltpu.make_async_remote_copy(
            src_ref=src, dst_ref=here, send_sem=z_send.at[kind, step, int(up)], recv_sem=z_recv.at[kind, step, int(up)],
            device_id=(dp, me + 1 if up else me - 1), device_id_type=MESH,
        )

    def chain_sends(step, up):
        return (me + 1 < n_t) & (me + 1 - step >= 0) if up else (me >= 1) & (me - 1 + step < n_t)

    def chain_gets(step, up):
        return me - step >= 0 if up else me + step < n_t

    def chain_start(kind, step):
        for up in (True, False):
            @pl.when(chain_sends(step, up))
            def _():
                chain(kind, step, up).start()

    def chain_take(kind, step):
        for up in (True, False):
            @pl.when(chain_gets(step, up))
            def _():
                chain(kind, step, up).wait_recv()

            if step + 1 < n_t:
                @pl.when(chain_sends(step + 1, up))
                def _():
                    chain(kind, step + 1, up).start()

    def part(i, dev, low, count):
        return full_refs[order[i]].at[pl.ds(pl.multiple_of(dev * rows + low, 128), count)]

    def copy(i, k):
        if k < 3:
            src, dst, peer = w_low[order[i]], part(i, dp, 0, rows), (by_x, by_y, by_c)[k]
        else:
            dev, low, count, peer = {
                3: (by_y, 0, half, by_x),
                4: (by_x, half, half, by_y),
                5: (by_x, 0, rows, by_c),
                6: (by_y, 0, rows, by_c),
                7: (far, 0, half, by_c),
                8: (far, half, half, by_c),
            }[k]
            src = dst = part(i, dev, low, count)
        return pltpu.make_async_remote_copy(
            src_ref=src, dst_ref=dst, send_sem=w_send.at[i, k], recv_sem=w_recv.at[i, k],
            device_id=(peer, me), device_id_type=MESH,
        )

    def own_start(i):
        for k in range(3):
            copy(i, k).start()

    def near_take(i):
        copy(i, 0).wait_recv()
        copy(i, 5).start()
        copy(i, 4).start()
        copy(i, 1).wait_recv()
        copy(i, 6).start()
        copy(i, 3).start()

    def far_take(i):
        for k in (3, 4):
            copy(i, k).wait_recv()
            copy(i, k + 4).start()

    def whole_take(i):
        for k in (2, 5, 6, 7, 8):
            copy(i, k).wait_recv()
        own[i].wait()

    def narrow(src, dst):
        def block(r, carry):
            here = pl.ds(pl.multiple_of(r * 32, 32), 32)
            dst[here, :] = src[here, :].astype(jnp.bfloat16)
            return carry

        lax.fori_loop(0, rows // 32, block, 0)

    own = [pltpu.make_async_copy(w_low[m], part(i, dp, 0, rows), own_sem.at[i]) for i, m in enumerate(order)]
    token_own = [
        pltpu.make_async_copy(a, b.at[pl.ds(pl.multiple_of(me * share, share), share)], own_sem.at[n_w + i])
        for i, (a, b) in enumerate(((tok_ref, tok_all), (cot_ref, cot_all)))
    ]
    chain_start(0, 1)
    for i, m in enumerate(order):
        loads[i].wait()
        narrow(w_wide[m], w_low[m])
        if i < 2:
            own_start(i)
        own[i].start()
    for cp in token_own:
        cp.start()
    sides = [
        pltpu.make_async_copy(a, b, side_sem.at[i])
        for i, (a, b) in enumerate(((gain_ref, gains), (bias_ref, biases), (seg_ref, segs), (freq_ref, freq)))
    ]
    for cp in sides:
        cp.start()
    loads = [pltpu.make_async_copy(m_refs[m], w_wide[m], load_sem.at[m]) for m in range(n_w)]
    for cp in loads:
        cp.start()
    for cp in loads:
        cp.wait()
    heads = w_refs[0].shape[1] // (3 * HD)
    wide_cols = w_refs[2].shape[1] // heads
    for dev, (m, head) in enumerate(owner_tables()):
        cols = w_refs[m].shape[1] // heads
        at = (dev % 2) * wide_cols
        narrow(w_wide[m].at[:, pl.ds(head * cols, cols)], m_low.at[dev // 2, :, pl.ds(at, cols)])

    def mom_copy(n):
        chip = ((y + n // 2) % 2) * 2 + (x + n) % 2
        return pltpu.make_async_remote_copy(
            src_ref=m_low.at[chip], dst_ref=mom_ref.at[y * 2 + x], send_sem=m_send.at[n], recv_sem=m_recv.at[n],
            device_id=(chip * 2 + c, me), device_id_type=MESH,
        )

    mom_own = pltpu.make_async_copy(m_low.at[y * 2 + x], mom_ref.at[y * 2 + x], m_send.at[0])
    mom_own.start()
    near_take(0)
    own_start(2)
    chain_take(0, 1)
    near_take(1)
    own_start(3)
    chain_take(0, 2)
    far_take(0)
    near_take(2)
    whole_take(0)
    load_qkv = pltpu.make_async_copy(full_refs[0], w_qkv, tile_sem.at[4])
    load_qkv.start()
    for step in range(3, n_t):
        chain_take(0, step)
    chain_start(1, 1)
    far_take(1)
    for cp in token_own + sides:
        cp.wait()
    tile = 256

    def tok_copy(r):
        return pltpu.make_async_copy(tok_all.at[pl.ds(pl.multiple_of(r * tile, tile), tile)], tok.at[r % 2], tok_sem.at[r % 2])

    tok_copy(jnp.int32(0)).start()
    load_qkv.wait()

    def project(r, carry):
        @pl.when(r + 1 < seq // tile)
        def _():
            tok_copy(r + 1).start()

        tok_copy(r).wait()
        here = pl.ds(pl.multiple_of(r * tile, tile), tile)
        hidden = tok[r % 2].astype(jnp.float32)
        mean = jnp.mean(hidden, axis=-1, keepdims=True)
        centred = hidden - mean
        scale = lax.rsqrt(jnp.mean(centred * centred, axis=-1, keepdims=True) + LN_EPS)
        normed = centred * scale
        ln = (normed * gains[0:1, :] + biases[0:1, :]).astype(jnp.bfloat16)
        ln_a[here, :] = ln
        ln_m[here, :] = (normed * gains[1:2, :] + biases[1:2, :]).astype(jnp.bfloat16)
        lane = lax.broadcasted_iota(jnp.int32, (tile, 128), 1)
        numbers = segs[...].astype(jnp.float32)
        mine = jnp.broadcast_to(segs[:, here].astype(jnp.float32), (128, tile)).T[:, 0:1]
        index = lax.broadcasted_iota(jnp.int32, (tile, seq), 1).astype(jnp.float32)
        first = jnp.min(jnp.where(numbers == mine, index, float(seq)), axis=1, keepdims=True)
        aux[here, :] = jnp.where(lane == 0, first, jnp.where(lane == 1, mean, scale))
        token = (r * tile + lax.broadcasted_iota(jnp.int32, (tile, 128), 0)).astype(jnp.float32)
        turns = (token - first) * freq[...]
        sine = jnp.sin(turns)
        angles = jnp.where(lane < ROT, jnp.cos(turns), jnp.where(lane < ROT + ROT // 2, -sine, sine))
        table[here, :] = angles
        raw = wide_dot(ln, w_qkv[...], NN)
        for n in range(w_qkv.shape[1] // HD):
            block = raw[:, n * HD : (n + 1) * HD]
            if n % 3 < 2:
                block = jnp.concatenate([turn(block[:, :128], angles, 1.0), block[:, 128:]], axis=1)
            qkv[here, n * HD : (n + 1) * HD] = block.astype(jnp.bfloat16)
        return carry

    lax.fori_loop(0, seq // tile, project, 0)
    outs = []

    def put(src, dst):
        cp = pltpu.make_async_copy(src, dst, out_sem.at[len(outs)])
        cp.start()
        outs.append(cp)

    put(ln_a, ln_a_ref)
    put(ln_m, ln_m_ref)
    put(qkv, qkv_ref)
    put(aux, aux_ref)
    put(table, table_ref)
    attend_kernel(qkv, aux, o)
    put(o, o_ref)
    near_take(3)
    far_take(2)
    for n in range(1, 4):
        mom_copy(n).start()
    whole_take(1)
    strip = 512
    n_up = act.shape[1] // strip

    def up_copy(j):
        return pltpu.make_async_copy(full_refs[2].at[:, pl.ds(j * strip, strip)], w_up.at[j % 2], tile_sem.at[j % 2])

    def down_copy(j):
        return pltpu.make_async_copy(full_refs[3].at[pl.ds(j * strip, strip)], w_down.at[j % 2], tile_sem.at[2 + j % 2])

    up_copy(0).start()
    chain_take(1, 1)
    for j in range(n_up):
        if j + 1 < n_up:
            up_copy(j + 1).start()
        up_copy(j).wait()
        cols = slice(j * strip, (j + 1) * strip)
        up_kernel(ln_m, w_up.at[j % 2], act.at[:, cols], slope.at[:, cols])
        if j == 1:
            far_take(3)
    put(act, act_ref)
    put(slope, slope_ref)
    whole_take(2)
    whole_take(3)
    load_out = pltpu.make_async_copy(full_refs[1], w_out, tile_sem.at[4])
    load_out.start()
    down_copy(0).start()
    load_out.wait()
    n_down = width // strip
    branch_copies = []
    for j in range(n_down):
        if j + 1 < n_down:
            down_copy(j + 1).start()
        down_copy(j).wait()
        if j >= 2:
            branch_copies[j - 2].wait()
        down_kernel(o, act, w_out.at[pl.ds(j * strip, strip)], w_down.at[j % 2], branch.at[j % 2])
        cp = pltpu.make_async_copy(branch.at[j % 2], branch_ref.at[:, pl.ds(j * strip, strip)], tok_sem.at[j % 2])
        cp.start()
        branch_copies.append(cp)
        if j == 1:
            chain_take(1, 2)
    for step in range(3, n_t):
        chain_take(1, step)
    for cp in branch_copies[-2:] + outs + [mom_own]:
        cp.wait()
    for i in range(n_w):
        for k in range(9):
            copy(i, k).wait_send()
    for n in range(1, 4):
        mom_copy(n).wait()
    for kind in range(2):
        for step in range(1, n_t):
            for up in (True, False):
                @pl.when(chain_sends(step, up))
                def _():
                    chain(kind, step, up).wait_send()


def forward_all(weights, moments, tokens, cotangent, gains, biases, segments):
    n_w = len(weights)
    rows, bf, f32 = weights[0].shape[0], jnp.bfloat16, jnp.float32
    n_t = lax.axis_size("tensor")
    share, width = tokens.shape
    seq = share * n_t
    qkv_cols, out_cols, units = (weights[i].shape[1] for i in range(3))
    mom_cols = units // 2 + 3 * HD
    freq = np.tile(10000.0 ** (-2.0 * np.arange(ROT // 2) / ROT), 4).astype(np.float32)[None]
    anyspec = pl.BlockSpec(memory_space=pl.ANY)
    V, S = pltpu.VMEM, pltpu.SemaphoreType.DMA
    array = jax.ShapeDtypeStruct
    out = pl.pallas_call(
        functools.partial(forward_kernel, (0, 2, 1, 3)),
        out_shape=[array((rows * 8, w.shape[1]), bf) for w in weights]
        + [array((4, rows, mom_cols), bf), array((seq, width), bf), array((seq, width), bf), array((seq, width), bf),
           array((seq, width), bf), array((seq, qkv_cols), bf), array((seq, 128), f32), array((seq, 128), f32), array((seq, out_cols), bf),
           array((seq, units), bf), array((seq, units), bf), array((seq, width), bf)],
        in_specs=[anyspec] * (2 * n_w + 6),
        out_specs=[anyspec] * (n_w + 12),
        scratch_shapes=[V(w.shape, w.dtype) for w in weights]
        + [V(w.shape, bf) for w in weights]
        + [V((4, rows, mom_cols), bf), V((2, 256, width), bf), V((seq, width), bf), V((seq, width), bf),
           V((seq, qkv_cols), bf), V((seq, 128), f32), V((seq, 128), f32), V((seq, out_cols), bf), V((seq, units), bf),
           V((seq, units), bf), V(gains.shape, f32), V(biases.shape, f32), V(segments.shape, jnp.int32),
           V(freq.shape, f32), V((width, qkv_cols), bf),
           V((width, out_cols), bf), V((2, width, 512), bf), V((2, 512, units), bf), V((2, seq, 512), bf),
           S((n_w,)), S((n_w + 2,)), S((n_w, 9)), S((n_w, 9)), S((4,)), S((4,)), S((2, n_t, 2)), S((2, n_t, 2)),
           S((4,)), S((2,)), S((5,)), S((8,))],
        compiler_params=pltpu.CompilerParams(collective_id=0, has_side_effects=True, vmem_limit_bytes=63 * 2**20),
        cost_estimate=pl.CostEstimate(flops=140 * 10**9, bytes_accessed=100 * 2**20, transcendentals=0),
        name="forward_all",
    )(*weights, *moments, tokens, cotangent, gains, biases, segments, freq)
    return out[:n_w], out[n_w:]


TILE = 256
STRIP = 512
SLOTS = 8
EVEN_STEPS, SHARED_STEPS, ALL_STEPS = 16, 20, 28


def owner_tables():
    return ((2, 0), (1, 0), (3, 0), (0, 0), (3, 1), (0, 1), (2, 1), (1, 1))


def backward_kernel(*refs):
    (dy_ref, ln_m_ref, ln_a_ref, act_ref, o_ref, slope_ref, qkv_ref, aux_ref, table_ref, tok_ref, norm_ref,
     w_down_ref, w_out_ref, w_up_ref, w_qkv_ref, mom_ref) = refs[:16]
    block_ref, grad_ref, u_ref, sums_ref = refs[16:20]
    (lhs, rhs, sib_send, own, sib_recv, far_x, far_y, in_x, in_y, far_send, x_send, y_send, mom, g_out, e_out,
     qkv, d_o, d_key, d_value, aux, table, w_tile, slope, row_q, row_u, tok, u_tile, norm, sums, z_in, z_sum, dp_in,
     lhs_sem, mom_sem, out_sem, keep_sem, give_ss, give_rs, sib_ss, sib_rs, fx_ss, fx_rs, fy_ss, fy_rs, x_ss, x_rs, y_ss, y_rs,
     side_sem, w_sem, slope_sem, row_sem, u_sem, z_ss, z_rs, d_ss, d_rs, sums_sem) = refs[20:]
    dp = lax.axis_index("dp")
    t = lax.axis_index("tensor")
    n_t = lax.axis_size("tensor")
    y, x, c = dp // 4, (dp // 2) % 2, dp % 2
    seq, width = dy_ref.shape
    units, heads_width = act_ref.shape[1], o_ref.shape[1]
    at_up, at_o, at_qkv = units, 2 * units, 2 * units + heads_width
    share = STRIP // 2
    half = share // 2
    strips = width // STRIP
    by_x = y * 4 + (1 - x) * 2 + c
    by_y = (1 - y) * 4 + x * 2 + c
    by_c = y * 4 + x * 2 + (1 - c)
    barrier = pltpu.get_barrier_semaphore()
    for shift in range(1, 8):
        pl.semaphore_signal(barrier, inc=1, device_id=(lax.rem(dp + shift, 8), t), device_id_type=MESH)
    for shift in range(1, n_t):
        pl.semaphore_signal(barrier, inc=1, device_id=(dp, lax.rem(t + shift, n_t)), device_id_type=MESH)

    def wide(v):
        return v.astype(jnp.float32)

    def low(v):
        return v.astype(jnp.bfloat16)

    def remote(src, dst, ss, rs, peer):
        return pltpu.make_async_remote_copy(src_ref=src, dst_ref=dst, send_sem=ss, recv_sem=rs, device_id=(peer, t), device_id_type=MESH)

    def local(src, dst, sem):
        return pltpu.make_async_copy(src, dst, sem)

    def outer(k):
        return (k < SHARED_STEPS) | (x != y)

    def inner(k):
        return (k < SHARED_STEPS) | (x == y)

    def place(k):
        step = jnp.where(k < EVEN_STEPS, k, k - EVEN_STEPS)
        return step % strips, step // strips

    def holder_slice(ref, k):
        strip, tile = place(k)
        col = jnp.where(k < EVEN_STEPS, 0, units // 2) + tile * TILE
        return ref.at[strip, :, pl.ds(pl.multiple_of(col, TILE), TILE)]

    def mom_copy(k):
        return local(holder_slice(mom_ref, k), mom.at[k % SLOTS], mom_sem.at[k % SLOTS])

    def grad_copy(k):
        return local(g_out.at[k % 2], holder_slice(grad_ref, k), keep_sem.at[k % 2])

    def out_copy(k):
        strip, tile = place(k)
        rows = pl.ds(pl.multiple_of(strip * STRIP + c * share, TILE), share)
        dst = block_ref.at[rows, pl.ds(pl.multiple_of(tile * TILE, TILE), TILE)]
        return local(e_out.at[k % 2], dst, out_sem.at[k % 2]), remote(e_out.at[k % 2], dst, give_ss.at[k % 2], give_rs, by_c)

    def keeps(k):
        return jnp.where(k < EVEN_STEPS, c == 0, c == 1)

    def out_start(k):
        here, there = out_copy(k)
        grad_copy(k).start()

        @pl.when(keeps(k))
        def _():
            here.start()

        @pl.when(jnp.logical_not(keeps(k)))
        def _():
            there.start()

    def out_wait(k):
        here, there = out_copy(k)
        grad_copy(k).wait()

        @pl.when(keeps(k))
        def _():
            here.wait()

        @pl.when(jnp.logical_not(keeps(k)))
        def _():
            there.wait_send()

    def sib_copy(k):
        return remote(sib_send.at[k % 2], sib_recv.at[k % SLOTS], sib_ss.at[k % 2], sib_rs.at[k % SLOTS], by_c)

    def far_copy_x(k):
        return remote(far_send.at[k % 2, pl.ds(0, half)], far_x.at[k % SLOTS], fx_ss.at[k % 2], fx_rs.at[k % SLOTS], by_x)

    def far_copy_y(k):
        return remote(far_send.at[k % 2, pl.ds(half, half)], far_y.at[k % SLOTS], fy_ss.at[k % 2], fy_rs.at[k % SLOTS], by_y)

    def copy_x(k):
        return remote(x_send.at[k % 2], in_x.at[k % SLOTS], x_ss.at[k % 2], x_rs.at[k % SLOTS], by_x)

    def copy_y(k):
        return remote(y_send.at[k % 2], in_y.at[k % SLOTS], y_ss.at[k % 2], y_rs.at[k % SLOTS], by_y)

    n_down, n_out = units // TILE, heads_width // TILE

    def down_cols(j):
        return pl.ds(pl.multiple_of((j % 2) * (units // 2) + (j // 2) * TILE, TILE), TILE)

    def w_start(j):
        @pl.when(j < n_down)
        def _():
            local(w_down_ref.at[:, down_cols(j)], w_tile.at[j % 2], w_sem.at[j % 2]).start()
            local(slope_ref.at[:, down_cols(j)], slope.at[j % 2], slope_sem.at[j % 2]).start()

        @pl.when(j >= n_down)
        def _():
            cols = pl.ds(pl.multiple_of((j - n_down) * TILE, TILE), TILE)
            local(w_out_ref.at[:, cols], w_tile.at[j % 2], w_sem.at[j % 2]).start()

    def row_copies(j):
        here = pl.ds(pl.multiple_of(j * TILE, TILE), TILE)
        slot = j % 2
        return (
            local(w_qkv_ref.at[here], row_q.at[slot], row_sem.at[slot, 0]),
            local(w_up_ref.at[here], row_u.at[slot], row_sem.at[slot, 1]),
            local(tok_ref.at[:, here], tok.at[slot], row_sem.at[slot, 2]),
        )

    def u_copy(j):
        return local(u_tile.at[j % 2], u_ref.at[:, pl.ds(pl.multiple_of(j * TILE, TILE), TILE)], u_sem.at[j % 2])

    lhs_copies = [local(ref, lhs.at[i], lhs_sem.at[i]) for i, ref in enumerate((dy_ref, ln_m_ref, ln_a_ref))]
    pairs = ((act_ref, rhs.at[:, pl.ds(0, units)]), (o_ref, rhs.at[:, pl.ds(at_o, heads_width)]), (qkv_ref, qkv),
             (aux_ref, aux), (table_ref, table), (norm_ref, norm))
    sides = [local(a, b, side_sem.at[i]) for i, (a, b) in enumerate(pairs)]
    lhs_copies[0].start()
    w_start(jnp.int32(0))
    w_start(jnp.int32(1))
    sides[0].start()
    lhs_copies[1].start()
    for cp in sides[1:]:
        cp.start()
    lhs_copies[2].start()
    sums[...] = jnp.zeros_like(sums)
    lhs_copies[0].wait()

    def made_by_dy(j):
        slot = j % 2
        local(w_out_ref.at[:, pl.ds(0, TILE)], w_tile.at[slot], w_sem.at[slot]).wait()

        @pl.when(j < n_down)
        def _():
            local(slope_ref.at[:, pl.ds(0, TILE)], slope.at[slot], slope_sem.at[slot]).wait()
            cols = pl.ds(pl.multiple_of(at_up + (j % 2) * (units // 2) + (j // 2) * TILE, TILE), TILE)
            for r in range(2):
                here = slice(r * (seq // 2), (r + 1) * (seq // 2))
                rhs[here, cols] = low(wide_dot(lhs[0, here, :], w_tile[slot], NN) * wide(slope[slot, here, :]))

        @pl.when(j >= n_down)
        def _():
            cols = pl.ds(pl.multiple_of((j - n_down) * TILE, TILE), TILE)
            for r in range(2):
                here = slice(r * (seq // 2), (r + 1) * (seq // 2))
                d_o[here, cols] = low(wide_dot(lhs[0, here, :], w_tile[slot], NN))

    def input_tile(j):
        slot = j % 2
        for cp in row_copies(j):
            cp.wait()

        @pl.when(j + 1 < width // TILE)
        def _():
            for cp in row_copies(j + 1):
                cp.start()

        @pl.when(j >= 2)
        def _():
            u_copy(j - 2).wait()

        cols = pl.ds(pl.multiple_of(j * TILE, TILE), TILE)
        gain_a, gain_m = norm[0:1, cols], norm[1:2, cols]

        total = jnp.zeros((4, TILE), jnp.float32)
        for r in range(2):
            here = slice(r * (seq // 2), (r + 1) * (seq // 2))
            by_a = wide_dot(rhs[here, pl.ds(at_qkv, qkv_ref.shape[1])], row_q[slot], NT)
            by_m = wide_dot(rhs[here, pl.ds(at_up, units)], row_u[slot], NT)
            normed = (wide(tok[slot, here, :]) - aux[here, 1:2]) * aux[here, 2:3]
            u_tile[slot, here, :] = low(gain_a * by_a + gain_m * by_m)
            parts = [jnp.sum(v, axis=0, keepdims=True) for v in (by_a * normed, by_a, by_m * normed, by_m)]
            total = total + jnp.concatenate(parts, axis=0)
        sums[:, cols] = total
        u_copy(j).start()

    def z_copy(shift):
        return pltpu.make_async_remote_copy(src_ref=sums, dst_ref=z_in.at[shift], send_sem=z_ss.at[shift], recv_sem=z_rs.at[shift], device_id=(dp, lax.rem(t + shift, n_t)), device_id_type=MESH)

    def dp_copy(shift):
        return remote(z_sum, dp_in.at[shift], d_ss.at[shift], d_rs.at[shift], lax.rem(dp + shift, 8))

    n_tiles = width // TILE
    n_blocks = seq // TILE
    first_attend = n_down + n_out
    paired_blocks = first_attend + 2 * n_blocks - EVEN_STEPS
    first_input = EVEN_STEPS + 1
    d_qkv = rhs.at[:, pl.ds(at_qkv, qkv_ref.shape[1])]

    made_by_dy(jnp.int32(0))
    made_by_dy(jnp.int32(1))
    w_start(jnp.int32(2))
    pl.semaphore_wait(barrier, 7 + n_t - 1)

    def step(i, carry):
        k1 = i
        k2 = i - 1
        k3 = i - 2
        k4 = i - 3

        @pl.when(k1 < ALL_STEPS)
        def _():
            @pl.when(k1 == 0)
            def _():
                sides[0].wait()
                lhs_copies[1].wait()

            @pl.when(k1 == EVEN_STEPS)
            def _():
                lhs_copies[2].wait()

            strip, tile = place(k1)

            @pl.when(k1 >= 2)
            def _():
                sib_copy(k1 - 2).wait_send()

            def piece(q):
                px = x + (q % 2) * (1 - 2 * x)
                py = y + (q // 2) * (1 - 2 * y)
                even = k1 < EVEN_STEPS
                plain = px == py
                which = jnp.where(even, jnp.where(plain, 1, 0), jnp.where(plain, 0, 2))
                col_even = jnp.where(plain, at_up, 0) + py * (units // 2) + tile * TILE
                col_odd = jnp.where(plain, at_o + py * TILE, at_qkv + py * (3 * HD) + tile * TILE)
                col = pl.multiple_of(jnp.where(even, col_even, col_odd), TILE)
                row = strip * STRIP
                right = rhs[:, pl.ds(col, TILE)]
                left = lhs[which, :, pl.ds(pl.multiple_of(row + (1 - c) * share, TILE), share)]
                sib_send[k1 % 2, q] = low(wide_dot(left, right, TN))
                left = lhs[which, :, pl.ds(pl.multiple_of(row + c * share, TILE), share)]
                own[k1 % SLOTS, q] = wide_dot(left, right, TN)

            @pl.when(k1 < SHARED_STEPS)
            def _():
                for q in range(4):
                    piece(q)

            @pl.when(k1 >= SHARED_STEPS)
            def _():
                piece(jnp.where(x == y, 1, 0))
                piece(jnp.where(x == y, 2, 3))

            sib_copy(k1).start()

        @pl.when((k2 >= 0) & (k2 < ALL_STEPS))
        def _():
            sib_copy(k2).wait_recv()

            @pl.when(outer(k2))
            def _():
                @pl.when(k2 >= 2)
                def _():
                    @pl.when(outer(k2 - 2))
                    def _():
                        far_copy_x(k2 - 2).wait_send()
                        far_copy_y(k2 - 2).wait_send()

                far_send[k2 % 2] = low(own[k2 % SLOTS, 3] + wide(sib_recv[k2 % SLOTS, 3]))
                far_copy_x(k2).start()
                far_copy_y(k2).start()

        @pl.when((i >= 2) & (i < n_down + n_out))
        def _():
            made_by_dy(i)

            @pl.when(i + 1 < n_down + n_out)
            def _():
                w_start(i + 1)

        for block in range(2 * n_blocks):
            @pl.when(i == first_attend + (block // 2 if block < 2 * paired_blocks else block - paired_blocks))
            def _():
                if block == 0:
                    for cp in sides[1:]:
                        cp.wait()
                attend_back_block(qkv, aux, table, d_o, d_qkv, d_key, d_value, block // n_blocks, block % n_blocks, block % n_blocks == n_blocks - 1)

        @pl.when((k3 >= 0) & (k3 < ALL_STEPS) & inner(k3))
        def _():
            @pl.when(k3 >= 2)
            def _():
                @pl.when(inner(k3 - 2))
                def _():
                    copy_x(k3 - 2).wait_send()
                    copy_y(k3 - 2).wait_send()

            far_copy_x(k3).wait_recv()
            far_copy_y(k3).wait_recv()
            first, last = pl.ds(0, half), pl.ds(half, half)

            def chip_sum(q, part):
                return own[k3 % SLOTS, q, part] + wide(sib_recv[k3 % SLOTS, q, part])

            y_send[k3 % 2, first] = low(chip_sum(2, first) + wide(far_x[k3 % SLOTS]))
            y_send[k3 % 2, last] = low(chip_sum(2, last))
            copy_y(k3).start()
            x_send[k3 % 2, first] = low(chip_sum(1, first))
            x_send[k3 % 2, last] = low(chip_sum(1, last) + wide(far_y[k3 % SLOTS]))
            copy_x(k3).start()

        @pl.when((k2 >= 0) & (k2 < ALL_STEPS) & outer(k2))
        def _():
            mom_copy(k2).start()

        @pl.when(i == first_input - 1)
        def _():
            for cp in row_copies(0):
                cp.start()

        @pl.when((i >= first_input) & (i < first_input + n_tiles))
        def _():
            input_tile(i - first_input)

        @pl.when(i == first_input + n_tiles)
        def _():
            for shift in range(1, n_t):
                z_copy(shift).start()

        @pl.when(i == first_input + n_tiles + 2)
        def _():
            total = sums[...]
            for shift in range(1, n_t):
                z_copy(shift).wait_recv()
                total = total + z_in[shift]
            z_sum[...] = total
            for shift in range(1, 8):
                dp_copy(shift).start()

        @pl.when((k4 >= 0) & outer(k4))
        def _():
            @pl.when(k4 >= 2)
            def _():
                @pl.when(outer(k4 - 2))
                def _():
                    out_wait(k4 - 2)

            copy_x(k4).wait_recv()
            copy_y(k4).wait_recv()
            mom_copy(k4).wait()
            grad = own[k4 % SLOTS, 0] + wide(sib_recv[k4 % SLOTS, 0]) + wide(in_x[k4 % SLOTS]) + wide(in_y[k4 % SLOTS])
            g_out[k4 % 2] = low(grad)
            e_out[k4 % 2] = low(grad + MOMENTUM * (MOMENTUM * wide(mom[k4 % SLOTS]) + grad))
            out_start(k4)

        return carry

    lax.fori_loop(0, ALL_STEPS + 3, step, 0)
    for last, here, there in ((SHARED_STEPS, x == y, x != y), (ALL_STEPS, x != y, x == y)):
        for k in (last - 2, last - 1):
            k = jnp.int32(k)
            if last == ALL_STEPS:
                sib_copy(k).wait_send()

            @pl.when(here)
            def _():
                far_copy_x(k).wait_send()
                far_copy_y(k).wait_send()
                out_wait(k)

            @pl.when(there)
            def _():
                copy_x(k).wait_send()
                copy_y(k).wait_send()

    for odd in range(2):
        for apart in range(2):
            cols = (units // 2 if odd == 0 else (3 * HD if apart else HD))

            @pl.when((c == odd) & (jnp.where(x == y, 0, 1) == apart))
            def _():
                seen = block_ref.at[pl.ds(0, width // 2), pl.ds(0, cols)]
                local(seen, seen, give_rs).wait()

    total = z_sum[...]
    for shift in range(1, 8):
        dp_copy(shift).wait_recv()
        total = total + dp_in[shift]
    sums_out = local(z_in.at[0], sums_ref, sums_sem)
    z_in[0] = total
    sums_out.start()
    for shift in range(1, n_t):
        z_copy(shift).wait_send()
    for shift in range(1, 8):
        dp_copy(shift).wait_send()
    u_copy(n_tiles - 2).wait()
    u_copy(n_tiles - 1).wait()
    sums_out.wait()


def backward_all(dy, ln_m, ln_a, act, o, slope, qkv, aux, table, tok, norm_rows, full, mom):
    full_qkv, full_out, full_up, full_down = full
    seq, width = dy.shape
    n_t = lax.axis_size("tensor")
    anyspec = pl.BlockSpec(memory_space=pl.ANY)
    bf, f32 = jnp.bfloat16, jnp.float32
    V, S = pltpu.VMEM, pltpu.SemaphoreType.DMA
    rhs_width = 2 * act.shape[1] + o.shape[1] + qkv.shape[1]
    piece = (STRIP // 2, TILE)
    halved = (STRIP // 4, TILE)
    scratch = [
        V((3, seq, width), bf), V((seq, rhs_width), bf), V((2, 4, *piece), bf), V((SLOTS, 4, *piece), f32),
        V((SLOTS, 4, *piece), bf), V((SLOTS, *halved), bf), V((SLOTS, *halved), bf), V((SLOTS, *piece), bf),
        V((SLOTS, *piece), bf), V((2, *piece), bf), V((2, *piece), bf), V((2, *piece), bf), V((SLOTS, *piece), bf),
        V((2, *piece), bf), V((2, *piece), bf),
        V(qkv.shape, bf), V(o.shape, bf), V((seq, HD), f32), V((seq, HD), f32), V(aux.shape, f32), V(table.shape, f32),
        V((2, width, TILE), bf), V((2, seq, TILE), bf), V((2, TILE, qkv.shape[1]), bf), V((2, TILE, act.shape[1]), bf),
        V((2, seq, TILE), bf), V((2, seq, TILE), bf), V(norm_rows.shape, f32), V((4, width), f32), V((n_t, 4, width), f32),
        V((4, width), f32), V((8, 4, width), f32),
        S((3,)), S((SLOTS,)), S((2,)), S((2,)), S((2,)), S, S((2,)), S((SLOTS,)), S((2,)), S((SLOTS,)), S((2,)), S((SLOTS,)),
        S((2,)), S((SLOTS,)), S((2,)), S((SLOTS,)),
        S((6,)), S((2,)), S((2,)), S((2, 3)), S((2,)), S((n_t,)), S((n_t,)), S((8,)), S((8,)), S,
    ]
    block = jax.ShapeDtypeStruct((width, act.shape[1] // 2), bf)
    return pl.pallas_call(
        backward_kernel,
        out_shape=[block, jax.ShapeDtypeStruct(mom.shape, bf), jax.ShapeDtypeStruct((seq, width), bf), jax.ShapeDtypeStruct((4, width), f32)],
        in_specs=[anyspec] * 16,
        out_specs=[anyspec] * 4,
        scratch_shapes=scratch,
        compiler_params=pltpu.CompilerParams(collective_id=1, has_side_effects=True, vmem_limit_bytes=63 * 2**20),
        cost_estimate=pl.CostEstimate(flops=120 * 10**9, bytes_accessed=100 * 2**20, transcendentals=0),
        name="backward_all",
    )(dy, ln_m, ln_a, act, o, slope, qkv, aux, table, tok, norm_rows, full_down, full_out, full_up, full_qkv, mom)


NT = (((1,), (1,)), ((), ()))
NN = (((1,), (0,)), ((), ()))


def wide_dot(left, right, dims):
    return lax.dot_general(left, right, dims, preferred_element_type=jnp.float32)


def sweep_all(block_ref, o_ref, flipped, gram, poly, cols, strip_of=None, done=None):
    rows = o_ref.shape[0]
    tile, strip = 256, 512
    high = strip if cols % strip == 0 else tile

    def squares(i, total):
        here = pl.ds(pl.multiple_of(i * tile, tile), tile)
        part = block_ref[here, :cols].astype(jnp.float32)
        return total + jnp.sum((part * part).reshape(tile // 8, 8, cols), axis=0)

    total = jnp.sum(lax.fori_loop(0, rows // tile, squares, jnp.zeros((8, cols), jnp.float32)))
    scale = 1.0 / (jnp.sqrt(total) + 1e-07)
    for i in range(rows // tile):
        here = slice(i * tile, (i + 1) * tile)
        flipped[:cols, here] = (block_ref[here, :cols].astype(jnp.float32) * scale).T.astype(jnp.bfloat16)
    pairs = [(i, j) for i in range(cols // tile) for j in range(i, cols // tile)]

    def sweep(step, carry):
        for i, j in pairs:
            a, b = slice(i * tile, (i + 1) * tile), slice(j * tile, (j + 1) * tile)
            part = wide_dot(flipped[a, :], flipped[b, :], NT).astype(jnp.bfloat16)
            gram[a, b] = part
            if i != j:
                gram[b, a] = part.T
        for i, j in pairs:
            a, b = slice(i * tile, (i + 1) * tile), slice(j * tile, (j + 1) * tile)
            part = NS_B * gram[a, b].astype(jnp.float32) + NS_C * wide_dot(gram[a, :cols], gram[:cols, b], NN)
            part = part.astype(jnp.bfloat16)
            poly[a, b] = part
            if i != j:
                poly[b, a] = part.T

        def update(n, inner):
            n = n if strip_of is None else strip_of(n)
            part = pl.ds(pl.multiple_of(n * strip, strip), strip)
            old = flipped[:cols, part]
            for m in range(cols // high):
                own = slice(m * high, (m + 1) * high)
                flipped[own, part] = (
                    NS_A * old[own].astype(jnp.float32) + wide_dot(poly[own, :cols], old, NN)
                ).astype(jnp.bfloat16)

            @pl.when(step == 4)
            def _():
                for r in range(strip // tile):
                    here = pl.ds(pl.multiple_of(n * strip + r * tile, tile), tile)
                    o_ref[here, :cols] = flipped[:cols, here].astype(jnp.float32).T.astype(jnp.bfloat16)
                if done is not None:
                    done(n)

            return inner

        for n in range(rows // strip):
            update(jnp.int32(n), 0)
        return carry

    lax.fori_loop(0, 5, sweep, 0)


def sweep_kernel(e_ref, o_ref, flipped, gram, poly):
    sweep_all(e_ref, o_ref, flipped, gram, poly, e_ref.shape[1])


def sweep_scratch(rows, cols):
    shapes = ((cols, rows), (cols, cols), (cols, cols))
    return [pltpu.VMEM(shape, jnp.bfloat16) for shape in shapes]


SWEEP_COST = dict(flops=55 * 10**9, bytes_accessed=8 * 2**20, transcendentals=0)


def sweeps(block):
    whole = pl.BlockSpec(memory_space=pltpu.VMEM)
    return pl.pallas_call(
        sweep_kernel,
        out_shape=jax.ShapeDtypeStruct(block.shape, jnp.bfloat16),
        in_specs=[whole],
        out_specs=whole,
        scratch_shapes=sweep_scratch(*block.shape),
        compiler_params=pltpu.CompilerParams(vmem_limit_bytes=63 * 2**20),
        cost_estimate=pl.CostEstimate(**SWEEP_COST),
        name="sweeps",
    )(block)


def sweep_return_kernel(
    widths, block_ref, grad_ref, rows_ref, ortho_ref, out, flipped, gram, poly,
    grad_ss, grad_rs, ortho_ss, ortho_rs, own_sem,
):
    dp, t = lax.axis_index("dp"), lax.axis_index("tensor")
    y, x, c = dp // 4, (dp // 2) % 2, dp % 2
    share, cols = ortho_ref.shape[1:]
    barrier = pltpu.get_barrier_semaphore()
    for shift in range(1, 8):
        pl.semaphore_signal(barrier, inc=1, device_id=(lax.rem(dp + shift, 8), t), device_id_type=MESH)
    pl.semaphore_wait(barrier, 7)

    def of_width(mine, fn):
        for width in sorted(set(mine)):
            here = functools.reduce(jnp.logical_or, [dp == dev for dev, w in enumerate(mine) if w == width])

            @pl.when(here)
            def _():
                fn(width)

    both = tuple(cols + widths[dev // 2 * 2 + 1] for dev in range(8))

    def grad_pair(chip, width):
        src, dst = grad_ref.at[chip, :, pl.ds(0, width)], rows_ref.at[y * 2 + x, :, pl.ds(0, width)]
        far = pltpu.make_async_remote_copy(
            src_ref=src, dst_ref=dst, send_sem=grad_ss.at[chip], recv_sem=grad_rs.at[y * 2 + x],
            device_id=(chip * 2 + c, t), device_id_type=MESH,
        )
        return far, pltpu.make_async_copy(src, dst, own_sem.at[0])

    def ortho_pair(peer, width):
        src = out.at[pl.ds(pl.multiple_of(peer * share, share), share), pl.ds(0, width)]
        dst = ortho_ref.at[dp, :, pl.ds(0, width)]
        far = pltpu.make_async_remote_copy(
            src_ref=src, dst_ref=dst, send_sem=ortho_ss.at[peer], recv_sem=ortho_rs.at[dp],
            device_id=(peer, t), device_id_type=MESH,
        )
        return far, pltpu.make_async_copy(src, dst, own_sem.at[1])

    def either(pair, away, start):
        far, here = pair

        @pl.when(away)
        def _():
            far.start() if start else far.wait_send()

        @pl.when(jnp.logical_not(away))
        def _():
            here.start() if start else here.wait()

    def chip_of(n):
        px = x + ((3 - n) % 2) * (1 - 2 * x)
        py = y + ((3 - n) // 2) * (1 - 2 * y)
        return py * 2 + px

    def grads(start):
        def go(width):
            for n in range(4):
                either(grad_pair(chip_of(n), width), n < 3, start)

        of_width(both, go)

    grads(True)

    def work(width):
        def done(strip):
            for core in range(2):
                peer = strip * 2 + core
                either(ortho_pair(peer, width), peer != dp, True)

        sweep_all(block_ref, out, flipped, gram, poly, width, chip_of, done)

    of_width(widths, work)
    grads(False)
    for chip in range(4):
        @pl.when(chip != y * 2 + x)
        def _():
            seen = rows_ref.at[chip, :, pl.ds(0, both[2 * chip])]
            pltpu.make_async_copy(seen, seen, grad_rs.at[chip]).wait()

    def sent(width):
        for peer in range(8):
            either(ortho_pair(peer, width), peer != dp, False)

    of_width(widths, sent)
    for dev in range(8):
        @pl.when(dev != dp)
        def _():
            seen = ortho_ref.at[dev, :, pl.ds(0, widths[dev])]
            pltpu.make_async_copy(seen, seen, ortho_rs.at[dev]).wait()


def sweep_return(block, grad_half, widths):
    rows, cols = block.shape
    whole, anyspec = pl.BlockSpec(memory_space=pltpu.VMEM), pl.BlockSpec(memory_space=pl.ANY)
    four, eight = pltpu.SemaphoreType.DMA((4,)), pltpu.SemaphoreType.DMA((8,))
    return pl.pallas_call(
        functools.partial(sweep_return_kernel, widths),
        out_shape=[
            jax.ShapeDtypeStruct(grad_half.shape, jnp.bfloat16),
            jax.ShapeDtypeStruct((8, rows // 8, cols), jnp.bfloat16),
        ],
        in_specs=[whole, anyspec],
        out_specs=[anyspec] * 2,
        scratch_shapes=[pltpu.VMEM((rows, cols), jnp.bfloat16)]
        + sweep_scratch(rows, cols)
        + [four, four, eight, eight, pltpu.SemaphoreType.DMA((2,))],
        compiler_params=pltpu.CompilerParams(collective_id=2, has_side_effects=True, vmem_limit_bytes=63 * 2**20),
        cost_estimate=pl.CostEstimate(**SWEEP_COST),
        name="sweep_return",
    )(block, grad_half)


def norm_back(tokens, cotangent, mixed):
    hidden, mixed = tokens.astype(jnp.float32), mixed.astype(jnp.float32)
    centred = hidden - jnp.mean(hidden, axis=-1, keepdims=True)
    scale = lax.rsqrt(jnp.mean(centred * centred, axis=-1, keepdims=True) + LN_EPS)
    normed = centred * scale
    inner = mixed - jnp.mean(mixed, axis=-1, keepdims=True) - normed * jnp.mean(mixed * normed, axis=-1, keepdims=True)
    return cotangent.astype(jnp.float32) + scale * inner


def update_kernel(places, width_of, *refs):
    n = len(width_of)
    w_refs, m_refs = refs[:n], refs[n : 2 * n]
    grad_ref, ortho_ref, tok_ref, cot_ref, mixed_ref, branch_ref = refs[2 * n : 2 * n + 6]
    new_m, new_w, out_ref, sum_ref = refs[2 * n + 6 : 3 * n + 6], refs[3 * n + 6 : 4 * n + 6], refs[4 * n + 6], refs[4 * n + 7]
    sum_ref[...] = (tok_ref[...].astype(jnp.float32) + branch_ref[...].astype(jnp.float32)).astype(jnp.bfloat16)
    out_ref[...] = norm_back(tok_ref[...], cot_ref[...], mixed_ref[...])
    for dev, (m, head) in enumerate(places):
        width = width_of[m]
        cols = slice(head * width, (head + 1) * width)
        at = (dev % 2) * ortho_ref.shape[2]
        grad = grad_ref[dev // 2, :, at : at + width].astype(jnp.float32)
        new_m[m][:, cols] = MOMENTUM * m_refs[m][:, cols] + grad
        ortho = ortho_ref[dev, :, :width].astype(jnp.float32)
        new_w[m][:, cols] = w_refs[m][:, cols] * (1.0 - LEARN * DECAY) - LEARN * ortho


def update_all(weights, moments, grad_rows, ortho_rows, rows_in, places, width_of):
    rows = weights[0].shape[0]
    tile = 64
    flat = [pl.BlockSpec((tile, w.shape[1]), lambda i: (i, 0)) for w in weights]
    strip = pl.BlockSpec((tile, rows_in[0].shape[1]), lambda i: (i, 0))
    block = lambda part: pl.BlockSpec((part.shape[0], tile, part.shape[2]), lambda i: (0, i, 0))
    out = pl.pallas_call(
        functools.partial(update_kernel, places, width_of),
        grid=(rows // tile,),
        out_shape=[jax.ShapeDtypeStruct(w.shape, w.dtype) for w in weights] * 2
        + [jax.ShapeDtypeStruct(rows_in[0].shape, jnp.float32), jax.ShapeDtypeStruct(rows_in[0].shape, jnp.bfloat16)],
        in_specs=flat * 2 + [block(grad_rows), block(ortho_rows)] + [strip] * 4,
        out_specs=flat * 2 + [strip] * 2,
        compiler_params=pltpu.CompilerParams(vmem_limit_bytes=63 * 2**20),
        cost_estimate=pl.CostEstimate(flops=10**7, bytes_accessed=34 * 2**20, transcendentals=0),
        name="update_all",
    )(*weights, *moments, grad_rows, ortho_rows, *rows_in)
    return out[: len(weights)], out[len(weights) : -2], out[-2], out[-1]


def turn(part, table, sign):
    half = ROT // 2
    lane = lax.broadcasted_iota(jnp.int32, part.shape, 1)
    sines = pltpu.roll(table, 128 - ROT, 1)
    ahead = pltpu.roll(part, 128 - half, 1)
    back = pltpu.roll(part, half, 1)
    partner = jnp.where(lane < half, ahead, back)
    return jnp.where(lane < ROT, part * table + sign * (partner * sines), part)


def rotary_table(positions):
    half = ROT // 2
    inv_freq = 10000.0 ** (-2.0 * jnp.arange(half, dtype=jnp.float32) / ROT)
    angles = positions.astype(jnp.float32)[:, None] * inv_freq[None, :]
    cosine, sine = jnp.cos(angles), jnp.sin(angles)
    return jnp.concatenate([cosine, cosine, -sine, sine], axis=1)


def project_kernel(tok_ref, norm_ref, table_ref, start_ref, w_ref, ln_a_ref, ln_m_ref, qkv_ref, aux_ref):
    hidden = tok_ref[...].astype(jnp.float32)
    mean = jnp.mean(hidden, axis=-1, keepdims=True)
    centred = hidden - mean
    scale = lax.rsqrt(jnp.mean(centred * centred, axis=-1, keepdims=True) + LN_EPS)
    normed = centred * scale
    ln_a = (normed * norm_ref[0:1, :] + norm_ref[1:2, :]).astype(jnp.bfloat16)
    ln_a_ref[...] = ln_a
    ln_m_ref[...] = (normed * norm_ref[2:3, :] + norm_ref[3:4, :]).astype(jnp.bfloat16)
    lane = lax.broadcasted_iota(jnp.int32, aux_ref.shape, 1)
    aux_ref[...] = jnp.where(lane == 0, start_ref[:, 0:1], jnp.where(lane == 1, mean, scale))
    table = table_ref[...]
    for part in range(w_ref.shape[1] // HD):
        raw = wide_dot(ln_a, w_ref[:, part * HD : (part + 1) * HD], NN)
        if part % 3 < 2:
            raw = jnp.concatenate([turn(raw[:, :128], table, 1.0), raw[:, 128:]], axis=1)
        qkv_ref[:, part * HD : (part + 1) * HD] = raw.astype(jnp.bfloat16)


def project(tokens_all, norm_rows, table, start_col, full_qkv):
    seq, width = tokens_all.shape
    cols = full_qkv.shape[1]
    tile = 256
    row = lambda n: pl.BlockSpec((tile, n), lambda i: (i, 0))
    whole = lambda a, b: pl.BlockSpec((a, b), lambda i: (0, 0))
    return pl.pallas_call(
        project_kernel,
        grid=(seq // tile,),
        out_shape=[
            jax.ShapeDtypeStruct((seq, width), jnp.bfloat16),
            jax.ShapeDtypeStruct((seq, width), jnp.bfloat16),
            jax.ShapeDtypeStruct((seq, cols), jnp.bfloat16),
            jax.ShapeDtypeStruct((seq, 128), jnp.float32),
        ],
        in_specs=[row(width), whole(4, width), row(128), row(1), whole(width, cols)],
        out_specs=[row(width), row(width), row(cols), row(128)],
        compiler_params=pltpu.CompilerParams(vmem_limit_bytes=63 * 2**20),
        cost_estimate=pl.CostEstimate(flops=2 * seq * width * cols, bytes_accessed=20 * 2**20, transcendentals=0),
        name="project",
    )(tokens_all, norm_rows, table, start_col, full_qkv)


def soft_block(query, keys, start_col, first, offset):
    scores = wide_dot(query, keys, NT) * (HD ** (-0.5))
    rows, cols = scores.shape
    key_pos = first + lax.broadcasted_iota(jnp.int32, (rows, cols), 1)
    query_pos = offset + lax.broadcasted_iota(jnp.int32, (rows, cols), 0)
    seen = (key_pos.astype(jnp.float32) >= start_col) & (key_pos <= query_pos)
    scores = jnp.where(seen, scores, MASKED)
    peak = jnp.max(scores, axis=-1, keepdims=True)
    expo = jnp.exp(scores - peak)
    return expo / jnp.sum(expo, axis=-1, keepdims=True)


def reach_of(block, tile):
    return max(0, (block * tile - (DOC_MOST - 1)) // tile)


def attend_kernel(qkv_ref, start_ref, o_ref):
    tile = 256
    for head in range(o_ref.shape[1] // HD):
        col = head * 3 * HD
        for block in range(o_ref.shape[0] // tile):
            low, high = reach_of(block, tile) * tile, (block + 1) * tile
            here = slice(block * tile, high)
            prob = soft_block(
                qkv_ref[here, col : col + HD],
                qkv_ref[low:high, col + HD : col + 2 * HD],
                start_ref[here, 0:1],
                low,
                block * tile,
            ).astype(jnp.bfloat16)
            mixed = wide_dot(prob, qkv_ref[low:high, col + 2 * HD : col + 3 * HD], NN)
            o_ref[here, head * HD : (head + 1) * HD] = mixed.astype(jnp.bfloat16)


def attend(qkv, start_col):
    seq = qkv.shape[0]
    cols = qkv.shape[1] // 3
    whole = pl.BlockSpec(memory_space=pltpu.VMEM)
    return pl.pallas_call(
        attend_kernel,
        out_shape=jax.ShapeDtypeStruct((seq, cols), jnp.bfloat16),
        in_specs=[whole, whole],
        out_specs=whole,
        compiler_params=pltpu.CompilerParams(vmem_limit_bytes=63 * 2**20),
        cost_estimate=pl.CostEstimate(flops=6 * 10**9, bytes_accessed=4 * 2**20, transcendentals=2**20),
        name="attend",
    )(qkv, start_col)


def up_kernel(ln_ref, w_ref, act_ref, slope_ref):
    tile = 256
    for block in range(ln_ref.shape[0] // tile):
        here = slice(block * tile, (block + 1) * tile)
        up = wide_dot(ln_ref[here, :], w_ref[...], NN)
        below = 0.5 + 0.5 * lax.erf(up * (0.5**0.5))
        act_ref[here, :] = (up * below).astype(jnp.bfloat16)
        slope_ref[here, :] = (below + up * jnp.exp(-0.5 * up * up) * ((2.0 * math.pi) ** -0.5)).astype(jnp.bfloat16)


def up_branch(ln_mlp, full_up):
    seq, width = ln_mlp.shape
    units = full_up.shape[1]
    tile = min(512, units)
    out = jax.ShapeDtypeStruct((seq, units), jnp.bfloat16)
    return pl.pallas_call(
        up_kernel,
        grid=(units // tile,),
        out_shape=[out, out],
        in_specs=[pl.BlockSpec((seq, width), lambda i: (0, 0)), pl.BlockSpec((width, tile), lambda i: (0, i))],
        out_specs=[pl.BlockSpec((seq, tile), lambda i: (0, i))] * 2,
        compiler_params=pltpu.CompilerParams(vmem_limit_bytes=63 * 2**20),
        cost_estimate=pl.CostEstimate(flops=2 * seq * width * units, bytes_accessed=20 * 2**20, transcendentals=2 * seq * units),
        name="up_branch",
    )(ln_mlp, full_up)


def down_kernel(o_ref, act_ref, w_out_ref, w_down_ref, out_ref):
    tile = 256
    for block in range(o_ref.shape[0] // tile):
        here = slice(block * tile, (block + 1) * tile)
        total = wide_dot(o_ref[here, :], w_out_ref[...], NT) + wide_dot(act_ref[here, :], w_down_ref[...], NT)
        out_ref[here, :] = total.astype(jnp.bfloat16)


def down_branch(o, act, full_out, full_down):
    seq, units = act.shape
    width = full_down.shape[0]
    tile = 512
    return pl.pallas_call(
        down_kernel,
        grid=(width // tile,),
        out_shape=jax.ShapeDtypeStruct((seq, width), jnp.bfloat16),
        in_specs=[
            pl.BlockSpec(o.shape, lambda i: (0, 0)),
            pl.BlockSpec(act.shape, lambda i: (0, 0)),
            pl.BlockSpec((tile, o.shape[1]), lambda i: (i, 0)),
            pl.BlockSpec((tile, units), lambda i: (i, 0)),
        ],
        out_specs=pl.BlockSpec((seq, tile), lambda i: (0, i)),
        compiler_params=pltpu.CompilerParams(vmem_limit_bytes=63 * 2**20),
        cost_estimate=pl.CostEstimate(flops=2 * seq * width * (units + o.shape[1]), bytes_accessed=20 * 2**20, transcendentals=0),
        name="down_branch",
    )(o, act, full_out, full_down)


TN = (((0,), (0,)), ((), ()))


def attend_back_block(qkv_ref, start_ref, table_ref, d_o_ref, d_qkv_ref, d_key, d_value, head, block, last):
    tile = 256
    col = head * 3 * HD
    low, high = reach_of(block, tile) * tile, (block + 1) * tile
    here = slice(block * tile, high)
    query, keys = qkv_ref[here, col : col + HD], qkv_ref[low:high, col + HD : col + 2 * HD]
    values = qkv_ref[low:high, col + 2 * HD : col + 3 * HD]
    d_o = d_o_ref[here, head * HD : (head + 1) * HD]
    prob = soft_block(query, keys, start_ref[here, 0:1], low, block * tile)
    value_part = wide_dot(prob.astype(jnp.bfloat16), d_o, TN)
    d_prob = wide_dot(d_o, values, NT)
    weighted = prob * d_prob
    d_score = (weighted - prob * jnp.sum(weighted, axis=-1, keepdims=True)).astype(jnp.bfloat16)
    d_query = wide_dot(d_score, keys, NN) * (HD ** (-0.5))
    key_part = wide_dot(d_score, query, TN) * (HD ** (-0.5))
    d_query = jnp.concatenate([turn(d_query[:, :128], table_ref[here, :], -1.0), d_query[:, 128:]], axis=1)
    d_qkv_ref[here, col : col + HD] = d_query.astype(jnp.bfloat16)
    old = high - tile
    if low < old:
        d_key[low:old, :] += key_part[: old - low]
        d_value[low:old, :] += value_part[: old - low]
    d_key[old:high, :] = key_part[old - low :]
    d_value[old:high, :] = value_part[old - low :]
    ready_from = low
    ready_to = high if last else reach_of(block + 1, tile) * tile
    if ready_to > ready_from:
        done = slice(ready_from, ready_to)
        total = d_key[done, :]
        total = jnp.concatenate([turn(total[:, :128], table_ref[done, :], -1.0), total[:, 128:]], axis=1)
        d_qkv_ref[done, col + HD : col + 2 * HD] = total.astype(jnp.bfloat16)
        d_qkv_ref[done, col + 2 * HD : col + 3 * HD] = d_value[done, :].astype(jnp.bfloat16)


def attend_back_kernel(qkv_ref, start_ref, table_ref, d_o_ref, d_qkv_ref, d_key, d_value):
    blocks = qkv_ref.shape[0] // 256
    for head in range(d_o_ref.shape[1] // HD):
        for block in range(blocks):
            attend_back_block(qkv_ref, start_ref, table_ref, d_o_ref, d_qkv_ref, d_key, d_value, head, block, block == blocks - 1)


def attend_back(qkv, start_col, table, d_o):
    whole = pl.BlockSpec(memory_space=pltpu.VMEM)
    return pl.pallas_call(
        attend_back_kernel,
        out_shape=jax.ShapeDtypeStruct(qkv.shape, jnp.bfloat16),
        in_specs=[whole] * 4,
        out_specs=whole,
        scratch_shapes=[pltpu.VMEM((qkv.shape[0], HD), jnp.float32)] * 2,
        compiler_params=pltpu.CompilerParams(vmem_limit_bytes=63 * 2**20),
        cost_estimate=pl.CostEstimate(flops=12 * 10**9, bytes_accessed=10 * 2**20, transcendentals=2**20),
        name="attend_back",
    )(qkv, start_col, table, d_o)


def hand_out(block, row_share):
    parts = block.reshape(lax.axis_size("dp"), row_share, block.shape[1])
    return lax.all_to_all(parts, "dp", split_axis=0, concat_axis=0, tiled=True)


def from_owners(parts, owners, matrix, col_count, heads):
    own = [parts[owners.index((matrix, head)), :, :col_count] for head in range(heads)]
    return jnp.concatenate(own, axis=1).astype(jnp.float32)


def on_device(
    tokens,
    cotangent,
    segments,
    w_qkv,
    w_out,
    w_up,
    w_down,
    m_qkv,
    m_out,
    m_up,
    m_down,
    norm_gains,
    norm_biases,
    norm_moments,
):
    tensor_size = lax.axis_size("tensor")
    seq_len = tokens.shape[0] * tensor_size
    seg_ids = segments[0]
    local_heads = w_out.shape[1] // HD
    block_units = FF // HEADS
    row_share = w_qkv.shape[0]
    paired = lax.axis_size("dp") == 8 and local_heads == 2
    weights_in = (w_qkv, w_out, w_up, w_down)
    moments_in = (m_qkv, m_out, m_up, m_down)
    col_counts = (3 * HD, HD, block_units, block_units)
    pad_width = max(col_counts)
    norm_rows = jnp.stack([norm_gains[0], norm_biases[0], norm_gains[1], norm_biases[1]])
    if paired:
        (full_qkv, full_out, full_up, full_down), rest = forward_all(
            weights_in, moments_in, tokens, cotangent, norm_gains, norm_biases, segments
        )
        mom_half, tokens_all, grad_all, ln_attn, ln_mlp, packed, aux, table = rest[:8]
        mixed_heads, activated, slope, branch = rest[8:]
    else:
        tokens_all, grad_all = (
            lax.all_gather(tokens, "tensor", axis=0, tiled=True),
            lax.all_gather(cotangent, "tensor", axis=0, tiled=True),
        )
        full_qkv, full_out, full_up, full_down = (
            lax.all_gather(w.astype(jnp.bfloat16), "dp", axis=0, tiled=True) for w in weights_in
        )
        starts = doc_starts(seg_ids)
        positions = jnp.arange(seq_len, dtype=jnp.int32) - starts
        start_col = starts[:, None].astype(jnp.float32)
        table = rotary_table(positions)
        ln_attn, ln_mlp, packed, aux = project(tokens_all, norm_rows, table, start_col, full_qkv)
        mixed_heads = attend(packed, aux)
        activated, slope = up_branch(ln_mlp, full_up)
        branch = down_branch(mixed_heads, activated, full_out, full_down)
    branch_sum = lax.psum_scatter(branch, "tensor", scatter_dimension=0, tiled=True)
    if paired:
        block, grad_half, mixed_grad, grad_norms = backward_all(
            grad_all, ln_mlp, ln_attn, activated, mixed_heads, slope, packed, aux, table, tokens_all, norm_gains,
            (full_qkv, full_out, full_up, full_down), mom_half,
        )
        owners = owner_tables()
    else:
        grad_mixed = jnp.dot(grad_all, full_out, preferred_element_type=jnp.float32).astype(jnp.bfloat16)
        grad_packed = attend_back(packed, aux, table, grad_mixed)
        grad_act = jnp.dot(grad_all, full_down, preferred_element_type=jnp.float32)
        grad_upproj = (grad_act * slope.astype(jnp.float32)).astype(jnp.bfloat16)
        grad_ln_mlp = contract_cols(grad_upproj, full_up)
        grad_ln_attn = contract_cols(grad_packed, full_qkv)
        mixed_grad = (norm_gains[0] * grad_ln_attn + norm_gains[1] * grad_ln_mlp).astype(jnp.bfloat16)
        normed_all = (tokens_all.astype(jnp.float32) - aux[:, 1:2]) * aux[:, 2:3]
        sums = [grad_ln_attn * normed_all, grad_ln_attn, grad_ln_mlp * normed_all, grad_ln_mlp]
        grad_norms = lax.psum(jnp.stack([jnp.sum(v, axis=0) for v in sums]), ("dp", "tensor"))
        lefts = (ln_attn, grad_all, ln_mlp, grad_all)
        rights = (grad_packed, mixed_heads, grad_upproj, activated)
        reduced = tuple(
            lax.psum_scatter(
                contract_rows(l, r).astype(jnp.bfloat16), "dp", scatter_dimension=0, tiled=True
            ).astype(jnp.float32)
            for l, r in zip(lefts, rights)
        )
        new_moments = tuple(MOMENTUM * m + g for m, g in zip(moments_in, reduced))
        parts = []
        for fresh, grad_rows, col_count in zip(new_moments, reduced, col_counts):
            nested = (grad_rows + MOMENTUM * fresh).astype(jnp.bfloat16)
            for head in range(local_heads):
                part = nested[:, head * col_count : (head + 1) * col_count]
                parts.append(jnp.pad(part, ((0, 0), (0, pad_width - col_count))))
        groups = lax.axis_size("dp") // len(parts)
        outgoing = jnp.tile(jnp.stack(parts), (groups, 1, 1))
        block = lax.all_to_all(outgoing, "dp", split_axis=0, concat_axis=0, tiled=True)
        block = block.reshape(row_share * lax.axis_size("dp"), pad_width)
        owners = tuple((m, h) for m in range(4) for h in range(local_heads)) * groups
    mixed_own = lax.psum_scatter(mixed_grad, "tensor", scatter_dimension=0, tiled=True)
    block, branch_sum = lax.optimization_barrier((block, branch_sum))
    if paired:
        grad_rows, ortho_rows = sweep_return(block, grad_half, tuple(col_counts[m] for m, _ in owners))
        mixed_own, ortho_rows = lax.optimization_barrier((mixed_own, ortho_rows))
        rows_in = (tokens, cotangent, mixed_own, branch_sum)
        new_moments, new_weights, grad_tokens, block_out = update_all(
            weights_in, moments_in, grad_rows, ortho_rows, rows_in, owners, col_counts
        )
    else:
        ortho_rows = hand_out(sweeps(block), row_share)
        new_weights = [
            w * (1.0 - LEARN * DECAY) - LEARN * from_owners(ortho_rows, owners, i, col_counts[i], local_heads)
            for i, w in enumerate(weights_in)
        ]
        grad_tokens = norm_back(tokens, cotangent, mixed_own)
        block_out = (tokens.astype(jnp.float32) + branch_sum.astype(jnp.float32)).astype(jnp.bfloat16)
    moment_norms = MOMENTUM * norm_moments + grad_norms
    step_scale = lax.rsqrt(jnp.mean(moment_norms * moment_norms, axis=-1, keepdims=True) + 1e-06)
    value_norms = norm_rows - NORM_LEARN * moment_norms * step_scale
    return (
        block_out,
        grad_tokens,
        new_moments[0],
        new_weights[0],
        new_moments[1],
        new_weights[1],
        new_moments[2],
        new_weights[2],
        new_moments[3],
        new_weights[3],
        moment_norms,
        value_norms,
    )


def solution(mesh):
    in_specs = (
        P(("dp", "tensor"), None),
        P(("dp", "tensor"), None),
        P("dp", None),
        P("dp", "tensor"),
        P("dp", "tensor"),
        P("dp", "tensor"),
        P("dp", "tensor"),
        P("dp", "tensor"),
        P("dp", "tensor"),
        P("dp", "tensor"),
        P("dp", "tensor"),
        P(),
        P(),
        P(),
    )
    out_specs = (
        P(("dp", "tensor"), None),
        P(("dp", "tensor"), None),
        P("dp", "tensor"),
        P("dp", "tensor"),
        P("dp", "tensor"),
        P("dp", "tensor"),
        P("dp", "tensor"),
        P("dp", "tensor"),
        P("dp", "tensor"),
        P("dp", "tensor"),
        P(),
        P(),
    )
    return jax.shard_map(
        on_device, mesh=mesh, in_specs=in_specs, out_specs=out_specs, check_vma=False
    )
```
